32 devices in a mesh: dp: 2 (over x), expert: 16 (over z, y, core).
Axes of the slice: x: 2, y: 2, z: 4, core: 2. Of those that a mesh axis runs over, the one named last changes fastest.
Arguments:
- tokens: bfloat16 [2, 3072, 2048], P(None, ('dp', 'expert')), may hold values from -6 to 6
- segment: int32 [2, 3072], P(None, 'dp'), may hold values from 0 to 2, as said below
- routes: int32 [2, 3072, 6], P(None, ('dp', 'expert')), may hold values from 0 to 15, all different within a row; in each aligned block of 96 rows (0 to 95, 96 to 191, ..., all dimensions but the last counted through in order) at most 96 rows name the same one
- drop_order: int32 [2, 32, 96], P(None, ('dp', 'expert')), may hold values from 0 to 95, each once within a row
- cotangent: bfloat16 [2, 3072, 2048], P(None, ('dp', 'expert')), may hold values from -6 to 6
- attn_gain: bfloat16 [2048], P(('dp', 'expert')), may hold values from 0.5 to 1.5
- query_weight: bfloat16 [2048, 3072], P('dp', 'expert'), may hold values from -0.125 to 0.125
- down_latent: bfloat16 [2048, 576], P(('dp', 'expert')), may hold values from -0.125 to 0.125
- latent_gain: bfloat16 [512], P(('dp', 'expert')), may hold values from 0.5 to 1.5
- up_latent: bfloat16 [512, 4096], P('dp', 'expert'), may hold values from -0.25 to 0.25
- output_weight: bfloat16 [2048, 2048], P('expert', 'dp'), may hold values from -0.5 to 0.5
- ffn_gain: bfloat16 [2048], P(('dp', 'expert')), may hold values from 0.5 to 1.5
- router_weight: bfloat16 [2048, 16], P(('dp', 'expert')), may hold values from -0.0625 to 0.0625
- shared_gate: bfloat16 [2048, 2816], P('dp', 'expert'), may hold values from -0.125 to 0.125
- shared_up: bfloat16 [2048, 2816], P('dp', 'expert'), may hold values from -0.125 to 0.125
- shared_down: bfloat16 [2816, 2048], P('expert', 'dp'), may hold values from -0.109375 to 0.109375
- expert_gate: bfloat16 [16, 2048, 1408], P('expert', 'dp'), may hold values from -0.125 to 0.125
- expert_up: bfloat16 [16, 2048, 1408], P('expert', 'dp'), may hold values from -0.125 to 0.125
- expert_down: bfloat16 [16, 1408, 2048], P('expert', None, 'dp'), may hold values from -0.625 to 0.625
Outputs:
- mixed: float32 [2, 3072, 2048], P(None, ('dp', 'expert'))
- tokens_grad: float32 [2, 3072, 2048], P(None, ('dp', 'expert'))
- attn_gain_grad: float32 [2048], P(('dp', 'expert'))
- query_weight_grad: float32 [2048, 3072], P('dp', 'expert')
- down_latent_grad: float32 [2048, 576], P(('dp', 'expert'))
- latent_gain_grad: float32 [512], P(('dp', 'expert'))
- up_latent_grad: float32 [512, 4096], P('dp', 'expert')
- output_weight_grad: float32 [2048, 2048], P('expert', 'dp')
- ffn_gain_grad: float32 [2048], P(('dp', 'expert'))
- router_weight_grad: float32 [2048, 16], P(('dp', 'expert'))
- shared_gate_grad: float32 [2048, 2816], P('dp', 'expert')
- shared_up_grad: float32 [2048, 2816], P('dp', 'expert')
- shared_down_grad: float32 [2816, 2048], P('expert', 'dp')
- expert_gate_grad: float32 [16, 2048, 1408], P('expert', 'dp')
- expert_up_grad: float32 [16, 2048, 1408], P('expert', 'dp')
- expert_down_grad: float32 [16, 1408, 2048], P('expert', None, 'dp')
The draws below stay inside these ranges and needn't reach their ends.
Inputs may be any that keep to these rules, and one draw needn't show every extreme that they name: `segment`: in each group of 96 rows of a micro-batch the numbers never fall: a prompt of at least 32 tokens, then 2 continuations of 16 to 32 tokens, the first of exactly 32. `routes`: each row names 6 different experts; within one group of a micro-batch some expert may be named by every row. `drop_order`: each group's entries are a permutation of its 96 rows.
All inputs are finite; a program needn't handle non-finite values.
Results may differ from the reference program's by a relative error of at most 0.02.
Values may be sent and summed in bfloat16 or wider, within the bound.
A program may use at most 384 MiB of HBM per device.

```python
import math
import jax
import jax.numpy as jnp
import numpy as np
from jax import lax

D = 2048
H = 16
DN = 128
DR = 64
DV = 128
R = 512
FF = 1408
NSH = 2
TOP = 6
EXPERTS = 16
CLEN = 32
CONT = 2
MB_TOK = 96
MICRO = 2
CAP = 45
TOKENS_MB = 3072
N_DP = 2
N_EXPERT = 16


def draw_segment(key, part):
    key = jax.random.fold_in(key, 7)
    blocks = MICRO * TOKENS_MB // MB_TOK
    lengths = jax.random.randint(key, (blocks, CONT), CLEN // 2, CLEN + 1)
    lengths = lengths.at[:, 0].set(CLEN)
    prompt = MB_TOK - jnp.sum(lengths, axis=1)
    starts = prompt[:, None] + jnp.cumsum(lengths, axis=1) - lengths
    places = jnp.arange(MB_TOK, dtype=jnp.int32)
    segment = jnp.sum((places[None, :, None] >= starts[:, None, :]).astype(jnp.int32), axis=2)
    return segment.reshape(MICRO, TOKENS_MB).astype(jnp.int32)


def level_of(key, shape, pieces, smallest, largest):
    level, own = 1.0, jax.random.fold_in(key, 6)
    for dim, parts in pieces:
        draws = jnp.exp(jax.random.uniform(jax.random.fold_in(own, dim), (parts,), jnp.float32, smallest / len(pieces), largest / len(pieces)))
        level = level * jnp.repeat(draws, shape[dim] // parts).reshape([-1 if axis == dim else 1 for axis in range(len(shape))])
    return level


def routed_block(own_key, own, number, rows, number_of, top, limit, lean):
    order = jax.random.permutation(own_key, number_of)
    crowded, usual = shares(number_of, rows * top, limit, lean, True), shares(number_of, rows * top, limit, lean, False)
    places = jnp.arange(number_of)

    def named(sizes, rotation):
        used = int((sizes > 0).sum())
        fixed = max(1, used // 4)
        moved = fixed + (places - fixed + rotation * (used - fixed)) % max(1, number_of - fixed)
        return jnp.zeros((number_of,), jnp.int32).at[order[jnp.where(places < fixed, places, moved)]].set(jnp.asarray(sizes, jnp.int32))

    sizes = jnp.where(number % 4 == 0, named(crowded, number // 4), named(usual, number - number // 4 - 1))
    mixed = jax.random.permutation(jax.random.fold_in(own, 3), number_of)
    source_of, taker = mixed[0:number_of // 2 * 2:2], mixed[1:number_of // 2 * 2:2]
    slack = jnp.minimum(sizes[source_of] - 1, limit - sizes[taker]) // 2
    slack = jnp.where((source_of == order[0]) | (taker == order[0]) | (sizes[taker] == 0), 0, jnp.maximum(slack, 0))
    moved = jax.random.randint(jax.random.fold_in(own, 4), (number_of // 2,), 0, 1 << 20) % (slack + 1)
    sizes = sizes.at[source_of].add(-moved).at[taker].add(moved)
    items = jnp.searchsorted(jnp.cumsum(sizes), jnp.arange(rows * top), side="right").astype(jnp.int32)
    grid = items.reshape(top, rows).T
    grid = grid[jax.random.permutation(jax.random.fold_in(own, 1), rows)]
    rotation = jax.random.randint(jax.random.fold_in(own, 2), (rows, 1), 0, top)
    return jnp.take_along_axis(grid, (jnp.arange(top)[None, :] + rotation) % top, axis=1)


def shares(number_of, total, most, slope, full):
    loads = [(1 << 20) // math.isqrt(standing ** slope) + 1 for standing in range(1, number_of + 1)]
    largest = most if full else min(most, max(-(-total // number_of), total * loads[0] // sum(loads)))
    least = 1 if total - largest >= number_of - 1 else 0
    holding, spare = [largest] + [least] * (number_of - 1), total - largest - least * (number_of - 1)
    while spare > 0:
        candidates = [i for i in range(1, number_of) if holding[i] < largest] or [i for i in range(1, number_of) if holding[i] < most]
        whole, budget = sum([loads[i] for i in candidates]), spare
        for i in candidates:
            addition = min(most - holding[i], max(1, budget * loads[i] // whole), spare)
            holding[i] = holding[i] + addition
            spare = spare - addition
    return np.array(holding)


def bell_draw(own_key, shape, spread, most, split=(), kind=jnp.bfloat16):
    values = jax.random.normal(own_key, shape, jnp.float32) * spread
    if len(split) > 0:
        values = level_of(own_key, shape, split, -0.22, 0.18) * values
    return jnp.clip(values, min=-most, max=most).astype(kind)


def setup_inputs(seed: int = 0) -> dict:
    keys = jax.random.split(jax.random.key(seed), 20)
    tokens = bell_draw(keys[0], (MICRO, TOKENS_MB, D), 1.0, 6.0, ((1, 32),))
    segment = draw_segment(jax.random.fold_in(keys[19], 71), 0)
    routes_keys = jax.random.split(jax.random.fold_in(keys[2], 1), MICRO * TOKENS_MB // MB_TOK)
    routes_turns = jax.random.permutation(jax.random.fold_in(keys[2], 3), MICRO * TOKENS_MB // MB_TOK)
    routes = jax.vmap(lambda own, number: routed_block(jax.random.fold_in(keys[2], 2), own, number, MB_TOK, EXPERTS, TOP, MB_TOK, 2))(routes_keys, routes_turns).reshape((MICRO, TOKENS_MB, TOP))
    drop_order = jax.vmap(lambda own: jax.random.permutation(own, MB_TOK))(jax.random.split(keys[3], MICRO * (N_DP * N_EXPERT))).reshape((MICRO, N_DP * N_EXPERT, MB_TOK)).astype(jnp.int32)
    cotangent = bell_draw(keys[4], (MICRO, TOKENS_MB, D), 1.0, 6.0, ((1, 32),))
    attn_gain = jnp.clip(1.0 + 0.1 * jax.random.normal(keys[5], (D,), jnp.float32), 0.5, 1.5).astype(jnp.bfloat16)
    query_weight = bell_draw(keys[6], (D, H * (DN + DR)), D ** -0.5, 0.125, ((0, 2), (1, 16)))
    down_latent = bell_draw(keys[7], (D, R + DR), D ** -0.5, 0.125, ((0, 32),))
    latent_gain = jnp.clip(1.0 + 0.1 * jax.random.normal(keys[8], (R,), jnp.float32), 0.5, 1.5).astype(jnp.bfloat16)
    up_latent = bell_draw(keys[9], (R, H * (DN + DV)), R ** -0.5, 0.25, ((0, 2), (1, 16)))
    output_weight = bell_draw(keys[10], (H * DV, D), (H * DV // 16) ** -0.5, 0.5, ((0, 16), (1, 2)))
    ffn_gain = jnp.clip(1.0 + 0.1 * jax.random.normal(keys[11], (D,), jnp.float32), 0.5, 1.5).astype(jnp.bfloat16)
    router_weight = bell_draw(keys[12], (D, EXPERTS), (4 * D) ** -0.5, 0.0625, ((0, 32),))
    shared_gate = bell_draw(keys[13], (D, NSH * FF), D ** -0.5, 0.125, ((0, 2), (1, 16)))
    shared_up = bell_draw(keys[14], (D, NSH * FF), D ** -0.5, 0.125, ((0, 2), (1, 16)))
    shared_down = bell_draw(keys[15], (NSH * FF, D), (NSH * FF) ** -0.5, 0.109375, ((0, 16), (1, 2)))
    expert_gate = bell_draw(keys[16], (EXPERTS, D, FF), D ** -0.5, 0.125, ((0, 16), (1, 2)))
    expert_up = bell_draw(keys[17], (EXPERTS, D, FF), D ** -0.5, 0.125, ((0, 16), (1, 2)))
    expert_down = bell_draw(keys[18], (EXPERTS, FF, D), (FF // 16) ** -0.5, 0.625, ((0, 16), (2, 2)))
    return {"tokens": tokens, "segment": segment, "routes": routes, "drop_order": drop_order, "cotangent": cotangent, "attn_gain": attn_gain, "query_weight": query_weight, "down_latent": down_latent, "latent_gain": latent_gain, "up_latent": up_latent, "output_weight": output_weight, "ffn_gain": ffn_gain, "router_weight": router_weight, "shared_gate": shared_gate, "shared_up": shared_up, "shared_down": shared_down, "expert_gate": expert_gate, "expert_up": expert_up, "expert_down": expert_down}


EPS = 1e-06
HIGH = lax.Precision.HIGHEST

@jax.custom_vjp
def low(v):
    return lax.optimization_barrier(v.astype(jnp.bfloat16)).astype(jnp.float32)

@jax.custom_vjp
def low_back(v):
    return v

def low_keep(v):
    return (low(v), None)

def low_pass(kept, grad):
    return (grad,)

def back_keep(v):
    return (v, None)

def back_low(kept, grad):
    return (low(grad),)
low.defvjp(low_keep, low_pass)
low_back.defvjp(back_keep, back_low)

def product_high(former, latter):
    return jnp.dot(former, latter, precision=HIGH)

def rms_scale(values):
    return lax.rsqrt(lax.optimization_barrier(jnp.mean(values * values, axis=-1, keepdims=True)) + EPS)

def softmax_rows(values):
    row_top = lax.optimization_barrier(jnp.max(values, axis=-1, keepdims=True))
    powers = jnp.exp(values - row_top)
    return powers / lax.optimization_barrier(jnp.sum(powers, axis=-1, keepdims=True))

def rotate(values, cosine, sine_part):
    half = values.shape[-1] // 2
    turned = jnp.concatenate([-values[..., half:], values[..., :half]], axis=-1)
    return values * cosine + turned * sine_part

def layout(segment_row):
    places = jnp.arange(segment_row.shape[0], dtype=jnp.int32)
    prompt_len = jnp.sum((segment_row == 0).astype(jnp.int32))
    seg_start = lax.optimization_barrier(jnp.sum((segment_row[None, :] < segment_row[:, None]).astype(jnp.int32), axis=1))
    position = jnp.where(segment_row == 0, places, prompt_len + places - seg_start)
    allowed = (places[None, :] <= places[:, None]) & ((segment_row[None, :] == 0) | (segment_row[None, :] == segment_row[:, None]))
    return (position, allowed)

def angles(position):
    freq_index = jnp.arange(DR // 2, dtype=jnp.float32)
    frequency = jnp.exp(freq_index * (-2.0 * math.log(10000.0) / DR))
    turning = position.astype(jnp.float32)[:, None] * frequency[None, :]
    turning = jnp.concatenate([turning, turning], axis=1)
    return (jnp.cos(turning), jnp.sin(turning))

def attend_group(queries, key_nope, key_rope, values, segment_row):
    position, allowed = layout(segment_row)
    cosine, sine_part = angles(position)
    row_count = queries.shape[0]
    query_low = low(jnp.concatenate([queries[..., :DN], rotate(queries[..., DN:], cosine[:, None, :], sine_part[:, None, :])], axis=-1))
    key_turned = rotate(key_rope, cosine, sine_part)
    key_low = low(jnp.concatenate([key_nope, jnp.broadcast_to(key_turned[:, None, :], (row_count, H, DR))], axis=-1))
    scores = low_back(jnp.einsum('qhc,khc->hqk', query_low, key_low, precision=HIGH) * (DN + DR) ** (-0.5))
    scores = jnp.where(allowed[None], scores, -1e+30)
    probs = softmax_rows(scores)
    attended = jnp.einsum('hqk,khc->qhc', low(probs), low(values), precision=HIGH)
    return attended.reshape(row_count, H * DV)

def forward(inputs, segment_rows, route_rows, order_rows, attn_gain, query_weight, down_latent, latent_gain, up_latent, output_weight, ffn_gain, router_weight, shared_gate, shared_up, shared_down, expert_gate, expert_up, expert_down):
    blocks = TOKENS_MB // MB_TOK
    normed = low(inputs * rms_scale(inputs) * attn_gain)
    queries = low_back(product_high(normed, query_weight)).reshape(blocks, MB_TOK, H, DN + DR)
    latent_all = low_back(product_high(normed, down_latent))
    latent = latent_all[:, :R]
    latent_low = low(latent * rms_scale(latent) * latent_gain)
    keys_values = low_back(product_high(latent_low, up_latent)).reshape(blocks, MB_TOK, H, DN + DV)
    attended = jax.vmap(attend_group)(queries, keys_values[..., :DN], latent_all[:, R:].reshape(blocks, MB_TOK, DR), keys_values[..., DN:], segment_rows.reshape(blocks, MB_TOK))
    attended_low = low(low_back(attended.reshape(TOKENS_MB, H * DV)))
    residual = inputs + low_back(product_high(attended_low, output_weight))
    ffn_in = low(residual * rms_scale(residual) * ffn_gain)
    router_probs = softmax_rows(product_high(ffn_in, router_weight))
    chosen = lax.optimization_barrier(jnp.sum(jax.nn.one_hot(route_rows, EXPERTS, dtype=jnp.int32), axis=1)).reshape(blocks, MB_TOK, EXPERTS)
    order_blocks = order_rows.reshape(blocks, MB_TOK)
    earlier = (order_blocks[:, None, :] < order_blocks[:, :, None]).astype(jnp.int32)
    slot_rank = jnp.einsum('btu,bue->bte', earlier, chosen)
    slot_ids = jnp.arange(CAP, dtype=jnp.int32)
    route_map = ((slot_rank[..., None] == slot_ids) & (chosen[..., None] == 1)).astype(jnp.float32).transpose(0, 2, 3, 1)
    gate_values = router_probs.reshape(blocks, MB_TOK, EXPERTS) * chosen.astype(jnp.float32)
    ffn_blocks = ffn_in.reshape(blocks, MB_TOK, D)
    expert_rows = low_back(jnp.einsum('best,btd->besd', route_map, ffn_blocks, precision=HIGH))
    expert_rows = expert_rows.transpose(1, 0, 2, 3).reshape(EXPERTS, blocks * CAP, D)
    gate_part = low_back(jnp.einsum('end,edf->enf', expert_rows, expert_gate, precision=HIGH))
    up_part = low_back(jnp.einsum('end,edf->enf', expert_rows, expert_up, precision=HIGH))
    inner_low = low(jax.nn.silu(gate_part) * up_part)
    returned = low(low_back(jnp.einsum('enf,efd->end', inner_low, expert_down, precision=HIGH)))
    returned = returned.reshape(EXPERTS, blocks, CAP, D).transpose(1, 0, 2, 3)
    weight_map = route_map * gate_values.transpose(0, 2, 1)[:, :, None, :]
    mixture = jnp.einsum('best,besd->btd', weight_map, returned, precision=HIGH).reshape(TOKENS_MB, D)
    shared_g = low_back(product_high(ffn_in, shared_gate))
    shared_u = low_back(product_high(ffn_in, shared_up))
    shared_out = low_back(product_high(low(jax.nn.silu(shared_g) * shared_u), shared_down))
    return residual + shared_out + mixture

def reference(tokens, segment, routes, drop_order, cotangent, attn_gain, query_weight, down_latent, latent_gain, up_latent, output_weight, ffn_gain, router_weight, shared_gate, shared_up, shared_down, expert_gate, expert_up, expert_down):
    weights = tuple((matrix.astype(jnp.float32) for matrix in (attn_gain, query_weight, down_latent, latent_gain, up_latent, output_weight, ffn_gain, router_weight, shared_gate, shared_up, shared_down, expert_gate, expert_up, expert_down)))
    mixed_list = []
    grad_list = []
    totals = None
    for micro_step in range(MICRO):

        def micro_forward(inputs, *params):
            return forward(inputs, segment[micro_step], routes[micro_step], drop_order[micro_step], *params)
        mixed, pull_back = jax.vjp(micro_forward, tokens[micro_step].astype(jnp.float32), *weights)
        gradients = pull_back(cotangent[micro_step].astype(jnp.float32))
        mixed_list.append(mixed)
        grad_list.append(gradients[0])
        if totals is None:
            totals = gradients[1:]
        else:
            totals = tuple((running + addend for running, addend in zip(totals, gradients[1:])))
    grad_attn_gain, grad_query, grad_down_latent, grad_latent_gain, grad_up_latent, grad_output, grad_ffn_gain, grad_router, grad_shared_gate, grad_shared_up, grad_shared_down, grad_expert_gate, grad_expert_up, grad_expert_down = totals
    return (jnp.stack(mixed_list), jnp.stack(grad_list), grad_attn_gain, grad_query, grad_down_latent, grad_latent_gain, grad_up_latent, grad_output, grad_ffn_gain, grad_router, grad_shared_gate, grad_shared_up, grad_shared_down, grad_expert_gate, grad_expert_up, grad_expert_down)
```

```python
import math

import jax
import jax.numpy as jnp
from jax import lax
from jax.sharding import PartitionSpec as P

DN = 128
DR = 64
DV = 128
EPS = 1e-06
HIGH = lax.Precision.HIGHEST
F32 = jnp.float32
BF = jnp.bfloat16


def dot(former, latter):
    return jnp.dot(former, latter, preferred_element_type=F32)


def dot_left(former, latter):
    return lax.dot_general(former, latter, (((0,), (0,)), ((), ())), preferred_element_type=F32)


def dot_right(former, latter):
    return lax.dot_general(former, latter, (((1,), (1,)), ((), ())), preferred_element_type=F32)


def rms_scale(values):
    return lax.rsqrt(jnp.mean(values * values, axis=-1, keepdims=True) + EPS)


def norm_back(values, scale_rows, gain, out_grad):
    scaled = out_grad * gain
    inner = jnp.mean(scaled * values, axis=-1, keepdims=True)
    value_grad = scale_rows * scaled - values * scale_rows * scale_rows * scale_rows * inner
    return (value_grad, jnp.sum(out_grad * values * scale_rows, axis=0))


def rotate(values, cosine, sine_part):
    half = values.shape[-1] // 2
    turned = jnp.concatenate([-values[..., half:], values[..., :half]], axis=-1)
    return values * cosine + turned * sine_part


def unrotate(values, cosine, sine_part):
    half = values.shape[-1] // 2
    scaled = values * sine_part
    return values * cosine + jnp.concatenate([scaled[..., half:], -scaled[..., :half]], axis=-1)


def layouts(segment):
    places = jnp.arange(segment.shape[1], dtype=jnp.int32)
    prompt_len = jnp.sum((segment == 0).astype(jnp.int32), axis=1, keepdims=True)
    former = (segment[:, None, :] < segment[:, :, None]).astype(jnp.int32)
    seg_start = jnp.sum(former, axis=2)
    position = jnp.where(segment == 0, places[None], prompt_len + places[None] - seg_start)
    allowed = (places[None, None, :] <= places[None, :, None]) & (
        (segment[:, None, :] == 0) | (segment[:, None, :] == segment[:, :, None])
    )
    return (position, allowed)


def angles(position, row_count):
    freq_index = jnp.arange(DR // 2, dtype=F32)
    frequency = jnp.exp(freq_index * (-2.0 * math.log(10000.0) / DR))
    turning = jnp.arange(row_count, dtype=F32)[:, None] * frequency[None, :]
    table = jnp.concatenate([jnp.cos(turning), jnp.sin(turning)], axis=1)
    picks = (position.reshape(-1)[:, None] == jnp.arange(row_count)[None, :]).astype(F32)
    both = jnp.dot(picks, table, precision=HIGH)
    cosine, sine_part = both[:, : DR // 2], both[:, DR // 2 :]
    return (
        jnp.concatenate([cosine, cosine], axis=1),
        jnp.concatenate([sine_part, sine_part], axis=1),
    )


def on_device(
    tokens,
    segment,
    routes,
    drop_order,
    cotangent,
    attn_gain,
    query_weight,
    down_latent,
    latent_gain,
    up_latent,
    output_weight,
    ffn_gain,
    router_weight,
    shared_gate,
    shared_up,
    shared_down,
    expert_gate,
    expert_up,
    expert_down,
):
    n_e = lax.axis_size("expert")
    n_d = lax.axis_size("dp")
    me_e = lax.axis_index("expert")
    me_d = lax.axis_index("dp")
    micro, group_rows, width = tokens.shape
    own_rows = micro * group_rows
    span = n_e * own_rows
    groups = n_e * micro
    top = routes.shape[2]
    experts = n_e * expert_gate.shape[0]
    capacity = (5 * group_rows * top + 4 * experts - 1) // (4 * experts)
    slots = -(-capacity // 16) * 16
    rank_latent = latent_gain.shape[0] * n_e * n_d
    hidden = expert_gate.shape[2]

    def gather(values):
        return lax.all_gather(values, "expert", axis=0, tiled=True)

    def scatter(values):
        return lax.psum_scatter(values, "expert", scatter_dimension=0, tiled=True)

    def from_dp(values):
        blocks = [values]
        for step in range(1, n_d):
            pairs = [((i + step) % n_d, i) for i in range(n_d)]
            blocks.append(lax.ppermute(values, "dp", pairs))
        return blocks

    def whole(blocks, axis):
        size = blocks[0].shape[axis]
        shape = list(blocks[0].shape)
        shape[axis] = size * n_d
        total = jnp.zeros(shape, blocks[0].dtype)
        for step in range(n_d):
            at = lax.rem(me_d + step, n_d) * size
            total = lax.dynamic_update_slice_in_dim(total, blocks[step], at, axis)
        return total

    def sum_dp(values, axis):
        size = values.shape[axis] // n_d

        def part(step):
            at = lax.rem(me_d + step, n_d) * size
            return lax.dynamic_slice_in_dim(values, at, size, axis)

        total = part(0).astype(F32)
        for step in range(1, n_d):
            pairs = [(i, (i + step) % n_d) for i in range(n_d)]
            total = total + lax.ppermute(part(step).astype(BF), "dp", pairs).astype(F32)
        return total

    small_rows = attn_gain.shape[0]
    latent_all_width = down_latent.shape[1]
    latent_piece = latent_gain.shape[0]
    packed = jnp.concatenate(
        [
            down_latent,
            router_weight,
            attn_gain[:, None],
            ffn_gain[:, None],
            jnp.pad(latent_gain, (0, small_rows - latent_piece))[:, None],
        ],
        axis=1,
    )
    packed = lax.all_gather(packed, ("dp", "expert"), axis=0, tiled=True)
    down_all = packed[:, :latent_all_width]
    router_all = packed[:, latent_all_width : latent_all_width + experts]
    rest = packed[:, latent_all_width + experts :].astype(F32)
    attn_gain_all = rest[:, 0]
    ffn_gain_all = rest[:, 1]
    latent_gain_all = rest[:, 2].reshape(n_e * n_d, small_rows)[:, :latent_piece].reshape(-1)

    query_w = whole(from_dp(query_weight), 0)
    up_w = whole(from_dp(up_latent), 0)
    output_w = whole(from_dp(output_weight), 1)
    gate_w = whole(from_dp(expert_gate[0]), 0)
    up_e_w = whole(from_dp(expert_up[0]), 0)
    down_e_w = whole(from_dp(expert_down[0]), 1)
    shared_gate_w = whole(from_dp(shared_gate), 0)
    shared_up_w = whole(from_dp(shared_up), 0)
    shared_down_w = whole(from_dp(shared_down), 1)

    tokens_own = tokens.reshape(own_rows, width)
    tokens_all = gather(tokens_own)
    upstream_own = cotangent.reshape(own_rows, width)
    upstream_all = gather(upstream_own)

    chosen = jnp.sum(
        (routes[..., None] == jnp.arange(experts, dtype=jnp.int32)).astype(jnp.int32), axis=2
    )
    order = drop_order[:, 0]
    earlier = (order[:, None, :] < order[:, :, None]).astype(F32)
    rank = jnp.einsum("mtu,mue->mte", earlier, chosen.astype(F32)).astype(jnp.int32)
    code = jnp.where((chosen == 1) & (rank < capacity), rank, -1).reshape(own_rows, experts)
    code_all = gather(code)
    my_code = lax.dynamic_slice_in_dim(code_all, me_e, 1, 1).reshape(groups, group_rows)
    picks = my_code[:, None, :] == jnp.arange(slots, dtype=jnp.int32)[None, :, None]
    picks_low = picks.astype(BF)
    picks_f = picks.astype(F32)

    span_segment = (
        segment.reshape(micro, n_e, group_rows).transpose(1, 0, 2).reshape(groups, group_rows)
    )
    position, allowed = layouts(span_segment)
    cosine, sine_part = angles(position, group_rows)
    score_scale = (DN + DR) ** (-0.5)
    inputs_all = tokens_all.astype(F32)
    first_scale = rms_scale(inputs_all)
    normed = (inputs_all * first_scale * attn_gain_all).astype(BF)
    first_w = jnp.concatenate([query_w, down_all], axis=1)
    first_out = dot(normed, first_w)
    queries = first_out[:, : DN + DR]
    latent = first_out[:, DN + DR : DN + DR + rank_latent]
    key_rope = first_out[:, DN + DR + rank_latent :]
    latent_scale = rms_scale(latent)
    latent_low = (latent * latent_scale * latent_gain_all).astype(BF)
    keys_values = dot(latent_low, up_w)
    query_low = (
        jnp.concatenate(
            [queries[:, :DN], rotate(queries[:, DN:], cosine, sine_part)], axis=-1
        )
        .astype(BF)
        .reshape(groups, group_rows, DN + DR)
    )
    key_low = (
        jnp.concatenate([keys_values[:, :DN], rotate(key_rope, cosine, sine_part)], axis=-1)
        .astype(BF)
        .reshape(groups, group_rows, DN + DR)
    )
    value_low = keys_values[:, DN:].astype(BF).reshape(groups, group_rows, DV)
    scores = (
        jnp.einsum("bqc,bkc->bqk", query_low, key_low, preferred_element_type=F32) * score_scale
    )
    scores = jnp.where(allowed, scores, -1e30)
    row_top = jnp.max(scores, axis=-1, keepdims=True)
    powers = jnp.exp(scores - row_top)
    probs = powers / jnp.sum(powers, axis=-1, keepdims=True)
    probs_low = probs.astype(BF)
    attended_low = (
        jnp.einsum("bqk,bkc->bqc", probs_low, value_low, preferred_element_type=F32)
        .astype(BF)
        .reshape(span, DV)
    )
    attention_out = scatter(dot(attended_low, output_w).astype(BF))
    residual = tokens_own.astype(F32) + attention_out.astype(F32)

    second_scale = rms_scale(residual)
    ffn_in = (residual * second_scale * ffn_gain_all).astype(BF)
    ffn_all = gather(ffn_in)
    expert_rows = (
        jnp.einsum(
            "gst,gtd->gsd",
            picks_low,
            ffn_all.reshape(groups, group_rows, width),
            preferred_element_type=F32,
        )
        .astype(BF)
        .reshape(groups * slots, width)
    )
    slot_up = (
        jnp.einsum(
            "gst,gtd->gsd",
            picks_low,
            upstream_all.reshape(groups, group_rows, width),
            preferred_element_type=F32,
        )
        .astype(BF)
        .reshape(groups * slots, width)
    )
    router_probs = jax.nn.softmax(dot(ffn_all, router_all), axis=-1)
    my_probs = lax.dynamic_slice_in_dim(router_probs, me_e, 1, 1)
    slot_gate = jnp.sum(picks_f * my_probs.reshape(groups, 1, group_rows), axis=2).reshape(-1, 1)
    gate_part = dot(expert_rows, gate_w)
    up_part = dot(expert_rows, up_e_w)
    sigmoid = jax.nn.sigmoid(gate_part)
    silu = gate_part * sigmoid
    inner = silu * up_part
    inner_low = inner.astype(BF)
    returned = dot(inner_low, down_e_w).astype(BF)
    pick_gate = (picks_f * my_probs.reshape(groups, 1, group_rows)).astype(BF)
    routed = jnp.einsum(
        "gst,gsd->gtd",
        pick_gate,
        returned.reshape(groups, slots, width),
        preferred_element_type=F32,
    ).reshape(span, width)
    shared_g = dot(ffn_all, shared_gate_w)
    shared_u = dot(ffn_all, shared_up_w)
    shared_sigmoid = jax.nn.sigmoid(shared_g)
    shared_low = (shared_g * shared_sigmoid * shared_u).astype(BF)
    mixed = residual + scatter((dot(shared_low, shared_down_w) + routed).astype(BF)).astype(F32)

    shared_down_grad = dot_left(shared_low, upstream_all)
    shared_hidden = dot_right(upstream_all, shared_down_w)
    shared_gate_low = (
        shared_hidden * shared_u * shared_sigmoid * (1.0 + shared_g * (1.0 - shared_sigmoid))
    ).astype(BF)
    shared_up_low = (shared_hidden * shared_g * shared_sigmoid).astype(BF)
    shared_gate_grad = dot_left(ffn_all, shared_gate_low)
    shared_up_grad = dot_left(ffn_all, shared_up_low)
    raw_back = dot_right(slot_up, down_e_w)
    slot_dot = jnp.sum(inner * raw_back, axis=1)
    inner_grad = raw_back * slot_gate
    gate_low = (inner_grad * up_part * sigmoid * (1.0 + gate_part * (1.0 - sigmoid))).astype(BF)
    up_low = (inner_grad * silu).astype(BF)
    inner_scaled = (inner * slot_gate).astype(BF)
    expert_down_grad = dot_left(inner_scaled, slot_up)
    expert_gate_grad = dot_left(expert_rows, gate_low)
    expert_up_grad = dot_left(expert_rows, up_low)
    rows_grad = (dot_right(gate_low, gate_w) + dot_right(up_low, up_e_w)).astype(BF)
    row_dot = jnp.sum(picks_f * slot_dot.reshape(groups, slots, 1), axis=1).reshape(span, 1)
    own_column = (jnp.arange(experts) == me_e).astype(F32)[None, :]
    logit_part = row_dot * my_probs * (own_column - router_probs)
    logit_high = logit_part.astype(BF)
    logit_rest = (logit_part - logit_high.astype(F32)).astype(BF)
    logit_both = jnp.concatenate([logit_high, logit_rest], axis=1)
    router_both = dot_left(ffn_all, logit_both)
    router_grad = router_both[:, :experts] + router_both[:, experts:]
    ffn_grad = (
        dot_right(shared_gate_low, shared_gate_w)
        + dot_right(shared_up_low, shared_up_w)
        + dot_right(logit_both, jnp.concatenate([router_all, router_all], axis=1))
        + jnp.einsum(
            "gst,gsd->gtd",
            picks_low,
            rows_grad.reshape(groups, slots, width),
            preferred_element_type=F32,
        ).reshape(span, width)
    )
    ffn_grad = scatter(ffn_grad.astype(BF)).astype(F32)
    residual_part, ffn_gain_grad = norm_back(residual, second_scale, ffn_gain_all, ffn_grad)
    residual_grad = upstream_own.astype(F32) + residual_part
    residual_all = gather(residual_grad.astype(BF))

    output_weight_grad = dot_left(attended_low, residual_all)
    attended_grad = (
        dot_right(residual_all, output_w).astype(BF).reshape(groups, group_rows, DV)
    )
    value_grad = jnp.einsum("bqk,bqc->bkc", probs_low, attended_grad, preferred_element_type=F32)
    probs_grad = jnp.einsum("bqc,bkc->bqk", attended_grad, value_low, preferred_element_type=F32)
    score_grad = (
        probs * (probs_grad - jnp.sum(probs * probs_grad, axis=-1, keepdims=True))
    ).astype(BF)
    query_grad = (
        jnp.einsum("bqk,bkc->bqc", score_grad, key_low, preferred_element_type=F32) * score_scale
    ).reshape(span, DN + DR)
    key_grad = (
        jnp.einsum("bqk,bqc->bkc", score_grad, query_low, preferred_element_type=F32)
        * score_scale
    ).reshape(span, DN + DR)
    query_all = jnp.concatenate(
        [query_grad[:, :DN], unrotate(query_grad[:, DN:], cosine, sine_part)], axis=-1
    ).astype(BF)
    kv_grad = jnp.concatenate([key_grad[:, :DN], value_grad.reshape(span, DV)], axis=-1).astype(BF)
    rope_part = unrotate(key_grad[:, DN:], cosine, sine_part)
    up_latent_grad = dot_left(latent_low, kv_grad)
    latent_grad, latent_gain_grad = norm_back(
        latent, latent_scale, latent_gain_all, dot_right(kv_grad, up_w)
    )
    first_grad = jnp.concatenate(
        [query_all, latent_grad.astype(BF), rope_part.astype(BF)], axis=-1
    )
    first_w_grad = dot_left(normed, first_grad)
    query_weight_grad = first_w_grad[:, : DN + DR]
    down_grad = first_w_grad[:, DN + DR :]
    normed_grad = scatter(dot_right(first_grad, first_w).astype(BF)).astype(F32)
    own_inputs = tokens_own.astype(F32)
    input_part, attn_gain_grad = norm_back(
        own_inputs, rms_scale(own_inputs), attn_gain_all, normed_grad
    )
    tokens_grad = residual_grad + input_part

    small = jnp.concatenate(
        [
            down_grad,
            router_grad,
            attn_gain_grad[:, None],
            ffn_gain_grad[:, None],
            jnp.pad(
                latent_gain_grad.reshape(n_e * n_d, latent_piece),
                ((0, 0), (0, small_rows - latent_piece)),
            ).reshape(-1, 1),
        ],
        axis=1,
    )
    small = lax.psum_scatter(small, ("dp", "expert"), scatter_dimension=0, tiled=True)
    last = latent_all_width + experts
    shape = (micro, group_rows, width)
    return (
        mixed.reshape(shape),
        tokens_grad.reshape(shape),
        small[:, last],
        sum_dp(query_weight_grad, 0),
        small[:, :latent_all_width],
        small[:latent_piece, last + 2],
        sum_dp(up_latent_grad, 0),
        sum_dp(output_weight_grad, 1),
        small[:, last + 1],
        small[:, latent_all_width:last],
        sum_dp(shared_gate_grad, 0),
        sum_dp(shared_up_grad, 0),
        sum_dp(shared_down_grad, 1),
        sum_dp(expert_gate_grad, 0)[None],
        sum_dp(expert_up_grad, 0)[None],
        sum_dp(expert_down_grad, 1)[None],
    )


def solution(mesh):
    rows = P(None, ("dp", "expert"), None)
    split = P(("dp", "expert"))
    split_rows = P(("dp", "expert"), None)
    columns = P("dp", "expert")
    turned = P("expert", "dp")
    expert_in = P("expert", "dp", None)
    expert_out = P("expert", None, "dp")
    return jax.shard_map(
        on_device,
        mesh=mesh,
        in_specs=(
            rows,
            P(None, "dp"),
            rows,
            rows,
            rows,
            split,
            columns,
            split_rows,
            split,
            columns,
            turned,
            split,
            split_rows,
            columns,
            columns,
            turned,
            expert_in,
            expert_in,
            expert_out,
        ),
        out_specs=(
            rows,
            rows,
            split,
            columns,
            split_rows,
            split,
            columns,
            turned,
            split,
            split_rows,
            columns,
            columns,
            turned,
            expert_in,
            expert_in,
            expert_out,
        ),
        check_vma=False,
    )
```

```python
import math

import jax
import jax.numpy as jnp
from jax import lax
from jax.experimental import pallas as pl
from jax.experimental.pallas import tpu as pltpu
from jax.sharding import PartitionSpec as P

DN = 128
DR = 64
DV = 128
EPS = 1e-06
HIGH = lax.Precision.HIGHEST
F32 = jnp.float32
BF = jnp.bfloat16


def dot(former, latter):
    return jnp.dot(former, latter, preferred_element_type=F32)


def dot_left(former, latter):
    return lax.dot_general(former, latter, (((0,), (0,)), ((), ())), preferred_element_type=F32)


def dot_right(former, latter):
    return lax.dot_general(former, latter, (((1,), (1,)), ((), ())), preferred_element_type=F32)


def rms_scale(values):
    return lax.rsqrt(jnp.mean(values * values, axis=-1, keepdims=True) + EPS)


def norm_back(values, scale_rows, gain, out_grad):
    scaled = out_grad * gain
    inner = jnp.mean(scaled * values, axis=-1, keepdims=True)
    value_grad = scale_rows * scaled - values * scale_rows * scale_rows * scale_rows * inner
    return (value_grad, jnp.sum(out_grad * values * scale_rows, axis=0))


def rotate(values, cosine, sine_part):
    half = values.shape[-1] // 2
    turned = jnp.concatenate([-values[..., half:], values[..., :half]], axis=-1)
    return values * cosine + turned * sine_part


def unrotate(values, cosine, sine_part):
    half = values.shape[-1] // 2
    scaled = values * sine_part
    return values * cosine + jnp.concatenate([scaled[..., half:], -scaled[..., :half]], axis=-1)


def layouts(segment):
    places = jnp.arange(segment.shape[1], dtype=jnp.int32)
    prompt_len = jnp.sum((segment == 0).astype(jnp.int32), axis=1, keepdims=True)
    former = (segment[:, None, :] < segment[:, :, None]).astype(jnp.int32)
    seg_start = jnp.sum(former, axis=2)
    position = jnp.where(segment == 0, places[None], prompt_len + places[None] - seg_start)
    allowed = (places[None, None, :] <= places[None, :, None]) & (
        (segment[:, None, :] == 0) | (segment[:, None, :] == segment[:, :, None])
    )
    return (position, allowed)


def angles(position, row_count):
    freq_index = jnp.arange(DR // 2, dtype=F32)
    frequency = jnp.exp(freq_index * (-2.0 * math.log(10000.0) / DR))
    turning = jnp.arange(row_count, dtype=F32)[:, None] * frequency[None, :]
    table = jnp.concatenate([jnp.cos(turning), jnp.sin(turning)], axis=1)
    picks = (position.reshape(-1)[:, None] == jnp.arange(row_count)[None, :]).astype(F32)
    both = jnp.dot(picks, table, precision=HIGH)
    cosine, sine_part = both[:, : DR // 2], both[:, DR // 2 :]
    return (
        jnp.concatenate([cosine, cosine], axis=1),
        jnp.concatenate([sine_part, sine_part], axis=1),
    )


LINE = 4
PIECES = 3
MESH = pl.DeviceIdType.MESH
VMEM_LIMIT = 60 * 1024 * 1024


def place_of(me):
    return (me // 4, lax.rem(me // 2, 2), lax.rem(me, 2))


def index_of(line, pair, core):
    return line * 4 + pair * 2 + core


def greet(line, pair, core):
    barrier = pltpu.get_barrier_semaphore()

    def signal(target):
        pl.semaphore_signal(barrier, inc=1, device_id={"expert": target}, device_id_type=MESH)

    signal(index_of(line, pair, 1 - core))
    signal(index_of(line, 1 - pair, core))

    @pl.when(line > 0)
    def _():
        signal(index_of(line - 1, pair, core))

    @pl.when(line < LINE - 1)
    def _():
        signal(index_of(line + 1, pair, core))

    inner = jnp.where(line > 0, 1, 0) + jnp.where(line < LINE - 1, 1, 0)
    pl.semaphore_wait(barrier, 2 + inner)


def when(condition, action):
    if condition is None:
        action()
    else:
        pl.when(condition)(action)


def gather_kernel(own_ref, out_ref, own_sem, send_sem, recv_sem):
    me = lax.axis_index("expert")
    line, pair, core = place_of(me)
    rows = own_ref.shape[0] // PIECES
    greet(line, pair, core)
    local = pltpu.make_async_copy(own_ref, out_ref.at[me], own_sem)
    local.start()
    sent = []

    def push(condition, kind, origin, piece, target, source=None):
        block = out_ref.at[origin, pl.ds(piece * rows, rows)]
        copy = pltpu.make_async_remote_copy(
            src_ref=block if source is None else source,
            dst_ref=block,
            send_sem=send_sem.at[kind, origin, piece],
            recv_sem=recv_sem.at[origin, piece],
            device_id={"expert": target},
            device_id_type=MESH,
        )
        when(condition, copy.start)
        sent.append((condition, copy))

    def arrive(condition, origin, piece):
        block = out_ref.at[origin, pl.ds(piece * rows, rows)]
        copy = pltpu.make_async_remote_copy(
            src_ref=block,
            dst_ref=block,
            send_sem=send_sem.at[0, origin, piece],
            recv_sem=recv_sem.at[origin, piece],
            device_id={"expert": me},
            device_id_type=MESH,
        )
        when(condition, copy.wait_recv)

    left = index_of(line - 1, pair, core)
    right = index_of(line + 1, pair, core)
    across = index_of(line, 1 - pair, core)
    sibling = index_of(line, pair, 1 - core)
    for piece in range(PIECES):
        source = own_ref.at[pl.ds(piece * rows, rows)]
        push(line < LINE - 1, 1, me, piece, right, source)
        push(line > 0, 0, me, piece, left, source)
        push(None, 2, me, piece, across, source)
        push(None, 3, me, piece, sibling, source)

    def along(hop):
        for piece in range(PIECES):
            for side in (-1, 1):
                there = line + side * hop
                held = (there >= 0) & (there < LINE)
                origin = index_of(there, pair, core)
                arrive(held, origin, piece)
                if hop < LINE - 1:
                    further = held & ((line < LINE - 1) if side < 0 else (line > 0))
                    kind, target = (1, right) if side < 0 else (0, left)
                    push(further, kind, origin, piece, target)
                push(held, 2, origin, piece, across)
                push(held, 3, origin, piece, sibling)

    def over(hop):
        for piece in range(PIECES):
            for side in (-1, 1) if hop else (1,):
                there = line + side * hop
                held = (there >= 0) & (there < LINE) if hop else None
                origin = index_of(there, 1 - pair, core)
                arrive(held, origin, piece)
                push(held, 3, origin, piece, sibling)

    along(1)
    over(0)
    along(2)
    over(1)
    along(3)
    over(2)
    over(3)
    for other_line in range(LINE):
        for other_pair in range(2):
            for piece in range(PIECES):
                arrive(None, index_of(other_line, other_pair, 1 - core), piece)
    for condition, copy in sent:
        when(condition, copy.wait_send)
    local.wait()


def gather_rows(own, collective_id):
    count = lax.axis_size("expert")
    rows, width = own.shape
    out = pl.pallas_call(
        gather_kernel,
        out_shape=jax.ShapeDtypeStruct((count, rows, width), own.dtype),
        in_specs=[pl.BlockSpec(memory_space=pl.ANY)],
        out_specs=pl.BlockSpec(memory_space=pl.ANY),
        scratch_shapes=[
            pltpu.SemaphoreType.DMA,
            pltpu.SemaphoreType.DMA((4, count, PIECES)),
            pltpu.SemaphoreType.DMA((count, PIECES)),
        ],
        compiler_params=pltpu.CompilerParams(collective_id=collective_id, has_side_effects=True),
        name="gather_rows",
    )(own)
    return out.reshape(count * rows, width)


FAR_FIRST = ((3, 3, 0, 0), (2, 0, 3, 1), (1, 2, 1, 2), (0, 1, 2, 3))
COLUMNS = 512
STRIP = 16


def pick_by(line, table):
    value = jnp.int32(table[LINE - 1])
    for k in range(LINE - 2, -1, -1):
        value = jnp.where(line == k, jnp.int32(table[k]), value)
    return value


def scatter_kernel(with_slots, *refs):
    if with_slots:
        (
            l_ref, r_ref, q_ref, v_ref, out_ref, part, met, paired, passed,
            core_send, core_recv, pair_send, pair_recv, line_send, line_recv,
        ) = refs
    else:
        (
            l_ref, r_ref, out_ref, part, met, paired, passed,
            core_send, core_recv, pair_send, pair_recv, line_send, line_recv,
        ) = refs
    me = lax.axis_index("expert")
    line, pair, core = place_of(me)
    rows, width = out_ref.shape
    piece_rows = rows // PIECES
    greet(line, pair, core)
    sibling = index_of(line, pair, 1 - core)
    across = index_of(line, 1 - pair, core)
    sent = []

    def produce(dest, target, added):
        start = pl.multiple_of(dest * rows, 64)

        @pl.loop(0, width // COLUMNS)
        def _(tile):
            columns = pl.ds(pl.multiple_of(tile * COLUMNS, COLUMNS), COLUMNS)
            total = jnp.dot(
                l_ref[pl.ds(start, rows), :], r_ref[:, columns], preferred_element_type=F32
            )
            if with_slots:
                per = q_ref.shape[1]
                count = rows // per
                total = total + jnp.concatenate(
                    [
                        jnp.dot(
                            q_ref[dest * count + k],
                            v_ref[dest * count + k, :, columns],
                            preferred_element_type=F32,
                        )
                        for k in range(count)
                    ],
                    axis=0,
                )
            if added:
                total = total + target[:, columns].astype(F32)
            target[:, columns] = total.astype(BF)

    def send(condition, source, dest, send_at, recv_at, target):
        copy = pltpu.make_async_remote_copy(
            src_ref=source,
            dst_ref=dest,
            send_sem=send_at,
            recv_sem=recv_at,
            device_id={"expert": target},
            device_id_type=MESH,
        )
        when(condition, copy.start)
        sent.append((condition, copy))

    def await_block(condition, block, recv_at, send_at):
        copy = pltpu.make_async_remote_copy(
            src_ref=block,
            dst_ref=block,
            send_sem=send_at,
            recv_sem=recv_at,
            device_id={"expert": me},
            device_id_type=MESH,
        )
        when(condition, copy.wait_recv)

    dest_line = [pick_by(line, FAR_FIRST[step]) for step in range(LINE)]

    def chip(i):
        return (dest_line[i // 2], (1 - pair) if i % 2 == 0 else pair)

    def meet(i):
        await_block(None, met.at[i], core_recv.at[i], core_send.at[i])
        there, other = chip(i)
        produce(index_of(there, other, core), met.at[i], True)
        if i % 2 == 0:
            for piece in range(PIECES):
                at = pl.ds(piece * piece_rows, piece_rows)
                send(
                    None,
                    met.at[i, at],
                    paired.at[i // 2, at],
                    pair_send.at[i // 2, piece],
                    pair_recv.at[i // 2, piece],
                    across,
                )

    for i in range(2 * LINE):
        there, other = chip(i)
        produce(index_of(there, other, 1 - core), part.at[i], False)
        send(None, part.at[i], met.at[i], core_send.at[i], core_recv.at[i], sibling)
        if i > 0:
            meet(i - 1)
    meet(2 * LINE - 1)

    def add_strips(target, first, others):
        @pl.loop(0, piece_rows // STRIP)
        def _(strip):
            for columns in range(0, width, COLUMNS):
                at = pl.ds(pl.multiple_of(first + strip * STRIP, STRIP), STRIP)
                cols = pl.ds(columns, COLUMNS)
                total = None
                for other in others:
                    term = other[at, cols].astype(F32)
                    total = term if total is None else total + term
                target[at, cols] = total.astype(target.dtype)

    for step in range(LINE - 1):
        there = dest_line[step]
        ahead = there > line
        way = jnp.where(ahead, 1, -1)
        behind = line - way
        held = (behind >= 0) & (behind < LINE)
        target = index_of(line + way, pair, core)
        slot = jnp.where((there == line + way) & (way < 0), LINE, there)
        for piece in range(PIECES):
            first = piece * piece_rows
            at = pl.ds(first, piece_rows)
            await_block(
                None, paired.at[step, at], pair_recv.at[step, piece], pair_send.at[step, piece]
            )
            await_block(
                held, passed.at[there, at], line_recv.at[there, piece], line_send.at[step, piece]
            )

            @pl.when(held)
            def _():
                add_strips(
                    paired.at[step],
                    first,
                    [paired.at[step], met.at[2 * step + 1], passed.at[there]],
                )

            @pl.when(jnp.logical_not(held))
            def _():
                add_strips(paired.at[step], first, [paired.at[step], met.at[2 * step + 1]])

            send(
                None,
                paired.at[step, at],
                passed.at[slot, at],
                line_send.at[step, piece],
                line_recv.at[slot, piece],
                target,
            )
    step = LINE - 1
    from_left, from_right = line > 0, line < LINE - 1
    for piece in range(PIECES):
        first = piece * piece_rows
        at = pl.ds(first, piece_rows)
        await_block(
            None, paired.at[step, at], pair_recv.at[step, piece], pair_send.at[step, piece]
        )
        add_strips(out_ref, first, [paired.at[step], met.at[2 * step + 1]])
        for held, slot in ((from_left, line), (from_right, LINE)):
            await_block(
                held, passed.at[slot, at], line_recv.at[slot, piece], line_send.at[0, piece]
            )

            @pl.when(held)
            def _():
                add_strips(out_ref, first, [out_ref, passed.at[slot]])

    for condition, copy in sent:
        when(condition, copy.wait_send)


def scatter_rows(left, right, collective_id, picks=None, values=None):
    count = lax.axis_size("expert")
    rows = left.shape[0] // count
    width = right.shape[1]
    operands = [left, right] if picks is None else [left, right, picks, values]
    block = (rows, width)
    return pl.pallas_call(
        lambda *refs: scatter_kernel(picks is not None, *refs),
        out_shape=jax.ShapeDtypeStruct(block, F32),
        in_specs=[pl.BlockSpec(memory_space=pltpu.VMEM)] * len(operands),
        out_specs=pl.BlockSpec(memory_space=pltpu.VMEM),
        scratch_shapes=[
            pltpu.VMEM((2 * LINE,) + block, BF),
            pltpu.VMEM((2 * LINE,) + block, BF),
            pltpu.VMEM((LINE,) + block, BF),
            pltpu.VMEM((LINE + 1,) + block, BF),
            pltpu.SemaphoreType.DMA((2 * LINE,)),
            pltpu.SemaphoreType.DMA((2 * LINE,)),
            pltpu.SemaphoreType.DMA((LINE, PIECES)),
            pltpu.SemaphoreType.DMA((LINE, PIECES)),
            pltpu.SemaphoreType.DMA((LINE, PIECES)),
            pltpu.SemaphoreType.DMA((LINE + 1, PIECES)),
        ],
        compiler_params=pltpu.CompilerParams(
            collective_id=collective_id, has_side_effects=True, vmem_limit_bytes=VMEM_LIMIT
        ),
        name="scatter_rows",
    )(*operands)


def on_device(
    tokens,
    segment,
    routes,
    drop_order,
    cotangent,
    attn_gain,
    query_weight,
    down_latent,
    latent_gain,
    up_latent,
    output_weight,
    ffn_gain,
    router_weight,
    shared_gate,
    shared_up,
    shared_down,
    expert_gate,
    expert_up,
    expert_down,
):
    n_e = lax.axis_size("expert")
    n_d = lax.axis_size("dp")
    me_e = lax.axis_index("expert")
    me_d = lax.axis_index("dp")
    micro, group_rows, width = tokens.shape
    own_rows = micro * group_rows
    span = n_e * own_rows
    groups = n_e * micro
    top = routes.shape[2]
    experts = n_e * expert_gate.shape[0]
    capacity = (5 * group_rows * top + 4 * experts - 1) // (4 * experts)
    slots = -(-capacity // 16) * 16
    rank_latent = latent_gain.shape[0] * n_e * n_d
    hidden = expert_gate.shape[2]

    def gather(values):
        return lax.all_gather(values, "expert", axis=0, tiled=True)

    def scatter(values):
        return lax.psum_scatter(values, "expert", scatter_dimension=0, tiled=True)

    def from_dp(values):
        blocks = [values]
        for step in range(1, n_d):
            pairs = [((i + step) % n_d, i) for i in range(n_d)]
            blocks.append(lax.ppermute(values, "dp", pairs))
        return blocks

    def whole(blocks, axis):
        size = blocks[0].shape[axis]
        shape = list(blocks[0].shape)
        shape[axis] = size * n_d
        total = jnp.zeros(shape, blocks[0].dtype)
        for step in range(n_d):
            at = lax.rem(me_d + step, n_d) * size
            total = lax.dynamic_update_slice_in_dim(total, blocks[step], at, axis)
        return total

    def sum_dp(values, axis):
        size = values.shape[axis] // n_d

        def part(step):
            at = lax.rem(me_d + step, n_d) * size
            return lax.dynamic_slice_in_dim(values, at, size, axis)

        total = part(0).astype(F32)
        for step in range(1, n_d):
            pairs = [(i, (i + step) % n_d) for i in range(n_d)]
            total = total + lax.ppermute(part(step).astype(BF), "dp", pairs).astype(F32)
        return total

    small_rows = attn_gain.shape[0]
    latent_all_width = down_latent.shape[1]
    latent_piece = latent_gain.shape[0]
    packed = jnp.concatenate(
        [
            down_latent,
            router_weight,
            attn_gain[:, None],
            ffn_gain[:, None],
            jnp.pad(latent_gain, (0, small_rows - latent_piece))[:, None],
        ],
        axis=1,
    )
    packed = lax.all_gather(packed, ("dp", "expert"), axis=0, tiled=True)
    down_all = packed[:, :latent_all_width]
    router_all = packed[:, latent_all_width : latent_all_width + experts]
    rest = packed[:, latent_all_width + experts :].astype(F32)
    attn_gain_all = rest[:, 0]
    ffn_gain_all = rest[:, 1]
    latent_gain_all = rest[:, 2].reshape(n_e * n_d, small_rows)[:, :latent_piece].reshape(-1)

    query_w = whole(from_dp(query_weight), 0)
    up_w = whole(from_dp(up_latent), 0)
    output_w = whole(from_dp(output_weight), 1)
    gate_w = whole(from_dp(expert_gate[0]), 0)
    up_e_w = whole(from_dp(expert_up[0]), 0)
    down_e_w = whole(from_dp(expert_down[0]), 1)
    shared_gate_w = whole(from_dp(shared_gate), 0)
    shared_up_w = whole(from_dp(shared_up), 0)
    shared_down_w = whole(from_dp(shared_down), 1)

    tokens_own = tokens.reshape(own_rows, width)
    tokens_all = gather_rows(tokens_own, 1)
    upstream_own = cotangent.reshape(own_rows, width)
    upstream_all = gather(upstream_own)

    chosen = jnp.sum(
        (routes[..., None] == jnp.arange(experts, dtype=jnp.int32)).astype(jnp.int32), axis=2
    )
    order = drop_order[:, 0]
    earlier = (order[:, None, :] < order[:, :, None]).astype(F32)
    rank = jnp.einsum("mtu,mue->mte", earlier, chosen.astype(F32)).astype(jnp.int32)
    code = jnp.where((chosen == 1) & (rank < capacity), rank, -1).reshape(own_rows, experts)
    code_all = gather(code)
    my_code = lax.dynamic_slice_in_dim(code_all, me_e, 1, 1).reshape(groups, group_rows)
    picks = my_code[:, None, :] == jnp.arange(slots, dtype=jnp.int32)[None, :, None]
    picks_low = picks.astype(BF)
    picks_f = picks.astype(F32)

    span_segment = (
        segment.reshape(micro, n_e, group_rows).transpose(1, 0, 2).reshape(groups, group_rows)
    )
    position, allowed = layouts(span_segment)
    cosine, sine_part = angles(position, group_rows)
    score_scale = (DN + DR) ** (-0.5)
    inputs_all = tokens_all.astype(F32)
    first_scale = rms_scale(inputs_all)
    normed = (inputs_all * first_scale * attn_gain_all).astype(BF)
    first_w = jnp.concatenate([query_w, down_all], axis=1)
    first_out = dot(normed, first_w)
    queries = first_out[:, : DN + DR]
    latent = first_out[:, DN + DR : DN + DR + rank_latent]
    key_rope = first_out[:, DN + DR + rank_latent :]
    latent_scale = rms_scale(latent)
    latent_low = (latent * latent_scale * latent_gain_all).astype(BF)
    keys_values = dot(latent_low, up_w)
    query_low = (
        jnp.concatenate(
            [queries[:, :DN], rotate(queries[:, DN:], cosine, sine_part)], axis=-1
        )
        .astype(BF)
        .reshape(groups, group_rows, DN + DR)
    )
    key_low = (
        jnp.concatenate([keys_values[:, :DN], rotate(key_rope, cosine, sine_part)], axis=-1)
        .astype(BF)
        .reshape(groups, group_rows, DN + DR)
    )
    value_low = keys_values[:, DN:].astype(BF).reshape(groups, group_rows, DV)
    scores = (
        jnp.einsum("bqc,bkc->bqk", query_low, key_low, preferred_element_type=F32) * score_scale
    )
    scores = jnp.where(allowed, scores, -1e30)
    row_top = jnp.max(scores, axis=-1, keepdims=True)
    powers = jnp.exp(scores - row_top)
    probs = powers / jnp.sum(powers, axis=-1, keepdims=True)
    probs_low = probs.astype(BF)
    attended_low = (
        jnp.einsum("bqk,bkc->bqc", probs_low, value_low, preferred_element_type=F32)
        .astype(BF)
        .reshape(span, DV)
    )
    residual = tokens_own.astype(F32) + scatter_rows(attended_low, output_w, 2)

    second_scale = rms_scale(residual)
    ffn_in = (residual * second_scale * ffn_gain_all).astype(BF)
    ffn_all = gather_rows(ffn_in, 1)
    expert_rows = (
        jnp.einsum(
            "gst,gtd->gsd",
            picks_low,
            ffn_all.reshape(groups, group_rows, width),
            preferred_element_type=F32,
        )
        .astype(BF)
        .reshape(groups * slots, width)
    )
    slot_up = (
        jnp.einsum(
            "gst,gtd->gsd",
            picks_low,
            upstream_all.reshape(groups, group_rows, width),
            preferred_element_type=F32,
        )
        .astype(BF)
        .reshape(groups * slots, width)
    )
    router_probs = jax.nn.softmax(dot(ffn_all, router_all), axis=-1)
    my_probs = lax.dynamic_slice_in_dim(router_probs, me_e, 1, 1)
    slot_gate = jnp.sum(picks_f * my_probs.reshape(groups, 1, group_rows), axis=2).reshape(-1, 1)
    gate_part = dot(expert_rows, gate_w)
    up_part = dot(expert_rows, up_e_w)
    sigmoid = jax.nn.sigmoid(gate_part)
    silu = gate_part * sigmoid
    inner = silu * up_part
    inner_low = inner.astype(BF)
    returned = dot(inner_low, down_e_w).astype(BF)
    pick_gate = (picks_f * my_probs.reshape(groups, 1, group_rows)).astype(BF)
    routed = jnp.einsum(
        "gst,gsd->gtd",
        pick_gate,
        returned.reshape(groups, slots, width),
        preferred_element_type=F32,
    ).reshape(span, width)
    shared_g = dot(ffn_all, shared_gate_w)
    shared_u = dot(ffn_all, shared_up_w)
    shared_sigmoid = jax.nn.sigmoid(shared_g)
    shared_low = (shared_g * shared_sigmoid * shared_u).astype(BF)
    mixed = residual + scatter((dot(shared_low, shared_down_w) + routed).astype(BF)).astype(F32)

    shared_down_grad = dot_left(shared_low, upstream_all)
    shared_hidden = dot_right(upstream_all, shared_down_w)
    shared_gate_low = (
        shared_hidden * shared_u * shared_sigmoid * (1.0 + shared_g * (1.0 - shared_sigmoid))
    ).astype(BF)
    shared_up_low = (shared_hidden * shared_g * shared_sigmoid).astype(BF)
    shared_gate_grad = dot_left(ffn_all, shared_gate_low)
    shared_up_grad = dot_left(ffn_all, shared_up_low)
    raw_back = dot_right(slot_up, down_e_w)
    slot_dot = jnp.sum(inner * raw_back, axis=1)
    inner_grad = raw_back * slot_gate
    gate_low = (inner_grad * up_part * sigmoid * (1.0 + gate_part * (1.0 - sigmoid))).astype(BF)
    up_low = (inner_grad * silu).astype(BF)
    inner_scaled = (inner * slot_gate).astype(BF)
    expert_down_grad = dot_left(inner_scaled, slot_up)
    expert_gate_grad = dot_left(expert_rows, gate_low)
    expert_up_grad = dot_left(expert_rows, up_low)
    rows_grad = (dot_right(gate_low, gate_w) + dot_right(up_low, up_e_w)).astype(BF)
    row_dot = jnp.sum(picks_f * slot_dot.reshape(groups, slots, 1), axis=1).reshape(span, 1)
    own_column = (jnp.arange(experts) == me_e).astype(F32)[None, :]
    logit_part = row_dot * my_probs * (own_column - router_probs)
    logit_high = logit_part.astype(BF)
    logit_rest = (logit_part - logit_high.astype(F32)).astype(BF)
    logit_both = jnp.concatenate([logit_high, logit_rest], axis=1)
    router_both = dot_left(ffn_all, logit_both)
    router_grad = router_both[:, :experts] + router_both[:, experts:]
    ffn_grad = scatter_rows(
        jnp.concatenate([shared_gate_low, shared_up_low, logit_both], axis=1),
        jnp.concatenate([shared_gate_w, shared_up_w, router_all, router_all], axis=1).T,
        3,
        picks_low.transpose(0, 2, 1),
        rows_grad.reshape(groups, slots, width),
    )
    residual_part, ffn_gain_grad = norm_back(residual, second_scale, ffn_gain_all, ffn_grad)
    residual_grad = upstream_own.astype(F32) + residual_part
    residual_all = gather_rows(residual_grad.astype(BF), 1)

    output_weight_grad = dot_left(attended_low, residual_all)
    attended_grad = (
        dot_right(residual_all, output_w).astype(BF).reshape(groups, group_rows, DV)
    )
    value_grad = jnp.einsum("bqk,bqc->bkc", probs_low, attended_grad, preferred_element_type=F32)
    probs_grad = jnp.einsum("bqc,bkc->bqk", attended_grad, value_low, preferred_element_type=F32)
    score_grad = (
        probs * (probs_grad - jnp.sum(probs * probs_grad, axis=-1, keepdims=True))
    ).astype(BF)
    query_grad = (
        jnp.einsum("bqk,bkc->bqc", score_grad, key_low, preferred_element_type=F32) * score_scale
    ).reshape(span, DN + DR)
    key_grad = (
        jnp.einsum("bqk,bqc->bkc", score_grad, query_low, preferred_element_type=F32)
        * score_scale
    ).reshape(span, DN + DR)
    query_all = jnp.concatenate(
        [query_grad[:, :DN], unrotate(query_grad[:, DN:], cosine, sine_part)], axis=-1
    ).astype(BF)
    kv_grad = jnp.concatenate([key_grad[:, :DN], value_grad.reshape(span, DV)], axis=-1).astype(BF)
    rope_part = unrotate(key_grad[:, DN:], cosine, sine_part)
    up_latent_grad = dot_left(latent_low, kv_grad)
    latent_grad, latent_gain_grad = norm_back(
        latent, latent_scale, latent_gain_all, dot_right(kv_grad, up_w)
    )
    first_grad = jnp.concatenate(
        [query_all, latent_grad.astype(BF), rope_part.astype(BF)], axis=-1
    )
    first_w_grad = dot_left(normed, first_grad)
    query_weight_grad = first_w_grad[:, : DN + DR]
    down_grad = first_w_grad[:, DN + DR :]
    normed_grad = scatter_rows(first_grad, first_w.T, 4)
    own_inputs = tokens_own.astype(F32)
    input_part, attn_gain_grad = norm_back(
        own_inputs, rms_scale(own_inputs), attn_gain_all, normed_grad
    )
    tokens_grad = residual_grad + input_part

    small = jnp.concatenate(
        [
            down_grad,
            router_grad,
            attn_gain_grad[:, None],
            ffn_gain_grad[:, None],
            jnp.pad(
                latent_gain_grad.reshape(n_e * n_d, latent_piece),
                ((0, 0), (0, small_rows - latent_piece)),
            ).reshape(-1, 1),
        ],
        axis=1,
    )
    small = lax.psum_scatter(
        small.astype(BF), ("dp", "expert"), scatter_dimension=0, tiled=True
    ).astype(F32)
    last = latent_all_width + experts
    shape = (micro, group_rows, width)
    return (
        mixed.reshape(shape),
        tokens_grad.reshape(shape),
        small[:, last],
        sum_dp(query_weight_grad, 0),
        small[:, :latent_all_width],
        small[:latent_piece, last + 2],
        sum_dp(up_latent_grad, 0),
        sum_dp(output_weight_grad, 1),
        small[:, last + 1],
        small[:, latent_all_width:last],
        sum_dp(shared_gate_grad, 0),
        sum_dp(shared_up_grad, 0),
        sum_dp(shared_down_grad, 1),
        sum_dp(expert_gate_grad, 0)[None],
        sum_dp(expert_up_grad, 0)[None],
        sum_dp(expert_down_grad, 1)[None],
    )


def solution(mesh):
    rows = P(None, ("dp", "expert"), None)
    split = P(("dp", "expert"))
    split_rows = P(("dp", "expert"), None)
    columns = P("dp", "expert")
    turned = P("expert", "dp")
    expert_in = P("expert", "dp", None)
    expert_out = P("expert", None, "dp")
    return jax.shard_map(
        on_device,
        mesh=mesh,
        in_specs=(
            rows,
            P(None, "dp"),
            rows,
            rows,
            rows,
            split,
            columns,
            split_rows,
            split,
            columns,
            turned,
            split,
            split_rows,
            columns,
            columns,
            turned,
            expert_in,
            expert_in,
            expert_out,
        ),
        out_specs=(
            rows,
            rows,
            split,
            columns,
            split_rows,
            split,
            columns,
            turned,
            split,
            split_rows,
            columns,
            columns,
            turned,
            expert_in,
            expert_in,
            expert_out,
        ),
        check_vma=False,
    )
```

```python
import math

import jax
import jax.numpy as jnp
from jax import lax
from jax.experimental import pallas as pl
from jax.experimental.pallas import tpu as pltpu
from jax.sharding import PartitionSpec as P

DN = 128
DR = 64
DV = 128
EPS = 1e-06
HIGH = lax.Precision.HIGHEST
F32 = jnp.float32
BF = jnp.bfloat16


def dot(former, latter):
    return jnp.dot(former, latter, preferred_element_type=F32)


def dot_left(former, latter):
    return lax.dot_general(former, latter, (((0,), (0,)), ((), ())), preferred_element_type=F32)


def dot_right(former, latter):
    return lax.dot_general(former, latter, (((1,), (1,)), ((), ())), preferred_element_type=F32)


def rms_scale(values):
    return lax.rsqrt(jnp.mean(values * values, axis=-1, keepdims=True) + EPS)


def norm_back(values, scale_rows, gain, out_grad):
    scaled = out_grad * gain
    inner = jnp.mean(scaled * values, axis=-1, keepdims=True)
    value_grad = scale_rows * scaled - values * scale_rows * scale_rows * scale_rows * inner
    return (value_grad, jnp.sum(out_grad * values * scale_rows, axis=0))


def layouts(segment):
    places = jnp.arange(segment.shape[1], dtype=jnp.int32)
    prompt_len = jnp.sum((segment == 0).astype(jnp.int32), axis=1, keepdims=True)
    former = (segment[:, None, :] < segment[:, :, None]).astype(jnp.int32)
    seg_start = jnp.sum(former, axis=2)
    position = jnp.where(segment == 0, places[None], prompt_len + places[None] - seg_start)
    allowed = (places[None, None, :] <= places[None, :, None]) & (
        (segment[:, None, :] == 0) | (segment[:, None, :] == segment[:, :, None])
    )
    return (position, allowed)


def angles(position, row_count):
    freq_index = jnp.arange(DR // 2, dtype=F32)
    frequency = jnp.exp(freq_index * (-2.0 * math.log(10000.0) / DR))
    turning = jnp.arange(row_count, dtype=F32)[:, None] * frequency[None, :]
    cosine, sine_part = jnp.cos(turning), jnp.sin(turning)
    table = jnp.concatenate([cosine] * 4 + [-sine_part, sine_part] * 2, axis=1)
    picks = (position.reshape(-1)[:, None] == jnp.arange(row_count)[None, :]).astype(F32)
    return jnp.dot(picks, table, precision=HIGH)


LINE = 4
PIECES = 3
MESH = pl.DeviceIdType.MESH
VMEM_LIMIT = 60 * 1024 * 1024


def place_of(me):
    return (me // 4, lax.rem(me // 2, 2), lax.rem(me, 2))


def index_of(line, pair, core):
    return line * 4 + pair * 2 + core


def greet(line, pair, core, others=0):
    barrier = pltpu.get_barrier_semaphore()

    def signal(target):
        pl.semaphore_signal(barrier, inc=1, device_id={"expert": target}, device_id_type=MESH)

    signal(index_of(line, pair, 1 - core))
    signal(index_of(line, 1 - pair, core))

    @pl.when(line > 0)
    def _():
        signal(index_of(line - 1, pair, core))

    @pl.when(line < LINE - 1)
    def _():
        signal(index_of(line + 1, pair, core))

    inner = jnp.where(line > 0, 1, 0) + jnp.where(line < LINE - 1, 1, 0)
    pl.semaphore_wait(barrier, 2 + others + inner)


def greet_dp(others):
    barrier = pltpu.get_barrier_semaphore()
    me_d, n_d = lax.axis_index("dp"), lax.axis_size("dp")
    if others:
        for step in range(1, n_d):
            pl.semaphore_signal(
                barrier,
                inc=1,
                device_id={"dp": lax.rem(me_d + step, n_d)},
                device_id_type=MESH,
            )


def ride(sources, targets, send_sem, recv_sem):
    me_d, n_d = lax.axis_index("dp"), lax.axis_size("dp")
    copies = []
    for number, (source, target) in enumerate(zip(sources, targets)):
        for step in range(1, n_d):
            copy = pltpu.make_async_remote_copy(
                src_ref=source.at[step - 1],
                dst_ref=target.at[step - 1],
                send_sem=send_sem.at[number, step - 1],
                recv_sem=recv_sem.at[number, step - 1],
                device_id={"dp": lax.rem(me_d + step, n_d)},
                device_id_type=MESH,
            )
            copy.start()
            copies.append(copy)
    return copies


def when(condition, action):
    if condition is None:
        action()
    else:
        pl.when(condition)(action)


def gather_kernel(axes, riders, *refs):
    count = len(axes)
    refs = list(refs)

    def take(number):
        taken = refs[:number]
        del refs[:number]
        return taken

    (own_ref,), blocks, sources = take(1), take(count), take(riders)
    (out_ref,), wholes, targets = take(1), take(count), take(riders)
    own_sem, send_sem, recv_sem, block_sem, block_send, block_recv, ride_send, ride_recv = refs
    me = lax.axis_index("expert")
    line, pair, core = place_of(me)
    rows = own_ref.shape[0] // PIECES
    me_d, n_d = lax.axis_index("dp"), lax.axis_size("dp")
    others = n_d - 1 if count + riders else 0
    greet_dp(others)
    greet(line, pair, core, others)
    local = [pltpu.make_async_copy(own_ref, out_ref.at[me], own_sem)]
    sent = []

    def push(condition, kind, origin, piece, target, source=None):
        block = out_ref.at[origin, pl.ds(piece * rows, rows)]
        copy = pltpu.make_async_remote_copy(
            src_ref=block if source is None else source,
            dst_ref=block,
            send_sem=send_sem.at[kind, origin, piece],
            recv_sem=recv_sem.at[origin, piece],
            device_id={"expert": target},
            device_id_type=MESH,
        )
        when(condition, copy.start)
        sent.append((condition, copy))

    def arrive(condition, origin, piece):
        block = out_ref.at[origin, pl.ds(piece * rows, rows)]
        copy = pltpu.make_async_remote_copy(
            src_ref=block,
            dst_ref=block,
            send_sem=send_sem.at[0, origin, piece],
            recv_sem=recv_sem.at[origin, piece],
            device_id={"expert": me},
            device_id_type=MESH,
        )
        when(condition, copy.wait_recv)

    left = index_of(line - 1, pair, core)
    right = index_of(line + 1, pair, core)
    across = index_of(line, 1 - pair, core)
    sibling = index_of(line, pair, 1 - core)
    for piece in range(PIECES):
        source = own_ref.at[pl.ds(piece * rows, rows)]
        push(line < LINE - 1, 1, me, piece, right, source)
        push(line > 0, 0, me, piece, left, source)
        push(None, 2, me, piece, across, source)
        push(None, 3, me, piece, sibling, source)
    ridden = ride(sources, targets, ride_send, ride_recv)
    incoming = []
    for number, (block, whole, axis) in enumerate(zip(blocks, wholes, axes)):
        size = block.shape[axis]

        def part(owner):
            at = pl.ds(pl.multiple_of(owner * size, size), size)
            return whole.at[at] if axis == 0 else whole.at[:, at]

        local.append(pltpu.make_async_copy(block, part(me_d), block_sem.at[number]))
        for step in range(1, n_d):
            copy = pltpu.make_async_remote_copy(
                src_ref=block,
                dst_ref=part(me_d),
                send_sem=block_send.at[number, step - 1],
                recv_sem=block_recv.at[number, step - 1],
                device_id={"dp": lax.rem(me_d + step, n_d)},
                device_id_type=MESH,
            )
            copy.start()
            sent.append((None, copy))
            source = part(lax.rem(me_d - step + n_d, n_d))
            incoming.append(
                pltpu.make_async_remote_copy(
                    src_ref=source,
                    dst_ref=source,
                    send_sem=block_send.at[number, step - 1],
                    recv_sem=block_recv.at[number, step - 1],
                    device_id={"dp": me_d},
                    device_id_type=MESH,
                )
            )
    for copy in local:
        copy.start()

    def along(hop):
        for piece in range(PIECES):
            for side in (-1, 1):
                there = line + side * hop
                held = (there >= 0) & (there < LINE)
                origin = index_of(there, pair, core)
                arrive(held, origin, piece)
                if hop < LINE - 1:
                    further = held & ((line < LINE - 1) if side < 0 else (line > 0))
                    kind, target = (1, right) if side < 0 else (0, left)
                    push(further, kind, origin, piece, target)
                push(held, 2, origin, piece, across)
                push(held, 3, origin, piece, sibling)

    def over(hop):
        for piece in range(PIECES):
            for side in (-1, 1) if hop else (1,):
                there = line + side * hop
                held = (there >= 0) & (there < LINE) if hop else None
                origin = index_of(there, 1 - pair, core)
                arrive(held, origin, piece)
                push(held, 3, origin, piece, sibling)

    along(1)
    over(0)
    along(2)
    over(1)
    along(3)
    over(2)
    over(3)
    for other_line in range(LINE):
        for other_pair in range(2):
            for piece in range(PIECES):
                arrive(None, index_of(other_line, other_pair, 1 - core), piece)
    for copy in incoming:
        copy.wait_recv()
    for copy in ridden:
        copy.wait()
    for condition, copy in sent:
        when(condition, copy.wait_send)
    for copy in local:
        copy.wait()


def gather_rows(own, collective_id, blocks=(), axes=(), riders=()):
    count = lax.axis_size("expert")
    n_d = lax.axis_size("dp")
    rows, width = own.shape
    shapes = [jax.ShapeDtypeStruct((count, rows, width), own.dtype)]
    for block, axis in zip(blocks, axes):
        shape = list(block.shape)
        shape[axis] *= n_d
        shapes.append(jax.ShapeDtypeStruct(tuple(shape), block.dtype))
    shapes += [jax.ShapeDtypeStruct(rider.shape, rider.dtype) for rider in riders]
    number, carried, others = max(1, len(axes)), max(1, len(riders)), max(1, n_d - 1)
    out = pl.pallas_call(
        lambda *refs: gather_kernel(axes, len(riders), *refs),
        out_shape=shapes,
        in_specs=[pl.BlockSpec(memory_space=pl.ANY)] * len(shapes),
        out_specs=[pl.BlockSpec(memory_space=pl.ANY)] * len(shapes),
        scratch_shapes=[
            pltpu.SemaphoreType.DMA,
            pltpu.SemaphoreType.DMA((4, count, PIECES)),
            pltpu.SemaphoreType.DMA((count, PIECES)),
            pltpu.SemaphoreType.DMA((number,)),
            pltpu.SemaphoreType.DMA((number, others)),
            pltpu.SemaphoreType.DMA((number, others)),
            pltpu.SemaphoreType.DMA((carried, others)),
            pltpu.SemaphoreType.DMA((carried, others)),
        ],
        compiler_params=pltpu.CompilerParams(collective_id=collective_id, has_side_effects=True),
        name="gather_rows",
    )(own, *blocks, *riders)
    return [out[0].reshape(count * rows, width)] + list(out[1:])


FAR_FIRST = ((3, 3, 0, 0), (2, 0, 3, 1), (1, 2, 1, 2), (0, 1, 2, 3))
COLUMNS = 512
STRIP = 16


def pick_by(line, table):
    value = jnp.int32(table[LINE - 1])
    for k in range(LINE - 2, -1, -1):
        value = jnp.where(line == k, jnp.int32(table[k]), value)
    return value


def scatter_kernel(kind, riders, *refs):
    refs = list(refs)

    def take(number):
        taken = refs[:number]
        del refs[:number]
        return taken

    with_slots = kind == "slots"
    l_ref, r_ref = take(2)
    q_ref, v_ref = take(2) if with_slots else (None, None)
    (extra_ref,) = take(1) if kind == "extra" else (None,)
    sources, (out_ref,), targets = take(riders), take(1), take(riders)
    (
        part, met, paired, passed, core_send, core_recv, pair_send, pair_recv,
        line_send, line_recv, ride_send, ride_recv,
    ) = refs
    me = lax.axis_index("expert")
    line, pair, core = place_of(me)
    rows, width = out_ref.shape
    piece_rows = rows // PIECES
    others = lax.axis_size("dp") - 1 if riders else 0
    greet_dp(others)
    greet(line, pair, core, others)
    ridden = ride(sources, targets, ride_send, ride_recv)
    sibling = index_of(line, pair, 1 - core)
    across = index_of(line, 1 - pair, core)
    sent = []

    def produce(dest, target, added):
        dense = rows if extra_ref is None else rows - extra_ref.shape[1]
        start = pl.multiple_of(dest * dense, 64)

        @pl.loop(0, width // COLUMNS)
        def _(tile):
            columns = pl.ds(pl.multiple_of(tile * COLUMNS, COLUMNS), COLUMNS)
            total = jnp.dot(
                l_ref[pl.ds(start, dense), :], r_ref[:, columns], preferred_element_type=F32
            )
            if with_slots:
                per = q_ref.shape[1]
                count = rows // per
                total = total + jnp.concatenate(
                    [
                        jnp.dot(
                            q_ref[dest * count + k],
                            v_ref[dest * count + k, :, columns],
                            preferred_element_type=F32,
                        )
                        for k in range(count)
                    ],
                    axis=0,
                )
            if added:
                total = total + target[:dense, columns].astype(F32)
            target[:dense, columns] = total.astype(BF)
            if extra_ref is not None:
                last = extra_ref[dest, :, columns]
                if added:
                    last = last.astype(F32) + target[dense:, columns].astype(F32)
                target[dense:, columns] = last.astype(BF)

    def send(condition, source, dest, send_at, recv_at, target):
        copy = pltpu.make_async_remote_copy(
            src_ref=source,
            dst_ref=dest,
            send_sem=send_at,
            recv_sem=recv_at,
            device_id={"expert": target},
            device_id_type=MESH,
        )
        when(condition, copy.start)
        sent.append((condition, copy))

    def await_block(condition, block, recv_at, send_at):
        copy = pltpu.make_async_remote_copy(
            src_ref=block,
            dst_ref=block,
            send_sem=send_at,
            recv_sem=recv_at,
            device_id={"expert": me},
            device_id_type=MESH,
        )
        when(condition, copy.wait_recv)

    dest_line = [pick_by(line, FAR_FIRST[step]) for step in range(LINE)]

    def chip(i):
        return (dest_line[i // 2], (1 - pair) if i % 2 == 0 else pair)

    def meet(i):
        await_block(None, met.at[i], core_recv.at[i], core_send.at[i])
        there, other = chip(i)
        produce(index_of(there, other, core), met.at[i], True)
        if i % 2 == 0:
            for piece in range(PIECES):
                at = pl.ds(piece * piece_rows, piece_rows)
                send(
                    None,
                    met.at[i, at],
                    paired.at[i // 2, at],
                    pair_send.at[i // 2, piece],
                    pair_recv.at[i // 2, piece],
                    across,
                )

    for i in range(2 * LINE):
        there, other = chip(i)
        produce(index_of(there, other, 1 - core), part.at[i], False)
        send(None, part.at[i], met.at[i], core_send.at[i], core_recv.at[i], sibling)
        if i > 0:
            meet(i - 1)
    meet(2 * LINE - 1)

    def add_strips(target, first, others):
        @pl.loop(0, piece_rows // STRIP)
        def _(strip):
            for columns in range(0, width, COLUMNS):
                at = pl.ds(pl.multiple_of(first + strip * STRIP, STRIP), STRIP)
                cols = pl.ds(columns, COLUMNS)
                total = None
                for other in others:
                    term = other[at, cols].astype(F32)
                    total = term if total is None else total + term
                target[at, cols] = total.astype(target.dtype)

    for step in range(LINE - 1):
        there = dest_line[step]
        ahead = there > line
        way = jnp.where(ahead, 1, -1)
        behind = line - way
        held = (behind >= 0) & (behind < LINE)
        target = index_of(line + way, pair, core)
        slot = jnp.where((there == line + way) & (way < 0), LINE, there)
        for piece in range(PIECES):
            first = piece * piece_rows
            at = pl.ds(first, piece_rows)
            await_block(
                None, paired.at[step, at], pair_recv.at[step, piece], pair_send.at[step, piece]
            )
            await_block(
                held, passed.at[there, at], line_recv.at[there, piece], line_send.at[step, piece]
            )

            @pl.when(held)
            def _():
                add_strips(
                    paired.at[step],
                    first,
                    [paired.at[step], met.at[2 * step + 1], passed.at[there]],
                )

            @pl.when(jnp.logical_not(held))
            def _():
                add_strips(paired.at[step], first, [paired.at[step], met.at[2 * step + 1]])

            send(
                None,
                paired.at[step, at],
                passed.at[slot, at],
                line_send.at[step, piece],
                line_recv.at[slot, piece],
                target,
            )
    step = LINE - 1
    from_left, from_right = line > 0, line < LINE - 1
    for piece in range(PIECES):
        first = piece * piece_rows
        at = pl.ds(first, piece_rows)
        await_block(
            None, paired.at[step, at], pair_recv.at[step, piece], pair_send.at[step, piece]
        )
        add_strips(out_ref, first, [paired.at[step], met.at[2 * step + 1]])
        for held, slot in ((from_left, line), (from_right, LINE)):
            await_block(
                held, passed.at[slot, at], line_recv.at[slot, piece], line_send.at[0, piece]
            )

            @pl.when(held)
            def _():
                add_strips(out_ref, first, [out_ref, passed.at[slot]])

    for condition, copy in sent:
        when(condition, copy.wait_send)
    for copy in ridden:
        copy.wait()


def scatter_rows(left, right, collective_id, picks=None, values=None, extra=None, riders=()):
    count = lax.axis_size("expert")
    rows = left.shape[0] // count
    width = right.shape[1]
    operands, kind = [left, right], "plain"
    if picks is not None:
        operands, kind = [left, right, picks, values], "slots"
    if extra is not None:
        operands, kind = [left, right, extra], "extra"
        rows += extra.shape[1]
    block = (rows, width)
    in_vmem, anywhere = pl.BlockSpec(memory_space=pltpu.VMEM), pl.BlockSpec(memory_space=pl.ANY)
    carried, others = max(1, len(riders)), max(1, lax.axis_size("dp") - 1)
    return pl.pallas_call(
        lambda *refs: scatter_kernel(kind, len(riders), *refs),
        out_shape=[jax.ShapeDtypeStruct(block, F32)]
        + [jax.ShapeDtypeStruct(rider.shape, rider.dtype) for rider in riders],
        in_specs=[in_vmem] * len(operands) + [anywhere] * len(riders),
        out_specs=[in_vmem] + [anywhere] * len(riders),
        scratch_shapes=[
            pltpu.VMEM((2 * LINE,) + block, BF),
            pltpu.VMEM((2 * LINE,) + block, BF),
            pltpu.VMEM((LINE,) + block, BF),
            pltpu.VMEM((LINE + 1,) + block, BF),
            pltpu.SemaphoreType.DMA((2 * LINE,)),
            pltpu.SemaphoreType.DMA((2 * LINE,)),
            pltpu.SemaphoreType.DMA((LINE, PIECES)),
            pltpu.SemaphoreType.DMA((LINE, PIECES)),
            pltpu.SemaphoreType.DMA((LINE, PIECES)),
            pltpu.SemaphoreType.DMA((LINE + 1, PIECES)),
            pltpu.SemaphoreType.DMA((carried, others)),
            pltpu.SemaphoreType.DMA((carried, others)),
        ],
        compiler_params=pltpu.CompilerParams(
            collective_id=collective_id, has_side_effects=True, vmem_limit_bytes=VMEM_LIMIT
        ),
        name="scatter_rows",
    )(*operands, *riders)


TILE_GROUPS = 4
SCALE = (DN + DR) ** (-0.5)


def half_turn(values):
    lane = lax.broadcasted_iota(jnp.int32, values.shape, 1)
    lower = (lane // (DR // 2)) % 2 == 0
    return jnp.where(lower, pltpu.roll(values, 128 - DR // 2, 1), pltpu.roll(values, DR // 2, 1))


def softmax_scores(query, key, mask):
    scores = jnp.where(mask > 0, dot_right(query, key) * SCALE, -1e30)
    powers = jnp.exp(scores - jnp.max(scores, axis=-1, keepdims=True))
    return powers / jnp.sum(powers, axis=-1, keepdims=True)


def attention_forward_kernel(
    x_ref, gain_ref, first_ref, latent_gain_ref, up_ref, trig_ref, mask_ref,
    normed_ref, query_ref, key_ref, value_ref, unit_ref, low_ref, scale_ref, attended_ref,
):
    rank = up_ref.shape[0]
    inputs = x_ref[...].astype(F32)
    scale = lax.rsqrt(jnp.mean(inputs * inputs, axis=1, keepdims=True) + EPS)
    normed_ref[...] = (inputs * scale * gain_ref[...]).astype(BF)
    out = dot(normed_ref[...], first_ref[...])
    latent = out[:, DN : DN + rank]
    latent_scale = lax.rsqrt(jnp.mean(latent * latent, axis=1, keepdims=True) + EPS)
    scale_ref[...] = latent_scale
    unit = latent * latent_scale
    unit_ref[...] = unit.astype(BF)
    low_ref[...] = (unit * latent_gain_ref[...]).astype(BF)
    keys_values = dot(low_ref[...], up_ref[...])
    rope = out[:, DN + rank :]
    turned = rope * trig_ref[:, :128] + half_turn(rope) * trig_ref[:, 128:]
    lane = lax.broadcasted_iota(jnp.int32, turned.shape, 1)
    query_ref[:, :DN] = out[:, :DN].astype(BF)
    query_ref[:, DN:] = jnp.where(lane < DR, turned, 0.0).astype(BF)
    key_ref[:, :DN] = keys_values[:, :DN].astype(BF)
    key_ref[:, DN:] = jnp.where(lane < DR, pltpu.roll(turned, DR, 1), 0.0).astype(BF)
    value_ref[...] = keys_values[:, DN:].astype(BF)
    per = mask_ref.shape[1]
    for group in range(mask_ref.shape[0]):
        at = pl.ds(group * per, per)
        probs = softmax_scores(query_ref[at], key_ref[at], mask_ref[group])
        attended_ref[at] = dot(probs.astype(BF), value_ref[at]).astype(BF)


def attention_forward(x, gain, first_w, latent_gain, up_w, trig, mask):
    groups, per, _ = mask.shape
    width, rank = first_w.shape[0], up_w.shape[0]
    span, rows = groups * per, TILE_GROUPS * per

    def tile(columns):
        return pl.BlockSpec((rows, columns), lambda i: (i, 0))

    def fixed(shape):
        return pl.BlockSpec(shape, lambda i: (0, 0))

    outs = (width, 2 * DN, 2 * DN, DV, rank, rank, 1, DV)
    kinds = (BF, BF, BF, BF, BF, BF, F32, BF)
    return pl.pallas_call(
        attention_forward_kernel,
        grid=(groups // TILE_GROUPS,),
        in_specs=[
            tile(width),
            fixed((1, width)),
            fixed(first_w.shape),
            fixed((1, rank)),
            fixed(up_w.shape),
            tile(trig.shape[1]),
            pl.BlockSpec((TILE_GROUPS, per, per), lambda i: (i, 0, 0)),
        ],
        out_specs=[tile(columns) for columns in outs],
        out_shape=[jax.ShapeDtypeStruct((span, c), k) for c, k in zip(outs, kinds)],
        compiler_params=pltpu.CompilerParams(vmem_limit_bytes=VMEM_LIMIT),
        name="attention_forward",
    )(x, gain[None], first_w, latent_gain[None], up_w, trig, mask)


def attention_backward_kernel(
    r_ref, output_ref, attended_ref, query_ref, key_ref, value_ref, mask_ref, trig_ref,
    unit_ref, low_ref, scale_ref, latent_gain_ref, up_ref, normed_ref,
    grad_ref, output_grad_ref, up_grad_ref, first_grad_ref, gain_grad_ref, kv_ref,
):
    step = pl.program_id(0)
    rank = up_ref.shape[0]
    per = mask_ref.shape[1]

    @pl.when(step == 0)
    def _():
        output_grad_ref[...] = jnp.zeros_like(output_grad_ref)
        up_grad_ref[...] = jnp.zeros_like(up_grad_ref)
        first_grad_ref[...] = jnp.zeros_like(first_grad_ref)
        gain_grad_ref[...] = jnp.zeros_like(gain_grad_ref)

    attended_grad = dot_right(r_ref[...], output_ref[...]).astype(BF)
    output_grad_ref[...] += dot_left(attended_ref[...], r_ref[...])
    for group in range(mask_ref.shape[0]):
        at = pl.ds(group * per, per)
        upper = attended_grad[group * per : (group + 1) * per]
        probs = softmax_scores(query_ref[at], key_ref[at], mask_ref[group])
        value_grad = dot_left(probs.astype(BF), upper)
        probs_grad = dot_right(upper, value_ref[at])
        inner = jnp.sum(probs * probs_grad, axis=1, keepdims=True)
        score_grad = (probs * (probs_grad - inner)).astype(BF)
        query_grad = dot(score_grad, key_ref[at]) * SCALE
        key_grad = dot_left(score_grad, query_ref[at]) * SCALE
        kv_ref[at, :DN] = key_grad[:, :DN].astype(BF)
        kv_ref[at, DN:] = value_grad.astype(BF)
        grad_ref[at, :DN] = query_grad[:, :DN].astype(BF)
        rope = query_grad[:, DN:] + pltpu.roll(key_grad[:, DN:], DR, 1)
        rope = rope * trig_ref[at, :128] + half_turn(rope * trig_ref[at, 128:])
        grad_ref[at, DN + rank :] = rope.astype(BF)
    out_grad = dot_right(kv_ref[...], up_ref[...])
    unit = unit_ref[...].astype(F32)
    gain_grad_ref[...] += jnp.sum(out_grad * unit, axis=0, keepdims=True)
    scaled = out_grad * latent_gain_ref[...]
    inner = jnp.mean(scaled * unit, axis=1, keepdims=True)
    grad_ref[:, DN : DN + rank] = (scale_ref[...] * (scaled - unit * inner)).astype(BF)
    up_grad_ref[...] += dot_left(low_ref[...], kv_ref[...])
    first_grad_ref[...] += dot_left(normed_ref[...], grad_ref[...])


def attention_backward(residual_all, output_w, stored, mask, trig, latent_gain, up_w):
    normed, query, key, value, unit, low, scale, attended = stored
    groups, per, _ = mask.shape
    width, rank = residual_all.shape[1], up_w.shape[0]
    span, rows = groups * per, TILE_GROUPS * per
    first_width = 2 * DN + rank

    def tile(columns):
        return pl.BlockSpec((rows, columns), lambda i: (i, 0))

    def fixed(shape):
        return pl.BlockSpec(shape, lambda i: (0, 0))

    sums = (output_w.shape, up_w.shape, (width, first_width), (1, rank))
    return pl.pallas_call(
        attention_backward_kernel,
        grid=(groups // TILE_GROUPS,),
        in_specs=[
            tile(width),
            fixed(output_w.shape),
            tile(DV),
            tile(2 * DN),
            tile(2 * DN),
            tile(DV),
            pl.BlockSpec((TILE_GROUPS, per, per), lambda i: (i, 0, 0)),
            tile(trig.shape[1]),
            tile(rank),
            tile(rank),
            tile(1),
            fixed((1, rank)),
            fixed(up_w.shape),
            tile(width),
        ],
        out_specs=[tile(first_width)] + [fixed(shape) for shape in sums],
        out_shape=[jax.ShapeDtypeStruct((span, first_width), BF)]
        + [jax.ShapeDtypeStruct(shape, F32) for shape in sums],
        scratch_shapes=[pltpu.VMEM((rows, DN + DV), BF)],
        compiler_params=pltpu.CompilerParams(vmem_limit_bytes=VMEM_LIMIT),
        name="attention_backward",
    )(
        residual_all, output_w, attended, query, key, value, mask, trig,
        unit, low, scale, latent_gain[None], up_w, normed,
    )


def on_device(
    tokens,
    segment,
    routes,
    drop_order,
    cotangent,
    attn_gain,
    query_weight,
    down_latent,
    latent_gain,
    up_latent,
    output_weight,
    ffn_gain,
    router_weight,
    shared_gate,
    shared_up,
    shared_down,
    expert_gate,
    expert_up,
    expert_down,
):
    n_e = lax.axis_size("expert")
    n_d = lax.axis_size("dp")
    me_e = lax.axis_index("expert")
    me_d = lax.axis_index("dp")
    micro, group_rows, width = tokens.shape
    own_rows = micro * group_rows
    span = n_e * own_rows
    groups = n_e * micro
    top = routes.shape[2]
    experts = n_e * expert_gate.shape[0]
    capacity = (5 * group_rows * top + 4 * experts - 1) // (4 * experts)
    slots = -(-capacity // 16) * 16
    rank_latent = latent_gain.shape[0] * n_e * n_d
    hidden = expert_gate.shape[2]

    def gather(values):
        return lax.all_gather(values, "expert", axis=0, tiled=True)

    def scatter(values):
        return lax.psum_scatter(values, "expert", scatter_dimension=0, tiled=True)

    def from_dp(values):
        blocks = [values]
        for step in range(1, n_d):
            pairs = [((i + step) % n_d, i) for i in range(n_d)]
            blocks.append(lax.ppermute(values, "dp", pairs))
        return blocks

    def whole(blocks, axis):
        size = blocks[0].shape[axis]
        shape = list(blocks[0].shape)
        shape[axis] = size * n_d
        total = jnp.zeros(shape, blocks[0].dtype)
        for step in range(n_d):
            at = lax.rem(me_d + step, n_d) * size
            total = lax.dynamic_update_slice_in_dim(total, blocks[step], at, axis)
        return total

    def sum_dp(values, axis):
        size = values.shape[axis] // n_d

        def part(step):
            at = lax.rem(me_d + step, n_d) * size
            return lax.dynamic_slice_in_dim(values, at, size, axis)

        total = part(0).astype(F32)
        for step in range(1, n_d):
            pairs = [(i, (i + step) % n_d) for i in range(n_d)]
            total = total + lax.ppermute(part(step).astype(BF), "dp", pairs).astype(F32)
        return total

    def grad_dp(left, right, axis):
        size = (left, right)[axis].shape[1] // n_d
        parts = []
        for step in range(n_d):
            at = lax.rem(me_d + step, n_d) * size
            if axis == 0:
                part = dot_left(lax.dynamic_slice_in_dim(left, at, size, 1), right)
            else:
                part = dot_left(left, lax.dynamic_slice_in_dim(right, at, size, 1))
            parts.append(part.astype(BF) if step else part)
        return (stack(parts[1:]), parts[0])

    def split_dp(values, axis):
        size = values.shape[axis] // n_d
        parts = []
        for step in range(n_d):
            at = lax.rem(me_d + step, n_d) * size
            parts.append(lax.dynamic_slice_in_dim(values, at, size, axis))
        return (stack([part.astype(BF) for part in parts[1:]]), parts[0])

    def stack(parts):
        return parts[0][None] if len(parts) == 1 else jnp.stack(parts)

    def add_all(total, parts):
        for step in range(n_d - 1):
            total = total + parts[step].astype(F32)
        return total

    small_rows = attn_gain.shape[0]
    latent_all_width = down_latent.shape[1]
    latent_piece = latent_gain.shape[0]
    packed = jnp.concatenate(
        [
            down_latent,
            router_weight,
            attn_gain[:, None],
            ffn_gain[:, None],
            jnp.pad(latent_gain, (0, small_rows - latent_piece))[:, None],
        ],
        axis=1,
    )
    packed = lax.all_gather(packed, ("dp", "expert"), axis=0, tiled=True)
    down_all = packed[:, :latent_all_width]
    router_all = packed[:, latent_all_width : latent_all_width + experts]
    rest = packed[:, latent_all_width + experts :].astype(F32)
    attn_gain_all = rest[:, 0]
    ffn_gain_all = rest[:, 1]
    latent_gain_all = rest[:, 2].reshape(n_e * n_d, small_rows)[:, :latent_piece].reshape(-1)

    gate_w = whole(from_dp(expert_gate[0]), 0)
    up_e_w = whole(from_dp(expert_up[0]), 0)
    down_e_w = whole(from_dp(expert_down[0]), 1)

    chosen = jnp.sum(
        (routes[..., None] == jnp.arange(experts, dtype=jnp.int32)).astype(jnp.int32), axis=2
    )
    order = drop_order[:, 0]
    earlier = (order[:, None, :] < order[:, :, None]).astype(F32)
    rank = jnp.einsum("mtu,mue->mte", earlier, chosen.astype(F32)).astype(jnp.int32)
    code = jnp.where((chosen == 1) & (rank < capacity), rank, -1).reshape(own_rows, experts)

    tokens_own = tokens.reshape(own_rows, width)
    code_lanes = -(-experts // 128) * 128
    code_low = jnp.pad(code.astype(BF), ((0, 0), (0, code_lanes - experts)))
    tokens_all, query_w, up_w, output_w, shared_gate_w, shared_up_w, shared_down_w = gather_rows(
        jnp.concatenate([tokens_own, code_low], axis=1),
        5,
        (query_weight, up_latent, output_weight, shared_gate, shared_up, shared_down),
        (0, 0, 1, 0, 0, 1),
    )
    upstream_own = cotangent.reshape(own_rows, width)
    upstream_later, tokens_all = lax.optimization_barrier((upstream_own, tokens_all))
    upstream_all = gather(upstream_later)
    code_all = tokens_all[:, width : width + experts].astype(jnp.int32)
    my_code = lax.dynamic_slice_in_dim(code_all, me_e, 1, 1).reshape(groups, group_rows)
    picks = my_code[:, None, :] == jnp.arange(slots, dtype=jnp.int32)[None, :, None]
    picks_low = picks.astype(BF)
    picks_f = picks.astype(F32)

    span_segment = (
        segment.reshape(micro, n_e, group_rows).transpose(1, 0, 2).reshape(groups, group_rows)
    )
    position, allowed = layouts(span_segment)
    mask = allowed.astype(F32)
    trig = angles(position, group_rows)
    first_w = jnp.concatenate(
        [
            query_w[:, :DN],
            down_all[:, :rank_latent],
            query_w[:, DN:],
            down_all[:, rank_latent:],
        ],
        axis=1,
    )
    stored = attention_forward(
        tokens_all, attn_gain_all, first_w, latent_gain_all, up_w, trig, mask
    )
    residual = tokens_own.astype(F32) + scatter_rows(stored[-1], output_w, 2)[0]

    second_scale = rms_scale(residual)
    ffn_in = (residual * second_scale * ffn_gain_all).astype(BF)
    ffn_all = gather_rows(ffn_in, 1)[0]
    expert_rows = (
        jnp.einsum(
            "gst,gtd->gsd",
            picks_low,
            ffn_all.reshape(groups, group_rows, width),
            preferred_element_type=F32,
        )
        .astype(BF)
        .reshape(groups * slots, width)
    )
    slot_up = (
        jnp.einsum(
            "gst,gtd->gsd",
            picks_low,
            upstream_all.reshape(groups, group_rows, width),
            preferred_element_type=F32,
        )
        .astype(BF)
        .reshape(groups * slots, width)
    )
    router_probs = jax.nn.softmax(dot(ffn_all, router_all), axis=-1)
    my_probs = lax.dynamic_slice_in_dim(router_probs, me_e, 1, 1)
    slot_gate = jnp.sum(picks_f * my_probs.reshape(groups, 1, group_rows), axis=2).reshape(-1, 1)
    gate_part = dot(expert_rows, gate_w)
    up_part = dot(expert_rows, up_e_w)
    sigmoid = jax.nn.sigmoid(gate_part)
    silu = gate_part * sigmoid
    inner = silu * up_part
    inner_low = inner.astype(BF)
    returned = dot(inner_low, down_e_w).astype(BF)
    pick_gate = (picks_f * my_probs.reshape(groups, 1, group_rows)).astype(BF)
    routed = jnp.einsum(
        "gst,gsd->gtd",
        pick_gate,
        returned.reshape(groups, slots, width),
        preferred_element_type=F32,
    ).reshape(span, width)
    shared_g = dot(ffn_all, shared_gate_w)
    shared_u = dot(ffn_all, shared_up_w)
    shared_sigmoid = jax.nn.sigmoid(shared_g)
    shared_low = (shared_g * shared_sigmoid * shared_u).astype(BF)
    mixed = residual + scatter((dot(shared_low, shared_down_w) + routed).astype(BF)).astype(F32)

    shared_down_grad = dot_left(shared_low, upstream_all)
    shared_hidden = dot_right(upstream_all, shared_down_w)
    shared_gate_low = (
        shared_hidden * shared_u * shared_sigmoid * (1.0 + shared_g * (1.0 - shared_sigmoid))
    ).astype(BF)
    shared_up_low = (shared_hidden * shared_g * shared_sigmoid).astype(BF)
    shared_gate_grad = dot_left(ffn_all, shared_gate_low)
    shared_up_grad = dot_left(ffn_all, shared_up_low)
    raw_back = dot_right(slot_up, down_e_w)
    slot_dot = jnp.sum(inner * raw_back, axis=1)
    inner_grad = raw_back * slot_gate
    gate_low = (inner_grad * up_part * sigmoid * (1.0 + gate_part * (1.0 - sigmoid))).astype(BF)
    up_low = (inner_grad * silu).astype(BF)
    inner_scaled = (inner * slot_gate).astype(BF)
    down_later, down_now = grad_dp(inner_scaled, slot_up, 1)
    gate_later, gate_now = grad_dp(expert_rows, gate_low, 0)
    up_later, up_now = grad_dp(expert_rows, up_low, 0)
    rows_grad = (dot_right(gate_low, gate_w) + dot_right(up_low, up_e_w)).astype(BF)
    row_dot = jnp.sum(picks_f * slot_dot.reshape(groups, slots, 1), axis=1).reshape(span, 1)
    own_column = (jnp.arange(experts) == me_e).astype(F32)[None, :]
    logit_part = row_dot * my_probs * (own_column - router_probs)
    logit_high = logit_part.astype(BF)
    logit_rest = (logit_part - logit_high.astype(F32)).astype(BF)
    logit_both = jnp.concatenate([logit_high, logit_rest], axis=1)
    router_both = dot_left(ffn_all, logit_both)
    router_grad = router_both[:, :experts] + router_both[:, experts:]
    shared_down_later, shared_down_now = split_dp(shared_down_grad, 1)
    shared_gate_later, shared_gate_now = split_dp(shared_gate_grad, 0)
    shared_up_later, shared_up_now = split_dp(shared_up_grad, 0)
    ffn_grad, down_parts = scatter_rows(
        jnp.concatenate([shared_gate_low, shared_up_low, logit_both], axis=1),
        jnp.concatenate([shared_gate_w, shared_up_w, router_all, router_all], axis=1).T,
        3,
        picks_low.transpose(0, 2, 1),
        rows_grad.reshape(groups, slots, width),
        riders=(down_later,),
    )
    residual_part, ffn_gain_grad = norm_back(residual, second_scale, ffn_gain_all, ffn_grad)
    residual_grad = upstream_own.astype(F32) + residual_part
    (
        residual_all,
        gate_parts,
        shared_down_parts,
        shared_gate_parts,
        shared_up_parts,
    ) = gather_rows(
        residual_grad.astype(BF),
        6,
        riders=(gate_later, shared_down_later, shared_gate_later, shared_up_later),
    )

    first_grad, output_weight_grad, up_latent_grad, first_w_grad, latent_gain_grad = (
        attention_backward(residual_all, output_w, stored, mask, trig, latent_gain_all, up_w)
    )
    rope_at = DN + rank_latent
    query_weight_grad = jnp.concatenate(
        [first_w_grad[:, :DN], first_w_grad[:, rope_at : rope_at + DR]], axis=1
    )
    down_grad = jnp.concatenate(
        [first_w_grad[:, DN:rope_at], first_w_grad[:, rope_at + DR :]], axis=1
    )
    attn_gain_grad = jnp.sum(first_w_grad * first_w.astype(F32), axis=1) / attn_gain_all
    small = jnp.concatenate(
        [
            down_grad,
            router_grad,
            attn_gain_grad[:, None],
            ffn_gain_grad[:, None],
            jnp.pad(
                latent_gain_grad.reshape(n_e * n_d, latent_piece),
                ((0, 0), (0, small_rows - latent_piece)),
            ).reshape(-1, 1),
        ],
        axis=1,
    )
    small_width = -(-small.shape[1] // 128) * 128
    small = jnp.pad(small, ((0, 0), (0, small_width - small.shape[1]))).astype(BF)
    small = small.reshape(n_d, n_e, small_rows, small_width).transpose(1, 0, 2, 3)
    small = small.reshape(n_e, -1, width)
    extra_rows = small.shape[1]
    small = jnp.pad(small, ((0, 0), (0, -extra_rows % 48), (0, 0)))
    query_later, query_now = split_dp(query_weight_grad, 0)
    latent_later, latent_now = split_dp(up_latent_grad, 0)
    output_later, output_now = split_dp(output_weight_grad, 1)
    summed, up_parts, query_parts, latent_parts, output_parts = scatter_rows(
        first_grad,
        first_w.T,
        4,
        extra=small,
        riders=(up_later, query_later, latent_later, output_later),
    )
    normed_grad = summed[:own_rows]
    small = summed[own_rows : own_rows + extra_rows].reshape(n_d * small_rows, small_width)
    small = sum_dp(small, 0)
    own_inputs = tokens_own.astype(F32)
    input_part, _ = norm_back(own_inputs, rms_scale(own_inputs), attn_gain_all, normed_grad)
    tokens_grad = residual_grad + input_part
    last = latent_all_width + experts
    shape = (micro, group_rows, width)
    return (
        mixed.reshape(shape),
        tokens_grad.reshape(shape),
        small[:, last],
        add_all(query_now, query_parts),
        small[:, :latent_all_width],
        small[:latent_piece, last + 2],
        add_all(latent_now, latent_parts),
        add_all(output_now, output_parts),
        small[:, last + 1],
        small[:, latent_all_width:last],
        add_all(shared_gate_now, shared_gate_parts),
        add_all(shared_up_now, shared_up_parts),
        add_all(shared_down_now, shared_down_parts),
        add_all(gate_now, gate_parts)[None],
        add_all(up_now, up_parts)[None],
        add_all(down_now, down_parts)[None],
    )


def solution(mesh):
    rows = P(None, ("dp", "expert"), None)
    split = P(("dp", "expert"))
    split_rows = P(("dp", "expert"), None)
    columns = P("dp", "expert")
    turned = P("expert", "dp")
    expert_in = P("expert", "dp", None)
    expert_out = P("expert", None, "dp")
    return jax.shard_map(
        on_device,
        mesh=mesh,
        in_specs=(
            rows,
            P(None, "dp"),
            rows,
            rows,
            rows,
            split,
            columns,
            split_rows,
            split,
            columns,
            turned,
            split,
            split_rows,
            columns,
            columns,
            turned,
            expert_in,
            expert_in,
            expert_out,
        ),
        out_specs=(
            rows,
            rows,
            split,
            columns,
            split_rows,
            split,
            columns,
            turned,
            split,
            split_rows,
            columns,
            columns,
            turned,
            expert_in,
            expert_in,
            expert_out,
        ),
        check_vma=False,
    )
```

```python
import math

import jax
import jax.numpy as jnp
from jax import lax
from jax.experimental import pallas as pl
from jax.experimental.pallas import tpu as pltpu
from jax.sharding import PartitionSpec as P

DN = 128
DR = 64
DV = 128
EPS = 1e-06
HIGH = lax.Precision.HIGHEST
F32 = jnp.float32
BF = jnp.bfloat16


def dot(former, latter):
    return jnp.dot(former, latter, preferred_element_type=F32)


def dot_left(former, latter):
    return lax.dot_general(former, latter, (((0,), (0,)), ((), ())), preferred_element_type=F32)


def dot_right(former, latter):
    return lax.dot_general(former, latter, (((1,), (1,)), ((), ())), preferred_element_type=F32)


def rms_scale(values):
    return lax.rsqrt(jnp.mean(values * values, axis=-1, keepdims=True) + EPS)


def norm_back(values, scale_rows, gain, out_grad):
    scaled = out_grad * gain
    inner = jnp.mean(scaled * values, axis=-1, keepdims=True)
    value_grad = scale_rows * scaled - values * scale_rows * scale_rows * scale_rows * inner
    return (value_grad, jnp.sum(out_grad * values * scale_rows, axis=0))


def positions(segment):
    places = jnp.arange(segment.shape[1], dtype=jnp.int32)
    prompt_len = jnp.sum((segment == 0).astype(jnp.int32), axis=1, keepdims=True)
    former = (segment[:, None, :] < segment[:, :, None]).astype(jnp.int32)
    seg_start = jnp.sum(former, axis=2)
    return jnp.where(segment == 0, places[None], prompt_len + places[None] - seg_start)


def angles(position, row_count):
    freq_index = jnp.arange(DR // 2, dtype=F32)
    frequency = jnp.exp(freq_index * (-2.0 * math.log(10000.0) / DR))
    turning = jnp.arange(row_count, dtype=F32)[:, None] * frequency[None, :]
    cosine, sine_part = jnp.cos(turning), jnp.sin(turning)
    table = jnp.concatenate([cosine] * 4 + [-sine_part, sine_part] * 2, axis=1)
    picks = (position.reshape(-1)[:, None] == jnp.arange(row_count)[None, :]).astype(F32)
    return jnp.dot(picks, table, precision=HIGH)


LINE = 4
PIECES = 3
MESH = pl.DeviceIdType.MESH
VMEM_LIMIT = 60 * 1024 * 1024


def place_of(me):
    return (me // 4, lax.rem(me // 2, 2), lax.rem(me, 2))


def index_of(line, pair, core):
    return line * 4 + pair * 2 + core


def greet(line, pair, core, others=0):
    barrier = pltpu.get_barrier_semaphore()

    def signal(target):
        pl.semaphore_signal(barrier, inc=1, device_id={"expert": target}, device_id_type=MESH)

    signal(index_of(line, pair, 1 - core))
    signal(index_of(line, 1 - pair, core))

    @pl.when(line > 0)
    def _():
        signal(index_of(line - 1, pair, core))

    @pl.when(line < LINE - 1)
    def _():
        signal(index_of(line + 1, pair, core))

    inner = jnp.where(line > 0, 1, 0) + jnp.where(line < LINE - 1, 1, 0)
    pl.semaphore_wait(barrier, 2 + others + inner)


def greet_dp(others):
    barrier = pltpu.get_barrier_semaphore()
    me_d, n_d = lax.axis_index("dp"), lax.axis_size("dp")
    if others:
        for step in range(1, n_d):
            pl.semaphore_signal(
                barrier,
                inc=1,
                device_id={"dp": lax.rem(me_d + step, n_d)},
                device_id_type=MESH,
            )


def ride(sources, targets, send_sem, recv_sem):
    me_d, n_d = lax.axis_index("dp"), lax.axis_size("dp")
    copies = []
    for number, (source, target) in enumerate(zip(sources, targets)):
        for step in range(1, n_d):
            copy = pltpu.make_async_remote_copy(
                src_ref=source.at[step - 1],
                dst_ref=target.at[step - 1],
                send_sem=send_sem.at[number, step - 1],
                recv_sem=recv_sem.at[number, step - 1],
                device_id={"dp": lax.rem(me_d + step, n_d)},
                device_id_type=MESH,
            )
            copy.start()
            copies.append(copy)
    return copies


def share(blocks, wholes, axes, own_sem, send_sem, recv_sem):
    me_d, n_d = lax.axis_index("dp"), lax.axis_size("dp")
    local, copies = [], []
    for number, (block, whole, axis) in enumerate(zip(blocks, wholes, axes)):
        size = block.shape[axis]
        at = pl.ds(pl.multiple_of(me_d * size, size), size)
        place = whole.at[at] if axis == 0 else whole.at[:, at]
        local.append(pltpu.make_async_copy(block, place, own_sem.at[number]))
        for step in range(1, n_d):
            copies.append(
                pltpu.make_async_remote_copy(
                    src_ref=block,
                    dst_ref=place,
                    send_sem=send_sem.at[number, step - 1],
                    recv_sem=recv_sem.at[number, step - 1],
                    device_id={"dp": lax.rem(me_d + step, n_d)},
                    device_id_type=MESH,
                )
            )
    for copy in copies + local:
        copy.start()
    return copies + local


def whole_shapes(blocks, axes):
    shapes = []
    for block, axis in zip(blocks, axes):
        shape = list(block.shape)
        shape[axis] *= lax.axis_size("dp")
        shapes.append(jax.ShapeDtypeStruct(tuple(shape), block.dtype))
    return shapes


def when(condition, action):
    if condition is None:
        action()
    else:
        pl.when(condition)(action)


def gather_kernel(axes, riders, *refs):
    count = len(axes)
    refs = list(refs)

    def take(number):
        taken = refs[:number]
        del refs[:number]
        return taken

    (own_ref,), blocks, sources = take(1), take(count), take(riders)
    (out_ref,), wholes, targets = take(1), take(count), take(riders)
    own_sem, send_sem, recv_sem, block_sem, block_send, block_recv, ride_send, ride_recv = refs
    me = lax.axis_index("expert")
    line, pair, core = place_of(me)
    rows = own_ref.shape[0] // PIECES
    others = lax.axis_size("dp") - 1 if count + riders else 0
    greet_dp(others)
    greet(line, pair, core, others)
    local = [pltpu.make_async_copy(own_ref, out_ref.at[me], own_sem)]
    sent = []

    def push(condition, kind, origin, piece, target, source=None):
        block = out_ref.at[origin, pl.ds(piece * rows, rows)]
        copy = pltpu.make_async_remote_copy(
            src_ref=block if source is None else source,
            dst_ref=block,
            send_sem=send_sem.at[kind, origin, piece],
            recv_sem=recv_sem.at[origin, piece],
            device_id={"expert": target},
            device_id_type=MESH,
        )
        when(condition, copy.start)
        sent.append((condition, copy))

    def arrive(condition, origin, piece):
        block = out_ref.at[origin, pl.ds(piece * rows, rows)]
        copy = pltpu.make_async_remote_copy(
            src_ref=block,
            dst_ref=block,
            send_sem=send_sem.at[0, origin, piece],
            recv_sem=recv_sem.at[origin, piece],
            device_id={"expert": me},
            device_id_type=MESH,
        )
        when(condition, copy.wait_recv)

    left = index_of(line - 1, pair, core)
    right = index_of(line + 1, pair, core)
    across = index_of(line, 1 - pair, core)
    sibling = index_of(line, pair, 1 - core)
    for piece in range(PIECES):
        source = own_ref.at[pl.ds(piece * rows, rows)]
        push(line < LINE - 1, 1, me, piece, right, source)
        push(line > 0, 0, me, piece, left, source)
        push(None, 2, me, piece, across, source)
        push(None, 3, me, piece, sibling, source)
    ridden = ride(sources, targets, ride_send, ride_recv)
    ridden += share(blocks, wholes, axes, block_sem, block_send, block_recv)
    for copy in local:
        copy.start()

    def along(hop):
        for piece in range(PIECES):
            for side in (-1, 1):
                there = line + side * hop
                held = (there >= 0) & (there < LINE)
                origin = index_of(there, pair, core)
                arrive(held, origin, piece)
                if hop < LINE - 1:
                    further = held & ((line < LINE - 1) if side < 0 else (line > 0))
                    kind, target = (1, right) if side < 0 else (0, left)
                    push(further, kind, origin, piece, target)
                push(held, 2, origin, piece, across)
                push(held, 3, origin, piece, sibling)

    def over(hop):
        for piece in range(PIECES):
            for side in (-1, 1) if hop else (1,):
                there = line + side * hop
                held = (there >= 0) & (there < LINE) if hop else None
                origin = index_of(there, 1 - pair, core)
                arrive(held, origin, piece)
                push(held, 3, origin, piece, sibling)

    along(1)
    over(0)
    along(2)
    over(1)
    along(3)
    over(2)
    over(3)
    for other_line in range(LINE):
        for other_pair in range(2):
            for piece in range(PIECES):
                arrive(None, index_of(other_line, other_pair, 1 - core), piece)
    for copy in ridden:
        copy.wait()
    for condition, copy in sent:
        when(condition, copy.wait_send)
    for copy in local:
        copy.wait()


def gather_rows(own, collective_id, blocks=(), axes=(), riders=()):
    count = lax.axis_size("expert")
    n_d = lax.axis_size("dp")
    rows, width = own.shape
    shapes = [jax.ShapeDtypeStruct((count, rows, width), own.dtype)]
    shapes += whole_shapes(blocks, axes)
    shapes += [jax.ShapeDtypeStruct(rider.shape, rider.dtype) for rider in riders]
    number, carried, others = max(1, len(axes)), max(1, len(riders)), max(1, n_d - 1)
    out = pl.pallas_call(
        lambda *refs: gather_kernel(axes, len(riders), *refs),
        out_shape=shapes,
        in_specs=[pl.BlockSpec(memory_space=pl.ANY)] * len(shapes),
        out_specs=[pl.BlockSpec(memory_space=pl.ANY)] * len(shapes),
        scratch_shapes=[
            pltpu.SemaphoreType.DMA,
            pltpu.SemaphoreType.DMA((4, count, PIECES)),
            pltpu.SemaphoreType.DMA((count, PIECES)),
            pltpu.SemaphoreType.DMA((number,)),
            pltpu.SemaphoreType.DMA((number, others)),
            pltpu.SemaphoreType.DMA((number, others)),
            pltpu.SemaphoreType.DMA((carried, others)),
            pltpu.SemaphoreType.DMA((carried, others)),
        ],
        compiler_params=pltpu.CompilerParams(collective_id=collective_id, has_side_effects=True),
        name="gather_rows",
    )(own, *blocks, *riders)
    return [out[0].reshape(count * rows, width)] + list(out[1:])


FAR_FIRST = ((3, 3, 0, 0), (2, 0, 3, 1), (1, 2, 1, 2), (0, 1, 2, 3))
COLUMNS = 512
STRIP = 16
EXTRA_ROWS = 48


def pick_by(line, table):
    value = jnp.int32(table[LINE - 1])
    for k in range(LINE - 2, -1, -1):
        value = jnp.where(line == k, jnp.int32(table[k]), value)
    return value


def scatter_kernel(kind, axes, riders, *refs):
    refs = list(refs)

    def take(number):
        taken = refs[:number]
        del refs[:number]
        return taken

    with_slots = kind == "slots"
    l_ref, r_ref = take(2)
    q_ref, v_ref = take(2) if with_slots else (None, None)
    (extra_ref,) = take(1) if kind == "extra" else (None,)
    count = len(axes)
    blocks, sources = take(count), take(riders)
    (out_ref,), wholes, targets = take(1), take(count), take(riders)
    (
        part, met, paired, passed, core_send, core_recv, pair_send, pair_recv,
        line_send, line_recv, block_sem, block_send, block_recv, ride_send, ride_recv,
    ) = refs
    me = lax.axis_index("expert")
    line, pair, core = place_of(me)
    rows, width = out_ref.shape
    piece_rows = rows // PIECES
    others = lax.axis_size("dp") - 1 if count + riders else 0
    greet_dp(others)
    greet(line, pair, core, others)
    ridden = ride(sources, targets, ride_send, ride_recv)
    ridden += share(blocks, wholes, axes, block_sem, block_send, block_recv)
    sibling = index_of(line, pair, 1 - core)
    across = index_of(line, 1 - pair, core)
    sent = []

    def produce(dest, target, added):
        extra = 0 if extra_ref is None else EXTRA_ROWS
        dense = rows - extra
        start = pl.multiple_of(dest * dense, 64)

        @pl.loop(0, width // COLUMNS)
        def _(tile):
            columns = pl.ds(pl.multiple_of(tile * COLUMNS, COLUMNS), COLUMNS)
            total = jnp.dot(
                l_ref[pl.ds(start, dense), :], r_ref[:, columns], preferred_element_type=F32
            )
            if with_slots:
                per = q_ref.shape[1]
                per_dest = rows // per
                total = total + jnp.concatenate(
                    [
                        jnp.dot(
                            q_ref[dest * per_dest + k],
                            v_ref[dest * per_dest + k, :, columns],
                            preferred_element_type=F32,
                        )
                        for k in range(per_dest)
                    ],
                    axis=0,
                )
            if added:
                total = total + target[:dense, columns].astype(F32)
            target[:dense, columns] = total.astype(BF)

        if extra:
            per, wide = extra_ref.shape[2:]
            if not added:
                target[dense:, :] = jnp.zeros((extra, width), BF)
            for unit in range(extra_ref.shape[0] * per // STRIP):
                owner, first = (unit * STRIP) // per, (unit * STRIP) % per
                high = unit % (extra // STRIP)
                left_at = (unit // (extra // STRIP)) * wide
                at = pl.ds(dense + high * STRIP, STRIP)
                term = extra_ref[owner, dest, pl.ds(first, STRIP), :]
                if added:
                    term = term.astype(F32) + target[at, left_at : left_at + wide].astype(F32)
                target[at, left_at : left_at + wide] = term.astype(BF)

    def send(condition, source, dest, send_at, recv_at, target):
        copy = pltpu.make_async_remote_copy(
            src_ref=source,
            dst_ref=dest,
            send_sem=send_at,
            recv_sem=recv_at,
            device_id={"expert": target},
            device_id_type=MESH,
        )
        when(condition, copy.start)
        sent.append((condition, copy))

    def await_block(condition, block, recv_at, send_at):
        copy = pltpu.make_async_remote_copy(
            src_ref=block,
            dst_ref=block,
            send_sem=send_at,
            recv_sem=recv_at,
            device_id={"expert": me},
            device_id_type=MESH,
        )
        when(condition, copy.wait_recv)

    dest_line = [pick_by(line, FAR_FIRST[step]) for step in range(LINE)]

    def chip(i):
        return (dest_line[i // 2], (1 - pair) if i % 2 == 0 else pair)

    def meet(i):
        await_block(None, met.at[i], core_recv.at[i], core_send.at[i])
        there, other = chip(i)
        produce(index_of(there, other, core), met.at[i], True)
        if i % 2 == 0:
            for piece in range(PIECES):
                at = pl.ds(piece * piece_rows, piece_rows)
                send(
                    None,
                    met.at[i, at],
                    paired.at[i // 2, at],
                    pair_send.at[i // 2, piece],
                    pair_recv.at[i // 2, piece],
                    across,
                )

    for i in range(2 * LINE):
        there, other = chip(i)
        produce(index_of(there, other, 1 - core), part.at[i], False)
        send(None, part.at[i], met.at[i], core_send.at[i], core_recv.at[i], sibling)
        if i > 0:
            meet(i - 1)
    meet(2 * LINE - 1)

    def add_strips(target, first, others):
        @pl.loop(0, piece_rows // STRIP)
        def _(strip):
            for columns in range(0, width, COLUMNS):
                at = pl.ds(pl.multiple_of(first + strip * STRIP, STRIP), STRIP)
                cols = pl.ds(columns, COLUMNS)
                total = None
                for other in others:
                    term = other[at, cols].astype(F32)
                    total = term if total is None else total + term
                target[at, cols] = total.astype(target.dtype)

    for step in range(LINE - 1):
        there = dest_line[step]
        ahead = there > line
        way = jnp.where(ahead, 1, -1)
        behind = line - way
        held = (behind >= 0) & (behind < LINE)
        target = index_of(line + way, pair, core)
        slot = jnp.where((there == line + way) & (way < 0), LINE, there)
        for piece in range(PIECES):
            first = piece * piece_rows
            at = pl.ds(first, piece_rows)
            await_block(
                None, paired.at[step, at], pair_recv.at[step, piece], pair_send.at[step, piece]
            )
            await_block(
                held, passed.at[there, at], line_recv.at[there, piece], line_send.at[step, piece]
            )

            @pl.when(held)
            def _():
                add_strips(
                    paired.at[step],
                    first,
                    [paired.at[step], met.at[2 * step + 1], passed.at[there]],
                )

            @pl.when(jnp.logical_not(held))
            def _():
                add_strips(paired.at[step], first, [paired.at[step], met.at[2 * step + 1]])

            send(
                None,
                paired.at[step, at],
                passed.at[slot, at],
                line_send.at[step, piece],
                line_recv.at[slot, piece],
                target,
            )
    step = LINE - 1
    from_left, from_right = line > 0, line < LINE - 1
    for piece in range(PIECES):
        first = piece * piece_rows
        at = pl.ds(first, piece_rows)
        await_block(
            None, paired.at[step, at], pair_recv.at[step, piece], pair_send.at[step, piece]
        )
        add_strips(out_ref, first, [paired.at[step], met.at[2 * step + 1]])
        for held, slot in ((from_left, line), (from_right, LINE)):
            await_block(
                held, passed.at[slot, at], line_recv.at[slot, piece], line_send.at[0, piece]
            )

            @pl.when(held)
            def _():
                add_strips(out_ref, first, [out_ref, passed.at[slot]])

    for condition, copy in sent:
        when(condition, copy.wait_send)
    for copy in ridden:
        copy.wait()


def scatter_rows(
    left, right, collective_id, picks=None, values=None, extra=None, blocks=(), axes=(), riders=()
):
    count = lax.axis_size("expert")
    rows = left.shape[0] // count
    width = right.shape[1]
    operands, kind = [left, right], "plain"
    if picks is not None:
        operands, kind = [left, right, picks, values], "slots"
    if extra is not None:
        operands, kind = [left, right, extra], "extra"
        rows += EXTRA_ROWS
    block = (rows, width)
    in_vmem, anywhere = pl.BlockSpec(memory_space=pltpu.VMEM), pl.BlockSpec(memory_space=pl.ANY)
    number, carried = max(1, len(axes)), max(1, len(riders))
    others = max(1, lax.axis_size("dp") - 1)
    return pl.pallas_call(
        lambda *refs: scatter_kernel(kind, axes, len(riders), *refs),
        out_shape=[jax.ShapeDtypeStruct(block, F32)]
        + whole_shapes(blocks, axes)
        + [jax.ShapeDtypeStruct(rider.shape, rider.dtype) for rider in riders],
        in_specs=[in_vmem] * len(operands) + [anywhere] * (len(axes) + len(riders)),
        out_specs=[in_vmem] + [anywhere] * (len(axes) + len(riders)),
        scratch_shapes=[
            pltpu.VMEM((2 * LINE,) + block, BF),
            pltpu.VMEM((2 * LINE,) + block, BF),
            pltpu.VMEM((LINE,) + block, BF),
            pltpu.VMEM((LINE + 1,) + block, BF),
            pltpu.SemaphoreType.DMA((2 * LINE,)),
            pltpu.SemaphoreType.DMA((2 * LINE,)),
            pltpu.SemaphoreType.DMA((LINE, PIECES)),
            pltpu.SemaphoreType.DMA((LINE, PIECES)),
            pltpu.SemaphoreType.DMA((LINE, PIECES)),
            pltpu.SemaphoreType.DMA((LINE + 1, PIECES)),
            pltpu.SemaphoreType.DMA((number,)),
            pltpu.SemaphoreType.DMA((number, others)),
            pltpu.SemaphoreType.DMA((number, others)),
            pltpu.SemaphoreType.DMA((carried, others)),
            pltpu.SemaphoreType.DMA((carried, others)),
        ],
        compiler_params=pltpu.CompilerParams(
            collective_id=collective_id, has_side_effects=True, vmem_limit_bytes=VMEM_LIMIT
        ),
        name="scatter_rows",
    )(*operands, *blocks, *riders)


TILE_GROUPS = 4
SCALE = (DN + DR) ** (-0.5)


def half_turn(values):
    lane = lax.broadcasted_iota(jnp.int32, values.shape, 1)
    lower = (lane // (DR // 2)) % 2 == 0
    return jnp.where(lower, pltpu.roll(values, 128 - DR // 2, 1), pltpu.roll(values, DR // 2, 1))


def group_mask(column_ref, row_ref):
    column, row = column_ref[...], row_ref[0]
    shape = (column.shape[0], row.shape[1])
    earlier = lax.broadcasted_iota(jnp.int32, shape, 1) <= lax.broadcasted_iota(
        jnp.int32, shape, 0
    )
    same = (column == row) | ((row % 4 == 0) & (column // 4 == row // 4))
    return earlier & same


def softmax_scores(query, key, mask):
    scores = jnp.where(mask, dot_right(query, key) * SCALE, -1e30)
    powers = jnp.exp(scores - jnp.max(scores, axis=-1, keepdims=True))
    return powers / jnp.sum(powers, axis=-1, keepdims=True)


def attention_forward_kernel(
    x_ref, gain_ref, first_ref, latent_gain_ref, up_ref, trig_ref, column_ref, row_ref,
    normed_ref, query_ref, key_ref, value_ref, unit_ref, low_ref, scale_ref, attended_ref,
):
    rank = up_ref.shape[0]
    inputs = x_ref[...].astype(F32)
    scale = lax.rsqrt(jnp.mean(inputs * inputs, axis=1, keepdims=True) + EPS)
    normed_ref[...] = (inputs * scale * gain_ref[...]).astype(BF)
    out = dot(normed_ref[...], first_ref[...])
    latent = out[:, DN : DN + rank]
    latent_scale = lax.rsqrt(jnp.mean(latent * latent, axis=1, keepdims=True) + EPS)
    scale_ref[...] = latent_scale
    unit = latent * latent_scale
    unit_ref[...] = unit.astype(BF)
    low_ref[...] = (unit * latent_gain_ref[...]).astype(BF)
    keys_values = dot(low_ref[...], up_ref[...])
    rope = out[:, DN + rank :]
    turned = rope * trig_ref[:, :128] + half_turn(rope) * trig_ref[:, 128:]
    lane = lax.broadcasted_iota(jnp.int32, turned.shape, 1)
    query_ref[:, :DN] = out[:, :DN].astype(BF)
    query_ref[:, DN:] = jnp.where(lane < DR, pltpu.roll(turned, DR, 1), 0.0).astype(BF)
    key_ref[:, :DN] = keys_values[:, :DN].astype(BF)
    key_ref[:, DN:] = jnp.where(lane < DR, turned, 0.0).astype(BF)
    value_ref[...] = keys_values[:, DN:].astype(BF)
    probs = softmax_scores(query_ref[...], key_ref[...], group_mask(column_ref, row_ref))
    attended_ref[...] = dot(probs.astype(BF), value_ref[...]).astype(BF)


def attention_forward(x, gain, first_w, latent_gain, up_w, trig, column, row):
    width, rank = first_w.shape[0], up_w.shape[0]
    span, rows = column.shape[0], row.shape[2]

    def tile(columns):
        return pl.BlockSpec((rows, columns), lambda i: (i, 0))

    def fixed(shape):
        return pl.BlockSpec(shape, lambda i: (0, 0))

    outs = (width, 2 * DN, 2 * DN, DV, rank, rank, 1, DV)
    kinds = (BF, BF, BF, BF, BF, BF, F32, BF)
    return pl.pallas_call(
        attention_forward_kernel,
        grid=(span // rows,),
        in_specs=[
            tile(width),
            fixed((1, width)),
            fixed(first_w.shape),
            fixed((1, rank)),
            fixed(up_w.shape),
            tile(trig.shape[1]),
            tile(1),
            pl.BlockSpec((1, 1, rows), lambda i: (i, 0, 0)),
        ],
        out_specs=[tile(columns) for columns in outs],
        out_shape=[jax.ShapeDtypeStruct((span, c), k) for c, k in zip(outs, kinds)],
        compiler_params=pltpu.CompilerParams(vmem_limit_bytes=VMEM_LIMIT),
        name="attention_forward",
    )(x, gain[None], first_w, latent_gain[None], up_w, trig, column, row)


def attention_backward_kernel(
    r_ref, output_ref, attended_ref, query_ref, key_ref, value_ref, column_ref, row_ref, trig_ref,
    unit_ref, low_ref, scale_ref, latent_gain_ref, up_ref, normed_ref,
    grad_ref, output_grad_ref, up_grad_ref, first_grad_ref, gain_grad_ref, kv_ref,
):
    step = pl.program_id(0)
    rank = up_ref.shape[0]

    @pl.when(step == 0)
    def _():
        output_grad_ref[...] = jnp.zeros_like(output_grad_ref)
        up_grad_ref[...] = jnp.zeros_like(up_grad_ref)
        first_grad_ref[...] = jnp.zeros_like(first_grad_ref)
        gain_grad_ref[...] = jnp.zeros_like(gain_grad_ref)

    attended_grad = dot_right(r_ref[...], output_ref[...]).astype(BF)
    output_grad_ref[...] += dot_left(attended_ref[...], r_ref[...])
    probs = softmax_scores(query_ref[...], key_ref[...], group_mask(column_ref, row_ref))
    kv_ref[:, DN:] = dot_left(probs.astype(BF), attended_grad).astype(BF)
    probs_grad = dot_right(attended_grad, value_ref[...])
    inner = jnp.sum(probs * probs_grad, axis=1, keepdims=True)
    score_grad = (probs * (probs_grad - inner)).astype(BF)
    query_grad = dot(score_grad, key_ref[...]) * SCALE
    key_grad = dot_left(score_grad, query_ref[...]) * SCALE
    kv_ref[:, :DN] = key_grad[:, :DN].astype(BF)
    grad_ref[:, :DN] = query_grad[:, :DN].astype(BF)
    rope = key_grad[:, DN:] + pltpu.roll(query_grad[:, DN:], DR, 1)
    rope = rope * trig_ref[:, :128] + half_turn(rope * trig_ref[:, 128:])
    grad_ref[:, DN + rank :] = rope.astype(BF)
    out_grad = dot_right(kv_ref[...], up_ref[...])
    unit = unit_ref[...].astype(F32)
    gain_grad_ref[...] += jnp.sum(out_grad * unit, axis=0, keepdims=True)
    scaled = out_grad * latent_gain_ref[...]
    inner = jnp.mean(scaled * unit, axis=1, keepdims=True)
    grad_ref[:, DN : DN + rank] = (scale_ref[...] * (scaled - unit * inner)).astype(BF)
    up_grad_ref[...] += dot_left(low_ref[...], kv_ref[...])
    first_grad_ref[...] += dot_left(normed_ref[...], grad_ref[...])


def attention_backward(residual_all, output_w, stored, column, row, trig, latent_gain, up_w):
    normed, query, key, value, unit, low, scale, attended = stored
    width, rank = residual_all.shape[1], up_w.shape[0]
    span, rows = column.shape[0], row.shape[2]
    first_width = 2 * DN + rank

    def tile(columns):
        return pl.BlockSpec((rows, columns), lambda i: (i, 0))

    def fixed(shape):
        return pl.BlockSpec(shape, lambda i: (0, 0))

    sums = (output_w.shape, up_w.shape, (width, first_width), (1, rank))
    return pl.pallas_call(
        attention_backward_kernel,
        grid=(span // rows,),
        in_specs=[
            tile(width),
            fixed(output_w.shape),
            tile(DV),
            tile(2 * DN),
            tile(2 * DN),
            tile(DV),
            tile(1),
            pl.BlockSpec((1, 1, rows), lambda i: (i, 0, 0)),
            tile(trig.shape[1]),
            tile(rank),
            tile(rank),
            tile(1),
            fixed((1, rank)),
            fixed(up_w.shape),
            tile(width),
        ],
        out_specs=[tile(first_width)] + [fixed(shape) for shape in sums],
        out_shape=[jax.ShapeDtypeStruct((span, first_width), BF)]
        + [jax.ShapeDtypeStruct(shape, F32) for shape in sums],
        scratch_shapes=[pltpu.VMEM((rows, DN + DV), BF)],
        compiler_params=pltpu.CompilerParams(vmem_limit_bytes=VMEM_LIMIT),
        name="attention_backward",
    )(
        residual_all, output_w, attended, query, key, value, column, row, trig,
        unit, low, scale, latent_gain[None], up_w, normed,
    )


HIDDEN = 256
ROUTER_AT = 448


def expert_layer_kernel(
    ffn_ref, y_ref, code_row_ref, code_column_ref, wide_ref, shared_down_ref,
    gate_w_ref, up_w_ref, down_w_ref,
    rows_ref, ups_ref, scaled_ref, gate_ref, up_ref, grad_ref, left_ref, mixed_ref,
    down_grad_ref, wide_grad_ref,
    inner_ref, returned_ref, slot_gate_ref, slot_dot_ref,
):
    step = pl.program_id(0)
    me = lax.axis_index("expert")
    experts = lax.axis_size("expert")
    groups, _, per = code_row_ref.shape
    slots = rows_ref.shape[0] // groups
    width = ffn_ref.shape[1]
    hidden = gate_w_ref.shape[1]

    @pl.when(step == 0)
    def _():
        down_grad_ref[...] = jnp.zeros_like(down_grad_ref)
        wide_grad_ref[...] = jnp.zeros_like(wide_grad_ref)

    out = dot(ffn_ref[...], wide_ref[...])
    gates, ups = out[:, :HIDDEN], out[:, HIDDEN:]
    last = out[:, 2 * HIDDEN - 128 :]
    lane = lax.broadcasted_iota(jnp.int32, last.shape, 1)
    first_lane = ROUTER_AT - (2 * HIDDEN - 128)
    logits = jnp.where((lane >= first_lane) & (lane < first_lane + experts), last, -1e30)
    powers = jnp.exp(logits - jnp.max(logits, axis=1, keepdims=True))
    probs = powers / jnp.sum(powers, axis=1, keepdims=True)
    own_lane = (lane == first_lane + me).astype(F32)
    own_probs = jnp.sum(probs * own_lane, axis=1, keepdims=True)
    sigmoid = 1.0 / (1.0 + jnp.exp(-gates))
    silu = gates * sigmoid
    shared_low = (silu * ups).astype(BF)
    back = dot_right(y_ref[...], shared_down_ref[...])
    left_ref[:, :HIDDEN] = (back * ups * sigmoid * (1.0 + gates * (1.0 - sigmoid))).astype(BF)
    shared_up_low = back * silu
    left_ref[:, HIDDEN : 2 * HIDDEN - 128] = shared_up_low[:, : HIDDEN - 128].astype(BF)
    shared_last = shared_up_low[:, HIDDEN - 128 :]
    down_grad_ref[...] += dot_left(shared_low, y_ref[...])

    square = (per, per)
    diagonal = lax.broadcasted_iota(jnp.int32, square, 0) == lax.broadcasted_iota(
        jnp.int32, square, 1
    )
    for group in range(groups):
        tokens_at = pl.ds(group * per, per)
        slots_at = pl.ds(group * slots, slots)
        slot_ids = lax.broadcasted_iota(jnp.int32, (slots, per), 0)
        picks = slot_ids == code_row_ref[group]
        picks_low = picks.astype(F32).astype(BF)
        rows_ref[slots_at] = dot(picks_low, ffn_ref[tokens_at]).astype(BF)
        ups_ref[slots_at] = dot(picks_low, y_ref[tokens_at]).astype(BF)
        own_column = own_probs[group * per : (group + 1) * per]
        own_row = jnp.sum(jnp.where(diagonal, own_column, 0.0), axis=0, keepdims=True)
        slot_gate_ref[slots_at] = jnp.sum(
            jnp.where(picks, own_row, 0.0), axis=1, keepdims=True
        )
    slot_dot_ref[...] = jnp.zeros_like(slot_dot_ref)

    def hidden_part(columns):
        gate_part = dot(rows_ref[...], gate_w_ref[:, columns])
        up_part = dot(rows_ref[...], up_w_ref[:, columns])
        raw = dot_right(ups_ref[...], down_w_ref[columns, :])
        slot_gate = slot_gate_ref[...]
        sigmoid = 1.0 / (1.0 + jnp.exp(-gate_part))
        silu = gate_part * sigmoid
        inner = silu * up_part
        slot_dot_ref[...] += jnp.sum(inner * raw, axis=1, keepdims=True)
        grad = raw * slot_gate
        inner_ref[:, columns] = inner.astype(BF)
        scaled_ref[:, columns] = (inner * slot_gate).astype(BF)
        gate_ref[:, columns] = (
            grad * up_part * sigmoid * (1.0 + gate_part * (1.0 - sigmoid))
        ).astype(BF)
        up_ref[:, columns] = (grad * silu).astype(BF)

    @pl.loop(0, hidden // HIDDEN)
    def _(tile):
        hidden_part(pl.ds(pl.multiple_of(tile * HIDDEN, HIDDEN), HIDDEN))

    if hidden % HIDDEN:
        hidden_part(pl.ds(hidden - hidden % HIDDEN, hidden % HIDDEN))

    @pl.loop(0, width // COLUMNS)
    def _(tile):
        columns = pl.ds(pl.multiple_of(tile * COLUMNS, COLUMNS), COLUMNS)
        returned_ref[:, columns] = dot(inner_ref[...], down_w_ref[:, columns]).astype(BF)
        grad_ref[:, columns] = (
            dot_right(gate_ref[...], gate_w_ref[columns, :])
            + dot_right(up_ref[...], up_w_ref[columns, :])
        ).astype(BF)

    for group in range(groups):
        tokens_at = pl.ds(group * per, per)
        slots_at = pl.ds(group * slots, slots)
        own_column = own_probs[group * per : (group + 1) * per]
        slot_lane = lax.broadcasted_iota(jnp.int32, (per, slots), 1)
        picks = slot_lane == code_column_ref[tokens_at]
        pick_gate = jnp.where(picks, own_column, 0.0).astype(BF)
        mixed_ref[tokens_at] = (
            dot(shared_low[group * per : (group + 1) * per], shared_down_ref[...])
            + dot(pick_gate, returned_ref[slots_at])
        ).astype(BF)
        small = (slots, slots)
        eye = lax.broadcasted_iota(jnp.int32, small, 0) == lax.broadcasted_iota(
            jnp.int32, small, 1
        )
        dot_row = jnp.sum(jnp.where(eye, slot_dot_ref[slots_at], 0.0), axis=0, keepdims=True)
        row_dot = jnp.sum(jnp.where(picks, dot_row, 0.0), axis=1, keepdims=True)
        at = slice(group * per, (group + 1) * per)
        logit_grad = row_dot * own_column * (own_lane[at] - probs[at])
        high = logit_grad.astype(BF)
        rest = logit_grad - high.astype(F32)
        left_ref[tokens_at, 2 * HIDDEN - 128 :] = jnp.where(
            lane[at] < first_lane,
            shared_last[at],
            high.astype(F32) + pltpu.roll(rest, experts, 1),
        ).astype(BF)
    wide_grad_ref[...] += dot_left(ffn_ref[...], left_ref[...])


def expert_layer(ffn_all, upstream_all, code, slots, wide, shared_down, weights):
    groups, per = code.shape
    span, width = ffn_all.shape
    gate_w, up_w, down_w = weights
    hidden = gate_w.shape[1]
    rows, slot_rows = TILE_GROUPS * per, TILE_GROUPS * slots
    total = groups * slots

    def tile(count, columns):
        return pl.BlockSpec((count, columns), lambda i: (i, 0))

    def fixed(shape):
        return pl.BlockSpec(shape, lambda i: (0, 0), pipeline_mode=pl.Buffered(1))

    def summed(shape):
        return pl.BlockSpec(shape, lambda i: (0, 0))

    outs = [(total, width)] * 2 + [(total, hidden)] * 3 + [(total, width)]
    outs += [(span, 2 * HIDDEN), (span, width)]
    sums = [shared_down.shape, wide.shape]
    return pl.pallas_call(
        expert_layer_kernel,
        grid=(groups // TILE_GROUPS,),
        in_specs=[
            tile(rows, width),
            tile(rows, width),
            pl.BlockSpec((TILE_GROUPS, 1, per), lambda i: (i, 0, 0)),
            tile(rows, 1),
            fixed(wide.shape),
            fixed(shared_down.shape),
            fixed(gate_w.shape),
            fixed(up_w.shape),
            fixed(down_w.shape),
        ],
        out_specs=[
            tile(slot_rows if shape[0] == total else rows, shape[1]) for shape in outs
        ]
        + [summed(shape) for shape in sums],
        out_shape=[jax.ShapeDtypeStruct(shape, BF) for shape in outs]
        + [jax.ShapeDtypeStruct(shape, F32) for shape in sums],
        scratch_shapes=[
            pltpu.VMEM((slot_rows, hidden), BF),
            pltpu.VMEM((slot_rows, width), BF),
            pltpu.VMEM((slot_rows, 1), F32),
            pltpu.VMEM((slot_rows, 1), F32),
        ],
        compiler_params=pltpu.CompilerParams(vmem_limit_bytes=VMEM_LIMIT),
        name="expert_layer",
    )(
        ffn_all, upstream_all, code[:, None, :], code.reshape(span, 1), wide, shared_down,
        gate_w, up_w, down_w,
    )


def on_device(
    tokens,
    segment,
    routes,
    drop_order,
    cotangent,
    attn_gain,
    query_weight,
    down_latent,
    latent_gain,
    up_latent,
    output_weight,
    ffn_gain,
    router_weight,
    shared_gate,
    shared_up,
    shared_down,
    expert_gate,
    expert_up,
    expert_down,
):
    n_e = lax.axis_size("expert")
    n_d = lax.axis_size("dp")
    me_e = lax.axis_index("expert")
    me_d = lax.axis_index("dp")
    micro, group_rows, width = tokens.shape
    own_rows = micro * group_rows
    span = n_e * own_rows
    groups = n_e * micro
    top = routes.shape[2]
    experts = n_e * expert_gate.shape[0]
    capacity = (5 * group_rows * top + 4 * experts - 1) // (4 * experts)
    slots = -(-capacity // 16) * 16
    rank_latent = latent_gain.shape[0] * n_e * n_d

    def gather(values):
        return lax.all_gather(values, "expert", axis=0, tiled=True)

    def scatter(values):
        return lax.psum_scatter(values, "expert", scatter_dimension=0, tiled=True)

    def sum_dp(values, axis):
        size = values.shape[axis] // n_d

        def part(step):
            at = lax.rem(me_d + step, n_d) * size
            return lax.dynamic_slice_in_dim(values, at, size, axis)

        total = part(0).astype(F32)
        for step in range(1, n_d):
            pairs = [(i, (i + step) % n_d) for i in range(n_d)]
            total = total + lax.ppermute(part(step).astype(BF), "dp", pairs).astype(F32)
        return total

    def grad_dp(left, right, axis):
        size = (left, right)[axis].shape[1] // n_d
        parts = []
        for step in range(n_d):
            at = lax.rem(me_d + step, n_d) * size
            if axis == 0:
                part = dot_left(lax.dynamic_slice_in_dim(left, at, size, 1), right)
            else:
                part = dot_left(left, lax.dynamic_slice_in_dim(right, at, size, 1))
            parts.append(part.astype(BF) if step else part)
        return (stack(parts[1:]), parts[0])

    def split_dp(values, axis):
        size = values.shape[axis] // n_d
        parts = []
        for step in range(n_d):
            at = lax.rem(me_d + step, n_d) * size
            parts.append(lax.dynamic_slice_in_dim(values, at, size, axis))
        return (stack([part.astype(BF) for part in parts[1:]]), parts[0])

    def stack(parts):
        return parts[0][None] if len(parts) == 1 else jnp.stack(parts)

    def add_all(total, parts):
        for step in range(n_d - 1):
            total = total + parts[step].astype(F32)
        return total

    small_rows = attn_gain.shape[0]
    latent_all_width = down_latent.shape[1]
    latent_piece = latent_gain.shape[0]
    packed = jnp.concatenate(
        [
            down_latent,
            router_weight,
            attn_gain[:, None],
            ffn_gain[:, None],
            jnp.pad(latent_gain, (0, small_rows - latent_piece))[:, None],
        ],
        axis=1,
    )
    packed = lax.all_gather(packed, ("dp", "expert"), axis=0, tiled=True)
    down_all = packed[:, :latent_all_width]
    router_all = packed[:, latent_all_width : latent_all_width + experts]
    rest = packed[:, latent_all_width + experts :].astype(F32)
    attn_gain_all = rest[:, 0]
    ffn_gain_all = rest[:, 1]
    latent_gain_all = rest[:, 2].reshape(n_e * n_d, small_rows)[:, :latent_piece].reshape(-1)

    chosen = jnp.sum(
        (routes[..., None] == jnp.arange(experts, dtype=jnp.int32)).astype(jnp.int32), axis=2
    )
    order = drop_order[:, 0]
    earlier = (order[:, None, :] < order[:, :, None]).astype(F32)
    rank = jnp.einsum("mtu,mue->mte", earlier, chosen.astype(F32)).astype(jnp.int32)
    code = jnp.where((chosen == 1) & (rank < capacity), rank, -1).reshape(own_rows, experts)

    tokens_own = tokens.reshape(own_rows, width)
    code_lanes = -(-experts // 128) * 128
    code_low = jnp.pad(code.astype(BF), ((0, 0), (0, code_lanes - experts)))
    (
        tokens_all,
        query_w,
        up_w,
        output_w,
        shared_gate_w,
        shared_up_w,
        shared_down_w,
        gate_w,
    ) = gather_rows(
        jnp.concatenate([tokens_own, code_low], axis=1),
        5,
        (
            query_weight,
            up_latent,
            output_weight,
            shared_gate,
            shared_up,
            shared_down,
            expert_gate[0],
        ),
        (0, 0, 1, 0, 0, 1, 0),
    )
    upstream_own = cotangent.reshape(own_rows, width)
    upstream_later, tokens_all = lax.optimization_barrier((upstream_own, tokens_all))
    upstream_all = gather(upstream_later)
    code_all = tokens_all[:, width : width + experts].astype(jnp.int32)
    my_code = lax.dynamic_slice_in_dim(code_all, me_e, 1, 1).reshape(groups, group_rows)
    picks = my_code[:, :, None] == jnp.arange(slots, dtype=jnp.int32)[None, None, :]
    picks_low = picks.astype(BF)

    span_segment = (
        segment.reshape(micro, n_e, group_rows).transpose(1, 0, 2).reshape(groups, group_rows)
    )
    trig = angles(positions(span_segment), group_rows)
    marks = span_segment + 4 * jnp.arange(groups, dtype=jnp.int32)[:, None]
    column = marks.reshape(span, 1)
    row = marks.reshape(groups // TILE_GROUPS, 1, TILE_GROUPS * group_rows)
    first_w = jnp.concatenate(
        [
            query_w[:, :DN],
            down_all[:, :rank_latent],
            down_all[:, rank_latent:],
            query_w[:, DN:],
        ],
        axis=1,
    )
    stored = attention_forward(
        tokens_all, attn_gain_all, first_w, latent_gain_all, up_w, trig, column, row
    )
    attention_out, up_e_w = scatter_rows(
        stored[-1], output_w, 2, blocks=(expert_up[0],), axes=(0,)
    )
    residual = tokens_own.astype(F32) + attention_out

    second_scale = rms_scale(residual)
    ffn_in = (residual * second_scale * ffn_gain_all).astype(BF)
    ffn_all, down_e_w = gather_rows(ffn_in, 1, (expert_down[0],), (1,))

    shared_hidden = shared_gate_w.shape[1]
    wide = jnp.concatenate(
        [
            jnp.pad(shared_gate_w, ((0, 0), (0, HIDDEN - shared_hidden))),
            jnp.pad(shared_up_w, ((0, 0), (0, ROUTER_AT - HIDDEN - shared_hidden))),
            jnp.pad(router_all, ((0, 0), (0, 2 * HIDDEN - ROUTER_AT - experts))),
        ],
        axis=1,
    )
    (
        expert_rows,
        slot_up,
        inner_scaled,
        gate_low,
        up_low,
        rows_grad,
        left,
        mixed_part,
        shared_down_grad,
        wide_grad,
    ) = expert_layer(
        ffn_all,
        upstream_all,
        my_code,
        slots,
        wide,
        jnp.pad(shared_down_w, ((0, HIDDEN - shared_hidden), (0, 0))),
        (gate_w, up_e_w, down_e_w),
    )
    mixed = residual + scatter(mixed_part).astype(F32)
    down_later, down_now = grad_dp(inner_scaled, slot_up, 1)
    gate_later, gate_now = grad_dp(expert_rows, gate_low, 0)
    up_later, up_now = grad_dp(expert_rows, up_low, 0)
    router_grad = (
        wide_grad[:, ROUTER_AT : ROUTER_AT + experts]
        + wide_grad[:, ROUTER_AT + experts : ROUTER_AT + 2 * experts]
    )
    shared_down_later, shared_down_now = split_dp(shared_down_grad[:shared_hidden], 1)
    shared_gate_later, shared_gate_now = split_dp(wide_grad[:, :shared_hidden], 0)
    shared_up_later, shared_up_now = split_dp(wide_grad[:, HIDDEN : HIDDEN + shared_hidden], 0)
    wide_again = jnp.concatenate(
        [wide[:, : ROUTER_AT + experts], router_all, wide[:, ROUTER_AT + 2 * experts :]], axis=1
    )
    ffn_grad, down_parts = scatter_rows(
        left,
        wide_again.T,
        3,
        picks_low,
        rows_grad.reshape(groups, slots, width),
        riders=(down_later,),
    )
    residual_part, ffn_gain_grad = norm_back(residual, second_scale, ffn_gain_all, ffn_grad)
    residual_grad = upstream_own.astype(F32) + residual_part
    (
        residual_all,
        gate_parts,
        shared_down_parts,
        shared_gate_parts,
        shared_up_parts,
    ) = gather_rows(
        residual_grad.astype(BF),
        6,
        riders=(gate_later, shared_down_later, shared_gate_later, shared_up_later),
    )

    first_grad, output_weight_grad, up_latent_grad, first_w_grad, latent_gain_grad = (
        attention_backward(
            residual_all, output_w, stored, column, row, trig, latent_gain_all, up_w
        )
    )
    rope_at = DN + latent_all_width
    query_weight_grad = jnp.concatenate(
        [first_w_grad[:, :DN], first_w_grad[:, rope_at:]], axis=1
    )
    down_grad = first_w_grad[:, DN:rope_at]
    attn_gain_grad = jnp.sum(first_w_grad * first_w.astype(F32), axis=1) / attn_gain_all
    small = jnp.concatenate(
        [
            down_grad,
            router_grad,
            attn_gain_grad[:, None],
            ffn_gain_grad[:, None],
            jnp.pad(
                latent_gain_grad.reshape(n_e * n_d, latent_piece),
                ((0, 0), (0, small_rows - latent_piece)),
            ).reshape(-1, 1),
        ],
        axis=1,
    )
    small_width = -(-small.shape[1] // 128) * 128
    small = jnp.pad(small, ((0, 0), (0, small_width - small.shape[1]))).astype(BF)
    small = small.reshape(n_d, n_e, small_rows, small_width)
    query_later, query_now = split_dp(query_weight_grad, 0)
    latent_later, latent_now = split_dp(up_latent_grad, 0)
    output_later, output_now = split_dp(output_weight_grad, 1)
    summed, up_parts, query_parts, latent_parts, output_parts = scatter_rows(
        first_grad,
        first_w.T,
        4,
        extra=small,
        riders=(up_later, query_later, latent_later, output_later),
    )
    normed_grad = summed[:own_rows]
    small = jnp.concatenate(
        [
            summed[own_rows:, k * small_width : (k + 1) * small_width]
            for k in range(width // small_width)
        ],
        axis=0,
    )[: n_d * small_rows]
    small = sum_dp(small, 0)
    own_inputs = tokens_own.astype(F32)
    input_part, _ = norm_back(own_inputs, rms_scale(own_inputs), attn_gain_all, normed_grad)
    tokens_grad = residual_grad + input_part
    last = latent_all_width + experts
    shape = (micro, group_rows, width)
    return (
        mixed.reshape(shape),
        tokens_grad.reshape(shape),
        small[:, last],
        add_all(query_now, query_parts),
        small[:, :latent_all_width],
        small[:latent_piece, last + 2],
        add_all(latent_now, latent_parts),
        add_all(output_now, output_parts),
        small[:, last + 1],
        small[:, latent_all_width:last],
        add_all(shared_gate_now, shared_gate_parts),
        add_all(shared_up_now, shared_up_parts),
        add_all(shared_down_now, shared_down_parts),
        add_all(gate_now, gate_parts)[None],
        add_all(up_now, up_parts)[None],
        add_all(down_now, down_parts)[None],
    )


def solution(mesh):
    rows = P(None, ("dp", "expert"), None)
    split = P(("dp", "expert"))
    split_rows = P(("dp", "expert"), None)
    columns = P("dp", "expert")
    turned = P("expert", "dp")
    expert_in = P("expert", "dp", None)
    expert_out = P("expert", None, "dp")
    return jax.shard_map(
        on_device,
        mesh=mesh,
        in_specs=(
            rows,
            P(None, "dp"),
            rows,
            rows,
            rows,
            split,
            columns,
            split_rows,
            split,
            columns,
            turned,
            split,
            split_rows,
            columns,
            columns,
            turned,
            expert_in,
            expert_in,
            expert_out,
        ),
        out_specs=(
            rows,
            rows,
            split,
            columns,
            split_rows,
            split,
            columns,
            turned,
            split,
            split_rows,
            columns,
            columns,
            turned,
            expert_in,
            expert_in,
            expert_out,
        ),
        check_vma=False,
    )
```

```python
import math

import jax
import jax.numpy as jnp
from jax import lax
from jax.experimental import pallas as pl
from jax.experimental.pallas import tpu as pltpu
from jax.sharding import PartitionSpec as P

DN = 128
DR = 64
DV = 128
EPS = 1e-06
HIGH = lax.Precision.HIGHEST
F32 = jnp.float32
BF = jnp.bfloat16


def dot(former, latter):
    return jnp.dot(former, latter, preferred_element_type=F32)


def dot_left(former, latter):
    return lax.dot_general(former, latter, (((0,), (0,)), ((), ())), preferred_element_type=F32)


def dot_right(former, latter):
    return lax.dot_general(former, latter, (((1,), (1,)), ((), ())), preferred_element_type=F32)


def rms_scale(values):
    return lax.rsqrt(jnp.mean(values * values, axis=-1, keepdims=True) + EPS)


def norm_back(values, scale_rows, gain, out_grad):
    scaled = out_grad * gain
    inner = jnp.mean(scaled * values, axis=-1, keepdims=True)
    value_grad = scale_rows * scaled - values * scale_rows * scale_rows * scale_rows * inner
    return (value_grad, jnp.sum(out_grad * values * scale_rows, axis=0))


def positions(segment):
    places = jnp.arange(segment.shape[1], dtype=jnp.int32)
    prompt_len = jnp.sum((segment == 0).astype(jnp.int32), axis=1, keepdims=True)
    former = (segment[:, None, :] < segment[:, :, None]).astype(jnp.int32)
    seg_start = jnp.sum(former, axis=2)
    return jnp.where(segment == 0, places[None], prompt_len + places[None] - seg_start)


def angles(position, row_count):
    freq_index = jnp.arange(DR // 2, dtype=F32)
    frequency = jnp.exp(freq_index * (-2.0 * math.log(10000.0) / DR))
    turning = jnp.arange(row_count, dtype=F32)[:, None] * frequency[None, :]
    cosine, sine_part = jnp.cos(turning), jnp.sin(turning)
    table = jnp.concatenate([cosine] * 4 + [-sine_part, sine_part] * 2, axis=1)
    picks = (position.reshape(-1)[:, None] == jnp.arange(row_count)[None, :]).astype(F32)
    return jnp.dot(picks, table, precision=HIGH)


LINE = 4
PIECES = 3
MESH = pl.DeviceIdType.MESH
VMEM_LIMIT = 60 * 1024 * 1024


def place_of(me):
    return (me // 4, lax.rem(me // 2, 2), lax.rem(me, 2))


def index_of(line, pair, core):
    return line * 4 + pair * 2 + core


def greet(line, pair, core, others=0):
    barrier = pltpu.get_barrier_semaphore()

    def signal(target):
        pl.semaphore_signal(barrier, inc=1, device_id={"expert": target}, device_id_type=MESH)

    signal(index_of(line, pair, 1 - core))
    signal(index_of(line, 1 - pair, core))

    @pl.when(line > 0)
    def _():
        signal(index_of(line - 1, pair, core))

    @pl.when(line < LINE - 1)
    def _():
        signal(index_of(line + 1, pair, core))

    inner = jnp.where(line > 0, 1, 0) + jnp.where(line < LINE - 1, 1, 0)
    pl.semaphore_wait(barrier, 2 + others + inner)


def greet_dp(others):
    barrier = pltpu.get_barrier_semaphore()
    me_d, n_d = lax.axis_index("dp"), lax.axis_size("dp")
    if others:
        for step in range(1, n_d):
            pl.semaphore_signal(
                barrier,
                inc=1,
                device_id={"dp": lax.rem(me_d + step, n_d)},
                device_id_type=MESH,
            )


def ride(sources, targets, send_sem, recv_sem):
    me_d, n_d = lax.axis_index("dp"), lax.axis_size("dp")
    copies = []
    for number, (source, target) in enumerate(zip(sources, targets)):
        parts = len(source.shape) == len(target.shape)
        for step in range(1, n_d):
            copy = pltpu.make_async_remote_copy(
                src_ref=source.at[step - 1] if parts else source,
                dst_ref=target.at[step - 1],
                send_sem=send_sem.at[number, step - 1],
                recv_sem=recv_sem.at[number, step - 1],
                device_id={"dp": lax.rem(me_d + step, n_d)},
                device_id_type=MESH,
            )
            copy.start()
            copies.append(copy)
    return copies


def landed(rider):
    array, rows = rider
    if rows is None:
        return jax.ShapeDtypeStruct(array.shape, array.dtype)
    shape = (lax.axis_size("dp") - 1, rows[1] - rows[0]) + array.shape[1:]
    return jax.ShapeDtypeStruct(shape, array.dtype)


def cut_rows(ref, rows):
    return ref if rows is None else ref.at[pl.ds(rows[0], rows[1] - rows[0])]


def when(condition, action):
    if condition is None:
        action()
    else:
        pl.when(condition)(action)


def gather_kernel(spans, *refs):
    riders = len(spans)
    refs = list(refs)

    def take(number):
        taken = refs[:number]
        del refs[:number]
        return taken

    (own_ref,), sources = take(1), take(riders)
    (out_ref,), targets = take(1), take(riders)
    own_sem, send_sem, recv_sem, ride_send, ride_recv = refs
    sources = [cut_rows(source, rows) for source, rows in zip(sources, spans)]
    me = lax.axis_index("expert")
    line, pair, core = place_of(me)
    rows = own_ref.shape[0] // PIECES
    others = lax.axis_size("dp") - 1 if riders else 0
    greet_dp(others)
    greet(line, pair, core, others)
    local = [pltpu.make_async_copy(own_ref, out_ref.at[me], own_sem)]
    sent = []

    def push(condition, kind, origin, piece, target, source=None):
        block = out_ref.at[origin, pl.ds(piece * rows, rows)]
        copy = pltpu.make_async_remote_copy(
            src_ref=block if source is None else source,
            dst_ref=block,
            send_sem=send_sem.at[kind, origin, piece],
            recv_sem=recv_sem.at[origin, piece],
            device_id={"expert": target},
            device_id_type=MESH,
        )
        when(condition, copy.start)
        sent.append((condition, copy))

    def arrive(condition, origin, piece):
        block = out_ref.at[origin, pl.ds(piece * rows, rows)]
        copy = pltpu.make_async_remote_copy(
            src_ref=block,
            dst_ref=block,
            send_sem=send_sem.at[0, origin, piece],
            recv_sem=recv_sem.at[origin, piece],
            device_id={"expert": me},
            device_id_type=MESH,
        )
        when(condition, copy.wait_recv)

    left = index_of(line - 1, pair, core)
    right = index_of(line + 1, pair, core)
    across = index_of(line, 1 - pair, core)
    sibling = index_of(line, pair, 1 - core)
    for piece in range(PIECES):
        source = own_ref.at[pl.ds(piece * rows, rows)]
        push(line < LINE - 1, 1, me, piece, right, source)
        push(line > 0, 0, me, piece, left, source)
        push(None, 2, me, piece, across, source)
        push(None, 3, me, piece, sibling, source)
    ridden = ride(sources, targets, ride_send, ride_recv)
    for copy in local:
        copy.start()

    def along(hop):
        for piece in range(PIECES):
            for side in (-1, 1):
                there = line + side * hop
                held = (there >= 0) & (there < LINE)
                origin = index_of(there, pair, core)
                arrive(held, origin, piece)
                if hop < LINE - 1:
                    further = held & ((line < LINE - 1) if side < 0 else (line > 0))
                    kind, target = (1, right) if side < 0 else (0, left)
                    push(further, kind, origin, piece, target)
                push(held, 2, origin, piece, across)
                push(held, 3, origin, piece, sibling)

    def over(hop):
        for piece in range(PIECES):
            for side in (-1, 1) if hop else (1,):
                there = line + side * hop
                held = (there >= 0) & (there < LINE) if hop else None
                origin = index_of(there, 1 - pair, core)
                arrive(held, origin, piece)
                push(held, 3, origin, piece, sibling)

    along(1)
    over(0)
    along(2)
    over(1)
    along(3)
    over(2)
    over(3)
    for other_line in range(LINE):
        for other_pair in range(2):
            for piece in range(PIECES):
                arrive(None, index_of(other_line, other_pair, 1 - core), piece)
    for copy in ridden:
        copy.wait()
    for condition, copy in sent:
        when(condition, copy.wait_send)
    for copy in local:
        copy.wait()


def gather_rows(own, collective_id, riders=()):
    count = lax.axis_size("expert")
    rows, width = own.shape
    shapes = [jax.ShapeDtypeStruct((count, rows, width), own.dtype)]
    shapes += [landed(rider) for rider in riders]
    carried, others = max(1, len(riders)), max(1, lax.axis_size("dp") - 1)
    out = pl.pallas_call(
        lambda *refs: gather_kernel([rider[1] for rider in riders], *refs),
        out_shape=shapes,
        in_specs=[pl.BlockSpec(memory_space=pl.ANY)] * len(shapes),
        out_specs=[pl.BlockSpec(memory_space=pl.ANY)] * len(shapes),
        scratch_shapes=[
            pltpu.SemaphoreType.DMA,
            pltpu.SemaphoreType.DMA((4, count, PIECES)),
            pltpu.SemaphoreType.DMA((count, PIECES)),
            pltpu.SemaphoreType.DMA((carried, others)),
            pltpu.SemaphoreType.DMA((carried, others)),
        ],
        compiler_params=pltpu.CompilerParams(collective_id=collective_id, has_side_effects=True),
        name="gather_rows",
    )(own, *[rider[0] for rider in riders])
    return [out[0].reshape(count * rows, width)] + list(out[1:])


FAR_FIRST = ((3, 3, 0, 0), (2, 0, 3, 1), (1, 2, 1, 2), (0, 1, 2, 3))
COLUMNS = 512
STRIP = 16
EXTRA_ROWS = 48


def pick_by(line, table):
    value = jnp.int32(table[LINE - 1])
    for k in range(LINE - 2, -1, -1):
        value = jnp.where(line == k, jnp.int32(table[k]), value)
    return value


def add_strips(target, first, count, others):
    @pl.loop(0, count // STRIP)
    def _(strip):
        for columns in range(0, target.shape[1], COLUMNS):
            at = pl.ds(pl.multiple_of(first + strip * STRIP, STRIP), STRIP)
            cols = pl.ds(columns, COLUMNS)
            total = None
            for other in others:
                term = other[at, cols].astype(F32)
                total = term if total is None else total + term
            target[at, cols] = total.astype(target.dtype)


def scatter_kernel(kind, spans, *refs):
    riders = len(spans)
    refs = list(refs)

    def take(number):
        taken = refs[:number]
        del refs[:number]
        return taken

    l_ref, r_ref = take(2)
    (extra_ref,) = take(1) if kind == "extra" else (None,)
    sources = [cut_rows(source, rows) for source, rows in zip(take(riders), spans)]
    (out_ref,), targets = take(1), take(riders)
    (
        part, met, paired, passed, core_send, core_recv, pair_send, pair_recv,
        line_send, line_recv, ride_send, ride_recv,
    ) = refs
    me = lax.axis_index("expert")
    line, pair, core = place_of(me)
    rows, width = out_ref.shape
    piece_rows = rows // PIECES
    others = lax.axis_size("dp") - 1 if riders else 0
    greet_dp(others)
    greet(line, pair, core, others)
    ridden = ride(sources, targets, ride_send, ride_recv)
    sibling = index_of(line, pair, 1 - core)
    across = index_of(line, 1 - pair, core)
    sent = []

    def produce(dest, target, added):
        extra = 0 if extra_ref is None else EXTRA_ROWS
        dense = rows - extra
        start = pl.multiple_of(dest * dense, 64)

        @pl.loop(0, width // COLUMNS)
        def _(tile):
            columns = pl.ds(pl.multiple_of(tile * COLUMNS, COLUMNS), COLUMNS)
            total = jnp.dot(
                l_ref[pl.ds(start, dense), :], r_ref[:, columns], preferred_element_type=F32
            )
            if added:
                total = total + target[:dense, columns].astype(F32)
            target[:dense, columns] = total.astype(BF)

        if extra:
            per, wide = extra_ref.shape[2:]
            if not added:
                target[dense:, :] = jnp.zeros((extra, width), BF)
            for unit in range(extra_ref.shape[0] * per // STRIP):
                owner, first = (unit * STRIP) // per, (unit * STRIP) % per
                high = unit % (extra // STRIP)
                left_at = (unit // (extra // STRIP)) * wide
                at = pl.ds(dense + high * STRIP, STRIP)
                term = extra_ref[owner, dest, pl.ds(first, STRIP), :]
                if added:
                    term = term.astype(F32) + target[at, left_at : left_at + wide].astype(F32)
                target[at, left_at : left_at + wide] = term.astype(BF)

    def send(condition, source, dest, send_at, recv_at, target):
        copy = pltpu.make_async_remote_copy(
            src_ref=source,
            dst_ref=dest,
            send_sem=send_at,
            recv_sem=recv_at,
            device_id={"expert": target},
            device_id_type=MESH,
        )
        when(condition, copy.start)
        sent.append((condition, copy))

    def await_block(condition, block, recv_at, send_at):
        copy = pltpu.make_async_remote_copy(
            src_ref=block,
            dst_ref=block,
            send_sem=send_at,
            recv_sem=recv_at,
            device_id={"expert": me},
            device_id_type=MESH,
        )
        when(condition, copy.wait_recv)

    dest_line = [pick_by(line, FAR_FIRST[step]) for step in range(LINE)]

    def chip(i):
        return (dest_line[i // 2], (1 - pair) if i % 2 == 0 else pair)

    def meet(i):
        await_block(None, met.at[i], core_recv.at[i], core_send.at[i])
        there, other = chip(i)
        produce(index_of(there, other, core), met.at[i], True)
        if i % 2 == 0:
            for piece in range(PIECES):
                at = pl.ds(piece * piece_rows, piece_rows)
                send(
                    None,
                    met.at[i, at],
                    paired.at[i // 2, at],
                    pair_send.at[i // 2, piece],
                    pair_recv.at[i // 2, piece],
                    across,
                )

    for i in range(2 * LINE):
        there, other = chip(i)
        produce(index_of(there, other, 1 - core), part.at[i], False)
        send(None, part.at[i], met.at[i], core_send.at[i], core_recv.at[i], sibling)
        if i > 0:
            meet(i - 1)
    meet(2 * LINE - 1)

    for step in range(LINE - 1):
        there = dest_line[step]
        ahead = there > line
        way = jnp.where(ahead, 1, -1)
        behind = line - way
        held = (behind >= 0) & (behind < LINE)
        target = index_of(line + way, pair, core)
        slot = jnp.where((there == line + way) & (way < 0), LINE, there)
        for piece in range(PIECES):
            first = piece * piece_rows
            at = pl.ds(first, piece_rows)
            await_block(
                None, paired.at[step, at], pair_recv.at[step, piece], pair_send.at[step, piece]
            )
            await_block(
                held, passed.at[there, at], line_recv.at[there, piece], line_send.at[step, piece]
            )

            @pl.when(held)
            def _():
                add_strips(
                    paired.at[step],
                    first,
                    piece_rows,
                    [paired.at[step], met.at[2 * step + 1], passed.at[there]],
                )

            @pl.when(jnp.logical_not(held))
            def _():
                add_strips(paired.at[step], first, piece_rows, [paired.at[step], met.at[2 * step + 1]])

            send(
                None,
                paired.at[step, at],
                passed.at[slot, at],
                line_send.at[step, piece],
                line_recv.at[slot, piece],
                target,
            )
    step = LINE - 1
    from_left, from_right = line > 0, line < LINE - 1
    for piece in range(PIECES):
        first = piece * piece_rows
        at = pl.ds(first, piece_rows)
        await_block(
            None, paired.at[step, at], pair_recv.at[step, piece], pair_send.at[step, piece]
        )
        add_strips(out_ref, first, piece_rows, [paired.at[step], met.at[2 * step + 1]])
        for held, slot in ((from_left, line), (from_right, LINE)):
            await_block(
                held, passed.at[slot, at], line_recv.at[slot, piece], line_send.at[0, piece]
            )

            @pl.when(held)
            def _():
                add_strips(out_ref, first, piece_rows, [out_ref, passed.at[slot]])

    for condition, copy in sent:
        when(condition, copy.wait_send)
    for copy in ridden:
        copy.wait()


def scatter_rows(left, right, collective_id, extra=None, riders=()):
    count = lax.axis_size("expert")
    rows = left.shape[0] // count
    width = right.shape[1]
    operands, kind = [left, right], "plain"
    if extra is not None:
        operands, kind = [left, right, extra], "extra"
        rows += EXTRA_ROWS
    block = (rows, width)
    in_vmem, anywhere = pl.BlockSpec(memory_space=pltpu.VMEM), pl.BlockSpec(memory_space=pl.ANY)
    carried = max(1, len(riders))
    others = max(1, lax.axis_size("dp") - 1)
    return pl.pallas_call(
        lambda *refs: scatter_kernel(kind, [rider[1] for rider in riders], *refs),
        out_shape=[jax.ShapeDtypeStruct(block, F32)]
        + [landed(rider) for rider in riders],
        in_specs=[in_vmem] * len(operands) + [anywhere] * len(riders),
        out_specs=[in_vmem] + [anywhere] * len(riders),
        scratch_shapes=[
            pltpu.VMEM((2 * LINE,) + block, BF),
            pltpu.VMEM((2 * LINE,) + block, BF),
            pltpu.VMEM((LINE,) + block, BF),
            pltpu.VMEM((LINE + 1,) + block, BF),
            pltpu.SemaphoreType.DMA((2 * LINE,)),
            pltpu.SemaphoreType.DMA((2 * LINE,)),
            pltpu.SemaphoreType.DMA((LINE, PIECES)),
            pltpu.SemaphoreType.DMA((LINE, PIECES)),
            pltpu.SemaphoreType.DMA((LINE, PIECES)),
            pltpu.SemaphoreType.DMA((LINE + 1, PIECES)),
            pltpu.SemaphoreType.DMA((carried, others)),
            pltpu.SemaphoreType.DMA((carried, others)),
        ],
        compiler_params=pltpu.CompilerParams(
            collective_id=collective_id, has_side_effects=True, vmem_limit_bytes=VMEM_LIMIT
        ),
        name="scatter_rows",
    )(*operands, *[rider[0] for rider in riders])


TILE_GROUPS = 4
SCALE = (DN + DR) ** (-0.5)


def half_turn(values):
    lane = lax.broadcasted_iota(jnp.int32, values.shape, 1)
    lower = (lane // (DR // 2)) % 2 == 0
    return jnp.where(lower, pltpu.roll(values, 128 - DR // 2, 1), pltpu.roll(values, DR // 2, 1))


def group_mask(column_ref, row_ref):
    column, row = column_ref[...], row_ref[0]
    shape = (column.shape[0], row.shape[1])
    earlier = lax.broadcasted_iota(jnp.int32, shape, 1) <= lax.broadcasted_iota(
        jnp.int32, shape, 0
    )
    same = (column == row) | ((row % 4 == 0) & (column // 4 == row // 4))
    return earlier & same


def softmax_scores(query, key, mask):
    scores = jnp.where(mask, dot_right(query, key) * SCALE, -1e30)
    powers = jnp.exp(scores - jnp.max(scores, axis=-1, keepdims=True))
    return powers / jnp.sum(powers, axis=-1, keepdims=True)


def attention_forward_kernel(
    x_ref, gain_ref, first_ref, latent_gain_ref, up_ref, trig_ref, column_ref, row_ref,
    normed_ref, query_ref, key_ref, value_ref, unit_ref, low_ref, scale_ref, attended_ref,
):
    rank = up_ref.shape[0]
    inputs = x_ref[...].astype(F32)
    scale = lax.rsqrt(jnp.mean(inputs * inputs, axis=1, keepdims=True) + EPS)
    normed_ref[...] = (inputs * scale * gain_ref[...]).astype(BF)
    out = dot(normed_ref[...], first_ref[...])
    latent = out[:, DN : DN + rank]
    latent_scale = lax.rsqrt(jnp.mean(latent * latent, axis=1, keepdims=True) + EPS)
    scale_ref[...] = latent_scale
    unit = latent * latent_scale
    unit_ref[...] = unit.astype(BF)
    low_ref[...] = (unit * latent_gain_ref[...]).astype(BF)
    keys_values = dot(low_ref[...], up_ref[...])
    rope = out[:, DN + rank :]
    turned = rope * trig_ref[:, :128] + half_turn(rope) * trig_ref[:, 128:]
    lane = lax.broadcasted_iota(jnp.int32, turned.shape, 1)
    query_ref[:, :DN] = out[:, :DN].astype(BF)
    query_ref[:, DN:] = jnp.where(lane < DR, pltpu.roll(turned, DR, 1), 0.0).astype(BF)
    key_ref[:, :DN] = keys_values[:, :DN].astype(BF)
    key_ref[:, DN:] = jnp.where(lane < DR, turned, 0.0).astype(BF)
    value_ref[...] = keys_values[:, DN:].astype(BF)
    probs = softmax_scores(query_ref[...], key_ref[...], group_mask(column_ref, row_ref))
    attended_ref[...] = dot(probs.astype(BF), value_ref[...]).astype(BF)


def attention_forward(x, gain, first_w, latent_gain, up_w, trig, column, row):
    width, rank = first_w.shape[0], up_w.shape[0]
    span, rows = column.shape[0], row.shape[2]

    def tile(columns):
        return pl.BlockSpec((rows, columns), lambda i: (i, 0))

    def fixed(shape):
        return pl.BlockSpec(shape, lambda i: (0, 0))

    outs = (width, 2 * DN, 2 * DN, DV, rank, rank, 1, DV)
    kinds = (BF, BF, BF, BF, BF, BF, F32, BF)
    return pl.pallas_call(
        attention_forward_kernel,
        grid=(span // rows,),
        in_specs=[
            tile(width),
            fixed((1, width)),
            fixed(first_w.shape),
            fixed((1, rank)),
            fixed(up_w.shape),
            tile(trig.shape[1]),
            tile(1),
            pl.BlockSpec((1, 1, rows), lambda i: (i, 0, 0)),
        ],
        out_specs=[tile(columns) for columns in outs],
        out_shape=[jax.ShapeDtypeStruct((span, c), k) for c, k in zip(outs, kinds)],
        compiler_params=pltpu.CompilerParams(vmem_limit_bytes=VMEM_LIMIT),
        name="attention_forward",
    )(x, gain[None], first_w, latent_gain[None], up_w, trig, column, row)


def attention_backward_kernel(
    r_ref, output_ref, attended_ref, query_ref, key_ref, value_ref, column_ref, row_ref, trig_ref,
    unit_ref, low_ref, scale_ref, latent_gain_ref, up_ref, normed_ref,
    grad_ref, output_grad_ref, up_grad_ref, first_grad_ref, gain_grad_ref, kv_ref,
):
    step = pl.program_id(0)
    rank = up_ref.shape[0]

    @pl.when(step == 0)
    def _():
        output_grad_ref[...] = jnp.zeros_like(output_grad_ref)
        up_grad_ref[...] = jnp.zeros_like(up_grad_ref)
        first_grad_ref[...] = jnp.zeros_like(first_grad_ref)
        gain_grad_ref[...] = jnp.zeros_like(gain_grad_ref)

    attended_grad = dot_right(r_ref[...], output_ref[...]).astype(BF)
    output_grad_ref[...] += dot_left(attended_ref[...], r_ref[...])
    probs = softmax_scores(query_ref[...], key_ref[...], group_mask(column_ref, row_ref))
    kv_ref[:, DN:] = dot_left(probs.astype(BF), attended_grad).astype(BF)
    probs_grad = dot_right(attended_grad, value_ref[...])
    inner = jnp.sum(probs * probs_grad, axis=1, keepdims=True)
    score_grad = (probs * (probs_grad - inner)).astype(BF)
    query_grad = dot(score_grad, key_ref[...]) * SCALE
    key_grad = dot_left(score_grad, query_ref[...]) * SCALE
    kv_ref[:, :DN] = key_grad[:, :DN].astype(BF)
    grad_ref[:, :DN] = query_grad[:, :DN].astype(BF)
    rope = key_grad[:, DN:] + pltpu.roll(query_grad[:, DN:], DR, 1)
    rope = rope * trig_ref[:, :128] + half_turn(rope * trig_ref[:, 128:])
    grad_ref[:, DN + rank :] = rope.astype(BF)
    out_grad = dot_right(kv_ref[...], up_ref[...])
    unit = unit_ref[...].astype(F32)
    gain_grad_ref[...] += jnp.sum(out_grad * unit, axis=0, keepdims=True)
    scaled = out_grad * latent_gain_ref[...]
    inner = jnp.mean(scaled * unit, axis=1, keepdims=True)
    grad_ref[:, DN : DN + rank] = (scale_ref[...] * (scaled - unit * inner)).astype(BF)
    up_grad_ref[...] += dot_left(low_ref[...], kv_ref[...])
    first_grad_ref[...] += dot_left(normed_ref[...], grad_ref[...])


def attention_backward(residual_all, output_w, stored, column, row, trig, latent_gain, up_w):
    normed, query, key, value, unit, low, scale, attended = stored
    width, rank = residual_all.shape[1], up_w.shape[0]
    span, rows = column.shape[0], row.shape[2]
    first_width = 2 * DN + rank

    def tile(columns):
        return pl.BlockSpec((rows, columns), lambda i: (i, 0))

    def fixed(shape):
        return pl.BlockSpec(shape, lambda i: (0, 0))

    sums = (output_w.shape, up_w.shape, (width, first_width), (1, rank))
    return pl.pallas_call(
        attention_backward_kernel,
        grid=(span // rows,),
        in_specs=[
            tile(width),
            fixed(output_w.shape),
            tile(DV),
            tile(2 * DN),
            tile(2 * DN),
            tile(DV),
            tile(1),
            pl.BlockSpec((1, 1, rows), lambda i: (i, 0, 0)),
            tile(trig.shape[1]),
            tile(rank),
            tile(rank),
            tile(1),
            fixed((1, rank)),
            fixed(up_w.shape),
            tile(width),
        ],
        out_specs=[tile(first_width)] + [fixed(shape) for shape in sums],
        out_shape=[jax.ShapeDtypeStruct((span, first_width), BF)]
        + [jax.ShapeDtypeStruct(shape, F32) for shape in sums],
        scratch_shapes=[pltpu.VMEM((rows, DN + DV), BF)],
        compiler_params=pltpu.CompilerParams(vmem_limit_bytes=VMEM_LIMIT),
        name="attention_backward",
    )(
        residual_all, output_w, attended, query, key, value, column, row, trig,
        unit, low, scale, latent_gain[None], up_w, normed,
    )


HIDDEN = 256
ROUTER_AT = 448


def expert_layer_kernel(
    splits,
    ffn_ref, y_ref, code_row_ref, code_column_ref, wide_ref, shared_down_ref, *refs,
):
    refs = list(refs)

    def take(number):
        taken = refs[:number]
        del refs[:number]
        return taken

    own_weights, came = take(3), take(len(splits))
    (
        rows_ref, ups_ref, scaled_ref, gate_ref, up_ref, mixed_ref,
        down_grad_out, wide_grad_out, sum_ref,
    ) = take(9)
    (
        gate_w_ref, up_w_ref, down_w_ref, load_sem, out_sem, down_grad_ref, wide_grad_ref,
        grad_ref, left_ref, inner_ref, returned_ref, slot_gate_ref, slot_dot_ref,
        part, kept, met, paired, passed,
        core_send, core_recv, pair_send, pair_recv, line_send, line_recv,
    ) = refs
    step = pl.program_id(0)
    me = lax.axis_index("expert")
    experts = lax.axis_size("expert")
    line, pair, core = place_of(me)
    me_d, n_d = lax.axis_index("dp"), lax.axis_size("dp")
    groups, _, per = code_row_ref.shape
    slots = rows_ref.shape[0] // groups
    width = ffn_ref.shape[1]
    hidden = gate_w_ref.shape[1]

    wholes = (gate_w_ref, up_w_ref, down_w_ref)
    loads = []

    def load(source, number, owner, start, count):
        axis = 1 if number == 2 else 0
        size = own_weights[number].shape[axis]
        at = pl.multiple_of(owner * size, size)
        if axis == 0:
            place = wholes[number].at[pl.ds(at + start, count)]
        else:
            place = wholes[number].at[:, pl.ds(at, size)]
        loads.append(pltpu.make_async_copy(source, place, load_sem.at[len(loads)]))

    for number in range(3):
        load(own_weights[number], number, me_d, 0, own_weights[number].shape[0])
    for source, (number, first, end) in zip(came, splits):
        for ahead in range(1, n_d):
            owner = lax.rem(me_d - ahead + n_d, n_d)
            load(source.at[ahead - 1], number, owner, first, end - first)

    @pl.when(step == 0)
    def _():
        for copy in loads:
            copy.start()
        greet(line, pair, core)
        down_grad_ref[...] = jnp.zeros_like(down_grad_ref)
        wide_grad_ref[...] = jnp.zeros_like(wide_grad_ref)

    out = dot(ffn_ref[...], wide_ref[...])
    gates, ups = out[:, :HIDDEN], out[:, HIDDEN:]
    last = out[:, 2 * HIDDEN - 128 :]
    lane = lax.broadcasted_iota(jnp.int32, last.shape, 1)
    first_lane = ROUTER_AT - (2 * HIDDEN - 128)
    logits = jnp.where((lane >= first_lane) & (lane < first_lane + experts), last, -1e30)
    powers = jnp.exp(logits - jnp.max(logits, axis=1, keepdims=True))
    probs = powers / jnp.sum(powers, axis=1, keepdims=True)
    own_lane = (lane == first_lane + me).astype(F32)
    own_probs = jnp.sum(probs * own_lane, axis=1, keepdims=True)
    sigmoid = 1.0 / (1.0 + jnp.exp(-gates))
    silu = gates * sigmoid
    shared_low = (silu * ups).astype(BF)
    back = dot_right(y_ref[...], shared_down_ref[...])
    left_ref[:, :HIDDEN] = (back * ups * sigmoid * (1.0 + gates * (1.0 - sigmoid))).astype(BF)
    shared_up_low = back * silu
    left_ref[:, HIDDEN : 2 * HIDDEN - 128] = shared_up_low[:, : HIDDEN - 128].astype(BF)
    shared_last = shared_up_low[:, HIDDEN - 128 :]
    down_grad_ref[...] += dot_left(shared_low, y_ref[...])

    square = (per, per)
    diagonal = lax.broadcasted_iota(jnp.int32, square, 0) == lax.broadcasted_iota(
        jnp.int32, square, 1
    )
    for group in range(groups):
        tokens_at = pl.ds(group * per, per)
        slots_at = pl.ds(group * slots, slots)
        slot_ids = lax.broadcasted_iota(jnp.int32, (slots, per), 0)
        picks = slot_ids == code_row_ref[group]
        picks_low = picks.astype(F32).astype(BF)
        rows_ref[slots_at] = dot(picks_low, ffn_ref[tokens_at]).astype(BF)
        ups_ref[slots_at] = dot(picks_low, y_ref[tokens_at]).astype(BF)
        own_column = own_probs[group * per : (group + 1) * per]
        own_row = jnp.sum(jnp.where(diagonal, own_column, 0.0), axis=0, keepdims=True)
        slot_gate_ref[slots_at] = jnp.sum(
            jnp.where(picks, own_row, 0.0), axis=1, keepdims=True
        )
    slot_dot_ref[...] = jnp.zeros_like(slot_dot_ref)

    @pl.when(step == 0)
    def _():
        for copy in loads:
            copy.wait()

    def hidden_part(columns):
        gate_part = dot(rows_ref[...], gate_w_ref[:, columns])
        up_part = dot(rows_ref[...], up_w_ref[:, columns])
        raw = dot_right(ups_ref[...], down_w_ref[columns, :])
        slot_gate = slot_gate_ref[...]
        sigmoid = 1.0 / (1.0 + jnp.exp(-gate_part))
        silu = gate_part * sigmoid
        inner = silu * up_part
        slot_dot_ref[...] += jnp.sum(inner * raw, axis=1, keepdims=True)
        grad = raw * slot_gate
        inner_ref[:, columns] = inner.astype(BF)
        scaled_ref[:, columns] = (inner * slot_gate).astype(BF)
        gate_ref[:, columns] = (
            grad * up_part * sigmoid * (1.0 + gate_part * (1.0 - sigmoid))
        ).astype(BF)
        up_ref[:, columns] = (grad * silu).astype(BF)

    @pl.loop(0, hidden // HIDDEN)
    def _(tile):
        hidden_part(pl.ds(pl.multiple_of(tile * HIDDEN, HIDDEN), HIDDEN))

    if hidden % HIDDEN:
        hidden_part(pl.ds(hidden - hidden % HIDDEN, hidden % HIDDEN))

    @pl.loop(0, width // COLUMNS)
    def _(tile):
        columns = pl.ds(pl.multiple_of(tile * COLUMNS, COLUMNS), COLUMNS)
        returned_ref[:, columns] = dot(inner_ref[...], down_w_ref[:, columns]).astype(BF)
        grad_ref[:, columns] = (
            dot_right(gate_ref[...], gate_w_ref[columns, :])
            + dot_right(up_ref[...], up_w_ref[columns, :])
        ).astype(BF)

    for group in range(groups):
        tokens_at = pl.ds(group * per, per)
        slots_at = pl.ds(group * slots, slots)
        own_column = own_probs[group * per : (group + 1) * per]
        slot_lane = lax.broadcasted_iota(jnp.int32, (per, slots), 1)
        picks = slot_lane == code_column_ref[tokens_at]
        pick_gate = jnp.where(picks, own_column, 0.0).astype(BF)
        mixed_ref[tokens_at] = (
            dot(shared_low[group * per : (group + 1) * per], shared_down_ref[...])
            + dot(pick_gate, returned_ref[slots_at])
        ).astype(BF)
        small = (slots, slots)
        eye = lax.broadcasted_iota(jnp.int32, small, 0) == lax.broadcasted_iota(
            jnp.int32, small, 1
        )
        dot_row = jnp.sum(jnp.where(eye, slot_dot_ref[slots_at], 0.0), axis=0, keepdims=True)
        row_dot = jnp.sum(jnp.where(picks, dot_row, 0.0), axis=1, keepdims=True)
        at = slice(group * per, (group + 1) * per)
        logit_grad = row_dot * own_column * (own_lane[at] - probs[at])
        high = logit_grad.astype(BF)
        rest = logit_grad - high.astype(F32)
        left_ref[tokens_at, 2 * HIDDEN - 128 :] = jnp.where(
            lane[at] < first_lane,
            shared_last[at],
            high.astype(F32) + pltpu.roll(rest, experts, 1),
        ).astype(BF)
    wide_grad_ref[...] += dot_left(ffn_ref[...], left_ref[...])

    rows = kept.shape[0]
    piece_rows = rows // PIECES
    sibling = index_of(line, pair, 1 - core)
    across = index_of(line, 1 - pair, core)
    steps = 2 * LINE

    def remote(source, dest, send_at, recv_at, target):
        return pltpu.make_async_remote_copy(
            src_ref=source,
            dst_ref=dest,
            send_sem=send_at,
            recv_sem=recv_at,
            device_id={"expert": target},
            device_id_type=MESH,
        )

    def to_sibling(i):
        return remote(part, met.at[i], core_send.at[i], core_recv.at[i], sibling)

    def to_pair(i, piece):
        at = pl.ds(piece * piece_rows, piece_rows)
        return remote(
            met.at[i, at],
            paired.at[i // 2, at],
            pair_send.at[i // 2, piece],
            pair_recv.at[i // 2, piece],
            across,
        )

    def meet(i):
        to_sibling(i).wait_recv()
        add_strips(met.at[i], 0, rows, [met.at[i], kept])

        @pl.when(lax.rem(i, 2) == 0)
        def _():
            for piece in range(PIECES):
                to_pair(i, piece).start()

    dest_line = [pick_by(line, FAR_FIRST[k]) for k in range(LINE)]

    def hop_facts(k):
        there = dest_line[k]
        way = jnp.where(there > line, 1, -1)
        behind = line - way
        held = (behind >= 0) & (behind < LINE)
        slot = jnp.where((there == line + way) & (way < 0), LINE, there)
        return (there, held, slot, index_of(line + way, pair, core))

    def along(k, piece):
        there, held, slot, target = hop_facts(k)
        at = pl.ds(piece * piece_rows, piece_rows)
        return remote(
            paired.at[k, at],
            passed.at[slot, at],
            line_send.at[k, piece],
            line_recv.at[slot, piece],
            target,
        )

    def came_along(slot, piece):
        at = pl.ds(piece * piece_rows, piece_rows)
        block = passed.at[slot, at]
        remote(block, block, line_send.at[0, piece], line_recv.at[slot, piece], me).wait_recv()

    def pair_arrived(k, piece):
        at = pl.ds(piece * piece_rows, piece_rows)
        block = paired.at[k, at]
        remote(block, block, pair_send.at[k, piece], pair_recv.at[k, piece], me).wait_recv()

    def hop(k, with_held):
        there = hop_facts(k)[0]
        for piece in range(PIECES):
            first = piece * piece_rows
            pair_arrived(k, piece)
            terms = [paired.at[k], met.at[2 * k + 1]]
            if with_held:
                came_along(there, piece)
                terms.append(passed.at[there])
            add_strips(paired.at[k], first, piece_rows, terms)
            along(k, piece).start()

    @pl.when(step > 0)
    def _():
        meet(step - 1)

    for k in range(LINE - 1):
        held = hop_facts(k)[1]
        if 2 * k + 3 < steps:

            @pl.when((step == 2 * k + 3) & jnp.logical_not(held))
            def _():
                hop(k, False)

        if 2 * k + 4 < steps:

            @pl.when((step == 2 * k + 4) & held)
            def _():
                hop(k, True)

    @pl.when(step > 0)
    def _():
        to_sibling(step - 1).wait_send()

    def produce(first, target):
        @pl.loop(0, width // COLUMNS)
        def _(tile):
            columns = pl.ds(pl.multiple_of(tile * COLUMNS, COLUMNS), COLUMNS)
            total = dot_right(left_ref[pl.ds(first, rows)], wide_ref[columns, :])
            for k in range(rows // per):
                group = first // per + k
                slot_lane = lax.broadcasted_iota(jnp.int32, (per, slots), 1)
                picks = slot_lane == code_column_ref[pl.ds(first + k * per, per)]
                scattered = dot(
                    picks.astype(F32).astype(BF),
                    grad_ref[pl.ds(group * slots, slots), columns],
                )
                target[pl.ds(k * per, per), columns] = (
                    total[k * per : (k + 1) * per] + scattered
                ).astype(BF)

    for which in range(2):

        @pl.when(core == which)
        def _():
            produce((1 - which) * rows, part)

    to_sibling(step).start()
    for which in range(2):

        @pl.when(core == which)
        def _():
            produce(which * rows, kept)

    @pl.when(step == steps - 1)
    def _():
        outs = [
            pltpu.make_async_copy(down_grad_ref, down_grad_out, out_sem.at[0]),
            pltpu.make_async_copy(wide_grad_ref, wide_grad_out, out_sem.at[1]),
        ]
        for copy in outs:
            copy.start()
        meet(steps - 1)
        last = LINE - 2
        held = hop_facts(last)[1]

        @pl.when(held)
        def _():
            hop(last, True)

        for piece in range(PIECES):
            first = piece * piece_rows
            pair_arrived(LINE - 1, piece)
            add_strips(
                sum_ref, first, piece_rows, [paired.at[LINE - 1], met.at[2 * LINE - 1]]
            )
            for has, slot in ((line > 0, line), (line < LINE - 1, LINE)):

                @pl.when(has)
                def _():
                    came_along(slot, piece)
                    add_strips(sum_ref, first, piece_rows, [sum_ref, passed.at[slot]])

        to_sibling(steps - 1).wait_send()
        for piece in range(PIECES):
            for k in range(LINE):
                to_pair(2 * k, piece).wait_send()
            for k in range(LINE - 1):
                along(k, piece).wait_send()
        for copy in outs:
            copy.wait()


def expert_layer(
    ffn_all, upstream_all, code, slots, wide, shared_down, weights, came, splits, collective_id
):
    groups, per = code.shape
    span, width = ffn_all.shape
    gate_w, up_w, down_w = weights
    hidden = gate_w.shape[1]
    n_d = lax.axis_size("dp")
    rows, slot_rows = TILE_GROUPS * per, TILE_GROUPS * slots
    total = groups * slots
    steps = 2 * LINE
    block = (rows // 2, width)

    def tile_of(i):
        line, pair, _ = place_of(lax.axis_index("expert"))
        there = pick_by(line, FAR_FIRST[LINE - 1])
        for k in range(LINE - 2, -1, -1):
            there = jnp.where(i // 2 == k, pick_by(line, FAR_FIRST[k]), there)
        return there * 2 + jnp.where(lax.rem(i, 2) == 0, 1 - pair, pair)

    def tile(count, columns):
        return pl.BlockSpec((count, columns), lambda i: (tile_of(i), 0))

    def fixed(shape):
        return pl.BlockSpec(shape, lambda i: (0, 0), pipeline_mode=pl.Buffered(1))

    anywhere = pl.BlockSpec(memory_space=pl.ANY)
    outs = [(total, width)] * 2 + [(total, hidden)] * 3 + [(span, width)]
    sums = [shared_down.shape, wide.shape]
    copies = 3 + len(came) * (n_d - 1)
    return pl.pallas_call(
        lambda *refs: expert_layer_kernel(splits, *refs),
        grid=(steps,),
        in_specs=[
            tile(rows, width),
            tile(rows, width),
            pl.BlockSpec((TILE_GROUPS, 1, per), lambda i: (tile_of(i), 0, 0)),
            tile(rows, 1),
            fixed(wide.shape),
            fixed(shared_down.shape),
        ]
        + [anywhere] * (3 + len(came)),
        out_specs=[
            tile(slot_rows if shape[0] == total else rows, shape[1]) for shape in outs
        ]
        + [anywhere] * 2
        + [pl.BlockSpec(block, lambda i: (0, 0))],
        out_shape=[jax.ShapeDtypeStruct(shape, BF) for shape in outs]
        + [jax.ShapeDtypeStruct(shape, F32) for shape in sums]
        + [jax.ShapeDtypeStruct(block, BF)],
        scratch_shapes=[
            pltpu.VMEM((gate_w.shape[0] * n_d, hidden), BF),
            pltpu.VMEM((up_w.shape[0] * n_d, hidden), BF),
            pltpu.VMEM((hidden, down_w.shape[1] * n_d), BF),
            pltpu.SemaphoreType.DMA((copies,)),
            pltpu.SemaphoreType.DMA((2,)),
            pltpu.VMEM(shared_down.shape, F32),
            pltpu.VMEM(wide.shape, F32),
            pltpu.VMEM((slot_rows, width), BF),
            pltpu.VMEM((rows, 2 * HIDDEN), BF),
            pltpu.VMEM((slot_rows, hidden), BF),
            pltpu.VMEM((slot_rows, width), BF),
            pltpu.VMEM((slot_rows, 1), F32),
            pltpu.VMEM((slot_rows, 1), F32),
            pltpu.VMEM(block, BF),
            pltpu.VMEM(block, BF),
            pltpu.VMEM((steps,) + block, BF),
            pltpu.VMEM((LINE,) + block, BF),
            pltpu.VMEM((LINE + 1,) + block, BF),
            pltpu.SemaphoreType.DMA((steps,)),
            pltpu.SemaphoreType.DMA((steps,)),
            pltpu.SemaphoreType.DMA((LINE, PIECES)),
            pltpu.SemaphoreType.DMA((LINE, PIECES)),
            pltpu.SemaphoreType.DMA((LINE, PIECES)),
            pltpu.SemaphoreType.DMA((LINE + 1, PIECES)),
        ],
        compiler_params=pltpu.CompilerParams(
            collective_id=collective_id,
            has_side_effects=True,
            vmem_limit_bytes=63 * 1024 * 1024,
        ),
        name="expert_layer",
    )(
        ffn_all, upstream_all, code[:, None, :], code.reshape(span, 1), wide, shared_down,
        gate_w, up_w, down_w, *came,
    )


def on_device(
    tokens,
    segment,
    routes,
    drop_order,
    cotangent,
    attn_gain,
    query_weight,
    down_latent,
    latent_gain,
    up_latent,
    output_weight,
    ffn_gain,
    router_weight,
    shared_gate,
    shared_up,
    shared_down,
    expert_gate,
    expert_up,
    expert_down,
):
    n_e = lax.axis_size("expert")
    n_d = lax.axis_size("dp")
    me_e = lax.axis_index("expert")
    me_d = lax.axis_index("dp")
    micro, group_rows, width = tokens.shape
    own_rows = micro * group_rows
    span = n_e * own_rows
    groups = n_e * micro
    top = routes.shape[2]
    experts = n_e * expert_gate.shape[0]
    capacity = (5 * group_rows * top + 4 * experts - 1) // (4 * experts)
    slots = -(-capacity // 16) * 16
    rank_latent = latent_gain.shape[0] * n_e * n_d

    def gather(values):
        return lax.all_gather(values, "expert", axis=0, tiled=True)

    def scatter(values):
        return lax.psum_scatter(values, "expert", scatter_dimension=0, tiled=True)

    def whole(own, parts, axis):
        size = own.shape[axis]
        shape = list(own.shape)
        shape[axis] = size * n_d
        total = jnp.zeros(shape, own.dtype)
        for step in range(n_d):
            at = lax.rem(me_d - step + n_d, n_d) * size
            block = parts[step - 1] if step else own
            total = lax.dynamic_update_slice_in_dim(total, block, at, axis)
        return total

    def sum_dp(values, axis):
        size = values.shape[axis] // n_d

        def part(step):
            at = lax.rem(me_d + step, n_d) * size
            return lax.dynamic_slice_in_dim(values, at, size, axis)

        total = part(0).astype(F32)
        for step in range(1, n_d):
            pairs = [(i, (i + step) % n_d) for i in range(n_d)]
            total = total + lax.ppermute(part(step).astype(BF), "dp", pairs).astype(F32)
        return total

    def grad_dp(left, right, axis):
        size = (left, right)[axis].shape[1] // n_d
        parts = []
        for step in range(n_d):
            at = lax.rem(me_d + step, n_d) * size
            if axis == 0:
                part = dot_left(lax.dynamic_slice_in_dim(left, at, size, 1), right)
            else:
                part = dot_left(left, lax.dynamic_slice_in_dim(right, at, size, 1))
            parts.append(part.astype(BF) if step else part)
        return (stack(parts[1:]), parts[0])

    def split_dp(values, axis):
        size = values.shape[axis] // n_d
        parts = []
        for step in range(n_d):
            at = lax.rem(me_d + step, n_d) * size
            parts.append(lax.dynamic_slice_in_dim(values, at, size, axis))
        return (stack([part.astype(BF) for part in parts[1:]]), parts[0])

    def stack(parts):
        return parts[0][None] if len(parts) == 1 else jnp.stack(parts)

    def add_all(total, parts):
        for step in range(n_d - 1):
            total = total + parts[step].astype(F32)
        return total

    small_rows = attn_gain.shape[0]
    latent_all_width = down_latent.shape[1]
    latent_piece = latent_gain.shape[0]
    packed = jnp.concatenate(
        [
            down_latent,
            router_weight,
            attn_gain[:, None],
            ffn_gain[:, None],
            jnp.pad(latent_gain, (0, small_rows - latent_piece))[:, None],
        ],
        axis=1,
    )
    packed = lax.all_gather(packed, ("dp", "expert"), axis=0, tiled=True)
    down_all = packed[:, :latent_all_width]
    router_all = packed[:, latent_all_width : latent_all_width + experts]
    rest = packed[:, latent_all_width + experts :].astype(F32)
    attn_gain_all = rest[:, 0]
    ffn_gain_all = rest[:, 1]
    latent_gain_all = rest[:, 2].reshape(n_e * n_d, small_rows)[:, :latent_piece].reshape(-1)

    chosen = jnp.sum(
        (routes[..., None] == jnp.arange(experts, dtype=jnp.int32)).astype(jnp.int32), axis=2
    )
    order = drop_order[:, 0]
    earlier = (order[:, None, :] < order[:, :, None]).astype(F32)
    rank = jnp.einsum("mtu,mue->mte", earlier, chosen.astype(F32)).astype(jnp.int32)
    code = jnp.where((chosen == 1) & (rank < capacity), rank, -1).reshape(own_rows, experts)

    tokens_own = tokens.reshape(own_rows, width)
    code_lanes = -(-experts // 128) * 128
    code_low = jnp.pad(code.astype(BF), ((0, 0), (0, code_lanes - experts)))
    own_gate, own_up, own_down = expert_gate[0], expert_up[0], expert_down[0]
    gate_half = own_gate.shape[0] // 2
    up_most = own_up.shape[0] * 3 // 4
    dense = (query_weight, up_latent, output_weight, shared_gate, shared_up, shared_down)
    came = gather_rows(
        jnp.concatenate([tokens_own, code_low], axis=1),
        5,
        riders=[(array, (0, array.shape[0])) for array in dense] + [(own_gate, (0, gate_half))],
    )
    tokens_all, gate_came = came[0], came[7]
    query_w, up_w, output_w, shared_gate_w, shared_up_w, shared_down_w = [
        whole(own, parts, axis)
        for own, parts, axis in zip(dense, came[1:7], (0, 0, 1, 0, 0, 1))
    ]
    upstream_own = cotangent.reshape(own_rows, width)
    upstream_later, tokens_all = lax.optimization_barrier((upstream_own, tokens_all))
    upstream_all = gather(upstream_later)
    code_all = tokens_all[:, width : width + experts].astype(jnp.int32)
    my_code = lax.dynamic_slice_in_dim(code_all, me_e, 1, 1).reshape(groups, group_rows)

    span_segment = (
        segment.reshape(micro, n_e, group_rows).transpose(1, 0, 2).reshape(groups, group_rows)
    )
    trig = angles(positions(span_segment), group_rows)
    marks = span_segment + 4 * jnp.arange(groups, dtype=jnp.int32)[:, None]
    column = marks.reshape(span, 1)
    row = marks.reshape(groups // TILE_GROUPS, 1, TILE_GROUPS * group_rows)
    first_w = jnp.concatenate(
        [
            query_w[:, :DN],
            down_all[:, :rank_latent],
            down_all[:, rank_latent:],
            query_w[:, DN:],
        ],
        axis=1,
    )
    stored = attention_forward(
        tokens_all, attn_gain_all, first_w, latent_gain_all, up_w, trig, column, row
    )
    attention_out, gate_came_last, up_came = scatter_rows(
        stored[-1],
        output_w,
        2,
        riders=[(own_gate, (gate_half, own_gate.shape[0])), (own_up, (0, up_most))],
    )
    residual = tokens_own.astype(F32) + attention_out

    second_scale = rms_scale(residual)
    ffn_in = (residual * second_scale * ffn_gain_all).astype(BF)
    ffn_all, up_came_last, down_came = gather_rows(
        ffn_in,
        1,
        riders=[(own_up, (up_most, own_up.shape[0])), (own_down, (0, own_down.shape[0]))],
    )

    shared_hidden = shared_gate_w.shape[1]
    wide = jnp.concatenate(
        [
            jnp.pad(shared_gate_w, ((0, 0), (0, HIDDEN - shared_hidden))),
            jnp.pad(shared_up_w, ((0, 0), (0, ROUTER_AT - HIDDEN - shared_hidden))),
            router_all,
            jnp.pad(router_all, ((0, 0), (0, 2 * HIDDEN - ROUTER_AT - 2 * experts))),
        ],
        axis=1,
    )
    (
        expert_rows,
        slot_up,
        inner_scaled,
        gate_low,
        up_low,
        mixed_part,
        shared_down_grad,
        wide_grad,
        ffn_grad,
    ) = expert_layer(
        ffn_all,
        upstream_all,
        my_code,
        slots,
        wide,
        jnp.pad(shared_down_w, ((0, HIDDEN - shared_hidden), (0, 0))),
        (own_gate, own_up, own_down),
        (gate_came, gate_came_last, up_came, up_came_last, down_came),
        (
            (0, 0, gate_half),
            (0, gate_half, own_gate.shape[0]),
            (1, 0, up_most),
            (1, up_most, own_up.shape[0]),
            (2, 0, own_down.shape[0]),
        ),
        3,
    )
    ffn_grad = ffn_grad.astype(F32)
    mixed = residual + scatter(mixed_part).astype(F32)
    down_later, down_now = grad_dp(inner_scaled, slot_up, 1)
    gate_later, gate_now = grad_dp(expert_rows, gate_low, 0)
    up_later, up_now = grad_dp(expert_rows, up_low, 0)
    router_grad = (
        wide_grad[:, ROUTER_AT : ROUTER_AT + experts]
        + wide_grad[:, ROUTER_AT + experts : ROUTER_AT + 2 * experts]
    )
    shared_down_later, shared_down_now = split_dp(shared_down_grad[:shared_hidden], 1)
    shared_gate_later, shared_gate_now = split_dp(wide_grad[:, :shared_hidden], 0)
    shared_up_later, shared_up_now = split_dp(wide_grad[:, HIDDEN : HIDDEN + shared_hidden], 0)
    residual_part, ffn_gain_grad = norm_back(residual, second_scale, ffn_gain_all, ffn_grad)
    residual_grad = upstream_own.astype(F32) + residual_part
    residual_all, down_parts, gate_parts = gather_rows(
        residual_grad.astype(BF), 6, riders=[(down_later, None), (gate_later, None)]
    )

    first_grad, output_weight_grad, up_latent_grad, first_w_grad, latent_gain_grad = (
        attention_backward(
            residual_all, output_w, stored, column, row, trig, latent_gain_all, up_w
        )
    )
    rope_at = DN + latent_all_width
    query_weight_grad = jnp.concatenate(
        [first_w_grad[:, :DN], first_w_grad[:, rope_at:]], axis=1
    )
    down_grad = first_w_grad[:, DN:rope_at]
    attn_gain_grad = jnp.sum(first_w_grad * first_w.astype(F32), axis=1) / attn_gain_all
    small = jnp.concatenate(
        [
            down_grad,
            router_grad,
            attn_gain_grad[:, None],
            ffn_gain_grad[:, None],
            jnp.pad(
                latent_gain_grad.reshape(n_e * n_d, latent_piece),
                ((0, 0), (0, small_rows - latent_piece)),
            ).reshape(-1, 1),
        ],
        axis=1,
    )
    small_width = -(-small.shape[1] // 128) * 128
    small = jnp.pad(small, ((0, 0), (0, small_width - small.shape[1]))).astype(BF)
    small = small.reshape(n_d, n_e, small_rows, small_width)
    query_later, query_now = split_dp(query_weight_grad, 0)
    latent_later, latent_now = split_dp(up_latent_grad, 0)
    output_later, output_now = split_dp(output_weight_grad, 1)
    (
        summed,
        up_parts,
        shared_down_parts,
        shared_gate_parts,
        shared_up_parts,
        query_parts,
        latent_parts,
        output_parts,
    ) = scatter_rows(
        first_grad,
        first_w.T,
        4,
        extra=small,
        riders=[
            (later, None)
            for later in (
                up_later,
                shared_down_later,
                shared_gate_later,
                shared_up_later,
                query_later,
                latent_later,
                output_later,
            )
        ],
    )
    normed_grad = summed[:own_rows]
    small = jnp.concatenate(
        [
            summed[own_rows:, k * small_width : (k + 1) * small_width]
            for k in range(width // small_width)
        ],
        axis=0,
    )[: n_d * small_rows]
    small = sum_dp(small, 0)
    own_inputs = tokens_own.astype(F32)
    input_part, _ = norm_back(own_inputs, rms_scale(own_inputs), attn_gain_all, normed_grad)
    tokens_grad = residual_grad + input_part
    last = latent_all_width + experts
    shape = (micro, group_rows, width)
    return (
        mixed.reshape(shape),
        tokens_grad.reshape(shape),
        small[:, last],
        add_all(query_now, query_parts),
        small[:, :latent_all_width],
        small[:latent_piece, last + 2],
        add_all(latent_now, latent_parts),
        add_all(output_now, output_parts),
        small[:, last + 1],
        small[:, latent_all_width:last],
        add_all(shared_gate_now, shared_gate_parts),
        add_all(shared_up_now, shared_up_parts),
        add_all(shared_down_now, shared_down_parts),
        add_all(gate_now, gate_parts)[None],
        add_all(up_now, up_parts)[None],
        add_all(down_now, down_parts)[None],
    )


def solution(mesh):
    rows = P(None, ("dp", "expert"), None)
    split = P(("dp", "expert"))
    split_rows = P(("dp", "expert"), None)
    columns = P("dp", "expert")
    turned = P("expert", "dp")
    expert_in = P("expert", "dp", None)
    expert_out = P("expert", None, "dp")
    return jax.shard_map(
        on_device,
        mesh=mesh,
        in_specs=(
            rows,
            P(None, "dp"),
            rows,
            rows,
            rows,
            split,
            columns,
            split_rows,
            split,
            columns,
            turned,
            split,
            split_rows,
            columns,
            columns,
            turned,
            expert_in,
            expert_in,
            expert_out,
        ),
        out_specs=(
            rows,
            rows,
            split,
            columns,
            split_rows,
            split,
            columns,
            turned,
            split,
            split_rows,
            columns,
            columns,
            turned,
            expert_in,
            expert_in,
            expert_out,
        ),
        check_vma=False,
    )
```

```python
import math

import jax
import jax.numpy as jnp
from jax import lax
from jax.experimental import pallas as pl
from jax.experimental.pallas import tpu as pltpu
from jax.sharding import PartitionSpec as P

DN = 128
DR = 64
DV = 128
EPS = 1e-06
HIGH = lax.Precision.HIGHEST
F32 = jnp.float32
BF = jnp.bfloat16


def dot(former, latter):
    return jnp.dot(former, latter, preferred_element_type=F32)


def dot_left(former, latter):
    return lax.dot_general(former, latter, (((0,), (0,)), ((), ())), preferred_element_type=F32)


def dot_right(former, latter):
    return lax.dot_general(former, latter, (((1,), (1,)), ((), ())), preferred_element_type=F32)


def rms_scale(values):
    return lax.rsqrt(jnp.mean(values * values, axis=-1, keepdims=True) + EPS)


def norm_back(values, scale_rows, gain, out_grad):
    scaled = out_grad * gain
    inner = jnp.mean(scaled * values, axis=-1, keepdims=True)
    value_grad = scale_rows * scaled - values * scale_rows * scale_rows * scale_rows * inner
    return (value_grad, jnp.sum(out_grad * values * scale_rows, axis=0))


def positions(segment):
    places = jnp.arange(segment.shape[1], dtype=jnp.int32)
    prompt_len = jnp.sum((segment == 0).astype(jnp.int32), axis=1, keepdims=True)
    former = (segment[:, None, :] < segment[:, :, None]).astype(jnp.int32)
    seg_start = jnp.sum(former, axis=2)
    return jnp.where(segment == 0, places[None], prompt_len + places[None] - seg_start)


def angles(position, row_count):
    freq_index = jnp.arange(DR // 2, dtype=F32)
    frequency = jnp.exp(freq_index * (-2.0 * math.log(10000.0) / DR))
    turning = jnp.arange(row_count, dtype=F32)[:, None] * frequency[None, :]
    cosine, sine_part = jnp.cos(turning), jnp.sin(turning)
    table = jnp.concatenate([cosine] * 4 + [-sine_part, sine_part] * 2, axis=1)
    picks = (position.reshape(-1)[:, None] == jnp.arange(row_count)[None, :]).astype(F32)
    return jnp.dot(picks, table, precision=HIGH)


LINE = 4
PIECES = 3
MESH = pl.DeviceIdType.MESH
VMEM_LIMIT = 60 * 1024 * 1024


def place_of(me):
    return (me // 4, lax.rem(me // 2, 2), lax.rem(me, 2))


def index_of(line, pair, core):
    return line * 4 + pair * 2 + core


def greet(line, pair, core, others=0):
    barrier = pltpu.get_barrier_semaphore()

    def signal(target):
        pl.semaphore_signal(barrier, inc=1, device_id={"expert": target}, device_id_type=MESH)

    signal(index_of(line, pair, 1 - core))
    signal(index_of(line, 1 - pair, core))

    @pl.when(line > 0)
    def _():
        signal(index_of(line - 1, pair, core))

    @pl.when(line < LINE - 1)
    def _():
        signal(index_of(line + 1, pair, core))

    inner = jnp.where(line > 0, 1, 0) + jnp.where(line < LINE - 1, 1, 0)
    pl.semaphore_wait(barrier, 2 + others + inner)


def greet_dp(others):
    barrier = pltpu.get_barrier_semaphore()
    me_d, n_d = lax.axis_index("dp"), lax.axis_size("dp")
    if others:
        for step in range(1, n_d):
            pl.semaphore_signal(
                barrier,
                inc=1,
                device_id={"dp": lax.rem(me_d + step, n_d)},
                device_id_type=MESH,
            )


def ride(sources, targets, send_sem, recv_sem, start=True):
    me_d, n_d = lax.axis_index("dp"), lax.axis_size("dp")
    copies = []
    for number, (source, target) in enumerate(zip(sources, targets)):
        parts = len(source.shape) == len(target.shape)
        for step in range(1, n_d):
            copy = pltpu.make_async_remote_copy(
                src_ref=source.at[step - 1] if parts else source,
                dst_ref=target.at[step - 1],
                send_sem=send_sem.at[number, step - 1],
                recv_sem=recv_sem.at[number, step - 1],
                device_id={"dp": lax.rem(me_d + step, n_d)},
                device_id_type=MESH,
            )
            if start:
                copy.start()
            copies.append(copy)
    return copies


def landed(rider):
    array, rows = rider
    if rows is None:
        return jax.ShapeDtypeStruct(array.shape, array.dtype)
    shape = (lax.axis_size("dp") - 1, rows[1] - rows[0]) + array.shape[1:]
    return jax.ShapeDtypeStruct(shape, array.dtype)


def cut_rows(ref, rows):
    return ref if rows is None else ref.at[pl.ds(rows[0], rows[1] - rows[0])]


def when(condition, action):
    if condition is None:
        action()
    else:
        pl.when(condition)(action)


def gather_kernel(spans, products, *refs):
    riders = len(spans)
    take = taker(refs)
    (own_ref,), sources = take(1), take(riders)
    products_in = take(5) if products else None
    (out_ref,), targets = take(1), take(riders)
    products_out = take(6) if products else None
    own_sem, send_sem, recv_sem, ride_send, ride_recv = take(5)
    if products:
        products = ExpertGradients(products_in, products_out, take(12))
    sources = [cut_rows(source, rows) for source, rows in zip(sources, spans)]
    me = lax.axis_index("expert")
    line, pair, core = place_of(me)
    rows = own_ref.shape[0] // PIECES
    others = lax.axis_size("dp") - 1 if riders or products else 0
    greet_dp(others)
    greet(line, pair, core, others)
    local = [pltpu.make_async_copy(own_ref, out_ref.at[me], own_sem)]
    sent = []

    def push(condition, kind, origin, piece, target, source=None):
        block = out_ref.at[origin, pl.ds(piece * rows, rows)]
        copy = pltpu.make_async_remote_copy(
            src_ref=block if source is None else source,
            dst_ref=block,
            send_sem=send_sem.at[kind, origin, piece],
            recv_sem=recv_sem.at[origin, piece],
            device_id={"expert": target},
            device_id_type=MESH,
        )
        when(condition, copy.start)
        sent.append((condition, copy))

    def arrive(condition, origin, piece):
        block = out_ref.at[origin, pl.ds(piece * rows, rows)]
        copy = pltpu.make_async_remote_copy(
            src_ref=block,
            dst_ref=block,
            send_sem=send_sem.at[0, origin, piece],
            recv_sem=recv_sem.at[origin, piece],
            device_id={"expert": me},
            device_id_type=MESH,
        )
        when(condition, copy.wait_recv)

    left = index_of(line - 1, pair, core)
    right = index_of(line + 1, pair, core)
    across = index_of(line, 1 - pair, core)
    sibling = index_of(line, pair, 1 - core)
    for piece in range(PIECES):
        source = own_ref.at[pl.ds(piece * rows, rows)]
        push(line < LINE - 1, 1, me, piece, right, source)
        push(line > 0, 0, me, piece, left, source)
        push(None, 2, me, piece, across, source)
        push(None, 3, me, piece, sibling, source)
    ridden = ride(sources, targets, ride_send, ride_recv)
    for copy in local:
        copy.start()
    if products:
        products.load()

    def work():
        if products:
            products.next()

    def along(hop):
        for piece in range(PIECES):
            for side in (-1, 1):
                there = line + side * hop
                held = (there >= 0) & (there < LINE)
                origin = index_of(there, pair, core)
                arrive(held, origin, piece)
                if hop < LINE - 1:
                    further = held & ((line < LINE - 1) if side < 0 else (line > 0))
                    kind, target = (1, right) if side < 0 else (0, left)
                    push(further, kind, origin, piece, target)
                push(held, 2, origin, piece, across)
                push(held, 3, origin, piece, sibling)
            work()

    def over(hop):
        for piece in range(PIECES):
            for side in (-1, 1) if hop else (1,):
                there = line + side * hop
                held = (there >= 0) & (there < LINE) if hop else None
                origin = index_of(there, 1 - pair, core)
                arrive(held, origin, piece)
                push(held, 3, origin, piece, sibling)
            work()

    along(1)
    over(0)
    along(2)
    over(1)
    along(3)
    over(2)
    over(3)
    for other_line in range(LINE):
        for other_pair in range(2):
            for piece in range(PIECES):
                arrive(None, index_of(other_line, other_pair, 1 - core), piece)
    if products:
        products.finish()
    for copy in ridden:
        copy.wait()
    for condition, copy in sent:
        when(condition, copy.wait_send)
    for copy in local:
        copy.wait()


class ExpertGradients:

    def __init__(self, operands, outs, scratch):
        self.sources = operands
        self.nows, self.landing, self.laters = outs[:3], outs[3:5], outs[5:6]
        self.held = scratch[:5]
        self.lows, self.stage = scratch[5:8], scratch[8]
        self.load_sem, self.out_sem, self.ride_sem = scratch[9:12]
        self.me_d, self.n_d = lax.axis_index("dp"), lax.axis_size("dp")
        self.pending, self.riding, self.count = [None, None], [], 0
        self.kinds = ((2, 1, 1), (0, 3, 0), (0, 4, 0))
        self.steps = self.all_steps()

    def load(self):
        self.loads = [
            pltpu.make_async_copy(source, held, self.load_sem.at[number])
            for number, (source, held) in enumerate(zip(self.sources, self.held))
        ]
        for copy in self.loads:
            copy.start()

    def chunk(self, number, owner, at):
        left, right, axis = self.kinds[number]
        left, right = self.held[left], self.held[right]
        shape = self.nows[number].shape
        count = chunk_rows(shape[0])
        if axis == 0:
            first = pl.multiple_of(owner * shape[0] + at * count, 128)
            return dot_left(left[:, pl.ds(first, count)], right[...])
        columns = pl.ds(pl.multiple_of(owner * shape[1], 128), shape[1])
        return dot_left(left[:, at * count : (at + 1) * count], right[:, columns])

    def all_steps(self):
        for copy in self.loads:
            copy.wait()
        for number in range(3):
            shape = self.nows[number].shape
            count = chunk_rows(shape[0])
            low = self.lows[number]
            for ahead in range(1, self.n_d):
                owner = lax.rem(self.me_d + ahead, self.n_d)
                for at in range(shape[0] // count):
                    low[ahead - 1, at * count : (at + 1) * count] = self.chunk(
                        number, owner, at
                    ).astype(BF)
                    if at == shape[0] // count - 1:
                        self.leave(number, ahead, low)
                    yield
        for number in range(3):
            shape = self.nows[number].shape
            count = chunk_rows(shape[0])
            for at in range(shape[0] // count):
                slot = self.count % 2
                if self.pending[slot] is not None:
                    self.pending[slot].wait()
                stage = self.stage.at[slot, :count, : shape[1]]
                stage[...] = self.chunk(number, self.me_d, at)
                copy = pltpu.make_async_copy(
                    stage,
                    self.nows[number].at[pl.ds(at * count, count)],
                    self.out_sem.at[slot],
                )
                copy.start()
                self.pending[slot] = copy
                self.count += 1
                yield

    def leave(self, number, ahead, low):
        if number == 2:
            copy = pltpu.make_async_copy(
                low.at[ahead - 1], self.laters[0].at[ahead - 1], self.load_sem.at[4 + ahead]
            )
        else:
            copy = pltpu.make_async_remote_copy(
                src_ref=low.at[ahead - 1],
                dst_ref=self.landing[number].at[ahead - 1],
                send_sem=self.ride_sem.at[0, number, ahead - 1],
                recv_sem=self.ride_sem.at[1, number, ahead - 1],
                device_id={"dp": lax.rem(self.me_d + ahead, self.n_d)},
                device_id_type=MESH,
            )
        copy.start()
        self.riding.append(copy)

    def next(self):
        next(self.steps, None)

    def finish(self):
        for _ in self.steps:
            pass
        for copy in self.riding + [copy for copy in self.pending if copy is not None]:
            copy.wait()


def chunk_rows(rows):
    return next(count for count in (256, 384, 352, 128, 64) if rows % count == 0)


def gradient_shapes(products, n_d):
    rows, ups, scaled, gate, up = products
    width, hidden = rows.shape[1], gate.shape[1]
    size = width // n_d
    nows = [(hidden, size), (size, hidden), (size, hidden)]
    shapes = [jax.ShapeDtypeStruct(shape, F32) for shape in nows]
    shapes += [jax.ShapeDtypeStruct((n_d - 1,) + shape, BF) for shape in nows]
    largest = max(hidden, size)
    scratch = [pltpu.VMEM(product.shape, BF) for product in products]
    scratch += [pltpu.VMEM((n_d - 1,) + shape, BF) for shape in nows]
    scratch += [
        pltpu.VMEM((2, 384, largest), F32),
        pltpu.SemaphoreType.DMA((5 + n_d,)),
        pltpu.SemaphoreType.DMA((2,)),
        pltpu.SemaphoreType.DMA((2, 3, n_d - 1)),
    ]
    return (shapes, scratch)


def gather_rows(own, collective_id, riders=(), products=()):
    count = lax.axis_size("expert")
    rows, width = own.shape
    shapes = [jax.ShapeDtypeStruct((count, rows, width), own.dtype)]
    shapes += [landed(rider) for rider in riders]
    n_d = lax.axis_size("dp")
    carried, others = max(1, len(riders)), max(1, n_d - 1)
    scratch = []
    if products:
        extra_shapes, scratch = gradient_shapes(products, n_d)
        shapes += extra_shapes
    out = pl.pallas_call(
        lambda *refs: gather_kernel([rider[1] for rider in riders], bool(products), *refs),
        out_shape=shapes,
        in_specs=[pl.BlockSpec(memory_space=pl.ANY)] * (1 + len(riders) + len(products)),
        out_specs=[pl.BlockSpec(memory_space=pl.ANY)] * len(shapes),
        scratch_shapes=[
            pltpu.SemaphoreType.DMA,
            pltpu.SemaphoreType.DMA((4, count, PIECES)),
            pltpu.SemaphoreType.DMA((count, PIECES)),
            pltpu.SemaphoreType.DMA((carried, others)),
            pltpu.SemaphoreType.DMA((carried, others)),
        ]
        + scratch,
        compiler_params=pltpu.CompilerParams(
            collective_id=collective_id, has_side_effects=True, vmem_limit_bytes=VMEM_LIMIT
        ),
        name="gather_rows",
    )(own, *[rider[0] for rider in riders], *products)
    return [out[0].reshape(count * rows, width)] + list(out[1:])


FAR_FIRST = ((3, 3, 0, 0), (2, 0, 3, 1), (1, 2, 1, 2), (0, 1, 2, 3))
COLUMNS = 512
STRIP = 16
EXTRA_ROWS = 48


def pick_by(line, table):
    value = jnp.int32(table[LINE - 1])
    for k in range(LINE - 2, -1, -1):
        value = jnp.where(line == k, jnp.int32(table[k]), value)
    return value


def add_strips(target, first, count, others):
    @pl.loop(0, count // STRIP)
    def _(strip):
        for columns in range(0, target.shape[1], COLUMNS):
            at = pl.ds(pl.multiple_of(first + strip * STRIP, STRIP), STRIP)
            cols = pl.ds(columns, COLUMNS)
            total = None
            for other in others:
                term = other[at, cols].astype(F32)
                total = term if total is None else total + term
            target[at, cols] = total.astype(target.dtype)


def step_scatter(step, buffers, semaphores):
    part, kept, met, paired, passed = buffers
    core_send, core_recv, pair_send, pair_recv, line_send, line_recv = semaphores
    me = lax.axis_index("expert")
    line, pair, core = place_of(me)
    rows = kept.shape[0]
    piece_rows = rows // PIECES
    sibling = index_of(line, pair, 1 - core)
    across = index_of(line, 1 - pair, core)
    steps = 2 * LINE

    def remote(source, dest, send_at, recv_at, target):
        return pltpu.make_async_remote_copy(
            src_ref=source,
            dst_ref=dest,
            send_sem=send_at,
            recv_sem=recv_at,
            device_id={"expert": target},
            device_id_type=MESH,
        )

    def to_sibling(i):
        return remote(part, met.at[i], core_send.at[i], core_recv.at[i], sibling)

    def to_pair(i, piece):
        at = pl.ds(piece * piece_rows, piece_rows)
        return remote(
            met.at[i, at],
            paired.at[i // 2, at],
            pair_send.at[i // 2, piece],
            pair_recv.at[i // 2, piece],
            across,
        )

    def meet(i):
        to_sibling(i).wait_recv()
        add_strips(met.at[i], 0, rows, [met.at[i], kept])

        @pl.when(lax.rem(i, 2) == 0)
        def _():
            for piece in range(PIECES):
                to_pair(i, piece).start()

    dest_line = [pick_by(line, FAR_FIRST[k]) for k in range(LINE)]

    def hop_facts(k):
        there = dest_line[k]
        way = jnp.where(there > line, 1, -1)
        behind = line - way
        held = (behind >= 0) & (behind < LINE)
        slot = jnp.where((there == line + way) & (way < 0), LINE, there)
        return (there, held, slot, index_of(line + way, pair, core))

    def along(k, piece):
        there, held, slot, target = hop_facts(k)
        at = pl.ds(piece * piece_rows, piece_rows)
        return remote(
            paired.at[k, at],
            passed.at[slot, at],
            line_send.at[k, piece],
            line_recv.at[slot, piece],
            target,
        )

    def came_along(slot, piece):
        at = pl.ds(piece * piece_rows, piece_rows)
        block = passed.at[slot, at]
        remote(block, block, line_send.at[0, piece], line_recv.at[slot, piece], me).wait_recv()

    def pair_arrived(k, piece):
        at = pl.ds(piece * piece_rows, piece_rows)
        block = paired.at[k, at]
        remote(block, block, pair_send.at[k, piece], pair_recv.at[k, piece], me).wait_recv()

    def hop(k, with_held):
        there = hop_facts(k)[0]
        for piece in range(PIECES):
            first = piece * piece_rows
            pair_arrived(k, piece)
            terms = [paired.at[k], met.at[2 * k + 1]]
            if with_held:
                came_along(there, piece)
                terms.append(passed.at[there])
            add_strips(paired.at[k], first, piece_rows, terms)
            along(k, piece).start()

    def advance(produce):
        @pl.when(step > 0)
        def _():
            meet(step - 1)

        for k in range(LINE - 1):
            held = hop_facts(k)[1]
            if 2 * k + 3 < steps:

                @pl.when((step == 2 * k + 3) & jnp.logical_not(held))
                def _():
                    hop(k, False)

            if 2 * k + 4 < steps:

                @pl.when((step == 2 * k + 4) & held)
                def _():
                    hop(k, True)

        @pl.when(step > 0)
        def _():
            to_sibling(step - 1).wait_send()

        for which in range(2):

            @pl.when(core == which)
            def _():
                produce((1 - which) * rows, part)

        to_sibling(step).start()
        for which in range(2):

            @pl.when(core == which)
            def _():
                produce(which * rows, kept)

    def finish(sum_ref):
        meet(steps - 1)
        last = LINE - 2

        @pl.when(hop_facts(last)[1])
        def _():
            hop(last, True)

        for piece in range(PIECES):
            first = piece * piece_rows
            pair_arrived(LINE - 1, piece)
            add_strips(
                sum_ref, first, piece_rows, [paired.at[LINE - 1], met.at[2 * LINE - 1]]
            )
            for has, slot in ((line > 0, line), (line < LINE - 1, LINE)):

                @pl.when(has)
                def _():
                    came_along(slot, piece)
                    add_strips(sum_ref, first, piece_rows, [sum_ref, passed.at[slot]])

        to_sibling(steps - 1).wait_send()
        for piece in range(PIECES):
            for k in range(LINE):
                to_pair(2 * k, piece).wait_send()
            for k in range(LINE - 1):
                along(k, piece).wait_send()

    return (advance, finish)


def step_buffers(block):
    return [
        pltpu.VMEM(block, BF),
        pltpu.VMEM(block, BF),
        pltpu.VMEM((2 * LINE,) + block, BF),
        pltpu.VMEM((LINE,) + block, BF),
        pltpu.VMEM((LINE + 1,) + block, BF),
        pltpu.SemaphoreType.DMA((2 * LINE,)),
        pltpu.SemaphoreType.DMA((2 * LINE,)),
        pltpu.SemaphoreType.DMA((LINE, PIECES)),
        pltpu.SemaphoreType.DMA((LINE, PIECES)),
        pltpu.SemaphoreType.DMA((LINE, PIECES)),
        pltpu.SemaphoreType.DMA((LINE + 1, PIECES)),
    ]


def step_tile(i):
    line, pair, _ = place_of(lax.axis_index("expert"))
    there = pick_by(line, FAR_FIRST[LINE - 1])
    for k in range(LINE - 2, -1, -1):
        there = jnp.where(i // 2 == k, pick_by(line, FAR_FIRST[k]), there)
    return there * 2 + jnp.where(lax.rem(i, 2) == 0, 1 - pair, pair)


def taker(refs):
    refs = list(refs)

    def take(number):
        taken = refs[:number]
        del refs[:number]
        return taken

    return take


def scatter_folded(fold, out_ref, buffers, semaphores):
    part, met, paired, passed = buffers
    core_send, core_recv, pair_send, pair_recv, line_send, line_recv = semaphores
    me = lax.axis_index("expert")
    line, pair, core = place_of(me)
    rows = out_ref.shape[0]
    sibling = index_of(line, pair, 1 - core)
    across = index_of(line, 1 - pair, core)
    sent = []

    def send(source, dest, send_at, recv_at, target):
        copy = pltpu.make_async_remote_copy(
            src_ref=source,
            dst_ref=dest,
            send_sem=send_at,
            recv_sem=recv_at,
            device_id={"expert": target},
            device_id_type=MESH,
        )
        copy.start()
        sent.append(copy)

    def await_block(block, recv_at, send_at):
        pltpu.make_async_remote_copy(
            src_ref=block,
            dst_ref=block,
            send_sem=send_at,
            recv_sem=recv_at,
            device_id={"expert": me},
            device_id_type=MESH,
        ).wait_recv()

    dest_line = [pick_by(line, FAR_FIRST[step]) for step in range(LINE)]

    def chip(i):
        return (dest_line[i // 2], (1 - pair) if i % 2 == 0 else pair)

    for i in range(2 * LINE):
        there, other = chip(i)
        fold(index_of(there, other, 1 - core), part.at[i])
        send(part.at[i], met.at[i], core_send.at[i], core_recv.at[i], sibling)
    for i in range(2 * LINE):
        there, other = chip(i)
        await_block(met.at[i], core_recv.at[i], core_send.at[i])
        fold(index_of(there, other, core), paired.at[LINE])
        add_strips(met.at[i], 0, rows, [met.at[i], paired.at[LINE]])
        if i % 2 == 0:
            send(met.at[i], paired.at[i // 2], pair_send.at[i // 2], pair_recv.at[i // 2], across)
    for step in range(LINE - 1):
        there = dest_line[step]
        way = jnp.where(there > line, 1, -1)
        behind = line - way
        held = (behind >= 0) & (behind < LINE)
        target = index_of(line + way, pair, core)
        slot = jnp.where((there == line + way) & (way < 0), LINE, there)
        await_block(paired.at[step], pair_recv.at[step], pair_send.at[step])
        add_strips(paired.at[step], 0, rows, [paired.at[step], met.at[2 * step + 1]])

        @pl.when(held)
        def _():
            await_block(passed.at[there], line_recv.at[there], line_send.at[step])
            add_strips(paired.at[step], 0, rows, [paired.at[step], passed.at[there]])

        send(paired.at[step], passed.at[slot], line_send.at[step], line_recv.at[slot], target)
    step = LINE - 1
    await_block(paired.at[step], pair_recv.at[step], pair_send.at[step])
    add_strips(out_ref, 0, rows, [paired.at[step], met.at[2 * step + 1]])
    for held, slot in ((line > 0, line), (line < LINE - 1, LINE)):

        @pl.when(held)
        def _():
            await_block(passed.at[slot], line_recv.at[slot], line_send.at[0])
            add_strips(out_ref, 0, rows, [out_ref, passed.at[slot]])

    for copy in sent:
        copy.wait_send()


TILE_GROUPS = 4
SCALE = (DN + DR) ** (-0.5)


def half_turn(values):
    lane = lax.broadcasted_iota(jnp.int32, values.shape, 1)
    lower = (lane // (DR // 2)) % 2 == 0
    return jnp.where(lower, pltpu.roll(values, 128 - DR // 2, 1), pltpu.roll(values, DR // 2, 1))


def group_mask(column_ref, row_ref):
    column, row = column_ref[...], row_ref[0]
    shape = (column.shape[0], row.shape[1])
    earlier = lax.broadcasted_iota(jnp.int32, shape, 1) <= lax.broadcasted_iota(
        jnp.int32, shape, 0
    )
    same = (column == row) | ((row % 4 == 0) & (column // 4 == row // 4))
    return earlier & same


def softmax_scores(query, key, mask):
    scores = jnp.where(mask, dot_right(query, key) * SCALE, -1e30)
    powers = jnp.exp(scores - jnp.max(scores, axis=-1, keepdims=True))
    return powers / jnp.sum(powers, axis=-1, keepdims=True)


def attention_forward_kernel(
    spans, x_ref, gain_ref, first_ref, latent_gain_ref, up_ref, trig_ref, column_ref, row_ref,
    output_ref, *refs,
):
    riders = len(spans)
    take = taker(refs)
    sources = [cut_rows(source, rows) for source, rows in zip(take(riders), spans)]
    normed_ref, query_ref, key_ref, value_ref, unit_ref, low_ref, scale_ref, attended_ref = take(8)
    (sum_ref,), targets = take(1), take(riders)
    buffers, semaphores, ride_sems = take(5), take(6), take(2)
    step = pl.program_id(0)

    @pl.when(step == 0)
    def _():
        others = lax.axis_size("dp") - 1 if riders else 0
        greet_dp(others)
        greet(*place_of(lax.axis_index("expert")), others)
        ride(sources, targets, *ride_sems)

    rank = up_ref.shape[0]
    inputs = x_ref[...].astype(F32)
    scale = lax.rsqrt(jnp.mean(inputs * inputs, axis=1, keepdims=True) + EPS)
    normed_ref[...] = (inputs * scale * gain_ref[...]).astype(BF)
    out = dot(normed_ref[...], first_ref[...])
    latent = out[:, DN : DN + rank]
    latent_scale = lax.rsqrt(jnp.mean(latent * latent, axis=1, keepdims=True) + EPS)
    scale_ref[...] = latent_scale
    unit = latent * latent_scale
    unit_ref[...] = unit.astype(BF)
    low_ref[...] = (unit * latent_gain_ref[...]).astype(BF)
    keys_values = dot(low_ref[...], up_ref[...])
    rope = out[:, DN + rank :]
    turned = rope * trig_ref[:, :128] + half_turn(rope) * trig_ref[:, 128:]
    lane = lax.broadcasted_iota(jnp.int32, turned.shape, 1)
    query_ref[:, :DN] = out[:, :DN].astype(BF)
    query_ref[:, DN:] = jnp.where(lane < DR, pltpu.roll(turned, DR, 1), 0.0).astype(BF)
    key_ref[:, :DN] = keys_values[:, :DN].astype(BF)
    key_ref[:, DN:] = jnp.where(lane < DR, turned, 0.0).astype(BF)
    value_ref[...] = keys_values[:, DN:].astype(BF)
    probs = softmax_scores(query_ref[...], key_ref[...], group_mask(column_ref, row_ref))
    attended_ref[...] = dot(probs.astype(BF), value_ref[...]).astype(BF)
    advance, finish = step_scatter(step, buffers, semaphores)

    def produce(first, target):
        rows, width = target.shape

        @pl.loop(0, width // COLUMNS)
        def _(tile):
            columns = pl.ds(pl.multiple_of(tile * COLUMNS, COLUMNS), COLUMNS)
            target[:, columns] = dot(
                attended_ref[pl.ds(first, rows)], output_ref[:, columns]
            ).astype(BF)

    advance(produce)

    @pl.when(step == 2 * LINE - 1)
    def _():
        finish(sum_ref)
        for copy in ride(sources, targets, *ride_sems, start=False):
            copy.wait()


def attention_forward(
    x, gain, first_w, latent_gain, up_w, trig, column, row, output_w, riders, collective_id
):
    width, rank = first_w.shape[0], up_w.shape[0]
    span, rows = column.shape[0], row.shape[2]

    def tile(columns):
        return pl.BlockSpec((rows, columns), lambda i: (step_tile(i), 0))

    def fixed(shape):
        return pl.BlockSpec(shape, lambda i: (0, 0), pipeline_mode=pl.Buffered(1))

    anywhere = pl.BlockSpec(memory_space=pl.ANY)
    block = (rows // 2, width)
    carried, others = max(1, len(riders)), max(1, lax.axis_size("dp") - 1)
    outs = (width, 2 * DN, 2 * DN, DV, rank, rank, 1, DV)
    kinds = (BF, BF, BF, BF, BF, BF, F32, BF)
    return pl.pallas_call(
        lambda *refs: attention_forward_kernel([rider[1] for rider in riders], *refs),
        grid=(span // rows,),
        in_specs=[
            tile(width),
            fixed((1, width)),
            fixed(first_w.shape),
            fixed((1, rank)),
            fixed(up_w.shape),
            tile(trig.shape[1]),
            tile(1),
            pl.BlockSpec((1, 1, rows), lambda i: (step_tile(i), 0, 0)),
            fixed(output_w.shape),
        ]
        + [anywhere] * len(riders),
        out_specs=[tile(columns) for columns in outs]
        + [pl.BlockSpec(block, lambda i: (0, 0))]
        + [anywhere] * len(riders),
        out_shape=[jax.ShapeDtypeStruct((span, c), k) for c, k in zip(outs, kinds)]
        + [jax.ShapeDtypeStruct(block, F32)]
        + [landed(rider) for rider in riders],
        scratch_shapes=step_buffers(block)
        + [pltpu.SemaphoreType.DMA((carried, others)) for _ in range(2)],
        compiler_params=pltpu.CompilerParams(
            collective_id=collective_id, has_side_effects=True, vmem_limit_bytes=VMEM_LIMIT
        ),
        name="attention_forward",
    )(
        x, gain[None], first_w, latent_gain[None], up_w, trig, column, row, output_w,
        *[rider[0] for rider in riders],
    )


def attention_backward_kernel(
    latent_piece, small_rows, spans,
    r_ref, output_ref, attended_ref, query_ref, key_ref, value_ref, column_ref, row_ref, trig_ref,
    unit_ref, low_ref, scale_ref, latent_gain_ref, up_ref, normed_ref, first_ref, turned_ref,
    side_ref, gain_ref, *refs,
):
    riders = len(spans)
    take = taker(refs)
    sources = [cut_rows(source, rows) for source, rows in zip(take(riders), spans)]
    (sum_ref, folded_ref), (query_out, up_out, output_out) = take(2), take(3)
    own_targets, targets = take(4), take(riders)
    grad_ref, kv_ref, output_grad_ref, up_grad_ref, first_grad_ref, gain_grad_ref = take(6)
    query_full, query_low, up_low, output_low, small_ref, folded_low = take(6)
    fold_buffers, fold_semaphores = take(4), take(6)
    buffers, semaphores, ride_sems, out_sem, own_sems = take(5), take(6), take(2), take(1)[0], take(2)
    step = pl.program_id(0)
    rank = up_ref.shape[0]
    n_d, me_d = lax.axis_size("dp"), lax.axis_index("dp")
    experts = lax.axis_size("expert")

    @pl.when(step == 0)
    def _():
        greet_dp(n_d - 1)
        greet(*place_of(lax.axis_index("expert")), n_d - 1)
        ride(sources, targets, *ride_sems)
        output_grad_ref[...] = jnp.zeros_like(output_grad_ref)
        up_grad_ref[...] = jnp.zeros_like(up_grad_ref)
        first_grad_ref[...] = jnp.zeros_like(first_grad_ref)
        gain_grad_ref[...] = jnp.zeros_like(gain_grad_ref)

    attended_grad = dot_right(r_ref[...], output_ref[...]).astype(BF)
    output_grad_ref[...] += dot_left(attended_ref[...], r_ref[...])
    probs = softmax_scores(query_ref[...], key_ref[...], group_mask(column_ref, row_ref))
    kv_ref[:, DN:] = dot_left(probs.astype(BF), attended_grad).astype(BF)
    probs_grad = dot_right(attended_grad, value_ref[...])
    inner = jnp.sum(probs * probs_grad, axis=1, keepdims=True)
    score_grad = (probs * (probs_grad - inner)).astype(BF)
    query_grad = dot(score_grad, key_ref[...]) * SCALE
    key_grad = dot_left(score_grad, query_ref[...]) * SCALE
    kv_ref[:, :DN] = key_grad[:, :DN].astype(BF)
    grad_ref[:, :DN] = query_grad[:, :DN].astype(BF)
    rope = key_grad[:, DN:] + pltpu.roll(query_grad[:, DN:], DR, 1)
    rope = rope * trig_ref[:, :128] + half_turn(rope * trig_ref[:, 128:])
    grad_ref[:, DN + rank :] = rope.astype(BF)
    out_grad = dot_right(kv_ref[...], up_ref[...])
    unit = unit_ref[...].astype(F32)
    gain_grad_ref[...] += jnp.sum(out_grad * unit, axis=0, keepdims=True)
    scaled = out_grad * latent_gain_ref[...]
    inner = jnp.mean(scaled * unit, axis=1, keepdims=True)
    grad_ref[:, DN : DN + rank] = (scale_ref[...] * (scaled - unit * inner)).astype(BF)
    up_grad_ref[...] += dot_left(low_ref[...], kv_ref[...])
    first_grad_ref[...] += dot_left(normed_ref[...], grad_ref[...])
    advance, finish = step_scatter(step, buffers, semaphores)

    def produce(first, target):
        rows, width = target.shape

        @pl.loop(0, width // COLUMNS)
        def _(tile):
            columns = pl.ds(pl.multiple_of(tile * COLUMNS, COLUMNS), COLUMNS)
            target[:, columns] = dot(
                grad_ref[pl.ds(first, rows)], turned_ref[:, columns]
            ).astype(BF)

    advance(produce)

    def part(array, number, owner):
        size = array.shape[1 if number == 2 else 0] // n_d
        at = pl.ds(pl.multiple_of(owner * size, size), size)
        return array.at[:, at] if number == 2 else array.at[at]

    def own_copies():
        copies = []
        for number, low in enumerate((query_low, up_low, output_low)):
            for ahead in range(1, n_d):
                owner = lax.rem(me_d + ahead, n_d)
                copies.append((part(low, number, owner), number, ahead))
        for ahead in range(1, n_d):
            copies.append((folded_low, 3, ahead))
        return [
            pltpu.make_async_remote_copy(
                src_ref=source,
                dst_ref=own_targets[number].at[ahead - 1],
                send_sem=own_sems[0].at[number, ahead - 1],
                recv_sem=own_sems[1].at[number, ahead - 1],
                device_id={"dp": lax.rem(me_d + ahead, n_d)},
                device_id_type=MESH,
            )
            for source, number, ahead in copies
        ]

    @pl.when(step == 2 * LINE - 1)
    def _():
        last = DN + rank
        strip = 256

        @pl.loop(0, first_grad_ref.shape[0] // strip)
        def _(tile):
            first = pl.multiple_of(tile * strip, strip)
            at = pl.ds(first, strip)
            sums = first_grad_ref[at]
            rope = sums[:, last:]
            query_full[at, :DN] = sums[:, :DN]
            query_full[at, DN:] = pltpu.roll(rope, DR, 1)
            query_low[at, :DN] = sums[:, :DN].astype(BF)
            query_low[at, DN:] = pltpu.roll(rope, DR, 1).astype(BF)
            small_ref[at, :rank] = sums[:, DN:last].astype(BF)
            gain_sum = jnp.sum(sums * first_ref[at].astype(F32), axis=1, keepdims=True)
            gain_sum = gain_sum / gain_ref[at]
            row = lax.broadcasted_iota(jnp.int32, (strip, rank), 0) + first
            index = lax.broadcasted_iota(jnp.int32, (strip, rank), 1)
            place = (index // latent_piece) * small_rows + index % latent_piece
            latent_sum = jnp.sum(
                jnp.where(row == place, gain_grad_ref[...], 0.0), axis=1, keepdims=True
            )
            lane = lax.broadcasted_iota(jnp.int32, rope.shape, 1)
            mixed = jnp.where(lane < DR, rope, side_ref[at].astype(F32))
            mixed = jnp.where(lane == DR + experts + 1, gain_sum, mixed)
            mixed = jnp.where(lane == DR + experts + 2, latent_sum, mixed)
            small_ref[at, rank:] = mixed.astype(BF)

        up_low[...] = up_grad_ref[...].astype(BF)
        output_low[...] = output_grad_ref[...].astype(BF)
        outs = [
            pltpu.make_async_copy(query_full, query_out, out_sem.at[0]),
            pltpu.make_async_copy(up_grad_ref, up_out, out_sem.at[1]),
            pltpu.make_async_copy(output_grad_ref, output_out, out_sem.at[2]),
        ]
        for copy in outs:
            copy.start()
        moves = own_copies()
        for copy in moves[: 3 * (n_d - 1)]:
            copy.start()

        def fold(dest, target):
            wide = small_ref.shape[1]
            total = folded_ref.shape[0] // STRIP
            target[...] = jnp.zeros(target.shape, BF)
            for unit in range(n_d * small_rows // STRIP):
                owner, first = (unit * STRIP) // small_rows, (unit * STRIP) % small_rows
                start = pl.multiple_of((owner * experts + dest) * small_rows + first, STRIP)
                target[
                    (unit % total) * STRIP : (unit % total + 1) * STRIP,
                    (unit // total) * wide : (unit // total + 1) * wide,
                ] = small_ref[pl.ds(start, STRIP)]

        scatter_folded(fold, folded_ref, fold_buffers, fold_semaphores)
        folded_low[...] = folded_ref[...].astype(BF)
        for copy in moves[3 * (n_d - 1) :]:
            copy.start()
        finish(sum_ref)
        for copy in moves + outs:
            copy.wait()
        for copy in ride(sources, targets, *ride_sems, start=False):
            copy.wait()


def attention_backward(
    residual_all, output_w, stored, column, row, trig, latent_gain, up_w, first_w, side, gain,
    latent_piece, small_rows, riders, collective_id,
):
    normed, query, key, value, unit, low, scale, attended = stored
    width, rank = residual_all.shape[1], up_w.shape[0]
    rows = row.shape[2]
    n_d = lax.axis_size("dp")
    first_width = 2 * DN + rank
    block = (rows // 2, width)
    folded = (EXTRA_ROWS, width)
    small = (width, rank + 128)

    def tile(columns):
        return pl.BlockSpec((rows, columns), lambda i: (step_tile(i), 0))

    def fixed(shape):
        return pl.BlockSpec(shape, lambda i: (0, 0), pipeline_mode=pl.Buffered(1))

    anywhere = pl.BlockSpec(memory_space=pl.ANY)
    carried, others = max(1, len(riders)), max(1, n_d - 1)
    query_shape, up_shape, output_shape = (width, 2 * DN), up_w.shape, output_w.shape
    to_others = [
        (n_d - 1, query_shape[0] // n_d, query_shape[1]),
        (n_d - 1, up_shape[0] // n_d, up_shape[1]),
        (n_d - 1, output_shape[0], output_shape[1] // n_d),
        (n_d - 1,) + folded,
    ]
    return pl.pallas_call(
        lambda *refs: attention_backward_kernel(
            latent_piece, small_rows, [rider[1] for rider in riders], *refs
        ),
        grid=(2 * LINE,),
        in_specs=[
            tile(width),
            fixed(output_w.shape),
            tile(DV),
            tile(2 * DN),
            tile(2 * DN),
            tile(DV),
            tile(1),
            pl.BlockSpec((1, 1, rows), lambda i: (step_tile(i), 0, 0)),
            tile(trig.shape[1]),
            tile(rank),
            tile(rank),
            tile(1),
            fixed((1, rank)),
            fixed(up_w.shape),
            tile(width),
            fixed(first_w.shape),
            fixed((first_width, width)),
            fixed(side.shape),
            fixed((width, 1)),
        ]
        + [anywhere] * len(riders),
        out_specs=[pl.BlockSpec(block, lambda i: (0, 0)), pl.BlockSpec(folded, lambda i: (0, 0))]
        + [anywhere] * (7 + len(riders)),
        out_shape=[
            jax.ShapeDtypeStruct(shape, F32)
            for shape in (block, folded, query_shape, up_shape, output_shape)
        ]
        + [jax.ShapeDtypeStruct(shape, BF) for shape in to_others]
        + [landed(rider) for rider in riders],
        scratch_shapes=[
            pltpu.VMEM((rows, first_width), BF),
            pltpu.VMEM((rows, DN + DV), BF),
            pltpu.VMEM(output_shape, F32),
            pltpu.VMEM(up_shape, F32),
            pltpu.VMEM((width, first_width), F32),
            pltpu.VMEM((1, rank), F32),
            pltpu.VMEM(query_shape, F32),
            pltpu.VMEM(query_shape, BF),
            pltpu.VMEM(up_shape, BF),
            pltpu.VMEM(output_shape, BF),
            pltpu.VMEM(small, BF),
            pltpu.VMEM(folded, BF),
            pltpu.VMEM((2 * LINE,) + folded, BF),
            pltpu.VMEM((2 * LINE,) + folded, BF),
            pltpu.VMEM((LINE + 1,) + folded, BF),
            pltpu.VMEM((LINE + 1,) + folded, BF),
            pltpu.SemaphoreType.DMA((2 * LINE,)),
            pltpu.SemaphoreType.DMA((2 * LINE,)),
            pltpu.SemaphoreType.DMA((LINE,)),
            pltpu.SemaphoreType.DMA((LINE,)),
            pltpu.SemaphoreType.DMA((LINE,)),
            pltpu.SemaphoreType.DMA((LINE + 1,)),
        ]
        + step_buffers(block)
        + [pltpu.SemaphoreType.DMA((carried, others)) for _ in range(2)]
        + [pltpu.SemaphoreType.DMA((3,))]
        + [pltpu.SemaphoreType.DMA((4, others)) for _ in range(2)],
        compiler_params=pltpu.CompilerParams(
            collective_id=collective_id, has_side_effects=True, vmem_limit_bytes=VMEM_LIMIT
        ),
        name="attention_backward",
    )(
        residual_all, output_w, attended, query, key, value, column, row, trig,
        unit, low, scale, latent_gain[None], up_w, normed, first_w, first_w.T, side,
        gain[:, None], *[rider[0] for rider in riders],
    )


HIDDEN = 256
ROUTER_AT = 448


def expert_layer_kernel(
    splits,
    ffn_ref, y_ref, code_row_ref, code_column_ref, wide_ref, shared_down_ref, *refs,
):
    take = taker(refs)
    own_weights, came = take(3), take(len(splits))
    (
        rows_ref, ups_ref, scaled_ref, gate_ref, up_ref, mixed_ref,
        down_grad_out, wide_grad_out, sum_ref,
    ) = take(9)
    (
        gate_w_ref, up_w_ref, down_w_ref, load_sem, out_sem, down_grad_ref, wide_grad_ref,
        grad_ref, left_ref, inner_ref, returned_ref, slot_gate_ref, slot_dot_ref,
        part, kept, met, paired, passed,
        core_send, core_recv, pair_send, pair_recv, line_send, line_recv,
    ) = take(24)
    step = pl.program_id(0)
    me = lax.axis_index("expert")
    experts = lax.axis_size("expert")
    line, pair, core = place_of(me)
    me_d, n_d = lax.axis_index("dp"), lax.axis_size("dp")
    groups, _, per = code_row_ref.shape
    slots = rows_ref.shape[0] // groups
    width = ffn_ref.shape[1]
    hidden = gate_w_ref.shape[1]

    wholes = (gate_w_ref, up_w_ref, down_w_ref)
    loads = []

    def load(source, number, owner, start, count):
        axis = 1 if number == 2 else 0
        size = own_weights[number].shape[axis]
        at = pl.multiple_of(owner * size, size)
        if axis == 0:
            place = wholes[number].at[pl.ds(at + start, count)]
        else:
            place = wholes[number].at[:, pl.ds(at, size)]
        loads.append(pltpu.make_async_copy(source, place, load_sem.at[len(loads)]))

    for number in range(3):
        load(own_weights[number], number, me_d, 0, own_weights[number].shape[0])
    for source, (number, first, end) in zip(came, splits):
        for ahead in range(1, n_d):
            owner = lax.rem(me_d - ahead + n_d, n_d)
            load(source.at[ahead - 1], number, owner, first, end - first)

    @pl.when(step == 0)
    def _():
        for copy in loads:
            copy.start()
        greet(line, pair, core)
        down_grad_ref[...] = jnp.zeros_like(down_grad_ref)
        wide_grad_ref[...] = jnp.zeros_like(wide_grad_ref)

    out = dot(ffn_ref[...], wide_ref[...])
    gates, ups = out[:, :HIDDEN], out[:, HIDDEN:]
    last = out[:, 2 * HIDDEN - 128 :]
    lane = lax.broadcasted_iota(jnp.int32, last.shape, 1)
    first_lane = ROUTER_AT - (2 * HIDDEN - 128)
    logits = jnp.where((lane >= first_lane) & (lane < first_lane + experts), last, -1e30)
    powers = jnp.exp(logits - jnp.max(logits, axis=1, keepdims=True))
    probs = powers / jnp.sum(powers, axis=1, keepdims=True)
    own_lane = (lane == first_lane + me).astype(F32)
    own_probs = jnp.sum(probs * own_lane, axis=1, keepdims=True)
    sigmoid = 1.0 / (1.0 + jnp.exp(-gates))
    silu = gates * sigmoid
    shared_low = (silu * ups).astype(BF)
    back = dot_right(y_ref[...], shared_down_ref[...])
    left_ref[:, :HIDDEN] = (back * ups * sigmoid * (1.0 + gates * (1.0 - sigmoid))).astype(BF)
    shared_up_low = back * silu
    left_ref[:, HIDDEN : 2 * HIDDEN - 128] = shared_up_low[:, : HIDDEN - 128].astype(BF)
    shared_last = shared_up_low[:, HIDDEN - 128 :]
    down_grad_ref[...] += dot_left(shared_low, y_ref[...])

    square = (per, per)
    diagonal = lax.broadcasted_iota(jnp.int32, square, 0) == lax.broadcasted_iota(
        jnp.int32, square, 1
    )
    for group in range(groups):
        tokens_at = pl.ds(group * per, per)
        slots_at = pl.ds(group * slots, slots)
        slot_ids = lax.broadcasted_iota(jnp.int32, (slots, per), 0)
        picks = slot_ids == code_row_ref[group]
        picks_low = picks.astype(F32).astype(BF)
        rows_ref[slots_at] = dot(picks_low, ffn_ref[tokens_at]).astype(BF)
        ups_ref[slots_at] = dot(picks_low, y_ref[tokens_at]).astype(BF)
        own_column = own_probs[group * per : (group + 1) * per]
        own_row = jnp.sum(jnp.where(diagonal, own_column, 0.0), axis=0, keepdims=True)
        slot_gate_ref[slots_at] = jnp.sum(
            jnp.where(picks, own_row, 0.0), axis=1, keepdims=True
        )
    slot_dot_ref[...] = jnp.zeros_like(slot_dot_ref)

    @pl.when(step == 0)
    def _():
        for copy in loads:
            copy.wait()

    def hidden_part(columns):
        gate_part = dot(rows_ref[...], gate_w_ref[:, columns])
        up_part = dot(rows_ref[...], up_w_ref[:, columns])
        raw = dot_right(ups_ref[...], down_w_ref[columns, :])
        slot_gate = slot_gate_ref[...]
        sigmoid = 1.0 / (1.0 + jnp.exp(-gate_part))
        silu = gate_part * sigmoid
        inner = silu * up_part
        slot_dot_ref[...] += jnp.sum(inner * raw, axis=1, keepdims=True)
        grad = raw * slot_gate
        inner_ref[:, columns] = inner.astype(BF)
        scaled_ref[:, columns] = (inner * slot_gate).astype(BF)
        gate_ref[:, columns] = (
            grad * up_part * sigmoid * (1.0 + gate_part * (1.0 - sigmoid))
        ).astype(BF)
        up_ref[:, columns] = (grad * silu).astype(BF)

    @pl.loop(0, hidden // HIDDEN)
    def _(tile):
        hidden_part(pl.ds(pl.multiple_of(tile * HIDDEN, HIDDEN), HIDDEN))

    if hidden % HIDDEN:
        hidden_part(pl.ds(hidden - hidden % HIDDEN, hidden % HIDDEN))

    @pl.loop(0, width // COLUMNS)
    def _(tile):
        columns = pl.ds(pl.multiple_of(tile * COLUMNS, COLUMNS), COLUMNS)
        returned_ref[:, columns] = dot(inner_ref[...], down_w_ref[:, columns]).astype(BF)
        grad_ref[:, columns] = (
            dot_right(gate_ref[...], gate_w_ref[columns, :])
            + dot_right(up_ref[...], up_w_ref[columns, :])
        ).astype(BF)

    for group in range(groups):
        tokens_at = pl.ds(group * per, per)
        slots_at = pl.ds(group * slots, slots)
        own_column = own_probs[group * per : (group + 1) * per]
        slot_lane = lax.broadcasted_iota(jnp.int32, (per, slots), 1)
        picks = slot_lane == code_column_ref[tokens_at]
        pick_gate = jnp.where(picks, own_column, 0.0).astype(BF)
        mixed_ref[tokens_at] = (
            dot(shared_low[group * per : (group + 1) * per], shared_down_ref[...])
            + dot(pick_gate, returned_ref[slots_at])
        ).astype(BF)
        small = (slots, slots)
        eye = lax.broadcasted_iota(jnp.int32, small, 0) == lax.broadcasted_iota(
            jnp.int32, small, 1
        )
        dot_row = jnp.sum(jnp.where(eye, slot_dot_ref[slots_at], 0.0), axis=0, keepdims=True)
        row_dot = jnp.sum(jnp.where(picks, dot_row, 0.0), axis=1, keepdims=True)
        at = slice(group * per, (group + 1) * per)
        logit_grad = row_dot * own_column * (own_lane[at] - probs[at])
        high = logit_grad.astype(BF)
        rest = logit_grad - high.astype(F32)
        left_ref[tokens_at, 2 * HIDDEN - 128 :] = jnp.where(
            lane[at] < first_lane,
            shared_last[at],
            high.astype(F32) + pltpu.roll(rest, experts, 1),
        ).astype(BF)
    wide_grad_ref[...] += dot_left(ffn_ref[...], left_ref[...])

    advance, finish = step_scatter(
        step, (part, kept, met, paired, passed),
        (core_send, core_recv, pair_send, pair_recv, line_send, line_recv),
    )
    rows = kept.shape[0]

    def produce(first, target):
        @pl.loop(0, width // COLUMNS)
        def _(tile):
            columns = pl.ds(pl.multiple_of(tile * COLUMNS, COLUMNS), COLUMNS)
            total = dot_right(left_ref[pl.ds(first, rows)], wide_ref[columns, :])
            for k in range(rows // per):
                group = first // per + k
                slot_lane = lax.broadcasted_iota(jnp.int32, (per, slots), 1)
                picks = slot_lane == code_column_ref[pl.ds(first + k * per, per)]
                scattered = dot(
                    picks.astype(F32).astype(BF),
                    grad_ref[pl.ds(group * slots, slots), columns],
                )
                target[pl.ds(k * per, per), columns] = (
                    total[k * per : (k + 1) * per] + scattered
                ).astype(BF)

    advance(produce)

    @pl.when(step == 2 * LINE - 1)
    def _():
        outs = [
            pltpu.make_async_copy(down_grad_ref, down_grad_out, out_sem.at[0]),
            pltpu.make_async_copy(wide_grad_ref, wide_grad_out, out_sem.at[1]),
        ]
        for copy in outs:
            copy.start()
        finish(sum_ref)
        for copy in outs:
            copy.wait()


def expert_layer(
    ffn_all, upstream_all, code, slots, wide, shared_down, weights, came, splits, collective_id
):
    groups, per = code.shape
    span, width = ffn_all.shape
    gate_w, up_w, down_w = weights
    hidden = gate_w.shape[1]
    n_d = lax.axis_size("dp")
    rows, slot_rows = TILE_GROUPS * per, TILE_GROUPS * slots
    total = groups * slots
    steps = 2 * LINE
    block = (rows // 2, width)

    def tile(count, columns):
        return pl.BlockSpec((count, columns), lambda i: (step_tile(i), 0))

    def fixed(shape):
        return pl.BlockSpec(shape, lambda i: (0, 0), pipeline_mode=pl.Buffered(1))

    anywhere = pl.BlockSpec(memory_space=pl.ANY)
    outs = [(total, width)] * 2 + [(total, hidden)] * 3 + [(span, width)]
    sums = [shared_down.shape, wide.shape]
    copies = 3 + len(came) * (n_d - 1)
    return pl.pallas_call(
        lambda *refs: expert_layer_kernel(splits, *refs),
        grid=(steps,),
        in_specs=[
            tile(rows, width),
            tile(rows, width),
            pl.BlockSpec((TILE_GROUPS, 1, per), lambda i: (step_tile(i), 0, 0)),
            tile(rows, 1),
            fixed(wide.shape),
            fixed(shared_down.shape),
        ]
        + [anywhere] * (3 + len(came)),
        out_specs=[
            tile(slot_rows if shape[0] == total else rows, shape[1]) for shape in outs
        ]
        + [anywhere] * 2
        + [pl.BlockSpec(block, lambda i: (0, 0))],
        out_shape=[jax.ShapeDtypeStruct(shape, BF) for shape in outs]
        + [jax.ShapeDtypeStruct(shape, F32) for shape in sums]
        + [jax.ShapeDtypeStruct(block, BF)],
        scratch_shapes=[
            pltpu.VMEM((gate_w.shape[0] * n_d, hidden), BF),
            pltpu.VMEM((up_w.shape[0] * n_d, hidden), BF),
            pltpu.VMEM((hidden, down_w.shape[1] * n_d), BF),
            pltpu.SemaphoreType.DMA((copies,)),
            pltpu.SemaphoreType.DMA((2,)),
            pltpu.VMEM(shared_down.shape, F32),
            pltpu.VMEM(wide.shape, F32),
            pltpu.VMEM((slot_rows, width), BF),
            pltpu.VMEM((rows, 2 * HIDDEN), BF),
            pltpu.VMEM((slot_rows, hidden), BF),
            pltpu.VMEM((slot_rows, width), BF),
            pltpu.VMEM((slot_rows, 1), F32),
            pltpu.VMEM((slot_rows, 1), F32),
        ]
        + step_buffers(block),
        compiler_params=pltpu.CompilerParams(
            collective_id=collective_id,
            has_side_effects=True,
            vmem_limit_bytes=63 * 1024 * 1024,
        ),
        name="expert_layer",
    )(
        ffn_all, upstream_all, code[:, None, :], code.reshape(span, 1), wide, shared_down,
        gate_w, up_w, down_w, *came,
    )


def on_device(
    tokens,
    segment,
    routes,
    drop_order,
    cotangent,
    attn_gain,
    query_weight,
    down_latent,
    latent_gain,
    up_latent,
    output_weight,
    ffn_gain,
    router_weight,
    shared_gate,
    shared_up,
    shared_down,
    expert_gate,
    expert_up,
    expert_down,
):
    n_e = lax.axis_size("expert")
    n_d = lax.axis_size("dp")
    me_e = lax.axis_index("expert")
    me_d = lax.axis_index("dp")
    micro, group_rows, width = tokens.shape
    own_rows = micro * group_rows
    span = n_e * own_rows
    groups = n_e * micro
    top = routes.shape[2]
    experts = n_e * expert_gate.shape[0]
    capacity = (5 * group_rows * top + 4 * experts - 1) // (4 * experts)
    slots = -(-capacity // 16) * 16
    rank_latent = latent_gain.shape[0] * n_e * n_d

    def gather(values):
        return lax.all_gather(values, "expert", axis=0, tiled=True)

    def scatter(values):
        return lax.psum_scatter(values, "expert", scatter_dimension=0, tiled=True)

    def whole(own, parts, axis):
        size = own.shape[axis]
        shape = list(own.shape)
        shape[axis] = size * n_d
        total = jnp.zeros(shape, own.dtype)
        for step in range(n_d):
            at = lax.rem(me_d - step + n_d, n_d) * size
            block = parts[step - 1] if step else own
            total = lax.dynamic_update_slice_in_dim(total, block, at, axis)
        return total

    def split_dp(values, axis):
        size = values.shape[axis] // n_d
        parts = []
        for step in range(n_d):
            at = lax.rem(me_d + step, n_d) * size
            parts.append(lax.dynamic_slice_in_dim(values, at, size, axis))
        return (stack([part.astype(BF) for part in parts[1:]]), parts[0])

    def stack(parts):
        return parts[0][None] if len(parts) == 1 else jnp.stack(parts)

    def add_all(total, parts):
        for step in range(n_d - 1):
            total = total + parts[step].astype(F32)
        return total

    small_rows = attn_gain.shape[0]
    latent_all_width = down_latent.shape[1]
    latent_piece = latent_gain.shape[0]
    packed = jnp.concatenate(
        [
            down_latent,
            router_weight,
            attn_gain[:, None],
            ffn_gain[:, None],
            jnp.pad(latent_gain, (0, small_rows - latent_piece))[:, None],
        ],
        axis=1,
    )
    packed = lax.all_gather(packed, ("dp", "expert"), axis=0, tiled=True)
    down_all = packed[:, :latent_all_width]
    router_all = packed[:, latent_all_width : latent_all_width + experts]
    rest = packed[:, latent_all_width + experts :].astype(F32)
    attn_gain_all = rest[:, 0]
    ffn_gain_all = rest[:, 1]
    latent_gain_all = rest[:, 2].reshape(n_e * n_d, small_rows)[:, :latent_piece].reshape(-1)

    chosen = jnp.sum(
        (routes[..., None] == jnp.arange(experts, dtype=jnp.int32)).astype(jnp.int32), axis=2
    )
    order = drop_order[:, 0]
    earlier = (order[:, None, :] < order[:, :, None]).astype(F32)
    rank = jnp.einsum("mtu,mue->mte", earlier, chosen.astype(F32)).astype(jnp.int32)
    code = jnp.where((chosen == 1) & (rank < capacity), rank, -1).reshape(own_rows, experts)

    tokens_own = tokens.reshape(own_rows, width)
    code_lanes = -(-experts // 128) * 128
    code_low = jnp.pad(code.astype(BF), ((0, 0), (0, code_lanes - experts)))
    own_gate, own_up, own_down = expert_gate[0], expert_up[0], expert_down[0]
    gate_half = own_gate.shape[0] // 2
    up_most = own_up.shape[0] * 3 // 4
    dense = (query_weight, up_latent, output_weight, shared_gate, shared_up, shared_down)
    came = gather_rows(
        jnp.concatenate([tokens_own, code_low], axis=1),
        5,
        riders=[(array, (0, array.shape[0])) for array in dense] + [(own_gate, (0, gate_half))],
    )
    tokens_all, gate_came = came[0], came[7]
    query_w, up_w, output_w, shared_gate_w, shared_up_w, shared_down_w = [
        whole(own, parts, axis)
        for own, parts, axis in zip(dense, came[1:7], (0, 0, 1, 0, 0, 1))
    ]
    upstream_own = cotangent.reshape(own_rows, width)
    upstream_later, tokens_all = lax.optimization_barrier((upstream_own, tokens_all))
    upstream_all = gather(upstream_later)
    code_all = tokens_all[:, width : width + experts].astype(jnp.int32)
    my_code = lax.dynamic_slice_in_dim(code_all, me_e, 1, 1).reshape(groups, group_rows)

    span_segment = (
        segment.reshape(micro, n_e, group_rows).transpose(1, 0, 2).reshape(groups, group_rows)
    )
    trig = angles(positions(span_segment), group_rows)
    marks = span_segment + 4 * jnp.arange(groups, dtype=jnp.int32)[:, None]
    column = marks.reshape(span, 1)
    row = marks.reshape(groups // TILE_GROUPS, 1, TILE_GROUPS * group_rows)
    first_w = jnp.concatenate(
        [
            query_w[:, :DN],
            down_all[:, :rank_latent],
            down_all[:, rank_latent:],
            query_w[:, DN:],
        ],
        axis=1,
    )
    came = attention_forward(
        tokens_all,
        attn_gain_all,
        first_w,
        latent_gain_all,
        up_w,
        trig,
        column,
        row,
        output_w,
        [(own_gate, (gate_half, own_gate.shape[0])), (own_up, (0, up_most))],
        2,
    )
    stored, attention_out, gate_came_last, up_came = came[:8], came[8], came[9], came[10]
    residual = tokens_own.astype(F32) + attention_out

    second_scale = rms_scale(residual)
    ffn_in = (residual * second_scale * ffn_gain_all).astype(BF)
    ffn_all, up_came_last, down_came = gather_rows(
        ffn_in,
        1,
        riders=[(own_up, (up_most, own_up.shape[0])), (own_down, (0, own_down.shape[0]))],
    )

    shared_hidden = shared_gate_w.shape[1]
    wide = jnp.concatenate(
        [
            jnp.pad(shared_gate_w, ((0, 0), (0, HIDDEN - shared_hidden))),
            jnp.pad(shared_up_w, ((0, 0), (0, ROUTER_AT - HIDDEN - shared_hidden))),
            router_all,
            jnp.pad(router_all, ((0, 0), (0, 2 * HIDDEN - ROUTER_AT - 2 * experts))),
        ],
        axis=1,
    )
    (
        expert_rows,
        slot_up,
        inner_scaled,
        gate_low,
        up_low,
        mixed_part,
        shared_down_grad,
        wide_grad,
        ffn_grad,
    ) = expert_layer(
        ffn_all,
        upstream_all,
        my_code,
        slots,
        wide,
        jnp.pad(shared_down_w, ((0, HIDDEN - shared_hidden), (0, 0))),
        (own_gate, own_up, own_down),
        (gate_came, gate_came_last, up_came, up_came_last, down_came),
        (
            (0, 0, gate_half),
            (0, gate_half, own_gate.shape[0]),
            (1, 0, up_most),
            (1, up_most, own_up.shape[0]),
            (2, 0, own_down.shape[0]),
        ),
        3,
    )
    ffn_grad = ffn_grad.astype(F32)
    mixed = residual + scatter(mixed_part).astype(F32)
    router_grad = (
        wide_grad[:, ROUTER_AT : ROUTER_AT + experts]
        + wide_grad[:, ROUTER_AT + experts : ROUTER_AT + 2 * experts]
    )
    shared_down_later, shared_down_now = split_dp(shared_down_grad[:shared_hidden], 1)
    shared_gate_later, shared_gate_now = split_dp(wide_grad[:, :shared_hidden], 0)
    shared_up_later, shared_up_now = split_dp(wide_grad[:, HIDDEN : HIDDEN + shared_hidden], 0)
    residual_part, ffn_gain_grad = norm_back(residual, second_scale, ffn_gain_all, ffn_grad)
    residual_grad = upstream_own.astype(F32) + residual_part
    (
        residual_all,
        down_now,
        gate_now,
        up_now,
        down_parts,
        gate_parts,
        up_later,
    ) = gather_rows(
        residual_grad.astype(BF),
        6,
        products=(expert_rows, slot_up, inner_scaled, gate_low, up_low),
    )

    side = jnp.concatenate(
        [
            jnp.zeros((width, DR), F32),
            router_grad,
            ffn_gain_grad[:, None],
            jnp.zeros((width, 128 - DR - experts - 1), F32),
        ],
        axis=1,
    ).astype(BF)
    (
        normed_grad,
        folded,
        query_full,
        up_latent_full,
        output_full,
        query_parts,
        latent_parts,
        output_parts,
        folded_parts,
        up_parts,
        shared_down_parts,
        shared_gate_parts,
        shared_up_parts,
    ) = attention_backward(
        residual_all,
        output_w,
        stored,
        column,
        row,
        trig,
        latent_gain_all,
        up_w,
        first_w,
        side,
        attn_gain_all,
        latent_piece,
        small_rows,
        [
            (later, None)
            for later in (up_later, shared_down_later, shared_gate_later, shared_up_later)
        ],
        4,
    )

    def own_part(values, axis):
        size = values.shape[axis] // n_d
        return lax.dynamic_slice_in_dim(values, me_d * size, size, axis)

    query_grad = add_all(own_part(query_full, 0), query_parts)[:, : DN + DR]
    up_latent_grad = add_all(own_part(up_latent_full, 0), latent_parts)
    output_grad = add_all(own_part(output_full, 1), output_parts)
    small_width = rank_latent + 128
    folded = add_all(folded, folded_parts)
    small = jnp.concatenate(
        [folded[:, k * small_width : (k + 1) * small_width] for k in range(width // small_width)],
        axis=0,
    )
    small = lax.dynamic_slice_in_dim(small, me_d * small_rows, small_rows, 0)
    own_inputs = tokens_own.astype(F32)
    input_part, _ = norm_back(own_inputs, rms_scale(own_inputs), attn_gain_all, normed_grad)
    tokens_grad = residual_grad + input_part
    last = latent_all_width + experts
    shape = (micro, group_rows, width)
    return (
        mixed.reshape(shape),
        tokens_grad.reshape(shape),
        small[:, last + 1],
        query_grad,
        small[:, :latent_all_width],
        small[:latent_piece, last + 2],
        up_latent_grad,
        output_grad,
        small[:, last],
        small[:, latent_all_width:last],
        add_all(shared_gate_now, shared_gate_parts),
        add_all(shared_up_now, shared_up_parts),
        add_all(shared_down_now, shared_down_parts),
        add_all(gate_now, gate_parts)[None],
        add_all(up_now, up_parts)[None],
        add_all(down_now, down_parts)[None],
    )


def solution(mesh):
    rows = P(None, ("dp", "expert"), None)
    split = P(("dp", "expert"))
    split_rows = P(("dp", "expert"), None)
    columns = P("dp", "expert")
    turned = P("expert", "dp")
    expert_in = P("expert", "dp", None)
    expert_out = P("expert", None, "dp")
    return jax.shard_map(
        on_device,
        mesh=mesh,
        in_specs=(
            rows,
            P(None, "dp"),
            rows,
            rows,
            rows,
            split,
            columns,
            split_rows,
            split,
            columns,
            turned,
            split,
            split_rows,
            columns,
            columns,
            turned,
            expert_in,
            expert_in,
            expert_out,
        ),
        out_specs=(
            rows,
            rows,
            split,
            columns,
            split_rows,
            split,
            columns,
            turned,
            split,
            split_rows,
            columns,
            columns,
            turned,
            expert_in,
            expert_in,
            expert_out,
        ),
        check_vma=False,
    )
```

```python
import math

import jax
import jax.numpy as jnp
from jax import lax
from jax.experimental import pallas as pl
from jax.experimental.pallas import tpu as pltpu
from jax.sharding import PartitionSpec as P

DN = 128
DR = 64
DV = 128
EPS = 1e-06
HIGH = lax.Precision.HIGHEST
F32 = jnp.float32
BF = jnp.bfloat16


def dot(former, latter):
    return jnp.dot(former, latter, preferred_element_type=F32)


def dot_left(former, latter):
    return lax.dot_general(former, latter, (((0,), (0,)), ((), ())), preferred_element_type=F32)


def dot_right(former, latter):
    return lax.dot_general(former, latter, (((1,), (1,)), ((), ())), preferred_element_type=F32)


def rms_scale(values):
    return lax.rsqrt(jnp.mean(values * values, axis=-1, keepdims=True) + EPS)


def norm_back(values, scale_rows, gain, out_grad):
    scaled = out_grad * gain
    inner = jnp.mean(scaled * values, axis=-1, keepdims=True)
    value_grad = scale_rows * scaled - values * scale_rows * scale_rows * scale_rows * inner
    return (value_grad, jnp.sum(out_grad * values * scale_rows, axis=0))


def positions(segment):
    places = jnp.arange(segment.shape[1], dtype=jnp.int32)
    prompt_len = jnp.sum((segment == 0).astype(jnp.int32), axis=1, keepdims=True)
    former = (segment[:, None, :] < segment[:, :, None]).astype(jnp.int32)
    seg_start = jnp.sum(former, axis=2)
    return jnp.where(segment == 0, places[None], prompt_len + places[None] - seg_start)


def angles(position, row_count):
    freq_index = jnp.arange(DR // 2, dtype=F32)
    frequency = jnp.exp(freq_index * (-2.0 * math.log(10000.0) / DR))
    turning = jnp.arange(row_count, dtype=F32)[:, None] * frequency[None, :]
    cosine, sine_part = jnp.cos(turning), jnp.sin(turning)
    table = jnp.concatenate([cosine] * 4 + [-sine_part, sine_part] * 2, axis=1)
    picks = (position.reshape(-1)[:, None] == jnp.arange(row_count)[None, :]).astype(F32)
    return jnp.dot(picks, table, precision=HIGH)


LINE = 4
PIECES = 3
MESH = pl.DeviceIdType.MESH
VMEM_LIMIT = 60 * 1024 * 1024


def place_of(me):
    return (me // 4, lax.rem(me // 2, 2), lax.rem(me, 2))


def index_of(line, pair, core):
    return line * 4 + pair * 2 + core


def greet(line, pair, core, others=0):
    barrier = pltpu.get_barrier_semaphore()

    def signal(target):
        pl.semaphore_signal(barrier, inc=1, device_id={"expert": target}, device_id_type=MESH)

    signal(index_of(line, pair, 1 - core))
    signal(index_of(line, 1 - pair, core))

    @pl.when(line > 0)
    def _():
        signal(index_of(line - 1, pair, core))

    @pl.when(line < LINE - 1)
    def _():
        signal(index_of(line + 1, pair, core))

    inner = jnp.where(line > 0, 1, 0) + jnp.where(line < LINE - 1, 1, 0)
    pl.semaphore_wait(barrier, 2 + others + inner)


def greet_dp(others):
    barrier = pltpu.get_barrier_semaphore()
    me_d, n_d = lax.axis_index("dp"), lax.axis_size("dp")
    if others:
        for step in range(1, n_d):
            pl.semaphore_signal(
                barrier,
                inc=1,
                device_id={"dp": lax.rem(me_d + step, n_d)},
                device_id_type=MESH,
            )


def ride(sources, targets, send_sem, recv_sem, start=True):
    me_d, n_d = lax.axis_index("dp"), lax.axis_size("dp")
    copies = []
    for number, (source, target) in enumerate(zip(sources, targets)):
        parts = len(source.shape) == len(target.shape)
        for step in range(1, n_d):
            copy = pltpu.make_async_remote_copy(
                src_ref=source.at[step - 1] if parts else source,
                dst_ref=target.at[step - 1],
                send_sem=send_sem.at[number, step - 1],
                recv_sem=recv_sem.at[number, step - 1],
                device_id={"dp": lax.rem(me_d + step, n_d)},
                device_id_type=MESH,
            )
            if start:
                copy.start()
            copies.append(copy)
    return copies


def landed(rider):
    array, rows = rider
    if rows is None:
        return jax.ShapeDtypeStruct(array.shape, array.dtype)
    shape = (lax.axis_size("dp") - 1, rows[1] - rows[0]) + array.shape[1:]
    return jax.ShapeDtypeStruct(shape, array.dtype)


def cut_rows(ref, rows):
    return ref if rows is None else ref.at[pl.ds(rows[0], rows[1] - rows[0])]


def when(condition, action):
    if condition is None:
        action()
    else:
        pl.when(condition)(action)


def gather_kernel(spans, products, *refs):
    riders = len(spans)
    take = taker(refs)
    (own_ref,), sources = take(1), take(riders)
    products_in = take(5) if products else None
    (out_ref,), targets = take(1), take(riders)
    products_out = take(6) if products else None
    own_sem, send_sem, recv_sem, ride_send, ride_recv = take(5)
    if products:
        products = ExpertGradients(products_in, products_out, take(12))
    sources = [cut_rows(source, rows) for source, rows in zip(sources, spans)]
    me = lax.axis_index("expert")
    line, pair, core = place_of(me)
    rows = own_ref.shape[0]
    sixth = rows // 6
    half = (rows - sixth) // 2
    spans_of = (pl.ds(0, sixth), pl.ds(sixth, half), pl.ds(sixth + half, half))
    others = lax.axis_size("dp") - 1 if riders or products else 0
    greet_dp(others)
    greet(line, pair, core, others)
    local = [pltpu.make_async_copy(own_ref, out_ref.at[me], own_sem)]
    sent = []

    def push(condition, kind, origin, piece, target, source=None):
        block = out_ref.at[origin, spans_of[piece]]
        copy = pltpu.make_async_remote_copy(
            src_ref=block if source is None else source,
            dst_ref=block,
            send_sem=send_sem.at[kind, origin, piece],
            recv_sem=recv_sem.at[origin, piece],
            device_id={"expert": target},
            device_id_type=MESH,
        )
        when(condition, copy.start)
        sent.append((condition, copy))

    def arrive(condition, origin, piece):
        block = out_ref.at[origin, spans_of[piece]]
        copy = pltpu.make_async_remote_copy(
            src_ref=block,
            dst_ref=block,
            send_sem=send_sem.at[0, origin, piece],
            recv_sem=recv_sem.at[origin, piece],
            device_id={"expert": me},
            device_id_type=MESH,
        )
        when(condition, copy.wait_recv)

    left = index_of(line - 1, pair, core)
    right = index_of(line + 1, pair, core)
    across = index_of(line, 1 - pair, core)
    sibling = index_of(line, pair, 1 - core)
    for piece in range(PIECES):
        source = own_ref.at[spans_of[piece]]
        push(line < LINE - 1, 1, me, piece, right, source)
        push(line > 0, 0, me, piece, left, source)
        push(None, 2, me, piece, across, source)
        push(None, 3, me, piece, sibling, source)
    ridden = ride(sources, targets, ride_send, ride_recv)
    for copy in local:
        copy.start()
    if products:
        products.load()

    def work():
        if products:
            products.next()

    def along(hop, piece):
        for side in (-1, 1):
            there = line + side * hop
            held = (there >= 0) & (there < LINE)
            origin = index_of(there, pair, core)
            arrive(held, origin, piece)
            pass_on(held, side, hop, origin, piece)
            if piece:
                push(held, 2, origin, piece, across)
            push(held, 3, origin, piece, sibling)
        work()

    def pass_on(held, side, hop, origin, piece):
        if hop < LINE - 1:
            further = held & ((line < LINE - 1) if side < 0 else (line > 0))
            kind, target = (1, right) if side < 0 else (0, left)
            push(further, kind, origin, piece, target)

    def over(hop, piece):
        for side in (-1, 1) if hop else (1,):
            there = line + side * hop
            held = (there >= 0) & (there < LINE) if hop else None
            origin = index_of(there, 1 - pair, core)
            arrive(held, origin, piece)
            if piece == 0 and hop:
                pass_on(held, side, hop, origin, piece)
            if piece == 0 and not hop:
                push(line < LINE - 1, 1, origin, piece, right)
                push(line > 0, 0, origin, piece, left)
            push(held, 3, origin, piece, sibling)
        work()

    over(0, 0)
    for hop in range(1, LINE):
        for piece in range(PIECES):
            along(hop, piece)
        over(hop, 0)
        for piece in range(1, PIECES):
            over(hop - 1, piece)
    for piece in range(1, PIECES):
        over(LINE - 1, piece)
    for other_line in range(LINE):
        for other_pair in range(2):
            for piece in range(PIECES):
                arrive(None, index_of(other_line, other_pair, 1 - core), piece)
    if products:
        products.finish()
    for copy in ridden:
        copy.wait()
    for condition, copy in sent:
        when(condition, copy.wait_send)
    for copy in local:
        copy.wait()


class ExpertGradients:

    def __init__(self, operands, outs, scratch):
        self.sources = operands
        self.nows, self.landing, self.laters = outs[:3], outs[3:5], outs[5:6]
        self.held = scratch[:5]
        self.lows, self.stage = scratch[5:8], scratch[8]
        self.load_sem, self.out_sem, self.ride_sem = scratch[9:12]
        self.me_d, self.n_d = lax.axis_index("dp"), lax.axis_size("dp")
        self.pending, self.riding, self.count = [None, None], [], 0
        self.kinds = ((2, 1, 1), (0, 3, 0), (0, 4, 0))
        self.steps = self.all_steps()

    def load(self):
        self.loads = [
            pltpu.make_async_copy(source, held, self.load_sem.at[number])
            for number, (source, held) in enumerate(zip(self.sources, self.held))
        ]
        for copy in self.loads:
            copy.start()

    def chunk(self, number, owner, at):
        left, right, axis = self.kinds[number]
        left, right = self.held[left], self.held[right]
        shape = self.nows[number].shape
        count = chunk_rows(shape[0])
        if axis == 0:
            first = pl.multiple_of(owner * shape[0] + at * count, 128)
            return dot_left(left[:, pl.ds(first, count)], right[...])
        columns = pl.ds(pl.multiple_of(owner * shape[1], 128), shape[1])
        return dot_left(left[:, at * count : (at + 1) * count], right[:, columns])

    def all_steps(self):
        for copy in self.loads:
            copy.wait()
        for number in range(3):
            shape = self.nows[number].shape
            count = chunk_rows(shape[0])
            low = self.lows[number]
            for ahead in range(1, self.n_d):
                owner = lax.rem(self.me_d + ahead, self.n_d)
                for at in range(shape[0] // count):
                    low[ahead - 1, at * count : (at + 1) * count] = self.chunk(
                        number, owner, at
                    ).astype(BF)
                    if at == shape[0] // count - 1:
                        self.leave(number, ahead, low)
                    yield
        for number in range(3):
            shape = self.nows[number].shape
            count = chunk_rows(shape[0])
            for at in range(shape[0] // count):
                slot = self.count % 2
                if self.pending[slot] is not None:
                    self.pending[slot].wait()
                stage = self.stage.at[slot, :count, : shape[1]]
                stage[...] = self.chunk(number, self.me_d, at)
                copy = pltpu.make_async_copy(
                    stage,
                    self.nows[number].at[pl.ds(at * count, count)],
                    self.out_sem.at[slot],
                )
                copy.start()
                self.pending[slot] = copy
                self.count += 1
                yield

    def leave(self, number, ahead, low):
        if number == 2:
            copy = pltpu.make_async_copy(
                low.at[ahead - 1], self.laters[0].at[ahead - 1], self.load_sem.at[4 + ahead]
            )
        else:
            copy = pltpu.make_async_remote_copy(
                src_ref=low.at[ahead - 1],
                dst_ref=self.landing[number].at[ahead - 1],
                send_sem=self.ride_sem.at[0, number, ahead - 1],
                recv_sem=self.ride_sem.at[1, number, ahead - 1],
                device_id={"dp": lax.rem(self.me_d + ahead, self.n_d)},
                device_id_type=MESH,
            )
        copy.start()
        self.riding.append(copy)

    def next(self):
        next(self.steps, None)

    def finish(self):
        for _ in self.steps:
            pass
        for copy in self.riding + [copy for copy in self.pending if copy is not None]:
            copy.wait()


def chunk_rows(rows):
    return next(count for count in (256, 384, 352, 128, 64) if rows % count == 0)


def gradient_shapes(products, n_d):
    rows, ups, scaled, gate, up = products
    width, hidden = rows.shape[1], gate.shape[1]
    size = width // n_d
    nows = [(hidden, size), (size, hidden), (size, hidden)]
    shapes = [jax.ShapeDtypeStruct(shape, F32) for shape in nows]
    shapes += [jax.ShapeDtypeStruct((n_d - 1,) + shape, BF) for shape in nows]
    largest = max(hidden, size)
    scratch = [pltpu.VMEM(product.shape, BF) for product in products]
    scratch += [pltpu.VMEM((n_d - 1,) + shape, BF) for shape in nows]
    scratch += [
        pltpu.VMEM((2, 384, largest), F32),
        pltpu.SemaphoreType.DMA((5 + n_d,)),
        pltpu.SemaphoreType.DMA((2,)),
        pltpu.SemaphoreType.DMA((2, 3, n_d - 1)),
    ]
    return (shapes, scratch)


def gather_rows(own, collective_id, riders=(), products=()):
    count = lax.axis_size("expert")
    rows, width = own.shape
    shapes = [jax.ShapeDtypeStruct((count, rows, width), own.dtype)]
    shapes += [landed(rider) for rider in riders]
    n_d = lax.axis_size("dp")
    carried, others = max(1, len(riders)), max(1, n_d - 1)
    scratch = []
    if products:
        extra_shapes, scratch = gradient_shapes(products, n_d)
        shapes += extra_shapes
    out = pl.pallas_call(
        lambda *refs: gather_kernel([rider[1] for rider in riders], bool(products), *refs),
        out_shape=shapes,
        in_specs=[pl.BlockSpec(memory_space=pl.ANY)] * (1 + len(riders) + len(products)),
        out_specs=[pl.BlockSpec(memory_space=pl.ANY)] * len(shapes),
        scratch_shapes=[
            pltpu.SemaphoreType.DMA,
            pltpu.SemaphoreType.DMA((4, count, PIECES)),
            pltpu.SemaphoreType.DMA((count, PIECES)),
            pltpu.SemaphoreType.DMA((carried, others)),
            pltpu.SemaphoreType.DMA((carried, others)),
        ]
        + scratch,
        compiler_params=pltpu.CompilerParams(
            collective_id=collective_id, has_side_effects=True, vmem_limit_bytes=VMEM_LIMIT
        ),
        name="gather_rows",
    )(own, *[rider[0] for rider in riders], *products)
    return [out[0].reshape(count * rows, width)] + list(out[1:])


FAR_FIRST = ((3, 3, 0, 0), (2, 0, 3, 1), (1, 2, 1, 2), (0, 1, 2, 3))
COLUMNS = 512
STRIP = 16
EXTRA_ROWS = 48


def pick_by(line, table):
    value = jnp.int32(table[LINE - 1])
    for k in range(LINE - 2, -1, -1):
        value = jnp.where(line == k, jnp.int32(table[k]), value)
    return value


def add_strips(target, first, count, others):
    @pl.loop(0, count // STRIP)
    def _(strip):
        for columns in range(0, target.shape[1], COLUMNS):
            at = pl.ds(pl.multiple_of(first + strip * STRIP, STRIP), STRIP)
            cols = pl.ds(columns, COLUMNS)
            total = None
            for other in others:
                term = other[at, cols].astype(F32)
                total = term if total is None else total + term
            target[at, cols] = total.astype(target.dtype)


def step_scatter(step, buffers, semaphores):
    part, kept, met, paired, passed = buffers
    core_send, core_recv, pair_send, pair_recv, line_send, line_recv = semaphores
    me = lax.axis_index("expert")
    line, pair, core = place_of(me)
    rows = kept.shape[0]
    piece_rows = rows // PIECES
    sibling = index_of(line, pair, 1 - core)
    across = index_of(line, 1 - pair, core)
    steps = 2 * LINE

    def remote(source, dest, send_at, recv_at, target):
        return pltpu.make_async_remote_copy(
            src_ref=source,
            dst_ref=dest,
            send_sem=send_at,
            recv_sem=recv_at,
            device_id={"expert": target},
            device_id_type=MESH,
        )

    def to_sibling(i):
        return remote(part, met.at[i], core_send.at[i], core_recv.at[i], sibling)

    def to_pair(i, piece):
        at = pl.ds(piece * piece_rows, piece_rows)
        return remote(
            met.at[i, at],
            paired.at[i // 2, at],
            pair_send.at[i // 2, piece],
            pair_recv.at[i // 2, piece],
            across,
        )

    def meet(i):
        to_sibling(i).wait_recv()
        add_strips(met.at[i], 0, rows, [met.at[i], kept])

        @pl.when(lax.rem(i, 2) == 0)
        def _():
            for piece in range(PIECES):
                to_pair(i, piece).start()

    dest_line = [pick_by(line, FAR_FIRST[k]) for k in range(LINE)]

    def hop_facts(k):
        there = dest_line[k]
        way = jnp.where(there > line, 1, -1)
        behind = line - way
        held = (behind >= 0) & (behind < LINE)
        slot = jnp.where((there == line + way) & (way < 0), LINE, there)
        return (there, held, slot, index_of(line + way, pair, core))

    def along(k, piece):
        there, held, slot, target = hop_facts(k)
        at = pl.ds(piece * piece_rows, piece_rows)
        return remote(
            paired.at[k, at],
            passed.at[slot, at],
            line_send.at[k, piece],
            line_recv.at[slot, piece],
            target,
        )

    def came_along(slot, piece):
        at = pl.ds(piece * piece_rows, piece_rows)
        block = passed.at[slot, at]
        remote(block, block, line_send.at[0, piece], line_recv.at[slot, piece], me).wait_recv()

    def pair_arrived(k, piece):
        at = pl.ds(piece * piece_rows, piece_rows)
        block = paired.at[k, at]
        remote(block, block, pair_send.at[k, piece], pair_recv.at[k, piece], me).wait_recv()

    def hop(k, with_held):
        there = hop_facts(k)[0]
        for piece in range(PIECES):
            first = piece * piece_rows
            pair_arrived(k, piece)
            terms = [paired.at[k], met.at[2 * k + 1]]
            if with_held:
                came_along(there, piece)
                terms.append(passed.at[there])
            add_strips(paired.at[k], first, piece_rows, terms)
            along(k, piece).start()

    def advance(produce):
        @pl.when(step > 0)
        def _():
            meet(step - 1)

        for k in range(LINE - 1):
            held = hop_facts(k)[1]
            if 2 * k + 3 < steps:

                @pl.when((step == 2 * k + 3) & jnp.logical_not(held))
                def _():
                    hop(k, False)

            if 2 * k + 4 < steps:

                @pl.when((step == 2 * k + 4) & held)
                def _():
                    hop(k, True)

        @pl.when(step > 0)
        def _():
            to_sibling(step - 1).wait_send()

        for which in range(2):

            @pl.when(core == which)
            def _():
                produce((1 - which) * rows, part)

        to_sibling(step).start()
        for which in range(2):

            @pl.when(core == which)
            def _():
                produce(which * rows, kept)

    def finish(sum_ref):
        meet(steps - 1)
        last = LINE - 2

        @pl.when(hop_facts(last)[1])
        def _():
            hop(last, True)

        for piece in range(PIECES):
            first = piece * piece_rows
            pair_arrived(LINE - 1, piece)
            add_strips(
                sum_ref, first, piece_rows, [paired.at[LINE - 1], met.at[2 * LINE - 1]]
            )
            for has, slot in ((line > 0, line), (line < LINE - 1, LINE)):

                @pl.when(has)
                def _():
                    came_along(slot, piece)
                    add_strips(sum_ref, first, piece_rows, [sum_ref, passed.at[slot]])

        to_sibling(steps - 1).wait_send()
        for piece in range(PIECES):
            for k in range(LINE):
                to_pair(2 * k, piece).wait_send()
            for k in range(LINE - 1):
                along(k, piece).wait_send()

    return (advance, finish)


def step_buffers(block):
    return [
        pltpu.VMEM(block, BF),
        pltpu.VMEM(block, BF),
        pltpu.VMEM((2 * LINE,) + block, BF),
        pltpu.VMEM((LINE,) + block, BF),
        pltpu.VMEM((LINE + 1,) + block, BF),
        pltpu.SemaphoreType.DMA((2 * LINE,)),
        pltpu.SemaphoreType.DMA((2 * LINE,)),
        pltpu.SemaphoreType.DMA((LINE, PIECES)),
        pltpu.SemaphoreType.DMA((LINE, PIECES)),
        pltpu.SemaphoreType.DMA((LINE, PIECES)),
        pltpu.SemaphoreType.DMA((LINE + 1, PIECES)),
    ]


def step_tile(i):
    line, pair, _ = place_of(lax.axis_index("expert"))
    there = pick_by(line, FAR_FIRST[LINE - 1])
    for k in range(LINE - 2, -1, -1):
        there = jnp.where(i // 2 == k, pick_by(line, FAR_FIRST[k]), there)
    return there * 2 + jnp.where(lax.rem(i, 2) == 0, 1 - pair, pair)


def taker(refs):
    refs = list(refs)

    def take(number):
        taken = refs[:number]
        del refs[:number]
        return taken

    return take


def scatter_folded(fold, out_ref, buffers, semaphores):
    part, met, paired, passed = buffers
    core_send, core_recv, pair_send, pair_recv, line_send, line_recv = semaphores
    me = lax.axis_index("expert")
    line, pair, core = place_of(me)
    rows = out_ref.shape[0]
    sibling = index_of(line, pair, 1 - core)
    across = index_of(line, 1 - pair, core)
    sent = []

    def send(source, dest, send_at, recv_at, target):
        copy = pltpu.make_async_remote_copy(
            src_ref=source,
            dst_ref=dest,
            send_sem=send_at,
            recv_sem=recv_at,
            device_id={"expert": target},
            device_id_type=MESH,
        )
        copy.start()
        sent.append(copy)

    def await_block(block, recv_at, send_at):
        pltpu.make_async_remote_copy(
            src_ref=block,
            dst_ref=block,
            send_sem=send_at,
            recv_sem=recv_at,
            device_id={"expert": me},
            device_id_type=MESH,
        ).wait_recv()

    dest_line = [pick_by(line, FAR_FIRST[step]) for step in range(LINE)]

    def chip(i):
        return (dest_line[i // 2], (1 - pair) if i % 2 == 0 else pair)

    for i in range(2 * LINE):
        there, other = chip(i)
        fold(index_of(there, other, 1 - core), part.at[i])
        send(part.at[i], met.at[i], core_send.at[i], core_recv.at[i], sibling)
    for i in range(2 * LINE):
        there, other = chip(i)
        await_block(met.at[i], core_recv.at[i], core_send.at[i])
        fold(index_of(there, other, core), paired.at[LINE])
        add_strips(met.at[i], 0, rows, [met.at[i], paired.at[LINE]])
        if i % 2 == 0:
            send(met.at[i], paired.at[i // 2], pair_send.at[i // 2], pair_recv.at[i // 2], across)
    for step in range(LINE - 1):
        there = dest_line[step]
        way = jnp.where(there > line, 1, -1)
        behind = line - way
        held = (behind >= 0) & (behind < LINE)
        target = index_of(line + way, pair, core)
        slot = jnp.where((there == line + way) & (way < 0), LINE, there)
        await_block(paired.at[step], pair_recv.at[step], pair_send.at[step])
        add_strips(paired.at[step], 0, rows, [paired.at[step], met.at[2 * step + 1]])

        @pl.when(held)
        def _():
            await_block(passed.at[there], line_recv.at[there], line_send.at[step])
            add_strips(paired.at[step], 0, rows, [paired.at[step], passed.at[there]])

        send(paired.at[step], passed.at[slot], line_send.at[step], line_recv.at[slot], target)
    step = LINE - 1
    await_block(paired.at[step], pair_recv.at[step], pair_send.at[step])
    add_strips(out_ref, 0, rows, [paired.at[step], met.at[2 * step + 1]])
    for held, slot in ((line > 0, line), (line < LINE - 1, LINE)):

        @pl.when(held)
        def _():
            await_block(passed.at[slot], line_recv.at[slot], line_send.at[0])
            add_strips(out_ref, 0, rows, [out_ref, passed.at[slot]])

    for copy in sent:
        copy.wait_send()


TILE_GROUPS = 4
SCALE = (DN + DR) ** (-0.5)


def half_turn(values):
    lane = lax.broadcasted_iota(jnp.int32, values.shape, 1)
    lower = (lane // (DR // 2)) % 2 == 0
    return jnp.where(lower, pltpu.roll(values, 128 - DR // 2, 1), pltpu.roll(values, DR // 2, 1))


def group_mask(column_ref, row_ref):
    column, row = column_ref[...], row_ref[0]
    shape = (column.shape[0], row.shape[1])
    earlier = lax.broadcasted_iota(jnp.int32, shape, 1) <= lax.broadcasted_iota(
        jnp.int32, shape, 0
    )
    same = (column == row) | ((row % 4 == 0) & (column // 4 == row // 4))
    return earlier & same


def softmax_scores(query, key, mask):
    scores = jnp.where(mask, dot_right(query, key) * SCALE, -1e30)
    powers = jnp.exp(scores - jnp.max(scores, axis=-1, keepdims=True))
    return powers / jnp.sum(powers, axis=-1, keepdims=True)


def attention_forward_kernel(
    spans, x_ref, gain_ref, first_ref, latent_gain_ref, up_ref, trig_ref, column_ref, row_ref,
    output_ref, *refs,
):
    riders = len(spans)
    take = taker(refs)
    sources = [cut_rows(source, rows) for source, rows in zip(take(riders), spans)]
    normed_ref, query_ref, key_ref, value_ref, unit_ref, low_ref, scale_ref, attended_ref = take(8)
    (sum_ref,), targets = take(1), take(riders)
    buffers, semaphores, ride_sems = take(5), take(6), take(2)
    step = pl.program_id(0)

    @pl.when(step == 0)
    def _():
        others = lax.axis_size("dp") - 1 if riders else 0
        greet_dp(others)
        greet(*place_of(lax.axis_index("expert")), others)
        ride(sources, targets, *ride_sems)

    rank = up_ref.shape[0]
    inputs = x_ref[...].astype(F32)
    scale = lax.rsqrt(jnp.mean(inputs * inputs, axis=1, keepdims=True) + EPS)
    normed_ref[...] = (inputs * scale * gain_ref[...]).astype(BF)
    out = dot(normed_ref[...], first_ref[...])
    latent = out[:, DN : DN + rank]
    latent_scale = lax.rsqrt(jnp.mean(latent * latent, axis=1, keepdims=True) + EPS)
    scale_ref[...] = latent_scale
    unit = latent * latent_scale
    unit_ref[...] = unit.astype(BF)
    low_ref[...] = (unit * latent_gain_ref[...]).astype(BF)
    keys_values = dot(low_ref[...], up_ref[...])
    rope = out[:, DN + rank :]
    turned = rope * trig_ref[:, :128] + half_turn(rope) * trig_ref[:, 128:]
    lane = lax.broadcasted_iota(jnp.int32, turned.shape, 1)
    query_ref[:, :DN] = out[:, :DN].astype(BF)
    query_ref[:, DN:] = jnp.where(lane < DR, pltpu.roll(turned, DR, 1), 0.0).astype(BF)
    key_ref[:, :DN] = keys_values[:, :DN].astype(BF)
    key_ref[:, DN:] = jnp.where(lane < DR, turned, 0.0).astype(BF)
    value_ref[...] = keys_values[:, DN:].astype(BF)
    probs = softmax_scores(query_ref[...], key_ref[...], group_mask(column_ref, row_ref))
    attended_ref[...] = dot(probs.astype(BF), value_ref[...]).astype(BF)
    advance, finish = step_scatter(step, buffers, semaphores)

    def produce(first, target):
        rows, width = target.shape

        @pl.loop(0, width // COLUMNS)
        def _(tile):
            columns = pl.ds(pl.multiple_of(tile * COLUMNS, COLUMNS), COLUMNS)
            target[:, columns] = dot(
                attended_ref[pl.ds(first, rows)], output_ref[:, columns]
            ).astype(BF)

    advance(produce)

    @pl.when(step == 2 * LINE - 1)
    def _():
        finish(sum_ref)
        for copy in ride(sources, targets, *ride_sems, start=False):
            copy.wait()


def attention_forward(
    x, gain, first_w, latent_gain, up_w, trig, column, row, output_w, riders, collective_id
):
    width, rank = first_w.shape[0], up_w.shape[0]
    span, rows = column.shape[0], row.shape[2]

    def tile(columns):
        return pl.BlockSpec((rows, columns), lambda i: (step_tile(i), 0))

    def fixed(shape):
        return pl.BlockSpec(shape, lambda i: (0, 0), pipeline_mode=pl.Buffered(1))

    anywhere = pl.BlockSpec(memory_space=pl.ANY)
    block = (rows // 2, width)
    carried, others = max(1, len(riders)), max(1, lax.axis_size("dp") - 1)
    outs = (width, 2 * DN, 2 * DN, DV, rank, rank, 1, DV)
    kinds = (BF, BF, BF, BF, BF, BF, F32, BF)
    return pl.pallas_call(
        lambda *refs: attention_forward_kernel([rider[1] for rider in riders], *refs),
        grid=(span // rows,),
        in_specs=[
            tile(width),
            fixed((1, width)),
            fixed(first_w.shape),
            fixed((1, rank)),
            fixed(up_w.shape),
            tile(trig.shape[1]),
            tile(1),
            pl.BlockSpec((1, 1, rows), lambda i: (step_tile(i), 0, 0)),
            fixed(output_w.shape),
        ]
        + [anywhere] * len(riders),
        out_specs=[tile(columns) for columns in outs]
        + [pl.BlockSpec(block, lambda i: (0, 0))]
        + [anywhere] * len(riders),
        out_shape=[jax.ShapeDtypeStruct((span, c), k) for c, k in zip(outs, kinds)]
        + [jax.ShapeDtypeStruct(block, F32)]
        + [landed(rider) for rider in riders],
        scratch_shapes=step_buffers(block)
        + [pltpu.SemaphoreType.DMA((carried, others)) for _ in range(2)],
        compiler_params=pltpu.CompilerParams(
            collective_id=collective_id, has_side_effects=True, vmem_limit_bytes=VMEM_LIMIT
        ),
        name="attention_forward",
    )(
        x, gain[None], first_w, latent_gain[None], up_w, trig, column, row, output_w,
        *[rider[0] for rider in riders],
    )


def attention_backward_kernel(
    latent_piece, small_rows, spans,
    r_ref, output_ref, attended_ref, query_ref, key_ref, value_ref, column_ref, row_ref, trig_ref,
    unit_ref, low_ref, scale_ref, latent_gain_ref, up_ref, normed_ref, first_ref, turned_ref,
    side_ref, gain_ref, *refs,
):
    riders = len(spans)
    take = taker(refs)
    sources = [cut_rows(source, rows) for source, rows in zip(take(riders), spans)]
    (sum_ref, folded_ref), (query_out, up_out, output_out) = take(2), take(3)
    own_targets, targets = take(4), take(riders)
    grad_ref, kv_ref, output_grad_ref, up_grad_ref, first_grad_ref, gain_grad_ref = take(6)
    query_full, query_low, up_low, output_low, small_ref, folded_low = take(6)
    fold_buffers, fold_semaphores = take(4), take(6)
    buffers, semaphores, ride_sems, out_sem, own_sems = take(5), take(6), take(2), take(1)[0], take(2)
    step = pl.program_id(0)
    rank = up_ref.shape[0]
    n_d, me_d = lax.axis_size("dp"), lax.axis_index("dp")
    experts = lax.axis_size("expert")

    @pl.when(step == 0)
    def _():
        greet_dp(n_d - 1)
        greet(*place_of(lax.axis_index("expert")), n_d - 1)
        ride(sources, targets, *ride_sems)
        output_grad_ref[...] = jnp.zeros_like(output_grad_ref)
        up_grad_ref[...] = jnp.zeros_like(up_grad_ref)
        first_grad_ref[...] = jnp.zeros_like(first_grad_ref)
        gain_grad_ref[...] = jnp.zeros_like(gain_grad_ref)

    attended_grad = dot_right(r_ref[...], output_ref[...]).astype(BF)
    output_grad_ref[...] += dot_left(attended_ref[...], r_ref[...])
    probs = softmax_scores(query_ref[...], key_ref[...], group_mask(column_ref, row_ref))
    kv_ref[:, DN:] = dot_left(probs.astype(BF), attended_grad).astype(BF)
    probs_grad = dot_right(attended_grad, value_ref[...])
    inner = jnp.sum(probs * probs_grad, axis=1, keepdims=True)
    score_grad = (probs * (probs_grad - inner)).astype(BF)
    query_grad = dot(score_grad, key_ref[...]) * SCALE
    key_grad = dot_left(score_grad, query_ref[...]) * SCALE
    kv_ref[:, :DN] = key_grad[:, :DN].astype(BF)
    grad_ref[:, :DN] = query_grad[:, :DN].astype(BF)
    rope = key_grad[:, DN:] + pltpu.roll(query_grad[:, DN:], DR, 1)
    rope = rope * trig_ref[:, :128] + half_turn(rope * trig_ref[:, 128:])
    grad_ref[:, DN + rank :] = rope.astype(BF)
    out_grad = dot_right(kv_ref[...], up_ref[...])
    unit = unit_ref[...].astype(F32)
    gain_grad_ref[...] += jnp.sum(out_grad * unit, axis=0, keepdims=True)
    scaled = out_grad * latent_gain_ref[...]
    inner = jnp.mean(scaled * unit, axis=1, keepdims=True)
    grad_ref[:, DN : DN + rank] = (scale_ref[...] * (scaled - unit * inner)).astype(BF)
    up_grad_ref[...] += dot_left(low_ref[...], kv_ref[...])
    first_grad_ref[...] += dot_left(normed_ref[...], grad_ref[...])
    advance, finish = step_scatter(step, buffers, semaphores)

    def produce(first, target):
        rows, width = target.shape

        @pl.loop(0, width // COLUMNS)
        def _(tile):
            columns = pl.ds(pl.multiple_of(tile * COLUMNS, COLUMNS), COLUMNS)
            target[:, columns] = dot(
                grad_ref[pl.ds(first, rows)], turned_ref[:, columns]
            ).astype(BF)

    advance(produce)

    def part(array, number, owner):
        size = array.shape[1 if number == 2 else 0] // n_d
        at = pl.ds(pl.multiple_of(owner * size, size), size)
        return array.at[:, at] if number == 2 else array.at[at]

    def own_copies():
        copies = []
        for number, low in enumerate((query_low, up_low, output_low)):
            for ahead in range(1, n_d):
                owner = lax.rem(me_d + ahead, n_d)
                copies.append((part(low, number, owner), number, ahead))
        for ahead in range(1, n_d):
            copies.append((folded_low, 3, ahead))
        return [
            pltpu.make_async_remote_copy(
                src_ref=source,
                dst_ref=own_targets[number].at[ahead - 1],
                send_sem=own_sems[0].at[number, ahead - 1],
                recv_sem=own_sems[1].at[number, ahead - 1],
                device_id={"dp": lax.rem(me_d + ahead, n_d)},
                device_id_type=MESH,
            )
            for source, number, ahead in copies
        ]

    @pl.when(step == 2 * LINE - 1)
    def _():
        last = DN + rank
        strip = 256

        @pl.loop(0, first_grad_ref.shape[0] // strip)
        def _(tile):
            first = pl.multiple_of(tile * strip, strip)
            at = pl.ds(first, strip)
            sums = first_grad_ref[at]
            rope = sums[:, last:]
            query_full[at, :DN] = sums[:, :DN]
            query_full[at, DN:] = pltpu.roll(rope, DR, 1)
            query_low[at, :DN] = sums[:, :DN].astype(BF)
            query_low[at, DN:] = pltpu.roll(rope, DR, 1).astype(BF)
            small_ref[at, :rank] = sums[:, DN:last].astype(BF)
            gain_sum = jnp.sum(sums * first_ref[at].astype(F32), axis=1, keepdims=True)
            gain_sum = gain_sum / gain_ref[at]
            row = lax.broadcasted_iota(jnp.int32, (strip, rank), 0) + first
            index = lax.broadcasted_iota(jnp.int32, (strip, rank), 1)
            place = (index // latent_piece) * small_rows + index % latent_piece
            latent_sum = jnp.sum(
                jnp.where(row == place, gain_grad_ref[...], 0.0), axis=1, keepdims=True
            )
            lane = lax.broadcasted_iota(jnp.int32, rope.shape, 1)
            mixed = jnp.where(lane < DR, rope, side_ref[at].astype(F32))
            mixed = jnp.where(lane == DR + experts + 1, gain_sum, mixed)
            mixed = jnp.where(lane == DR + experts + 2, latent_sum, mixed)
            small_ref[at, rank:] = mixed.astype(BF)

        up_low[...] = up_grad_ref[...].astype(BF)
        output_low[...] = output_grad_ref[...].astype(BF)
        outs = [
            pltpu.make_async_copy(query_full, query_out, out_sem.at[0]),
            pltpu.make_async_copy(up_grad_ref, up_out, out_sem.at[1]),
            pltpu.make_async_copy(output_grad_ref, output_out, out_sem.at[2]),
        ]
        for copy in outs:
            copy.start()
        moves = own_copies()
        for copy in moves[: 3 * (n_d - 1)]:
            copy.start()

        def fold(dest, target):
            wide = small_ref.shape[1]
            total = folded_ref.shape[0] // STRIP
            target[...] = jnp.zeros(target.shape, BF)
            for unit in range(n_d * small_rows // STRIP):
                owner, first = (unit * STRIP) // small_rows, (unit * STRIP) % small_rows
                start = pl.multiple_of((owner * experts + dest) * small_rows + first, STRIP)
                target[
                    (unit % total) * STRIP : (unit % total + 1) * STRIP,
                    (unit // total) * wide : (unit // total + 1) * wide,
                ] = small_ref[pl.ds(start, STRIP)]

        scatter_folded(fold, folded_ref, fold_buffers, fold_semaphores)
        folded_low[...] = folded_ref[...].astype(BF)
        for copy in moves[3 * (n_d - 1) :]:
            copy.start()
        finish(sum_ref)
        for copy in moves + outs:
            copy.wait()
        for copy in ride(sources, targets, *ride_sems, start=False):
            copy.wait()


def attention_backward(
    residual_all, output_w, stored, column, row, trig, latent_gain, up_w, first_w, side, gain,
    latent_piece, small_rows, riders, collective_id,
):
    normed, query, key, value, unit, low, scale, attended = stored
    width, rank = residual_all.shape[1], up_w.shape[0]
    rows = row.shape[2]
    n_d = lax.axis_size("dp")
    first_width = 2 * DN + rank
    block = (rows // 2, width)
    folded = (EXTRA_ROWS, width)
    small = (width, rank + 128)

    def tile(columns):
        return pl.BlockSpec((rows, columns), lambda i: (step_tile(i), 0))

    def fixed(shape):
        return pl.BlockSpec(shape, lambda i: (0, 0), pipeline_mode=pl.Buffered(1))

    anywhere = pl.BlockSpec(memory_space=pl.ANY)
    carried, others = max(1, len(riders)), max(1, n_d - 1)
    query_shape, up_shape, output_shape = (width, 2 * DN), up_w.shape, output_w.shape
    to_others = [
        (n_d - 1, query_shape[0] // n_d, query_shape[1]),
        (n_d - 1, up_shape[0] // n_d, up_shape[1]),
        (n_d - 1, output_shape[0], output_shape[1] // n_d),
        (n_d - 1,) + folded,
    ]
    return pl.pallas_call(
        lambda *refs: attention_backward_kernel(
            latent_piece, small_rows, [rider[1] for rider in riders], *refs
        ),
        grid=(2 * LINE,),
        in_specs=[
            tile(width),
            fixed(output_w.shape),
            tile(DV),
            tile(2 * DN),
            tile(2 * DN),
            tile(DV),
            tile(1),
            pl.BlockSpec((1, 1, rows), lambda i: (step_tile(i), 0, 0)),
            tile(trig.shape[1]),
            tile(rank),
            tile(rank),
            tile(1),
            fixed((1, rank)),
            fixed(up_w.shape),
            tile(width),
            fixed(first_w.shape),
            fixed((first_width, width)),
            fixed(side.shape),
            fixed((width, 1)),
        ]
        + [anywhere] * len(riders),
        out_specs=[pl.BlockSpec(block, lambda i: (0, 0)), pl.BlockSpec(folded, lambda i: (0, 0))]
        + [anywhere] * (7 + len(riders)),
        out_shape=[
            jax.ShapeDtypeStruct(shape, F32)
            for shape in (block, folded, query_shape, up_shape, output_shape)
        ]
        + [jax.ShapeDtypeStruct(shape, BF) for shape in to_others]
        + [landed(rider) for rider in riders],
        scratch_shapes=[
            pltpu.VMEM((rows, first_width), BF),
            pltpu.VMEM((rows, DN + DV), BF),
            pltpu.VMEM(output_shape, F32),
            pltpu.VMEM(up_shape, F32),
            pltpu.VMEM((width, first_width), F32),
            pltpu.VMEM((1, rank), F32),
            pltpu.VMEM(query_shape, F32),
            pltpu.VMEM(query_shape, BF),
            pltpu.VMEM(up_shape, BF),
            pltpu.VMEM(output_shape, BF),
            pltpu.VMEM(small, BF),
            pltpu.VMEM(folded, BF),
            pltpu.VMEM((2 * LINE,) + folded, BF),
            pltpu.VMEM((2 * LINE,) + folded, BF),
            pltpu.VMEM((LINE + 1,) + folded, BF),
            pltpu.VMEM((LINE + 1,) + folded, BF),
            pltpu.SemaphoreType.DMA((2 * LINE,)),
            pltpu.SemaphoreType.DMA((2 * LINE,)),
            pltpu.SemaphoreType.DMA((LINE,)),
            pltpu.SemaphoreType.DMA((LINE,)),
            pltpu.SemaphoreType.DMA((LINE,)),
            pltpu.SemaphoreType.DMA((LINE + 1,)),
        ]
        + step_buffers(block)
        + [pltpu.SemaphoreType.DMA((carried, others)) for _ in range(2)]
        + [pltpu.SemaphoreType.DMA((3,))]
        + [pltpu.SemaphoreType.DMA((4, others)) for _ in range(2)],
        compiler_params=pltpu.CompilerParams(
            collective_id=collective_id, has_side_effects=True, vmem_limit_bytes=VMEM_LIMIT
        ),
        name="attention_backward",
    )(
        residual_all, output_w, attended, query, key, value, column, row, trig,
        unit, low, scale, latent_gain[None], up_w, normed, first_w, first_w.T, side,
        gain[:, None], *[rider[0] for rider in riders],
    )


HIDDEN = 256
ROUTER_AT = 448


def logistic(values):
    return 0.5 * jnp.tanh(0.5 * values) + 0.5


def expert_layer_kernel(
    splits,
    ffn_ref, y_ref, code_row_ref, code_column_ref, wide_ref, shared_down_ref, *refs,
):
    take = taker(refs)
    own_weights, came = take(3), take(len(splits))
    (
        rows_ref, ups_ref, scaled_ref, gate_ref, up_ref, mixed_ref,
        down_grad_out, wide_grad_out, sum_ref,
    ) = take(9)
    (
        gate_w_ref, up_w_ref, down_w_ref, load_sem, out_sem, down_grad_ref, wide_grad_ref,
        grad_ref, left_ref, inner_ref, returned_ref, slot_gate_ref, slot_dot_ref,
        part, kept, met, paired, passed,
        core_send, core_recv, pair_send, pair_recv, line_send, line_recv,
    ) = take(24)
    step = pl.program_id(0)
    me = lax.axis_index("expert")
    experts = lax.axis_size("expert")
    line, pair, core = place_of(me)
    me_d, n_d = lax.axis_index("dp"), lax.axis_size("dp")
    groups, _, per = code_row_ref.shape
    slots = rows_ref.shape[0] // groups
    width = ffn_ref.shape[1]
    hidden = gate_w_ref.shape[1]

    wholes = (gate_w_ref, up_w_ref, down_w_ref)
    loads = []

    def load(source, number, owner, start, count):
        axis = 1 if number == 2 else 0
        size = own_weights[number].shape[axis]
        at = pl.multiple_of(owner * size, size)
        if axis == 0:
            place = wholes[number].at[pl.ds(at + start, count)]
        else:
            place = wholes[number].at[:, pl.ds(at, size)]
        loads.append(pltpu.make_async_copy(source, place, load_sem.at[len(loads)]))

    for number in range(3):
        load(own_weights[number], number, me_d, 0, own_weights[number].shape[0])
    for source, (number, first, end) in zip(came, splits):
        for ahead in range(1, n_d):
            owner = lax.rem(me_d - ahead + n_d, n_d)
            load(source.at[ahead - 1], number, owner, first, end - first)

    @pl.when(step == 0)
    def _():
        for copy in loads:
            copy.start()
        greet(line, pair, core)
        down_grad_ref[...] = jnp.zeros_like(down_grad_ref)
        wide_grad_ref[...] = jnp.zeros_like(wide_grad_ref)

    out = dot(ffn_ref[...], wide_ref[...])
    gates, ups = out[:, :HIDDEN], out[:, HIDDEN:]
    last = out[:, 2 * HIDDEN - 128 :]
    lane = lax.broadcasted_iota(jnp.int32, last.shape, 1)
    first_lane = ROUTER_AT - (2 * HIDDEN - 128)
    logits = jnp.where((lane >= first_lane) & (lane < first_lane + experts), last, -1e30)
    powers = jnp.exp(logits - jnp.max(logits, axis=1, keepdims=True))
    probs = powers / jnp.sum(powers, axis=1, keepdims=True)
    own_lane = (lane == first_lane + me).astype(F32)
    own_probs = jnp.sum(probs * own_lane, axis=1, keepdims=True)
    sigmoid = logistic(gates)
    silu = gates * sigmoid
    shared_low = (silu * ups).astype(BF)
    back = dot_right(y_ref[...], shared_down_ref[...])
    left_ref[:, :HIDDEN] = (back * ups * sigmoid * (1.0 + gates * (1.0 - sigmoid))).astype(BF)
    shared_up_low = back * silu
    left_ref[:, HIDDEN : 2 * HIDDEN - 128] = shared_up_low[:, : HIDDEN - 128].astype(BF)
    shared_last = shared_up_low[:, HIDDEN - 128 :]
    down_grad_ref[...] += dot_left(shared_low, y_ref[...])

    square = (per, per)
    diagonal = lax.broadcasted_iota(jnp.int32, square, 0) == lax.broadcasted_iota(
        jnp.int32, square, 1
    )
    for group in range(groups):
        tokens_at = pl.ds(group * per, per)
        slots_at = pl.ds(group * slots, slots)
        slot_ids = lax.broadcasted_iota(jnp.int32, (slots, per), 0)
        picks = slot_ids == code_row_ref[group]
        picks_low = picks.astype(F32).astype(BF)
        rows_ref[slots_at] = dot(picks_low, ffn_ref[tokens_at]).astype(BF)
        ups_ref[slots_at] = dot(picks_low, y_ref[tokens_at]).astype(BF)
        own_column = own_probs[group * per : (group + 1) * per]
        own_row = jnp.sum(jnp.where(diagonal, own_column, 0.0), axis=0, keepdims=True)
        slot_gate_ref[slots_at] = jnp.sum(
            jnp.where(picks, own_row, 0.0), axis=1, keepdims=True
        )
    slot_dot_ref[...] = jnp.zeros_like(slot_dot_ref)

    @pl.when(step == 0)
    def _():
        for copy in loads:
            copy.wait()

    def hidden_part(columns):
        gate_part = dot(rows_ref[...], gate_w_ref[:, columns])
        up_part = dot(rows_ref[...], up_w_ref[:, columns])
        raw = dot_right(ups_ref[...], down_w_ref[columns, :])
        slot_gate = slot_gate_ref[...]
        sigmoid = logistic(gate_part)
        silu = gate_part * sigmoid
        inner = silu * up_part
        slot_dot_ref[...] += jnp.sum(inner * raw, axis=1, keepdims=True)
        grad = raw * slot_gate
        inner_ref[:, columns] = inner.astype(BF)
        scaled_ref[:, columns] = (inner * slot_gate).astype(BF)
        gate_ref[:, columns] = (
            grad * up_part * sigmoid * (1.0 + gate_part * (1.0 - sigmoid))
        ).astype(BF)
        up_ref[:, columns] = (grad * silu).astype(BF)

    for first in range(0, hidden, HIDDEN):
        hidden_part(pl.ds(first, min(HIDDEN, hidden - first)))

    @pl.loop(0, width // COLUMNS)
    def _(tile):
        columns = pl.ds(pl.multiple_of(tile * COLUMNS, COLUMNS), COLUMNS)
        returned_ref[:, columns] = dot(inner_ref[...], down_w_ref[:, columns]).astype(BF)
        grad_ref[:, columns] = (
            dot_right(gate_ref[...], gate_w_ref[columns, :])
            + dot_right(up_ref[...], up_w_ref[columns, :])
        ).astype(BF)

    for group in range(groups):
        tokens_at = pl.ds(group * per, per)
        slots_at = pl.ds(group * slots, slots)
        own_column = own_probs[group * per : (group + 1) * per]
        slot_lane = lax.broadcasted_iota(jnp.int32, (per, slots), 1)
        picks = slot_lane == code_column_ref[tokens_at]
        pick_gate = jnp.where(picks, own_column, 0.0).astype(BF)
        mixed_ref[tokens_at] = (
            dot(shared_low[group * per : (group + 1) * per], shared_down_ref[...])
            + dot(pick_gate, returned_ref[slots_at])
        ).astype(BF)
        small = (slots, slots)
        eye = lax.broadcasted_iota(jnp.int32, small, 0) == lax.broadcasted_iota(
            jnp.int32, small, 1
        )
        dot_row = jnp.sum(jnp.where(eye, slot_dot_ref[slots_at], 0.0), axis=0, keepdims=True)
        row_dot = jnp.sum(jnp.where(picks, dot_row, 0.0), axis=1, keepdims=True)
        at = slice(group * per, (group + 1) * per)
        logit_grad = row_dot * own_column * (own_lane[at] - probs[at])
        high = logit_grad.astype(BF)
        rest = logit_grad - high.astype(F32)
        left_ref[tokens_at, 2 * HIDDEN - 128 :] = jnp.where(
            lane[at] < first_lane,
            shared_last[at],
            high.astype(F32) + pltpu.roll(rest, experts, 1),
        ).astype(BF)
    wide_grad_ref[...] += dot_left(ffn_ref[...], left_ref[...])

    advance, finish = step_scatter(
        step, (part, kept, met, paired, passed),
        (core_send, core_recv, pair_send, pair_recv, line_send, line_recv),
    )
    rows = kept.shape[0]

    def produce(first, target):
        @pl.loop(0, width // COLUMNS)
        def _(tile):
            columns = pl.ds(pl.multiple_of(tile * COLUMNS, COLUMNS), COLUMNS)
            total = dot_right(left_ref[pl.ds(first, rows)], wide_ref[columns, :])
            for k in range(rows // per):
                group = first // per + k
                slot_lane = lax.broadcasted_iota(jnp.int32, (per, slots), 1)
                picks = slot_lane == code_column_ref[pl.ds(first + k * per, per)]
                scattered = dot(
                    picks.astype(F32).astype(BF),
                    grad_ref[pl.ds(group * slots, slots), columns],
                )
                target[pl.ds(k * per, per), columns] = (
                    total[k * per : (k + 1) * per] + scattered
                ).astype(BF)

    advance(produce)

    @pl.when(step == 2 * LINE - 1)
    def _():
        outs = [
            pltpu.make_async_copy(down_grad_ref, down_grad_out, out_sem.at[0]),
            pltpu.make_async_copy(wide_grad_ref, wide_grad_out, out_sem.at[1]),
        ]
        for copy in outs:
            copy.start()
        finish(sum_ref)
        for copy in outs:
            copy.wait()


def expert_layer(
    ffn_all, upstream_all, code, slots, wide, shared_down, weights, came, splits, collective_id
):
    groups, per = code.shape
    span, width = ffn_all.shape
    gate_w, up_w, down_w = weights
    hidden = gate_w.shape[1]
    n_d = lax.axis_size("dp")
    rows, slot_rows = TILE_GROUPS * per, TILE_GROUPS * slots
    total = groups * slots
    steps = 2 * LINE
    block = (rows // 2, width)

    def tile(count, columns):
        return pl.BlockSpec((count, columns), lambda i: (step_tile(i), 0))

    def fixed(shape):
        return pl.BlockSpec(shape, lambda i: (0, 0), pipeline_mode=pl.Buffered(1))

    anywhere = pl.BlockSpec(memory_space=pl.ANY)
    outs = [(total, width)] * 2 + [(total, hidden)] * 3 + [(span, width)]
    sums = [shared_down.shape, wide.shape]
    copies = 3 + len(came) * (n_d - 1)
    return pl.pallas_call(
        lambda *refs: expert_layer_kernel(splits, *refs),
        grid=(steps,),
        in_specs=[
            tile(rows, width),
            tile(rows, width),
            pl.BlockSpec((TILE_GROUPS, 1, per), lambda i: (step_tile(i), 0, 0)),
            tile(rows, 1),
            fixed(wide.shape),
            fixed(shared_down.shape),
        ]
        + [anywhere] * (3 + len(came)),
        out_specs=[
            tile(slot_rows if shape[0] == total else rows, shape[1]) for shape in outs
        ]
        + [anywhere] * 2
        + [pl.BlockSpec(block, lambda i: (0, 0))],
        out_shape=[jax.ShapeDtypeStruct(shape, BF) for shape in outs]
        + [jax.ShapeDtypeStruct(shape, F32) for shape in sums]
        + [jax.ShapeDtypeStruct(block, BF)],
        scratch_shapes=[
            pltpu.VMEM((gate_w.shape[0] * n_d, hidden), BF),
            pltpu.VMEM((up_w.shape[0] * n_d, hidden), BF),
            pltpu.VMEM((hidden, down_w.shape[1] * n_d), BF),
            pltpu.SemaphoreType.DMA((copies,)),
            pltpu.SemaphoreType.DMA((2,)),
            pltpu.VMEM(shared_down.shape, F32),
            pltpu.VMEM(wide.shape, F32),
            pltpu.VMEM((slot_rows, width), BF),
            pltpu.VMEM((rows, 2 * HIDDEN), BF),
            pltpu.VMEM((slot_rows, hidden), BF),
            pltpu.VMEM((slot_rows, width), BF),
            pltpu.VMEM((slot_rows, 1), F32),
            pltpu.VMEM((slot_rows, 1), F32),
        ]
        + step_buffers(block),
        compiler_params=pltpu.CompilerParams(
            collective_id=collective_id,
            has_side_effects=True,
            vmem_limit_bytes=63 * 1024 * 1024,
        ),
        name="expert_layer",
    )(
        ffn_all, upstream_all, code[:, None, :], code.reshape(span, 1), wide, shared_down,
        gate_w, up_w, down_w, *came,
    )


def on_device(
    tokens,
    segment,
    routes,
    drop_order,
    cotangent,
    attn_gain,
    query_weight,
    down_latent,
    latent_gain,
    up_latent,
    output_weight,
    ffn_gain,
    router_weight,
    shared_gate,
    shared_up,
    shared_down,
    expert_gate,
    expert_up,
    expert_down,
):
    n_e = lax.axis_size("expert")
    n_d = lax.axis_size("dp")
    me_e = lax.axis_index("expert")
    me_d = lax.axis_index("dp")
    micro, group_rows, width = tokens.shape
    own_rows = micro * group_rows
    span = n_e * own_rows
    groups = n_e * micro
    top = routes.shape[2]
    experts = n_e * expert_gate.shape[0]
    capacity = (5 * group_rows * top + 4 * experts - 1) // (4 * experts)
    slots = -(-capacity // 16) * 16
    rank_latent = latent_gain.shape[0] * n_e * n_d

    def gather(values):
        return lax.all_gather(values, "expert", axis=0, tiled=True)

    def scatter(values):
        return lax.psum_scatter(values, "expert", scatter_dimension=0, tiled=True)

    def whole(own, parts, axis):
        size = own.shape[axis]
        shape = list(own.shape)
        shape[axis] = size * n_d
        total = jnp.zeros(shape, own.dtype)
        for step in range(n_d):
            at = lax.rem(me_d - step + n_d, n_d) * size
            block = parts[step - 1] if step else own
            total = lax.dynamic_update_slice_in_dim(total, block, at, axis)
        return total

    def split_dp(values, axis):
        size = values.shape[axis] // n_d
        parts = []
        for step in range(n_d):
            at = lax.rem(me_d + step, n_d) * size
            parts.append(lax.dynamic_slice_in_dim(values, at, size, axis))
        return (stack([part.astype(BF) for part in parts[1:]]), parts[0])

    def stack(parts):
        return parts[0][None] if len(parts) == 1 else jnp.stack(parts)

    def add_all(total, parts):
        for step in range(n_d - 1):
            total = total + parts[step].astype(F32)
        return total

    small_rows = attn_gain.shape[0]
    latent_all_width = down_latent.shape[1]
    latent_piece = latent_gain.shape[0]
    packed = jnp.concatenate(
        [
            down_latent,
            router_weight,
            attn_gain[:, None],
            ffn_gain[:, None],
            jnp.pad(latent_gain, (0, small_rows - latent_piece))[:, None],
        ],
        axis=1,
    )
    packed = lax.all_gather(packed, ("dp", "expert"), axis=0, tiled=True)
    down_all = packed[:, :latent_all_width]
    router_all = packed[:, latent_all_width : latent_all_width + experts]
    rest = packed[:, latent_all_width + experts :].astype(F32)
    attn_gain_all = rest[:, 0]
    ffn_gain_all = rest[:, 1]
    latent_gain_all = rest[:, 2].reshape(n_e * n_d, small_rows)[:, :latent_piece].reshape(-1)

    chosen = jnp.sum(
        (routes[..., None] == jnp.arange(experts, dtype=jnp.int32)).astype(jnp.int32), axis=2
    )
    order = drop_order[:, 0]
    earlier = (order[:, None, :] < order[:, :, None]).astype(F32)
    rank = jnp.einsum("mtu,mue->mte", earlier, chosen.astype(F32)).astype(jnp.int32)
    code = jnp.where((chosen == 1) & (rank < capacity), rank, -1).reshape(own_rows, experts)

    tokens_own = tokens.reshape(own_rows, width)
    code_lanes = -(-experts // 128) * 128
    code_low = jnp.pad(code.astype(BF), ((0, 0), (0, code_lanes - experts)))
    own_gate, own_up, own_down = expert_gate[0], expert_up[0], expert_down[0]
    gate_half = own_gate.shape[0] // 2
    up_most = own_up.shape[0] * 3 // 4
    dense = (query_weight, up_latent, output_weight, shared_gate, shared_up, shared_down)
    came = gather_rows(
        jnp.concatenate([tokens_own, code_low], axis=1),
        5,
        riders=[(array, (0, array.shape[0])) for array in dense] + [(own_gate, (0, gate_half))],
    )
    tokens_all, gate_came = came[0], came[7]
    query_w, up_w, output_w, shared_gate_w, shared_up_w, shared_down_w = [
        whole(own, parts, axis)
        for own, parts, axis in zip(dense, came[1:7], (0, 0, 1, 0, 0, 1))
    ]
    upstream_own = cotangent.reshape(own_rows, width)
    upstream_later, tokens_all = lax.optimization_barrier((upstream_own, tokens_all))
    upstream_all = gather(upstream_later)
    code_all = tokens_all[:, width : width + experts].astype(jnp.int32)
    my_code = lax.dynamic_slice_in_dim(code_all, me_e, 1, 1).reshape(groups, group_rows)

    span_segment = (
        segment.reshape(micro, n_e, group_rows).transpose(1, 0, 2).reshape(groups, group_rows)
    )
    trig = angles(positions(span_segment), group_rows)
    marks = span_segment + 4 * jnp.arange(groups, dtype=jnp.int32)[:, None]
    column = marks.reshape(span, 1)
    row = marks.reshape(groups // TILE_GROUPS, 1, TILE_GROUPS * group_rows)
    first_w = jnp.concatenate(
        [
            query_w[:, :DN],
            down_all[:, :rank_latent],
            down_all[:, rank_latent:],
            query_w[:, DN:],
        ],
        axis=1,
    )
    came = attention_forward(
        tokens_all,
        attn_gain_all,
        first_w,
        latent_gain_all,
        up_w,
        trig,
        column,
        row,
        output_w,
        [(own_gate, (gate_half, own_gate.shape[0])), (own_up, (0, up_most))],
        2,
    )
    stored, attention_out, gate_came_last, up_came = came[:8], came[8], came[9], came[10]
    residual = tokens_own.astype(F32) + attention_out

    second_scale = rms_scale(residual)
    ffn_in = (residual * second_scale * ffn_gain_all).astype(BF)
    ffn_all, up_came_last, down_came = gather_rows(
        ffn_in,
        1,
        riders=[(own_up, (up_most, own_up.shape[0])), (own_down, (0, own_down.shape[0]))],
    )

    shared_hidden = shared_gate_w.shape[1]
    wide = jnp.concatenate(
        [
            jnp.pad(shared_gate_w, ((0, 0), (0, HIDDEN - shared_hidden))),
            jnp.pad(shared_up_w, ((0, 0), (0, ROUTER_AT - HIDDEN - shared_hidden))),
            router_all,
            jnp.pad(router_all, ((0, 0), (0, 2 * HIDDEN - ROUTER_AT - 2 * experts))),
        ],
        axis=1,
    )
    (
        expert_rows,
        slot_up,
        inner_scaled,
        gate_low,
        up_low,
        mixed_part,
        shared_down_grad,
        wide_grad,
        ffn_grad,
    ) = expert_layer(
        ffn_all,
        upstream_all,
        my_code,
        slots,
        wide,
        jnp.pad(shared_down_w, ((0, HIDDEN - shared_hidden), (0, 0))),
        (own_gate, own_up, own_down),
        (gate_came, gate_came_last, up_came, up_came_last, down_came),
        (
            (0, 0, gate_half),
            (0, gate_half, own_gate.shape[0]),
            (1, 0, up_most),
            (1, up_most, own_up.shape[0]),
            (2, 0, own_down.shape[0]),
        ),
        3,
    )
    ffn_grad = ffn_grad.astype(F32)
    mixed = residual + scatter(mixed_part).astype(F32)
    router_grad = (
        wide_grad[:, ROUTER_AT : ROUTER_AT + experts]
        + wide_grad[:, ROUTER_AT + experts : ROUTER_AT + 2 * experts]
    )
    shared_down_later, shared_down_now = split_dp(shared_down_grad[:shared_hidden], 1)
    shared_gate_later, shared_gate_now = split_dp(wide_grad[:, :shared_hidden], 0)
    shared_up_later, shared_up_now = split_dp(wide_grad[:, HIDDEN : HIDDEN + shared_hidden], 0)
    residual_part, ffn_gain_grad = norm_back(residual, second_scale, ffn_gain_all, ffn_grad)
    residual_grad = upstream_own.astype(F32) + residual_part
    (
        residual_all,
        down_now,
        gate_now,
        up_now,
        down_parts,
        gate_parts,
        up_later,
    ) = gather_rows(
        residual_grad.astype(BF),
        6,
        products=(expert_rows, slot_up, inner_scaled, gate_low, up_low),
    )

    side = jnp.concatenate(
        [
            jnp.zeros((width, DR), F32),
            router_grad,
            ffn_gain_grad[:, None],
            jnp.zeros((width, 128 - DR - experts - 1), F32),
        ],
        axis=1,
    ).astype(BF)
    (
        normed_grad,
        folded,
        query_full,
        up_latent_full,
        output_full,
        query_parts,
        latent_parts,
        output_parts,
        folded_parts,
        up_parts,
        shared_down_parts,
        shared_gate_parts,
        shared_up_parts,
    ) = attention_backward(
        residual_all,
        output_w,
        stored,
        column,
        row,
        trig,
        latent_gain_all,
        up_w,
        first_w,
        side,
        attn_gain_all,
        latent_piece,
        small_rows,
        [
            (later, None)
            for later in (up_later, shared_down_later, shared_gate_later, shared_up_later)
        ],
        4,
    )

    def own_part(values, axis):
        size = values.shape[axis] // n_d
        return lax.dynamic_slice_in_dim(values, me_d * size, size, axis)

    query_grad = add_all(own_part(query_full, 0), query_parts)[:, : DN + DR]
    up_latent_grad = add_all(own_part(up_latent_full, 0), latent_parts)
    output_grad = add_all(own_part(output_full, 1), output_parts)
    small_width = rank_latent + 128
    folded = add_all(folded, folded_parts)
    small = jnp.concatenate(
        [folded[:, k * small_width : (k + 1) * small_width] for k in range(width // small_width)],
        axis=0,
    )
    small = lax.dynamic_slice_in_dim(small, me_d * small_rows, small_rows, 0)
    own_inputs = tokens_own.astype(F32)
    input_part, _ = norm_back(own_inputs, rms_scale(own_inputs), attn_gain_all, normed_grad)
    tokens_grad = residual_grad + input_part
    last = latent_all_width + experts
    shape = (micro, group_rows, width)
    return (
        mixed.reshape(shape),
        tokens_grad.reshape(shape),
        small[:, last + 1],
        query_grad,
        small[:, :latent_all_width],
        small[:latent_piece, last + 2],
        up_latent_grad,
        output_grad,
        small[:, last],
        small[:, latent_all_width:last],
        add_all(shared_gate_now, shared_gate_parts),
        add_all(shared_up_now, shared_up_parts),
        add_all(shared_down_now, shared_down_parts),
        add_all(gate_now, gate_parts)[None],
        add_all(up_now, up_parts)[None],
        add_all(down_now, down_parts)[None],
    )


def solution(mesh):
    rows = P(None, ("dp", "expert"), None)
    split = P(("dp", "expert"))
    split_rows = P(("dp", "expert"), None)
    columns = P("dp", "expert")
    turned = P("expert", "dp")
    expert_in = P("expert", "dp", None)
    expert_out = P("expert", None, "dp")
    return jax.shard_map(
        on_device,
        mesh=mesh,
        in_specs=(
            rows,
            P(None, "dp"),
            rows,
            rows,
            rows,
            split,
            columns,
            split_rows,
            split,
            columns,
            turned,
            split,
            split_rows,
            columns,
            columns,
            turned,
            expert_in,
            expert_in,
            expert_out,
        ),
        out_specs=(
            rows,
            rows,
            split,
            columns,
            split_rows,
            split,
            columns,
            turned,
            split,
            split_rows,
            columns,
            columns,
            turned,
            expert_in,
            expert_in,
            expert_out,
        ),
        check_vma=False,
    )
```

```python
import math

import jax
import jax.numpy as jnp
from jax import lax
from jax.experimental import pallas as pl
from jax.experimental.pallas import tpu as pltpu
from jax.sharding import PartitionSpec as P

DN = 128
DR = 64
DV = 128
EPS = 1e-06
HIGH = lax.Precision.HIGHEST
F32 = jnp.float32
BF = jnp.bfloat16


def dot(former, latter):
    return jnp.dot(former, latter, preferred_element_type=F32)


def dot_left(former, latter):
    return lax.dot_general(former, latter, (((0,), (0,)), ((), ())), preferred_element_type=F32)


def dot_right(former, latter):
    return lax.dot_general(former, latter, (((1,), (1,)), ((), ())), preferred_element_type=F32)


def rms_scale(values):
    return lax.rsqrt(jnp.mean(values * values, axis=-1, keepdims=True) + EPS)


def norm_back(values, scale_rows, gain, out_grad):
    scaled = out_grad * gain
    inner = jnp.mean(scaled * values, axis=-1, keepdims=True)
    value_grad = scale_rows * scaled - values * scale_rows * scale_rows * scale_rows * inner
    return (value_grad, jnp.sum(out_grad * values * scale_rows, axis=0))


def positions(segment):
    places = jnp.arange(segment.shape[1], dtype=jnp.int32)
    prompt_len = jnp.sum((segment == 0).astype(jnp.int32), axis=1, keepdims=True)
    former = (segment[:, None, :] < segment[:, :, None]).astype(jnp.int32)
    seg_start = jnp.sum(former, axis=2)
    return jnp.where(segment == 0, places[None], prompt_len + places[None] - seg_start)


def angles(position, row_count):
    freq_index = jnp.arange(DR // 2, dtype=F32)
    frequency = jnp.exp(freq_index * (-2.0 * math.log(10000.0) / DR))
    turning = jnp.arange(row_count, dtype=F32)[:, None] * frequency[None, :]
    cosine, sine_part = jnp.cos(turning), jnp.sin(turning)
    table = jnp.concatenate([cosine] * 4 + [-sine_part, sine_part] * 2, axis=1)
    picks = (position.reshape(-1)[:, None] == jnp.arange(row_count)[None, :]).astype(F32)
    return jnp.dot(picks, table, precision=HIGH)


LINE = 4
PIECES = 3
MESH = pl.DeviceIdType.MESH
VMEM_LIMIT = 60 * 1024 * 1024


def place_of(me):
    return (me // 4, lax.rem(me // 2, 2), lax.rem(me, 2))


def index_of(line, pair, core):
    return line * 4 + pair * 2 + core


def greet(line, pair, core, others=0):
    barrier = pltpu.get_barrier_semaphore()

    def signal(target):
        pl.semaphore_signal(barrier, inc=1, device_id={"expert": target}, device_id_type=MESH)

    signal(index_of(line, pair, 1 - core))
    signal(index_of(line, 1 - pair, core))

    @pl.when(line > 0)
    def _():
        signal(index_of(line - 1, pair, core))

    @pl.when(line < LINE - 1)
    def _():
        signal(index_of(line + 1, pair, core))

    inner = jnp.where(line > 0, 1, 0) + jnp.where(line < LINE - 1, 1, 0)
    pl.semaphore_wait(barrier, 2 + others + inner)


def greet_dp(others):
    barrier = pltpu.get_barrier_semaphore()
    me_d, n_d = lax.axis_index("dp"), lax.axis_size("dp")
    if others:
        for step in range(1, n_d):
            pl.semaphore_signal(
                barrier,
                inc=1,
                device_id={"dp": lax.rem(me_d + step, n_d)},
                device_id_type=MESH,
            )


def ride(sources, targets, send_sem, recv_sem, start=True):
    me_d, n_d = lax.axis_index("dp"), lax.axis_size("dp")
    copies = []
    for number, (source, target) in enumerate(zip(sources, targets)):
        parts = len(source.shape) == len(target.shape)
        for step in range(1, n_d):
            copy = pltpu.make_async_remote_copy(
                src_ref=source.at[step - 1] if parts else source,
                dst_ref=target.at[step - 1],
                send_sem=send_sem.at[number, step - 1],
                recv_sem=recv_sem.at[number, step - 1],
                device_id={"dp": lax.rem(me_d + step, n_d)},
                device_id_type=MESH,
            )
            if start:
                copy.start()
            copies.append(copy)
    return copies


def landed(rider):
    array, rows = rider
    if rows is None:
        return jax.ShapeDtypeStruct(array.shape, array.dtype)
    shape = (lax.axis_size("dp") - 1, rows[1] - rows[0]) + array.shape[1:]
    return jax.ShapeDtypeStruct(shape, array.dtype)


def cut_rows(ref, rows):
    return ref if rows is None else ref.at[pl.ds(rows[0], rows[1] - rows[0])]


def when(condition, action):
    if condition is None:
        action()
    else:
        pl.when(condition)(action)


def gather_kernel(spans, products, *refs):
    riders = len(spans)
    take = taker(refs)
    (own_ref,), sources = take(1), take(riders)
    products_in = take(5) if products else None
    (out_ref,), targets = take(1), take(riders)
    products_out = take(7) if products else None
    own_sem, send_sem, recv_sem, ride_send, ride_recv = take(5)
    if products:
        products = ExpertGradients(products_in, products_out, take(12))
    sources = [cut_rows(source, rows) for source, rows in zip(sources, spans)]
    me = lax.axis_index("expert")
    line, pair, core = place_of(me)
    rows = own_ref.shape[0]
    sixth = rows // 6
    half = (rows - sixth) // 2
    spans_of = (pl.ds(0, sixth), pl.ds(sixth, half), pl.ds(sixth + half, half))
    others = lax.axis_size("dp") - 1 if riders or products else 0
    greet_dp(others)
    greet(line, pair, core, others)
    local = [pltpu.make_async_copy(own_ref, out_ref.at[me], own_sem)]
    sent = []

    def push(condition, kind, origin, piece, target, source=None):
        block = out_ref.at[origin, spans_of[piece]]
        copy = pltpu.make_async_remote_copy(
            src_ref=block if source is None else source,
            dst_ref=block,
            send_sem=send_sem.at[kind, origin, piece],
            recv_sem=recv_sem.at[origin, piece],
            device_id={"expert": target},
            device_id_type=MESH,
        )
        when(condition, copy.start)
        sent.append((condition, copy))

    def arrive(condition, origin, piece):
        block = out_ref.at[origin, spans_of[piece]]
        copy = pltpu.make_async_remote_copy(
            src_ref=block,
            dst_ref=block,
            send_sem=send_sem.at[0, origin, piece],
            recv_sem=recv_sem.at[origin, piece],
            device_id={"expert": me},
            device_id_type=MESH,
        )
        when(condition, copy.wait_recv)

    left = index_of(line - 1, pair, core)
    right = index_of(line + 1, pair, core)
    across = index_of(line, 1 - pair, core)
    sibling = index_of(line, pair, 1 - core)
    for piece in range(PIECES):
        source = own_ref.at[spans_of[piece]]
        push(line < LINE - 1, 1, me, piece, right, source)
        push(line > 0, 0, me, piece, left, source)
        push(None, 2, me, piece, across, source)
        push(None, 3, me, piece, sibling, source)
    ridden = ride(sources, targets, ride_send, ride_recv)
    for copy in local:
        copy.start()
    if products:
        products.load()

    def work():
        if products:
            products.next()

    def along(hop, piece):
        for side in (-1, 1):
            there = line + side * hop
            held = (there >= 0) & (there < LINE)
            origin = index_of(there, pair, core)
            arrive(held, origin, piece)
            pass_on(held, side, hop, origin, piece)
            if piece:
                push(held, 2, origin, piece, across)
            push(held, 3, origin, piece, sibling)
        work()

    def pass_on(held, side, hop, origin, piece):
        if hop < LINE - 1:
            further = held & ((line < LINE - 1) if side < 0 else (line > 0))
            kind, target = (1, right) if side < 0 else (0, left)
            push(further, kind, origin, piece, target)

    def over(hop, piece):
        for side in (-1, 1) if hop else (1,):
            there = line + side * hop
            held = (there >= 0) & (there < LINE) if hop else None
            origin = index_of(there, 1 - pair, core)
            arrive(held, origin, piece)
            if piece == 0 and hop:
                pass_on(held, side, hop, origin, piece)
            if piece == 0 and not hop:
                push(line < LINE - 1, 1, origin, piece, right)
                push(line > 0, 0, origin, piece, left)
            push(held, 3, origin, piece, sibling)
        work()

    over(0, 0)
    for hop in range(1, LINE):
        for piece in range(PIECES):
            along(hop, piece)
        over(hop, 0)
        for piece in range(1, PIECES):
            over(hop - 1, piece)
    for piece in range(1, PIECES):
        over(LINE - 1, piece)
    for other_line in range(LINE):
        for other_pair in range(2):
            for piece in range(PIECES):
                arrive(None, index_of(other_line, other_pair, 1 - core), piece)
    if products:
        products.finish()
    for copy in ridden:
        copy.wait()
    for condition, copy in sent:
        when(condition, copy.wait_send)
    for copy in local:
        copy.wait()


class ExpertGradients:

    def __init__(self, operands, outs, scratch):
        self.sources = operands
        self.nows, self.landing, self.laters = outs[:3], outs[3:5], outs[5:7]
        self.held = scratch[:5]
        self.lows, self.stage = scratch[5:8], scratch[8]
        self.load_sem, self.out_sem, self.ride_sem = scratch[9:12]
        self.me_d, self.n_d = lax.axis_index("dp"), lax.axis_size("dp")
        self.pending, self.riding, self.count = [None, None], [], 0
        self.kinds = ((2, 1, 1), (0, 3, 0), (0, 4, 0))
        self.steps = self.all_steps()

    def load(self):
        self.loads = [
            pltpu.make_async_copy(source, held, self.load_sem.at[number])
            for number, (source, held) in enumerate(zip(self.sources, self.held))
        ]
        for copy in self.loads:
            copy.start()

    def chunk(self, number, owner, at):
        left, right, axis = self.kinds[number]
        left, right = self.held[left], self.held[right]
        shape = self.nows[number].shape
        count = chunk_rows(number, shape[0])
        if axis == 0:
            first = pl.multiple_of(owner * shape[0] + at * count, 128)
            return dot_left(left[:, pl.ds(first, count)], right[...])
        columns = pl.ds(pl.multiple_of(owner * shape[1], 128), shape[1])
        return dot_left(left[:, at * count : (at + 1) * count], right[:, columns])

    def all_steps(self):
        for copy in self.loads:
            copy.wait()
        for number in range(3):
            shape = self.nows[number].shape
            count = chunk_rows(number, shape[0])
            low = self.lows[number]
            for ahead in range(1, self.n_d):
                owner = lax.rem(self.me_d + ahead, self.n_d)
                for at in range(shape[0] // count):
                    low[ahead - 1, at * count : (at + 1) * count] = self.chunk(
                        number, owner, at
                    ).astype(BF)
                    if number == 1 and (at + 1) * count == shape[0] // 2:
                        self.leave(number, ahead, low.at[ahead - 1, : shape[0] // 2])
                    if at == shape[0] // count - 1:
                        first = shape[0] // 2 if number == 1 else 0
                        self.leave(2 + number // 2 if number else 0, ahead, low.at[ahead - 1, first:])
                    yield
        for number in range(3):
            shape = self.nows[number].shape
            count = chunk_rows(number, shape[0])
            for at in range(shape[0] // count):
                slot = self.count % 2
                if self.pending[slot] is not None:
                    self.pending[slot].wait()
                stage = self.stage.at[slot, :count, : shape[1]]
                stage[...] = self.chunk(number, self.me_d, at)
                copy = pltpu.make_async_copy(
                    stage,
                    self.nows[number].at[pl.ds(at * count, count)],
                    self.out_sem.at[slot],
                )
                copy.start()
                self.pending[slot] = copy
                self.count += 1
                yield

    def leave(self, kind, ahead, source):
        if kind >= 2:
            copy = pltpu.make_async_copy(
                source,
                self.laters[kind - 2].at[ahead - 1],
                self.load_sem.at[3 + 2 * ahead + kind - 2],
            )
        else:
            copy = pltpu.make_async_remote_copy(
                src_ref=source,
                dst_ref=self.landing[kind].at[ahead - 1],
                send_sem=self.ride_sem.at[0, kind, ahead - 1],
                recv_sem=self.ride_sem.at[1, kind, ahead - 1],
                device_id={"dp": lax.rem(self.me_d + ahead, self.n_d)},
                device_id_type=MESH,
            )
        copy.start()
        self.riding.append(copy)

    def next(self):
        next(self.steps, None)

    def finish(self):
        for _ in self.steps:
            pass
        for copy in self.riding + [copy for copy in self.pending if copy is not None]:
            copy.wait()


def chunk_rows(number, rows):
    return rows // 4 if number == 0 else min(256, rows // 2)


def gradient_shapes(products, n_d):
    rows, ups, scaled, gate, up = products
    width, hidden = rows.shape[1], gate.shape[1]
    size = width // n_d
    nows = [(hidden, size), (size, hidden), (size, hidden)]
    shapes = [jax.ShapeDtypeStruct(shape, F32) for shape in nows]
    sent = [nows[0], (size // 2, hidden), (size // 2, hidden), nows[2]]
    shapes += [jax.ShapeDtypeStruct((n_d - 1,) + shape, BF) for shape in sent]
    largest = max(hidden, size)
    scratch = [pltpu.VMEM(product.shape, BF) for product in products]
    scratch += [pltpu.VMEM((n_d - 1,) + shape, BF) for shape in nows]
    scratch += [
        pltpu.VMEM((2, 384, largest), F32),
        pltpu.SemaphoreType.DMA((5 + 2 * n_d,)),
        pltpu.SemaphoreType.DMA((2,)),
        pltpu.SemaphoreType.DMA((2, 3, n_d - 1)),
    ]
    return (shapes, scratch)


def gather_rows(own, collective_id, riders=(), products=()):
    count = lax.axis_size("expert")
    rows, width = own.shape
    shapes = [jax.ShapeDtypeStruct((count, rows, width), own.dtype)]
    shapes += [landed(rider) for rider in riders]
    n_d = lax.axis_size("dp")
    carried, others = max(1, len(riders)), max(1, n_d - 1)
    scratch = []
    if products:
        extra_shapes, scratch = gradient_shapes(products, n_d)
        shapes += extra_shapes
    out = pl.pallas_call(
        lambda *refs: gather_kernel([rider[1] for rider in riders], bool(products), *refs),
        out_shape=shapes,
        in_specs=[pl.BlockSpec(memory_space=pl.ANY)] * (1 + len(riders) + len(products)),
        out_specs=[pl.BlockSpec(memory_space=pl.ANY)] * len(shapes),
        scratch_shapes=[
            pltpu.SemaphoreType.DMA,
            pltpu.SemaphoreType.DMA((4, count, PIECES)),
            pltpu.SemaphoreType.DMA((count, PIECES)),
            pltpu.SemaphoreType.DMA((carried, others)),
            pltpu.SemaphoreType.DMA((carried, others)),
        ]
        + scratch,
        compiler_params=pltpu.CompilerParams(
            collective_id=collective_id, has_side_effects=True, vmem_limit_bytes=VMEM_LIMIT
        ),
        name="gather_rows",
    )(own, *[rider[0] for rider in riders], *products)
    return [out[0].reshape(count * rows, width)] + list(out[1:])


FAR_FIRST = ((3, 3, 0, 0), (2, 0, 3, 1), (1, 2, 1, 2), (0, 1, 2, 3))
COLUMNS = 512
STRIP = 16
EXTRA_ROWS = 48


def pick_by(line, table):
    value = jnp.int32(table[LINE - 1])
    for k in range(LINE - 2, -1, -1):
        value = jnp.where(line == k, jnp.int32(table[k]), value)
    return value


def add_strips(target, first, count, others):
    @pl.loop(0, count // STRIP)
    def _(strip):
        for columns in range(0, target.shape[1], COLUMNS):
            at = pl.ds(pl.multiple_of(first + strip * STRIP, STRIP), STRIP)
            cols = pl.ds(columns, COLUMNS)
            total = None
            for other in others:
                term = other[at, cols].astype(F32)
                total = term if total is None else total + term
            target[at, cols] = total.astype(target.dtype)


def step_scatter(step, buffers, semaphores):
    part, kept, met, paired, passed = buffers
    core_send, core_recv, pair_send, pair_recv, line_send, line_recv = semaphores
    me = lax.axis_index("expert")
    line, pair, core = place_of(me)
    rows = kept.shape[0]
    piece_rows = rows // PIECES
    sibling = index_of(line, pair, 1 - core)
    across = index_of(line, 1 - pair, core)
    steps = 2 * LINE

    def remote(source, dest, send_at, recv_at, target):
        return pltpu.make_async_remote_copy(
            src_ref=source,
            dst_ref=dest,
            send_sem=send_at,
            recv_sem=recv_at,
            device_id={"expert": target},
            device_id_type=MESH,
        )

    def to_sibling(i):
        return remote(part, met.at[i], core_send.at[i], core_recv.at[i], sibling)

    def to_pair(i, piece):
        at = pl.ds(piece * piece_rows, piece_rows)
        return remote(
            met.at[i, at],
            paired.at[i // 2, at],
            pair_send.at[i // 2, piece],
            pair_recv.at[i // 2, piece],
            across,
        )

    def meet(i):
        to_sibling(i).wait_recv()
        add_strips(met.at[i], 0, rows, [met.at[i], kept])

        @pl.when(lax.rem(i, 2) == 0)
        def _():
            for piece in range(PIECES):
                to_pair(i, piece).start()

    dest_line = [pick_by(line, FAR_FIRST[k]) for k in range(LINE)]

    def hop_facts(k):
        there = dest_line[k]
        way = jnp.where(there > line, 1, -1)
        behind = line - way
        held = (behind >= 0) & (behind < LINE)
        slot = jnp.where((there == line + way) & (way < 0), LINE, there)
        return (there, held, slot, index_of(line + way, pair, core))

    def along(k, piece):
        there, held, slot, target = hop_facts(k)
        at = pl.ds(piece * piece_rows, piece_rows)
        return remote(
            paired.at[k, at],
            passed.at[slot, at],
            line_send.at[k, piece],
            line_recv.at[slot, piece],
            target,
        )

    def came_along(slot, piece):
        at = pl.ds(piece * piece_rows, piece_rows)
        block = passed.at[slot, at]
        remote(block, block, line_send.at[0, piece], line_recv.at[slot, piece], me).wait_recv()

    def pair_arrived(k, piece):
        at = pl.ds(piece * piece_rows, piece_rows)
        block = paired.at[k, at]
        remote(block, block, pair_send.at[k, piece], pair_recv.at[k, piece], me).wait_recv()

    def hop(k, with_held):
        there = hop_facts(k)[0]
        for piece in range(PIECES):
            first = piece * piece_rows
            pair_arrived(k, piece)
            terms = [paired.at[k], met.at[2 * k + 1]]
            if with_held:
                came_along(there, piece)
                terms.append(passed.at[there])
            add_strips(paired.at[k], first, piece_rows, terms)
            along(k, piece).start()

    def advance(produce):
        @pl.when(step > 0)
        def _():
            meet(step - 1)

        for k in range(LINE - 1):
            held = hop_facts(k)[1]
            if 2 * k + 3 < steps:

                @pl.when((step == 2 * k + 3) & jnp.logical_not(held))
                def _():
                    hop(k, False)

            if 2 * k + 4 < steps:

                @pl.when((step == 2 * k + 4) & held)
                def _():
                    hop(k, True)

        @pl.when(step > 0)
        def _():
            to_sibling(step - 1).wait_send()

        for which in range(2):

            @pl.when(core == which)
            def _():
                produce((1 - which) * rows, part)

        to_sibling(step).start()
        for which in range(2):

            @pl.when(core == which)
            def _():
                produce(which * rows, kept)

    def finish(sum_ref):
        last_hop()
        last_sum(sum_ref)

    def last_hop():
        meet(steps - 1)
        last = LINE - 2

        @pl.when(hop_facts(last)[1])
        def _():
            hop(last, True)

    def last_sum(sum_ref):
        for piece in range(PIECES):
            first = piece * piece_rows
            pair_arrived(LINE - 1, piece)
            add_strips(
                sum_ref, first, piece_rows, [paired.at[LINE - 1], met.at[2 * LINE - 1]]
            )
            for has, slot in ((line > 0, line), (line < LINE - 1, LINE)):

                @pl.when(has)
                def _():
                    came_along(slot, piece)
                    add_strips(sum_ref, first, piece_rows, [sum_ref, passed.at[slot]])

        to_sibling(steps - 1).wait_send()
        for piece in range(PIECES):
            for k in range(LINE):
                to_pair(2 * k, piece).wait_send()
            for k in range(LINE - 1):
                along(k, piece).wait_send()

    return (advance, finish, last_hop, last_sum)


def step_buffers(block):
    return [
        pltpu.VMEM(block, BF),
        pltpu.VMEM(block, BF),
        pltpu.VMEM((2 * LINE,) + block, BF),
        pltpu.VMEM((LINE,) + block, BF),
        pltpu.VMEM((LINE + 1,) + block, BF),
        pltpu.SemaphoreType.DMA((2 * LINE,)),
        pltpu.SemaphoreType.DMA((2 * LINE,)),
        pltpu.SemaphoreType.DMA((LINE, PIECES)),
        pltpu.SemaphoreType.DMA((LINE, PIECES)),
        pltpu.SemaphoreType.DMA((LINE, PIECES)),
        pltpu.SemaphoreType.DMA((LINE + 1, PIECES)),
    ]


def step_tile(i):
    line, pair, _ = place_of(lax.axis_index("expert"))
    there = pick_by(line, FAR_FIRST[LINE - 1])
    for k in range(LINE - 2, -1, -1):
        there = jnp.where(i // 2 == k, pick_by(line, FAR_FIRST[k]), there)
    return there * 2 + jnp.where(lax.rem(i, 2) == 0, 1 - pair, pair)


def taker(refs):
    refs = list(refs)

    def take(number):
        taken = refs[:number]
        del refs[:number]
        return taken

    return take


def scatter_folded(fold, out_ref, buffers, semaphores):
    part, met, paired, passed = buffers
    core_send, core_recv, pair_send, pair_recv, line_send, line_recv = semaphores
    me = lax.axis_index("expert")
    line, pair, core = place_of(me)
    rows = out_ref.shape[0]
    sibling = index_of(line, pair, 1 - core)
    across = index_of(line, 1 - pair, core)
    sent = []

    def send(source, dest, send_at, recv_at, target):
        copy = pltpu.make_async_remote_copy(
            src_ref=source,
            dst_ref=dest,
            send_sem=send_at,
            recv_sem=recv_at,
            device_id={"expert": target},
            device_id_type=MESH,
        )
        copy.start()
        sent.append(copy)

    def await_block(block, recv_at, send_at):
        pltpu.make_async_remote_copy(
            src_ref=block,
            dst_ref=block,
            send_sem=send_at,
            recv_sem=recv_at,
            device_id={"expert": me},
            device_id_type=MESH,
        ).wait_recv()

    dest_line = [pick_by(line, FAR_FIRST[step]) for step in range(LINE)]

    def chip(i):
        return (dest_line[i // 2], (1 - pair) if i % 2 == 0 else pair)

    for i in range(2 * LINE):
        there, other = chip(i)
        fold(index_of(there, other, 1 - core), part.at[i])
        send(part.at[i], met.at[i], core_send.at[i], core_recv.at[i], sibling)
    for i in range(2 * LINE):
        there, other = chip(i)
        await_block(met.at[i], core_recv.at[i], core_send.at[i])
        fold(index_of(there, other, core), paired.at[LINE])
        add_strips(met.at[i], 0, rows, [met.at[i], paired.at[LINE]])
        if i % 2 == 0:
            send(met.at[i], paired.at[i // 2], pair_send.at[i // 2], pair_recv.at[i // 2], across)
    for step in range(LINE - 1):
        there = dest_line[step]
        way = jnp.where(there > line, 1, -1)
        behind = line - way
        held = (behind >= 0) & (behind < LINE)
        target = index_of(line + way, pair, core)
        slot = jnp.where((there == line + way) & (way < 0), LINE, there)
        await_block(paired.at[step], pair_recv.at[step], pair_send.at[step])
        add_strips(paired.at[step], 0, rows, [paired.at[step], met.at[2 * step + 1]])

        @pl.when(held)
        def _():
            await_block(passed.at[there], line_recv.at[there], line_send.at[step])
            add_strips(paired.at[step], 0, rows, [paired.at[step], passed.at[there]])

        send(paired.at[step], passed.at[slot], line_send.at[step], line_recv.at[slot], target)
    step = LINE - 1
    await_block(paired.at[step], pair_recv.at[step], pair_send.at[step])
    add_strips(out_ref, 0, rows, [paired.at[step], met.at[2 * step + 1]])
    for held, slot in ((line > 0, line), (line < LINE - 1, LINE)):

        @pl.when(held)
        def _():
            await_block(passed.at[slot], line_recv.at[slot], line_send.at[0])
            add_strips(out_ref, 0, rows, [out_ref, passed.at[slot]])

    for copy in sent:
        copy.wait_send()


TILE_GROUPS = 4
SCALE = (DN + DR) ** (-0.5)


def half_turn(values):
    lane = lax.broadcasted_iota(jnp.int32, values.shape, 1)
    lower = (lane // (DR // 2)) % 2 == 0
    return jnp.where(lower, pltpu.roll(values, 128 - DR // 2, 1), pltpu.roll(values, DR // 2, 1))


def group_mask(column_ref, row_ref):
    column, row = column_ref[...], row_ref[0]
    shape = (column.shape[0], row.shape[1])
    earlier = lax.broadcasted_iota(jnp.int32, shape, 1) <= lax.broadcasted_iota(
        jnp.int32, shape, 0
    )
    same = (column == row) | ((row % 4 == 0) & (column // 4 == row // 4))
    return earlier & same


def softmax_scores(query, key, mask):
    scores = jnp.where(mask, dot_right(query, key) * SCALE, -1e30)
    powers = jnp.exp(scores - jnp.max(scores, axis=-1, keepdims=True))
    return powers / jnp.sum(powers, axis=-1, keepdims=True)


def attention_forward_kernel(
    spans, x_ref, gain_ref, first_ref, latent_gain_ref, up_ref, trig_ref, column_ref, row_ref,
    output_ref, *refs,
):
    riders = len(spans)
    take = taker(refs)
    sources = [cut_rows(source, rows) for source, rows in zip(take(riders), spans)]
    normed_ref, query_ref, key_ref, value_ref, unit_ref, low_ref, scale_ref, attended_ref = take(8)
    (sum_ref,), targets = take(1), take(riders)
    buffers, semaphores, ride_sems = take(5), take(6), take(2)
    step = pl.program_id(0)

    @pl.when(step == 0)
    def _():
        others = lax.axis_size("dp") - 1 if riders else 0
        greet_dp(others)
        greet(*place_of(lax.axis_index("expert")), others)
        ride(sources, targets, *ride_sems)

    rank = up_ref.shape[0]
    inputs = x_ref[...].astype(F32)
    scale = lax.rsqrt(jnp.mean(inputs * inputs, axis=1, keepdims=True) + EPS)
    normed_ref[...] = (inputs * scale * gain_ref[...]).astype(BF)
    out = dot(normed_ref[...], first_ref[...])
    latent = out[:, DN : DN + rank]
    latent_scale = lax.rsqrt(jnp.mean(latent * latent, axis=1, keepdims=True) + EPS)
    scale_ref[...] = latent_scale
    unit = latent * latent_scale
    unit_ref[...] = unit.astype(BF)
    low_ref[...] = (unit * latent_gain_ref[...]).astype(BF)
    keys_values = dot(low_ref[...], up_ref[...])
    rope = out[:, DN + rank :]
    turned = rope * trig_ref[:, :128] + half_turn(rope) * trig_ref[:, 128:]
    lane = lax.broadcasted_iota(jnp.int32, turned.shape, 1)
    query_ref[:, :DN] = out[:, :DN].astype(BF)
    query_ref[:, DN:] = jnp.where(lane < DR, pltpu.roll(turned, DR, 1), 0.0).astype(BF)
    key_ref[:, :DN] = keys_values[:, :DN].astype(BF)
    key_ref[:, DN:] = jnp.where(lane < DR, turned, 0.0).astype(BF)
    value_ref[...] = keys_values[:, DN:].astype(BF)
    probs = softmax_scores(query_ref[...], key_ref[...], group_mask(column_ref, row_ref))
    attended_ref[...] = dot(probs.astype(BF), value_ref[...]).astype(BF)
    advance, finish, _, _ = step_scatter(step, buffers, semaphores)

    def produce(first, target):
        rows, width = target.shape

        @pl.loop(0, width // COLUMNS)
        def _(tile):
            columns = pl.ds(pl.multiple_of(tile * COLUMNS, COLUMNS), COLUMNS)
            target[:, columns] = dot(
                attended_ref[pl.ds(first, rows)], output_ref[:, columns]
            ).astype(BF)

    advance(produce)

    @pl.when(step == 2 * LINE - 1)
    def _():
        finish(sum_ref)
        for copy in ride(sources, targets, *ride_sems, start=False):
            copy.wait()


def attention_forward(
    x, gain, first_w, latent_gain, up_w, trig, column, row, output_w, riders, collective_id
):
    width, rank = first_w.shape[0], up_w.shape[0]
    span, rows = column.shape[0], row.shape[2]

    def tile(columns):
        return pl.BlockSpec((rows, columns), lambda i: (step_tile(i), 0))

    def fixed(shape):
        return pl.BlockSpec(shape, lambda i: (0, 0), pipeline_mode=pl.Buffered(1))

    anywhere = pl.BlockSpec(memory_space=pl.ANY)
    block = (rows // 2, width)
    carried, others = max(1, len(riders)), max(1, lax.axis_size("dp") - 1)
    outs = (width, 2 * DN, 2 * DN, DV, rank, rank, 1, DV)
    kinds = (BF, BF, BF, BF, BF, BF, F32, BF)
    return pl.pallas_call(
        lambda *refs: attention_forward_kernel([rider[1] for rider in riders], *refs),
        grid=(span // rows,),
        in_specs=[
            tile(width),
            fixed((1, width)),
            fixed(first_w.shape),
            fixed((1, rank)),
            fixed(up_w.shape),
            tile(trig.shape[1]),
            tile(1),
            pl.BlockSpec((1, 1, rows), lambda i: (step_tile(i), 0, 0)),
            fixed(output_w.shape),
        ]
        + [anywhere] * len(riders),
        out_specs=[tile(columns) for columns in outs]
        + [pl.BlockSpec(block, lambda i: (0, 0))]
        + [anywhere] * len(riders),
        out_shape=[jax.ShapeDtypeStruct((span, c), k) for c, k in zip(outs, kinds)]
        + [jax.ShapeDtypeStruct(block, F32)]
        + [landed(rider) for rider in riders],
        scratch_shapes=step_buffers(block)
        + [pltpu.SemaphoreType.DMA((carried, others)) for _ in range(2)],
        compiler_params=pltpu.CompilerParams(
            collective_id=collective_id, has_side_effects=True, vmem_limit_bytes=VMEM_LIMIT
        ),
        name="attention_forward",
    )(
        x, gain[None], first_w, latent_gain[None], up_w, trig, column, row, output_w,
        *[rider[0] for rider in riders],
    )


def attention_backward_kernel(
    latent_piece, small_rows, spans,
    r_ref, output_ref, attended_ref, query_ref, key_ref, value_ref, column_ref, row_ref, trig_ref,
    unit_ref, low_ref, scale_ref, latent_gain_ref, up_ref, normed_ref, first_ref,
    side_ref, gain_ref, down_now_ref, down_parts_ref, *refs,
):
    riders = len(spans)
    take = taker(refs)
    sources = [cut_rows(source, rows) for source, rows in zip(take(riders), spans)]
    (sum_ref, folded_ref, down_ref), (query_out, up_out, output_out) = take(3), take(3)
    own_targets, targets = take(4), take(riders)
    grad_ref, kv_ref, output_grad_ref, up_grad_ref, first_grad_ref, gain_grad_ref = take(6)
    query_full, query_low, up_low, output_low, small_ref, folded_low = take(6)
    fold_buffers, fold_semaphores = take(4), take(6)
    buffers, semaphores, ride_sems, out_sem, own_sems = take(5), take(6), take(2), take(1)[0], take(2)
    step = pl.program_id(0)
    rank = up_ref.shape[0]
    n_d, me_d = lax.axis_size("dp"), lax.axis_index("dp")
    experts = lax.axis_size("expert")

    @pl.when(step == 0)
    def _():
        greet_dp(n_d - 1)
        greet(*place_of(lax.axis_index("expert")), n_d - 1)
        ride(sources, targets, *ride_sems)
        output_grad_ref[...] = jnp.zeros_like(output_grad_ref)
        up_grad_ref[...] = jnp.zeros_like(up_grad_ref)
        first_grad_ref[...] = jnp.zeros_like(first_grad_ref)
        gain_grad_ref[...] = jnp.zeros_like(gain_grad_ref)

    down_total = down_now_ref[...]
    for ahead in range(1, n_d):
        down_total = down_total + down_parts_ref[ahead - 1].astype(F32)
    down_ref[...] = down_total
    attended_grad = dot_right(r_ref[...], output_ref[...]).astype(BF)
    output_grad_ref[...] += dot_left(attended_ref[...], r_ref[...])
    probs = softmax_scores(query_ref[...], key_ref[...], group_mask(column_ref, row_ref))
    kv_ref[:, DN:] = dot_left(probs.astype(BF), attended_grad).astype(BF)
    probs_grad = dot_right(attended_grad, value_ref[...])
    inner = jnp.sum(probs * probs_grad, axis=1, keepdims=True)
    score_grad = (probs * (probs_grad - inner)).astype(BF)
    query_grad = dot(score_grad, key_ref[...]) * SCALE
    key_grad = dot_left(score_grad, query_ref[...]) * SCALE
    kv_ref[:, :DN] = key_grad[:, :DN].astype(BF)
    grad_ref[:, :DN] = query_grad[:, :DN].astype(BF)
    rope = key_grad[:, DN:] + pltpu.roll(query_grad[:, DN:], DR, 1)
    rope = rope * trig_ref[:, :128] + half_turn(rope * trig_ref[:, 128:])
    grad_ref[:, DN + rank :] = rope.astype(BF)
    out_grad = dot_right(kv_ref[...], up_ref[...])
    unit = unit_ref[...].astype(F32)
    gain_grad_ref[...] += jnp.sum(out_grad * unit, axis=0, keepdims=True)
    scaled = out_grad * latent_gain_ref[...]
    inner = jnp.mean(scaled * unit, axis=1, keepdims=True)
    grad_ref[:, DN : DN + rank] = (scale_ref[...] * (scaled - unit * inner)).astype(BF)
    up_grad_ref[...] += dot_left(low_ref[...], kv_ref[...])
    first_grad_ref[...] += dot_left(normed_ref[...], grad_ref[...])
    advance, _, last_hop, last_sum = step_scatter(step, buffers, semaphores)

    def produce(first, target):
        rows, width = target.shape

        @pl.loop(0, width // COLUMNS)
        def _(tile):
            columns = pl.ds(pl.multiple_of(tile * COLUMNS, COLUMNS), COLUMNS)
            target[:, columns] = dot_right(
                grad_ref[pl.ds(first, rows)], first_ref[columns, :]
            ).astype(BF)

    advance(produce)

    def part(array, number, owner):
        size = array.shape[1 if number == 2 else 0] // n_d
        at = pl.ds(pl.multiple_of(owner * size, size), size)
        return array.at[:, at] if number == 2 else array.at[at]

    def own_copies():
        copies = []
        for number, low in enumerate((query_low, up_low, output_low)):
            for ahead in range(1, n_d):
                owner = lax.rem(me_d + ahead, n_d)
                copies.append((part(low, number, owner), number, ahead))
        for ahead in range(1, n_d):
            copies.append((folded_low, 3, ahead))
        return [
            pltpu.make_async_remote_copy(
                src_ref=source,
                dst_ref=own_targets[number].at[ahead - 1],
                send_sem=own_sems[0].at[number, ahead - 1],
                recv_sem=own_sems[1].at[number, ahead - 1],
                device_id={"dp": lax.rem(me_d + ahead, n_d)},
                device_id_type=MESH,
            )
            for source, number, ahead in copies
        ]

    @pl.when(step == 2 * LINE - 1)
    def _():
        last = DN + rank
        strip = 256

        @pl.loop(0, first_grad_ref.shape[0] // strip)
        def _(tile):
            first = pl.multiple_of(tile * strip, strip)
            at = pl.ds(first, strip)
            sums = first_grad_ref[at]
            rope = sums[:, last:]
            query_full[at, :DN] = sums[:, :DN]
            query_full[at, DN:] = pltpu.roll(rope, DR, 1)
            query_low[at, :DN] = sums[:, :DN].astype(BF)
            query_low[at, DN:] = pltpu.roll(rope, DR, 1).astype(BF)
            small_ref[at, :rank] = sums[:, DN:last].astype(BF)
            gain_sum = jnp.sum(sums * first_ref[at].astype(F32), axis=1, keepdims=True)
            gain_sum = gain_sum / gain_ref[at]
            row = lax.broadcasted_iota(jnp.int32, (strip, rank), 0) + first
            index = lax.broadcasted_iota(jnp.int32, (strip, rank), 1)
            place = (index // latent_piece) * small_rows + index % latent_piece
            latent_sum = jnp.sum(
                jnp.where(row == place, gain_grad_ref[...], 0.0), axis=1, keepdims=True
            )
            lane = lax.broadcasted_iota(jnp.int32, rope.shape, 1)
            mixed = jnp.where(lane < DR, rope, side_ref[at].astype(F32))
            mixed = jnp.where(lane == DR + experts + 1, gain_sum, mixed)
            mixed = jnp.where(lane == DR + experts + 2, latent_sum, mixed)
            small_ref[at, rank:] = mixed.astype(BF)

        up_low[...] = up_grad_ref[...].astype(BF)
        output_low[...] = output_grad_ref[...].astype(BF)
        outs = [
            pltpu.make_async_copy(query_full, query_out, out_sem.at[0]),
            pltpu.make_async_copy(up_grad_ref, up_out, out_sem.at[1]),
            pltpu.make_async_copy(output_grad_ref, output_out, out_sem.at[2]),
        ]
        for copy in outs:
            copy.start()
        moves = own_copies()
        for copy in moves[: 3 * (n_d - 1)]:
            copy.start()

        def fold(dest, target):
            wide = small_ref.shape[1]
            total = folded_ref.shape[0] // STRIP
            target[...] = jnp.zeros(target.shape, BF)
            for unit in range(n_d * small_rows // STRIP):
                owner, first = (unit * STRIP) // small_rows, (unit * STRIP) % small_rows
                start = pl.multiple_of((owner * experts + dest) * small_rows + first, STRIP)
                target[
                    (unit % total) * STRIP : (unit % total + 1) * STRIP,
                    (unit // total) * wide : (unit // total + 1) * wide,
                ] = small_ref[pl.ds(start, STRIP)]

        last_hop()
        scatter_folded(fold, folded_ref, fold_buffers, fold_semaphores)
        folded_low[...] = folded_ref[...].astype(BF)
        for copy in moves[3 * (n_d - 1) :]:
            copy.start()
        last_sum(sum_ref)
        for copy in moves + outs:
            copy.wait()
        for copy in ride(sources, targets, *ride_sems, start=False):
            copy.wait()


def attention_backward(
    residual_all, output_w, stored, column, row, trig, latent_gain, up_w, first_w, side, gain,
    latent_piece, small_rows, down_now, down_parts, riders, collective_id,
):
    normed, query, key, value, unit, low, scale, attended = stored
    width, rank = residual_all.shape[1], up_w.shape[0]
    rows = row.shape[2]
    n_d = lax.axis_size("dp")
    first_width = 2 * DN + rank
    block = (rows // 2, width)
    folded = (EXTRA_ROWS, width)
    small = (width, rank + 128)
    down_block = (down_now.shape[0] // (2 * LINE), down_now.shape[1])

    def tile(columns):
        return pl.BlockSpec((rows, columns), lambda i: (step_tile(i), 0))

    def fixed(shape):
        return pl.BlockSpec(shape, lambda i: (0, 0), pipeline_mode=pl.Buffered(1))

    anywhere = pl.BlockSpec(memory_space=pl.ANY)
    carried, others = max(1, len(riders)), max(1, n_d - 1)
    query_shape, up_shape, output_shape = (width, 2 * DN), up_w.shape, output_w.shape
    to_others = [
        (n_d - 1, query_shape[0] // n_d, query_shape[1]),
        (n_d - 1, up_shape[0] // n_d, up_shape[1]),
        (n_d - 1, output_shape[0], output_shape[1] // n_d),
        (n_d - 1,) + folded,
    ]
    return pl.pallas_call(
        lambda *refs: attention_backward_kernel(
            latent_piece, small_rows, [rider[1] for rider in riders], *refs
        ),
        grid=(2 * LINE,),
        in_specs=[
            tile(width),
            fixed(output_w.shape),
            tile(DV),
            tile(2 * DN),
            tile(2 * DN),
            tile(DV),
            tile(1),
            pl.BlockSpec((1, 1, rows), lambda i: (step_tile(i), 0, 0)),
            tile(trig.shape[1]),
            tile(rank),
            tile(rank),
            tile(1),
            fixed((1, rank)),
            fixed(up_w.shape),
            tile(width),
            fixed(first_w.shape),
            fixed(side.shape),
            fixed((width, 1)),
            pl.BlockSpec(down_block, lambda i: (i, 0)),
            pl.BlockSpec((n_d - 1,) + down_block, lambda i: (0, i, 0)),
        ]
        + [anywhere] * len(riders),
        out_specs=[
            pl.BlockSpec(block, lambda i: (0, 0)),
            pl.BlockSpec(folded, lambda i: (0, 0)),
            pl.BlockSpec(down_block, lambda i: (i, 0)),
        ]
        + [anywhere] * (7 + len(riders)),
        out_shape=[
            jax.ShapeDtypeStruct(shape, F32)
            for shape in (block, folded, down_now.shape, query_shape, up_shape, output_shape)
        ]
        + [jax.ShapeDtypeStruct(shape, BF) for shape in to_others]
        + [landed(rider) for rider in riders],
        scratch_shapes=[
            pltpu.VMEM((rows, first_width), BF),
            pltpu.VMEM((rows, DN + DV), BF),
            pltpu.VMEM(output_shape, F32),
            pltpu.VMEM(up_shape, F32),
            pltpu.VMEM((width, first_width), F32),
            pltpu.VMEM((1, rank), F32),
            pltpu.VMEM(query_shape, F32),
            pltpu.VMEM(query_shape, BF),
            pltpu.VMEM(up_shape, BF),
            pltpu.VMEM(output_shape, BF),
            pltpu.VMEM(small, BF),
            pltpu.VMEM(folded, BF),
            pltpu.VMEM((2 * LINE,) + folded, BF),
            pltpu.VMEM((2 * LINE,) + folded, BF),
            pltpu.VMEM((LINE + 1,) + folded, BF),
            pltpu.VMEM((LINE + 1,) + folded, BF),
            pltpu.SemaphoreType.DMA((2 * LINE,)),
            pltpu.SemaphoreType.DMA((2 * LINE,)),
            pltpu.SemaphoreType.DMA((LINE,)),
            pltpu.SemaphoreType.DMA((LINE,)),
            pltpu.SemaphoreType.DMA((LINE,)),
            pltpu.SemaphoreType.DMA((LINE + 1,)),
        ]
        + step_buffers(block)
        + [pltpu.SemaphoreType.DMA((carried, others)) for _ in range(2)]
        + [pltpu.SemaphoreType.DMA((3,))]
        + [pltpu.SemaphoreType.DMA((4, others)) for _ in range(2)],
        compiler_params=pltpu.CompilerParams(
            collective_id=collective_id, has_side_effects=True, vmem_limit_bytes=VMEM_LIMIT
        ),
        name="attention_backward",
    )(
        residual_all, output_w, attended, query, key, value, column, row, trig,
        unit, low, scale, latent_gain[None], up_w, normed, first_w, side,
        gain[:, None], down_now, down_parts, *[rider[0] for rider in riders],
    )


HIDDEN = 256
ROUTER_AT = 448


def logistic(values):
    return 0.5 * jnp.tanh(0.5 * values) + 0.5


def expert_layer_kernel(
    splits,
    ffn_ref, y_ref, code_row_ref, code_column_ref, wide_ref, shared_down_ref, *refs,
):
    take = taker(refs)
    own_weights, came = take(3), take(len(splits))
    (
        rows_ref, ups_ref, scaled_ref, gate_ref, up_ref, mixed_ref,
        down_grad_out, wide_grad_out, sum_ref,
    ) = take(9)
    (
        gate_w_ref, up_w_ref, down_w_ref, load_sem, out_sem, down_grad_ref, wide_grad_ref,
        grad_ref, left_ref, inner_ref, returned_ref, slot_gate_ref, slot_dot_ref,
        part, kept, met, paired, passed,
        core_send, core_recv, pair_send, pair_recv, line_send, line_recv,
    ) = take(24)
    step = pl.program_id(0)
    me = lax.axis_index("expert")
    experts = lax.axis_size("expert")
    line, pair, core = place_of(me)
    me_d, n_d = lax.axis_index("dp"), lax.axis_size("dp")
    groups, _, per = code_row_ref.shape
    slots = rows_ref.shape[0] // groups
    width = ffn_ref.shape[1]
    hidden = gate_w_ref.shape[1]

    wholes = (gate_w_ref, up_w_ref, down_w_ref)
    loads = []

    def load(source, number, owner, start, count):
        axis = 1 if number == 2 else 0
        size = own_weights[number].shape[axis]
        at = pl.multiple_of(owner * size, size)
        if axis == 0:
            place = wholes[number].at[pl.ds(at + start, count)]
        else:
            place = wholes[number].at[:, pl.ds(at, size)]
        loads.append(pltpu.make_async_copy(source, place, load_sem.at[len(loads)]))

    for number in range(3):
        load(own_weights[number], number, me_d, 0, own_weights[number].shape[0])
    for source, (number, first, end) in zip(came, splits):
        for ahead in range(1, n_d):
            owner = lax.rem(me_d - ahead + n_d, n_d)
            load(source.at[ahead - 1], number, owner, first, end - first)

    @pl.when(step == 0)
    def _():
        for copy in loads:
            copy.start()
        greet(line, pair, core)
        down_grad_ref[...] = jnp.zeros_like(down_grad_ref)
        wide_grad_ref[...] = jnp.zeros_like(wide_grad_ref)

    out = dot(ffn_ref[...], wide_ref[...])
    gates, ups = out[:, :HIDDEN], out[:, HIDDEN:]
    last = out[:, 2 * HIDDEN - 128 :]
    lane = lax.broadcasted_iota(jnp.int32, last.shape, 1)
    first_lane = ROUTER_AT - (2 * HIDDEN - 128)
    logits = jnp.where((lane >= first_lane) & (lane < first_lane + experts), last, -1e30)
    powers = jnp.exp(logits - jnp.max(logits, axis=1, keepdims=True))
    probs = powers / jnp.sum(powers, axis=1, keepdims=True)
    own_lane = (lane == first_lane + me).astype(F32)
    own_probs = jnp.sum(probs * own_lane, axis=1, keepdims=True)
    sigmoid = logistic(gates)
    silu = gates * sigmoid
    shared_low = (silu * ups).astype(BF)
    back = dot_right(y_ref[...], shared_down_ref[...])
    left_ref[:, :HIDDEN] = (back * ups * sigmoid * (1.0 + gates * (1.0 - sigmoid))).astype(BF)
    shared_up_low = back * silu
    left_ref[:, HIDDEN : 2 * HIDDEN - 128] = shared_up_low[:, : HIDDEN - 128].astype(BF)
    shared_last = shared_up_low[:, HIDDEN - 128 :]
    down_grad_ref[...] += dot_left(shared_low, y_ref[...])

    square = (per, per)
    diagonal = lax.broadcasted_iota(jnp.int32, square, 0) == lax.broadcasted_iota(
        jnp.int32, square, 1
    )
    for group in range(groups):
        tokens_at = pl.ds(group * per, per)
        slots_at = pl.ds(group * slots, slots)
        slot_ids = lax.broadcasted_iota(jnp.int32, (slots, per), 0)
        picks = slot_ids == code_row_ref[group]
        picks_low = picks.astype(F32).astype(BF)
        rows_ref[slots_at] = dot(picks_low, ffn_ref[tokens_at]).astype(BF)
        ups_ref[slots_at] = dot(picks_low, y_ref[tokens_at]).astype(BF)
        own_column = own_probs[group * per : (group + 1) * per]
        own_row = jnp.sum(jnp.where(diagonal, own_column, 0.0), axis=0, keepdims=True)
        slot_gate_ref[slots_at] = jnp.sum(
            jnp.where(picks, own_row, 0.0), axis=1, keepdims=True
        )
    slot_dot_ref[...] = jnp.zeros_like(slot_dot_ref)

    @pl.when(step == 0)
    def _():
        for copy in loads:
            copy.wait()

    def hidden_part(columns):
        gate_part = dot(rows_ref[...], gate_w_ref[:, columns])
        up_part = dot(rows_ref[...], up_w_ref[:, columns])
        raw = dot_right(ups_ref[...], down_w_ref[columns, :])
        slot_gate = slot_gate_ref[...]
        sigmoid = logistic(gate_part)
        silu = gate_part * sigmoid
        inner = silu * up_part
        slot_dot_ref[...] += jnp.sum(inner * raw, axis=1, keepdims=True)
        grad = raw * slot_gate
        inner_ref[:, columns] = inner.astype(BF)
        scaled_ref[:, columns] = (inner * slot_gate).astype(BF)
        gate_ref[:, columns] = (
            grad * up_part * sigmoid * (1.0 + gate_part * (1.0 - sigmoid))
        ).astype(BF)
        up_ref[:, columns] = (grad * silu).astype(BF)

    for first in range(0, hidden, HIDDEN):
        hidden_part(pl.ds(first, min(HIDDEN, hidden - first)))

    @pl.loop(0, width // COLUMNS)
    def _(tile):
        columns = pl.ds(pl.multiple_of(tile * COLUMNS, COLUMNS), COLUMNS)
        returned_ref[:, columns] = dot(inner_ref[...], down_w_ref[:, columns]).astype(BF)
        grad_ref[:, columns] = (
            dot_right(gate_ref[...], gate_w_ref[columns, :])
            + dot_right(up_ref[...], up_w_ref[columns, :])
        ).astype(BF)

    for group in range(groups):
        tokens_at = pl.ds(group * per, per)
        slots_at = pl.ds(group * slots, slots)
        own_column = own_probs[group * per : (group + 1) * per]
        slot_lane = lax.broadcasted_iota(jnp.int32, (per, slots), 1)
        picks = slot_lane == code_column_ref[tokens_at]
        pick_gate = jnp.where(picks, own_column, 0.0).astype(BF)
        mixed_ref[tokens_at] = (
            dot(shared_low[group * per : (group + 1) * per], shared_down_ref[...])
            + dot(pick_gate, returned_ref[slots_at])
        ).astype(BF)
        small = (slots, slots)
        eye = lax.broadcasted_iota(jnp.int32, small, 0) == lax.broadcasted_iota(
            jnp.int32, small, 1
        )
        dot_row = jnp.sum(jnp.where(eye, slot_dot_ref[slots_at], 0.0), axis=0, keepdims=True)
        row_dot = jnp.sum(jnp.where(picks, dot_row, 0.0), axis=1, keepdims=True)
        at = slice(group * per, (group + 1) * per)
        logit_grad = row_dot * own_column * (own_lane[at] - probs[at])
        high = logit_grad.astype(BF)
        rest = logit_grad - high.astype(F32)
        left_ref[tokens_at, 2 * HIDDEN - 128 :] = jnp.where(
            lane[at] < first_lane,
            shared_last[at],
            high.astype(F32) + pltpu.roll(rest, experts, 1),
        ).astype(BF)
    wide_grad_ref[...] += dot_left(ffn_ref[...], left_ref[...])

    advance, finish, _, _ = step_scatter(
        step, (part, kept, met, paired, passed),
        (core_send, core_recv, pair_send, pair_recv, line_send, line_recv),
    )
    rows = kept.shape[0]

    def produce(first, target):
        @pl.loop(0, width // COLUMNS)
        def _(tile):
            columns = pl.ds(pl.multiple_of(tile * COLUMNS, COLUMNS), COLUMNS)
            total = dot_right(left_ref[pl.ds(first, rows)], wide_ref[columns, :])
            for k in range(rows // per):
                group = first // per + k
                slot_lane = lax.broadcasted_iota(jnp.int32, (per, slots), 1)
                picks = slot_lane == code_column_ref[pl.ds(first + k * per, per)]
                scattered = dot(
                    picks.astype(F32).astype(BF),
                    grad_ref[pl.ds(group * slots, slots), columns],
                )
                target[pl.ds(k * per, per), columns] = (
                    total[k * per : (k + 1) * per] + scattered
                ).astype(BF)

    advance(produce)

    @pl.when(step == 2 * LINE - 1)
    def _():
        outs = [
            pltpu.make_async_copy(down_grad_ref, down_grad_out, out_sem.at[0]),
            pltpu.make_async_copy(wide_grad_ref, wide_grad_out, out_sem.at[1]),
        ]
        for copy in outs:
            copy.start()
        finish(sum_ref)
        for copy in outs:
            copy.wait()


def expert_layer(
    ffn_all, upstream_all, code, slots, wide, shared_down, weights, came, splits, collective_id
):
    groups, per = code.shape
    span, width = ffn_all.shape
    gate_w, up_w, down_w = weights
    hidden = gate_w.shape[1]
    n_d = lax.axis_size("dp")
    rows, slot_rows = TILE_GROUPS * per, TILE_GROUPS * slots
    total = groups * slots
    steps = 2 * LINE
    block = (rows // 2, width)

    def tile(count, columns):
        return pl.BlockSpec((count, columns), lambda i: (step_tile(i), 0))

    def fixed(shape):
        return pl.BlockSpec(shape, lambda i: (0, 0), pipeline_mode=pl.Buffered(1))

    anywhere = pl.BlockSpec(memory_space=pl.ANY)
    outs = [(total, width)] * 2 + [(total, hidden)] * 3 + [(span, width)]
    sums = [shared_down.shape, wide.shape]
    copies = 3 + len(came) * (n_d - 1)
    return pl.pallas_call(
        lambda *refs: expert_layer_kernel(splits, *refs),
        grid=(steps,),
        in_specs=[
            tile(rows, width),
            tile(rows, width),
            pl.BlockSpec((TILE_GROUPS, 1, per), lambda i: (step_tile(i), 0, 0)),
            tile(rows, 1),
            fixed(wide.shape),
            fixed(shared_down.shape),
        ]
        + [anywhere] * (3 + len(came)),
        out_specs=[
            tile(slot_rows if shape[0] == total else rows, shape[1]) for shape in outs
        ]
        + [anywhere] * 2
        + [pl.BlockSpec(block, lambda i: (0, 0))],
        out_shape=[jax.ShapeDtypeStruct(shape, BF) for shape in outs]
        + [jax.ShapeDtypeStruct(shape, F32) for shape in sums]
        + [jax.ShapeDtypeStruct(block, BF)],
        scratch_shapes=[
            pltpu.VMEM((gate_w.shape[0] * n_d, hidden), BF),
            pltpu.VMEM((up_w.shape[0] * n_d, hidden), BF),
            pltpu.VMEM((hidden, down_w.shape[1] * n_d), BF),
            pltpu.SemaphoreType.DMA((copies,)),
            pltpu.SemaphoreType.DMA((2,)),
            pltpu.VMEM(shared_down.shape, F32),
            pltpu.VMEM(wide.shape, F32),
            pltpu.VMEM((slot_rows, width), BF),
            pltpu.VMEM((rows, 2 * HIDDEN), BF),
            pltpu.VMEM((slot_rows, hidden), BF),
            pltpu.VMEM((slot_rows, width), BF),
            pltpu.VMEM((slot_rows, 1), F32),
            pltpu.VMEM((slot_rows, 1), F32),
        ]
        + step_buffers(block),
        compiler_params=pltpu.CompilerParams(
            collective_id=collective_id,
            has_side_effects=True,
            vmem_limit_bytes=63 * 1024 * 1024,
        ),
        name="expert_layer",
    )(
        ffn_all, upstream_all, code[:, None, :], code.reshape(span, 1), wide, shared_down,
        gate_w, up_w, down_w, *came,
    )


def on_device(
    tokens,
    segment,
    routes,
    drop_order,
    cotangent,
    attn_gain,
    query_weight,
    down_latent,
    latent_gain,
    up_latent,
    output_weight,
    ffn_gain,
    router_weight,
    shared_gate,
    shared_up,
    shared_down,
    expert_gate,
    expert_up,
    expert_down,
):
    n_e = lax.axis_size("expert")
    n_d = lax.axis_size("dp")
    me_e = lax.axis_index("expert")
    me_d = lax.axis_index("dp")
    micro, group_rows, width = tokens.shape
    own_rows = micro * group_rows
    span = n_e * own_rows
    groups = n_e * micro
    top = routes.shape[2]
    experts = n_e * expert_gate.shape[0]
    capacity = (5 * group_rows * top + 4 * experts - 1) // (4 * experts)
    slots = -(-capacity // 16) * 16
    rank_latent = latent_gain.shape[0] * n_e * n_d

    def gather(values):
        return lax.all_gather(values, "expert", axis=0, tiled=True)

    def scatter(values):
        return lax.psum_scatter(values, "expert", scatter_dimension=0, tiled=True)

    def whole(own, parts, axis):
        blocks = [own] + [parts[step - 1] for step in range(1, n_d)]
        ordered = [
            lax.select_n(lax.rem(me_d - owner + n_d, n_d), *blocks) for owner in range(n_d)
        ]
        return jnp.concatenate(ordered, axis=axis)

    def split_dp(values, axis):
        size = values.shape[axis] // n_d
        parts = []
        for step in range(n_d):
            at = lax.rem(me_d + step, n_d) * size
            parts.append(lax.dynamic_slice_in_dim(values, at, size, axis))
        return (stack([part.astype(BF) for part in parts[1:]]), parts[0])

    def stack(parts):
        return parts[0][None] if len(parts) == 1 else jnp.stack(parts)

    def add_all(total, parts):
        for step in range(n_d - 1):
            total = total + parts[step].astype(F32)
        return total

    small_rows = attn_gain.shape[0]
    latent_all_width = down_latent.shape[1]
    latent_piece = latent_gain.shape[0]
    packed = jnp.concatenate(
        [
            down_latent,
            router_weight,
            attn_gain[:, None],
            ffn_gain[:, None],
            jnp.pad(latent_gain, (0, small_rows - latent_piece))[:, None],
        ],
        axis=1,
    )
    packed = lax.all_gather(packed, ("dp", "expert"), axis=0, tiled=True)
    down_all = packed[:, :latent_all_width]
    router_all = packed[:, latent_all_width : latent_all_width + experts]
    rest = packed[:, latent_all_width + experts :].astype(F32)
    attn_gain_all = rest[:, 0]
    ffn_gain_all = rest[:, 1]
    latent_gain_all = rest[:, 2].reshape(n_e * n_d, small_rows)[:, :latent_piece].reshape(-1)

    chosen = jnp.sum(
        (routes[..., None] == jnp.arange(experts, dtype=jnp.int32)).astype(jnp.int32), axis=2
    )
    order = drop_order[:, 0]
    earlier = (order[:, None, :] < order[:, :, None]).astype(F32)
    rank = jnp.einsum("mtu,mue->mte", earlier, chosen.astype(F32)).astype(jnp.int32)
    code = jnp.where((chosen == 1) & (rank < capacity), rank, -1).reshape(own_rows, experts)

    tokens_own = tokens.reshape(own_rows, width)
    code_lanes = -(-experts // 128) * 128
    code_low = jnp.pad(code.astype(BF), ((0, 0), (0, code_lanes - experts)))
    own_gate, own_up, own_down = expert_gate[0], expert_up[0], expert_down[0]
    gate_first = own_gate.shape[0] // 4
    dense = (query_weight, up_latent, output_weight, shared_gate, shared_up, shared_down)
    came = gather_rows(
        jnp.concatenate([tokens_own, code_low], axis=1),
        5,
        riders=[(array, (0, array.shape[0])) for array in dense] + [(own_gate, (0, gate_first))],
    )
    tokens_all, gate_came = came[0], came[7]
    query_w, up_w, output_w, shared_gate_w, shared_up_w, shared_down_w = [
        whole(own, parts, axis)
        for own, parts, axis in zip(dense, came[1:7], (0, 0, 1, 0, 0, 1))
    ]
    upstream_own = cotangent.reshape(own_rows, width)
    upstream_later, tokens_all = lax.optimization_barrier((upstream_own, tokens_all))
    upstream_all = gather(upstream_later)
    code_all = tokens_all[:, width : width + experts].astype(jnp.int32)
    my_code = lax.dynamic_slice_in_dim(code_all, me_e, 1, 1).reshape(groups, group_rows)

    span_segment = (
        segment.reshape(micro, n_e, group_rows).transpose(1, 0, 2).reshape(groups, group_rows)
    )
    trig = angles(positions(span_segment), group_rows)
    marks = span_segment + 4 * jnp.arange(groups, dtype=jnp.int32)[:, None]
    column = marks.reshape(span, 1)
    row = marks.reshape(groups // TILE_GROUPS, 1, TILE_GROUPS * group_rows)
    first_w = jnp.concatenate(
        [
            query_w[:, :DN],
            down_all[:, :rank_latent],
            down_all[:, rank_latent:],
            query_w[:, DN:],
        ],
        axis=1,
    )
    came = attention_forward(
        tokens_all,
        attn_gain_all,
        first_w,
        latent_gain_all,
        up_w,
        trig,
        column,
        row,
        output_w,
        [(own_gate, (gate_first, own_gate.shape[0])), (own_up, (0, own_up.shape[0]))],
        2,
    )
    stored, attention_out, gate_came_last, up_came = came[:8], came[8], came[9], came[10]
    residual = tokens_own.astype(F32) + attention_out

    second_scale = rms_scale(residual)
    ffn_in = (residual * second_scale * ffn_gain_all).astype(BF)
    ffn_all, down_came = gather_rows(ffn_in, 1, riders=[(own_down, (0, own_down.shape[0]))])

    shared_hidden = shared_gate_w.shape[1]
    wide = jnp.concatenate(
        [
            jnp.pad(shared_gate_w, ((0, 0), (0, HIDDEN - shared_hidden))),
            jnp.pad(shared_up_w, ((0, 0), (0, ROUTER_AT - HIDDEN - shared_hidden))),
            router_all,
            jnp.pad(router_all, ((0, 0), (0, 2 * HIDDEN - ROUTER_AT - 2 * experts))),
        ],
        axis=1,
    )
    (
        expert_rows,
        slot_up,
        inner_scaled,
        gate_low,
        up_low,
        mixed_part,
        shared_down_grad,
        wide_grad,
        ffn_grad,
    ) = expert_layer(
        ffn_all,
        upstream_all,
        my_code,
        slots,
        wide,
        jnp.pad(shared_down_w, ((0, HIDDEN - shared_hidden), (0, 0))),
        (own_gate, own_up, own_down),
        (gate_came, gate_came_last, up_came, down_came),
        (
            (0, 0, gate_first),
            (0, gate_first, own_gate.shape[0]),
            (1, 0, own_up.shape[0]),
            (2, 0, own_down.shape[0]),
        ),
        3,
    )
    ffn_grad = ffn_grad.astype(F32)
    mixed = residual + scatter(mixed_part).astype(F32)
    router_grad = (
        wide_grad[:, ROUTER_AT : ROUTER_AT + experts]
        + wide_grad[:, ROUTER_AT + experts : ROUTER_AT + 2 * experts]
    )
    shared_down_later, shared_down_now = split_dp(shared_down_grad[:shared_hidden], 1)
    shared_gate_later, shared_gate_now = split_dp(wide_grad[:, :shared_hidden], 0)
    shared_up_later, shared_up_now = split_dp(wide_grad[:, HIDDEN : HIDDEN + shared_hidden], 0)
    residual_part, ffn_gain_grad = norm_back(residual, second_scale, ffn_gain_all, ffn_grad)
    residual_grad = upstream_own.astype(F32) + residual_part
    (
        residual_all,
        shared_down_parts,
        shared_gate_parts,
        shared_up_parts,
        down_now,
        gate_now,
        up_now,
        down_parts,
        gate_parts_first,
        gate_later,
        up_later,
    ) = gather_rows(
        residual_grad.astype(BF),
        6,
        riders=[
            (later, None) for later in (shared_down_later, shared_gate_later, shared_up_later)
        ],
        products=(expert_rows, slot_up, inner_scaled, gate_low, up_low),
    )

    side = jnp.concatenate(
        [
            jnp.zeros((width, DR), F32),
            router_grad,
            ffn_gain_grad[:, None],
            jnp.zeros((width, 128 - DR - experts - 1), F32),
        ],
        axis=1,
    ).astype(BF)
    (
        normed_grad,
        folded,
        down_grad,
        query_full,
        up_latent_full,
        output_full,
        query_parts,
        latent_parts,
        output_parts,
        folded_parts,
        gate_parts_last,
        up_parts,
    ) = attention_backward(
        residual_all,
        output_w,
        stored,
        column,
        row,
        trig,
        latent_gain_all,
        up_w,
        first_w,
        side,
        attn_gain_all,
        latent_piece,
        small_rows,
        down_now,
        down_parts,
        [(gate_later, None), (up_later, None)],
        4,
    )

    def own_part(values, axis):
        size = values.shape[axis] // n_d
        return lax.dynamic_slice_in_dim(values, me_d * size, size, axis)

    query_grad = add_all(own_part(query_full, 0), query_parts)[:, : DN + DR]
    up_latent_grad = add_all(own_part(up_latent_full, 0), latent_parts)
    output_grad = add_all(own_part(output_full, 1), output_parts)
    small_width = rank_latent + 128
    folded = add_all(folded, folded_parts)
    small = jnp.concatenate(
        [folded[:, k * small_width : (k + 1) * small_width] for k in range(width // small_width)],
        axis=0,
    )
    small = lax.dynamic_slice_in_dim(small, me_d * small_rows, small_rows, 0)
    own_inputs = tokens_own.astype(F32)
    input_part, _ = norm_back(own_inputs, rms_scale(own_inputs), attn_gain_all, normed_grad)
    tokens_grad = residual_grad + input_part
    last = latent_all_width + experts
    shape = (micro, group_rows, width)
    return (
        mixed.reshape(shape),
        tokens_grad.reshape(shape),
        small[:, last + 1],
        query_grad,
        small[:, :latent_all_width],
        small[:latent_piece, last + 2],
        up_latent_grad,
        output_grad,
        small[:, last],
        small[:, latent_all_width:last],
        add_all(shared_gate_now, shared_gate_parts),
        add_all(shared_up_now, shared_up_parts),
        add_all(shared_down_now, shared_down_parts),
        jnp.concatenate(
            [
                add_all(gate_now[: gate_now.shape[0] // 2], gate_parts_first),
                add_all(gate_now[gate_now.shape[0] // 2 :], gate_parts_last),
            ],
            axis=0,
        )[None],
        add_all(up_now, up_parts)[None],
        down_grad[None],
    )


def solution(mesh):
    rows = P(None, ("dp", "expert"), None)
    split = P(("dp", "expert"))
    split_rows = P(("dp", "expert"), None)
    columns = P("dp", "expert")
    turned = P("expert", "dp")
    expert_in = P("expert", "dp", None)
    expert_out = P("expert", None, "dp")
    return jax.shard_map(
        on_device,
        mesh=mesh,
        in_specs=(
            rows,
            P(None, "dp"),
            rows,
            rows,
            rows,
            split,
            columns,
            split_rows,
            split,
            columns,
            turned,
            split,
            split_rows,
            columns,
            columns,
            turned,
            expert_in,
            expert_in,
            expert_out,
        ),
        out_specs=(
            rows,
            rows,
            split,
            columns,
            split_rows,
            split,
            columns,
            turned,
            split,
            split_rows,
            columns,
            columns,
            turned,
            expert_in,
            expert_in,
            expert_out,
        ),
        check_vma=False,
    )
```

```python
import math

import jax
import jax.numpy as jnp
from jax import lax
from jax.experimental import pallas as pl
from jax.experimental.pallas import tpu as pltpu
from jax.sharding import PartitionSpec as P

DN = 128
DR = 64
DV = 128
EPS = 1e-06
HIGH = lax.Precision.HIGHEST
F32 = jnp.float32
BF = jnp.bfloat16


def dot(former, latter):
    return jnp.dot(former, latter, preferred_element_type=F32)


def dot_left(former, latter):
    return lax.dot_general(former, latter, (((0,), (0,)), ((), ())), preferred_element_type=F32)


def dot_right(former, latter):
    return lax.dot_general(former, latter, (((1,), (1,)), ((), ())), preferred_element_type=F32)


def rms_scale(values):
    return lax.rsqrt(jnp.mean(values * values, axis=-1, keepdims=True) + EPS)


def norm_back(values, scale_rows, gain, out_grad):
    scaled = out_grad * gain
    inner = jnp.mean(scaled * values, axis=-1, keepdims=True)
    value_grad = scale_rows * scaled - values * scale_rows * scale_rows * scale_rows * inner
    return (value_grad, jnp.sum(out_grad * values * scale_rows, axis=0))


def positions(segment):
    places = jnp.arange(segment.shape[1], dtype=jnp.int32)
    prompt_len = jnp.sum((segment == 0).astype(jnp.int32), axis=1, keepdims=True)
    former = (segment[:, None, :] < segment[:, :, None]).astype(jnp.int32)
    seg_start = jnp.sum(former, axis=2)
    return jnp.where(segment == 0, places[None], prompt_len + places[None] - seg_start)


def angles(position, row_count):
    freq_index = jnp.arange(DR // 2, dtype=F32)
    frequency = jnp.exp(freq_index * (-2.0 * math.log(10000.0) / DR))
    turning = jnp.arange(row_count, dtype=F32)[:, None] * frequency[None, :]
    cosine, sine_part = jnp.cos(turning), jnp.sin(turning)
    table = jnp.concatenate([cosine] * 4 + [-sine_part, sine_part] * 2, axis=1)
    picks = (position.reshape(-1)[:, None] == jnp.arange(row_count)[None, :]).astype(F32)
    return jnp.dot(picks, table, precision=HIGH)


LINE = 4
PIECES = 3
MESH = pl.DeviceIdType.MESH
VMEM_LIMIT = 60 * 1024 * 1024


def place_of(me):
    return (me // 4, lax.rem(me // 2, 2), lax.rem(me, 2))


def index_of(line, pair, core):
    return line * 4 + pair * 2 + core


def greet(line, pair, core, others=0):
    barrier = pltpu.get_barrier_semaphore()

    def signal(target):
        pl.semaphore_signal(barrier, inc=1, device_id={"expert": target}, device_id_type=MESH)

    signal(index_of(line, pair, 1 - core))
    signal(index_of(line, 1 - pair, core))

    @pl.when(line > 0)
    def _():
        signal(index_of(line - 1, pair, core))

    @pl.when(line < LINE - 1)
    def _():
        signal(index_of(line + 1, pair, core))

    inner = jnp.where(line > 0, 1, 0) + jnp.where(line < LINE - 1, 1, 0)
    pl.semaphore_wait(barrier, 2 + others + inner)


def greet_dp(others):
    barrier = pltpu.get_barrier_semaphore()
    me_d, n_d = lax.axis_index("dp"), lax.axis_size("dp")
    if others:
        for step in range(1, n_d):
            pl.semaphore_signal(
                barrier,
                inc=1,
                device_id={"dp": lax.rem(me_d + step, n_d)},
                device_id_type=MESH,
            )


def ride(sources, targets, send_sem, recv_sem, start=True):
    me_d, n_d = lax.axis_index("dp"), lax.axis_size("dp")
    copies = []
    for number, (source, target) in enumerate(zip(sources, targets)):
        parts = len(source.shape) == len(target.shape)
        for step in range(1, n_d):
            copy = pltpu.make_async_remote_copy(
                src_ref=source.at[step - 1] if parts else source,
                dst_ref=target.at[step - 1],
                send_sem=send_sem.at[number, step - 1],
                recv_sem=recv_sem.at[number, step - 1],
                device_id={"dp": lax.rem(me_d + step, n_d)},
                device_id_type=MESH,
            )
            if start:
                copy.start()
            copies.append(copy)
    return copies


def landed(rider):
    array, rows = rider
    if rows is None:
        return jax.ShapeDtypeStruct(array.shape, array.dtype)
    shape = (lax.axis_size("dp") - 1, rows[1] - rows[0]) + array.shape[1:]
    return jax.ShapeDtypeStruct(shape, array.dtype)


def cut_rows(ref, rows):
    return ref if rows is None else ref.at[pl.ds(rows[0], rows[1] - rows[0])]


def when(condition, action):
    if condition is None:
        action()
    else:
        pl.when(condition)(action)


def gather_kernel(spans, products, *refs):
    riders = len(spans)
    take = taker(refs)
    (own_ref,), sources = take(1), take(riders)
    products_in = take(5) if products else None
    (out_ref,), targets = take(1), take(riders)
    products_out = take(7) if products else None
    own_sem, send_sem, recv_sem, ride_send, ride_recv = take(5)
    if products:
        products = ExpertGradients(products_in, products_out, take(12))
    sources = [cut_rows(source, rows) for source, rows in zip(sources, spans)]
    me = lax.axis_index("expert")
    line, pair, core = place_of(me)
    rows = own_ref.shape[0]
    sixth = rows // 6
    half = (rows - sixth) // 2
    spans_of = (pl.ds(0, sixth), pl.ds(sixth, half), pl.ds(sixth + half, half))
    others = lax.axis_size("dp") - 1 if riders or products else 0
    greet_dp(others)
    greet(line, pair, core, others)
    local = [pltpu.make_async_copy(own_ref, out_ref.at[me], own_sem)]
    sent = []

    def push(condition, kind, origin, piece, target, source=None):
        block = out_ref.at[origin, spans_of[piece]]
        copy = pltpu.make_async_remote_copy(
            src_ref=block if source is None else source,
            dst_ref=block,
            send_sem=send_sem.at[kind, origin, piece],
            recv_sem=recv_sem.at[origin, piece],
            device_id={"expert": target},
            device_id_type=MESH,
        )
        when(condition, copy.start)
        sent.append((condition, copy))

    def arrive(condition, origin, piece):
        block = out_ref.at[origin, spans_of[piece]]
        copy = pltpu.make_async_remote_copy(
            src_ref=block,
            dst_ref=block,
            send_sem=send_sem.at[0, origin, piece],
            recv_sem=recv_sem.at[origin, piece],
            device_id={"expert": me},
            device_id_type=MESH,
        )
        when(condition, copy.wait_recv)

    left = index_of(line - 1, pair, core)
    right = index_of(line + 1, pair, core)
    across = index_of(line, 1 - pair, core)
    sibling = index_of(line, pair, 1 - core)
    for piece in range(PIECES):
        source = own_ref.at[spans_of[piece]]
        push(line < LINE - 1, 1, me, piece, right, source)
        push(line > 0, 0, me, piece, left, source)
        push(None, 2, me, piece, across, source)
        push(None, 3, me, piece, sibling, source)
    ridden = ride(sources, targets, ride_send, ride_recv)
    for copy in local:
        copy.start()
    if products:
        products.load()

    def work():
        if products:
            products.next()

    def along(hop, piece):
        for side in (-1, 1):
            there = line + side * hop
            held = (there >= 0) & (there < LINE)
            origin = index_of(there, pair, core)
            arrive(held, origin, piece)
            pass_on(held, side, hop, origin, piece)
            if piece:
                push(held, 2, origin, piece, across)
            push(held, 3, origin, piece, sibling)
        work()

    def pass_on(held, side, hop, origin, piece):
        if hop < LINE - 1:
            further = held & ((line < LINE - 1) if side < 0 else (line > 0))
            kind, target = (1, right) if side < 0 else (0, left)
            push(further, kind, origin, piece, target)

    def over(hop, piece):
        for side in (-1, 1) if hop else (1,):
            there = line + side * hop
            held = (there >= 0) & (there < LINE) if hop else None
            origin = index_of(there, 1 - pair, core)
            arrive(held, origin, piece)
            if piece == 0 and hop:
                pass_on(held, side, hop, origin, piece)
            if piece == 0 and not hop:
                push(line < LINE - 1, 1, origin, piece, right)
                push(line > 0, 0, origin, piece, left)
            push(held, 3, origin, piece, sibling)
        work()

    over(0, 0)
    for hop in range(1, LINE):
        for piece in range(PIECES):
            along(hop, piece)
        over(hop, 0)
        for piece in range(1, PIECES):
            over(hop - 1, piece)
    for piece in range(1, PIECES):
        over(LINE - 1, piece)
    for other_line in range(LINE):
        for other_pair in range(2):
            for piece in range(PIECES):
                arrive(None, index_of(other_line, other_pair, 1 - core), piece)
    if products:
        products.finish()
    for copy in ridden:
        copy.wait()
    for condition, copy in sent:
        when(condition, copy.wait_send)
    for copy in local:
        copy.wait()


class ExpertGradients:

    def __init__(self, operands, outs, scratch):
        self.sources = operands
        self.nows, self.landing, self.laters = outs[:3], outs[3:5], outs[5:7]
        self.held = scratch[:5]
        self.lows, self.stage = scratch[5:8], scratch[8]
        self.load_sem, self.out_sem, self.ride_sem = scratch[9:12]
        self.me_d, self.n_d = lax.axis_index("dp"), lax.axis_size("dp")
        self.pending, self.riding, self.count = [None, None], [], 0
        self.kinds = ((2, 1, 1), (0, 3, 0), (0, 4, 0))
        self.steps = self.all_steps()

    def load(self):
        self.loads = [
            pltpu.make_async_copy(source, held, self.load_sem.at[number])
            for number, (source, held) in enumerate(zip(self.sources, self.held))
        ]
        for copy in self.loads:
            copy.start()

    def chunk(self, number, owner, at):
        left, right, axis = self.kinds[number]
        left, right = self.held[left], self.held[right]
        shape = self.nows[number].shape
        count = chunk_rows(number, shape[0])
        if axis == 0:
            first = pl.multiple_of(owner * shape[0] + at * count, 128)
            return dot_left(left[:, pl.ds(first, count)], right[...])
        columns = pl.ds(pl.multiple_of(owner * shape[1], 128), shape[1])
        return dot_left(left[:, at * count : (at + 1) * count], right[:, columns])

    def all_steps(self):
        for copy in self.loads:
            copy.wait()
        for number in range(3):
            shape = self.nows[number].shape
            count = chunk_rows(number, shape[0])
            low = self.lows[number]
            for ahead in range(1, self.n_d):
                owner = lax.rem(self.me_d + ahead, self.n_d)
                for at in range(shape[0] // count):
                    low[ahead - 1, at * count : (at + 1) * count] = self.chunk(
                        number, owner, at
                    ).astype(BF)
                    if number == 1 and (at + 1) * count == shape[0] // 2:
                        self.leave(number, ahead, low.at[ahead - 1, : shape[0] // 2])
                    if at == shape[0] // count - 1:
                        first = shape[0] // 2 if number == 1 else 0
                        self.leave(2 + number // 2 if number else 0, ahead, low.at[ahead - 1, first:])
                    yield
        for number in range(3):
            shape = self.nows[number].shape
            count = chunk_rows(number, shape[0])
            for at in range(shape[0] // count):
                slot = self.count % 2
                if self.pending[slot] is not None:
                    self.pending[slot].wait()
                stage = self.stage.at[slot, :count, : shape[1]]
                stage[...] = self.chunk(number, self.me_d, at)
                copy = pltpu.make_async_copy(
                    stage,
                    self.nows[number].at[pl.ds(at * count, count)],
                    self.out_sem.at[slot],
                )
                copy.start()
                self.pending[slot] = copy
                self.count += 1
                yield

    def leave(self, kind, ahead, source):
        if kind >= 2:
            copy = pltpu.make_async_copy(
                source,
                self.laters[kind - 2].at[ahead - 1],
                self.load_sem.at[3 + 2 * ahead + kind - 2],
            )
        else:
            copy = pltpu.make_async_remote_copy(
                src_ref=source,
                dst_ref=self.landing[kind].at[ahead - 1],
                send_sem=self.ride_sem.at[0, kind, ahead - 1],
                recv_sem=self.ride_sem.at[1, kind, ahead - 1],
                device_id={"dp": lax.rem(self.me_d + ahead, self.n_d)},
                device_id_type=MESH,
            )
        copy.start()
        self.riding.append(copy)

    def next(self):
        next(self.steps, None)

    def finish(self):
        for _ in self.steps:
            pass
        for copy in self.riding + [copy for copy in self.pending if copy is not None]:
            copy.wait()


def chunk_rows(number, rows):
    return rows // 4 if number == 0 else min(256, rows // 2)


def gradient_shapes(products, n_d):
    rows, ups, scaled, gate, up = products
    width, hidden = rows.shape[1], gate.shape[1]
    size = width // n_d
    nows = [(hidden, size), (size, hidden), (size, hidden)]
    shapes = [jax.ShapeDtypeStruct(shape, F32) for shape in nows]
    sent = [nows[0], (size // 2, hidden), (size // 2, hidden), nows[2]]
    shapes += [jax.ShapeDtypeStruct((n_d - 1,) + shape, BF) for shape in sent]
    largest = max(hidden, size)
    scratch = [pltpu.VMEM(product.shape, BF) for product in products]
    scratch += [pltpu.VMEM((n_d - 1,) + shape, BF) for shape in nows]
    scratch += [
        pltpu.VMEM((2, 384, largest), F32),
        pltpu.SemaphoreType.DMA((5 + 2 * n_d,)),
        pltpu.SemaphoreType.DMA((2,)),
        pltpu.SemaphoreType.DMA((2, 3, n_d - 1)),
    ]
    return (shapes, scratch)


def gather_rows(own, collective_id, riders=(), products=()):
    count = lax.axis_size("expert")
    rows, width = own.shape
    shapes = [jax.ShapeDtypeStruct((count, rows, width), own.dtype)]
    shapes += [landed(rider) for rider in riders]
    n_d = lax.axis_size("dp")
    carried, others = max(1, len(riders)), max(1, n_d - 1)
    scratch = []
    if products:
        extra_shapes, scratch = gradient_shapes(products, n_d)
        shapes += extra_shapes
    out = pl.pallas_call(
        lambda *refs: gather_kernel([rider[1] for rider in riders], bool(products), *refs),
        out_shape=shapes,
        in_specs=[pl.BlockSpec(memory_space=pl.ANY)] * (1 + len(riders) + len(products)),
        out_specs=[pl.BlockSpec(memory_space=pl.ANY)] * len(shapes),
        scratch_shapes=[
            pltpu.SemaphoreType.DMA,
            pltpu.SemaphoreType.DMA((4, count, PIECES)),
            pltpu.SemaphoreType.DMA((count, PIECES)),
            pltpu.SemaphoreType.DMA((carried, others)),
            pltpu.SemaphoreType.DMA((carried, others)),
        ]
        + scratch,
        compiler_params=pltpu.CompilerParams(
            collective_id=collective_id, has_side_effects=True, vmem_limit_bytes=VMEM_LIMIT
        ),
        name="gather_rows",
    )(own, *[rider[0] for rider in riders], *products)
    return [out[0].reshape(count * rows, width)] + list(out[1:])


FAR_FIRST = ((3, 3, 0, 0), (2, 0, 3, 1), (1, 2, 1, 2), (0, 1, 2, 3))
COLUMNS = 512
STRIP = 16
EXTRA_ROWS = 48


def pick_by(line, table):
    value = jnp.int32(table[LINE - 1])
    for k in range(LINE - 2, -1, -1):
        value = jnp.where(line == k, jnp.int32(table[k]), value)
    return value


def add_strips(target, first, count, others):
    @pl.loop(0, count // STRIP)
    def _(strip):
        for columns in range(0, target.shape[1], COLUMNS):
            at = pl.ds(pl.multiple_of(first + strip * STRIP, STRIP), STRIP)
            cols = pl.ds(columns, COLUMNS)
            total = None
            for other in others:
                term = other[at, cols].astype(F32)
                total = term if total is None else total + term
            target[at, cols] = total.astype(target.dtype)


def step_scatter(step, buffers, semaphores):
    part, kept, met, paired, passed = buffers
    core_send, core_recv, pair_send, pair_recv, line_send, line_recv = semaphores
    me = lax.axis_index("expert")
    line, pair, core = place_of(me)
    rows = kept.shape[0]
    piece_rows = rows // PIECES
    sibling = index_of(line, pair, 1 - core)
    across = index_of(line, 1 - pair, core)
    steps = 2 * LINE

    def remote(source, dest, send_at, recv_at, target):
        return pltpu.make_async_remote_copy(
            src_ref=source,
            dst_ref=dest,
            send_sem=send_at,
            recv_sem=recv_at,
            device_id={"expert": target},
            device_id_type=MESH,
        )

    def to_sibling(i):
        return remote(part, met.at[i], core_send.at[i], core_recv.at[i], sibling)

    def to_pair(i, piece):
        at = pl.ds(piece * piece_rows, piece_rows)
        return remote(
            met.at[i, at],
            paired.at[i // 2, at],
            pair_send.at[i // 2, piece],
            pair_recv.at[i // 2, piece],
            across,
        )

    def meet(i):
        to_sibling(i).wait_recv()
        add_strips(met.at[i], 0, rows, [met.at[i], kept])

        @pl.when(lax.rem(i, 2) == 0)
        def _():
            for piece in range(PIECES):
                to_pair(i, piece).start()

    dest_line = [pick_by(line, FAR_FIRST[k]) for k in range(LINE)]

    def hop_facts(k):
        there = dest_line[k]
        way = jnp.where(there > line, 1, -1)
        behind = line - way
        held = (behind >= 0) & (behind < LINE)
        slot = jnp.where((there == line + way) & (way < 0), LINE, there)
        return (there, held, slot, index_of(line + way, pair, core))

    def along(k, piece):
        there, held, slot, target = hop_facts(k)
        at = pl.ds(piece * piece_rows, piece_rows)
        return remote(
            paired.at[k, at],
            passed.at[slot, at],
            line_send.at[k, piece],
            line_recv.at[slot, piece],
            target,
        )

    def came_along(slot, piece):
        at = pl.ds(piece * piece_rows, piece_rows)
        block = passed.at[slot, at]
        remote(block, block, line_send.at[0, piece], line_recv.at[slot, piece], me).wait_recv()

    def pair_arrived(k, piece):
        at = pl.ds(piece * piece_rows, piece_rows)
        block = paired.at[k, at]
        remote(block, block, pair_send.at[k, piece], pair_recv.at[k, piece], me).wait_recv()

    def hop(k, with_held):
        there = hop_facts(k)[0]
        for piece in range(PIECES):
            first = piece * piece_rows
            pair_arrived(k, piece)
            terms = [paired.at[k], met.at[2 * k + 1]]
            if with_held:
                came_along(there, piece)
                terms.append(passed.at[there])
            add_strips(paired.at[k], first, piece_rows, terms)
            along(k, piece).start()

    def advance(produce):
        @pl.when(step > 0)
        def _():
            meet(step - 1)

        for k in range(LINE - 1):
            held = hop_facts(k)[1]
            if 2 * k + 3 < steps:

                @pl.when((step == 2 * k + 3) & jnp.logical_not(held))
                def _():
                    hop(k, False)

            if 2 * k + 4 < steps:

                @pl.when((step == 2 * k + 4) & held)
                def _():
                    hop(k, True)

        @pl.when(step > 0)
        def _():
            to_sibling(step - 1).wait_send()

        for which in range(2):

            @pl.when(core == which)
            def _():
                produce((1 - which) * rows, part)

        to_sibling(step).start()
        for which in range(2):

            @pl.when(core == which)
            def _():
                produce(which * rows, kept)

    def finish(sum_ref):
        last_hop()
        last_sum(sum_ref)

    def last_hop():
        meet(steps - 1)
        last = LINE - 2

        @pl.when(hop_facts(last)[1])
        def _():
            hop(last, True)

    def last_sum(sum_ref):
        for piece in range(PIECES):
            first = piece * piece_rows
            pair_arrived(LINE - 1, piece)
            add_strips(
                sum_ref, first, piece_rows, [paired.at[LINE - 1], met.at[2 * LINE - 1]]
            )
            for has, slot in ((line > 0, line), (line < LINE - 1, LINE)):

                @pl.when(has)
                def _():
                    came_along(slot, piece)
                    add_strips(sum_ref, first, piece_rows, [sum_ref, passed.at[slot]])

        to_sibling(steps - 1).wait_send()
        for piece in range(PIECES):
            for k in range(LINE):
                to_pair(2 * k, piece).wait_send()
            for k in range(LINE - 1):
                along(k, piece).wait_send()

    return (advance, finish, last_hop, last_sum)


def step_buffers(block):
    return [
        pltpu.VMEM(block, BF),
        pltpu.VMEM(block, BF),
        pltpu.VMEM((2 * LINE,) + block, BF),
        pltpu.VMEM((LINE,) + block, BF),
        pltpu.VMEM((LINE + 1,) + block, BF),
        pltpu.SemaphoreType.DMA((2 * LINE,)),
        pltpu.SemaphoreType.DMA((2 * LINE,)),
        pltpu.SemaphoreType.DMA((LINE, PIECES)),
        pltpu.SemaphoreType.DMA((LINE, PIECES)),
        pltpu.SemaphoreType.DMA((LINE, PIECES)),
        pltpu.SemaphoreType.DMA((LINE + 1, PIECES)),
    ]


def step_tile(i):
    line, pair, _ = place_of(lax.axis_index("expert"))
    there = pick_by(line, FAR_FIRST[LINE - 1])
    for k in range(LINE - 2, -1, -1):
        there = jnp.where(i // 2 == k, pick_by(line, FAR_FIRST[k]), there)
    return there * 2 + jnp.where(lax.rem(i, 2) == 0, 1 - pair, pair)


def taker(refs):
    refs = list(refs)

    def take(number):
        taken = refs[:number]
        del refs[:number]
        return taken

    return take


def scatter_folded(fold, out_ref, buffers, semaphores):
    part, met, paired, passed = buffers
    core_send, core_recv, pair_send, pair_recv, line_send, line_recv = semaphores
    me = lax.axis_index("expert")
    line, pair, core = place_of(me)
    rows = out_ref.shape[0]
    sibling = index_of(line, pair, 1 - core)
    across = index_of(line, 1 - pair, core)
    sent = []

    def send(source, dest, send_at, recv_at, target):
        copy = pltpu.make_async_remote_copy(
            src_ref=source,
            dst_ref=dest,
            send_sem=send_at,
            recv_sem=recv_at,
            device_id={"expert": target},
            device_id_type=MESH,
        )
        copy.start()
        sent.append(copy)

    def await_block(block, recv_at, send_at):
        pltpu.make_async_remote_copy(
            src_ref=block,
            dst_ref=block,
            send_sem=send_at,
            recv_sem=recv_at,
            device_id={"expert": me},
            device_id_type=MESH,
        ).wait_recv()

    dest_line = [pick_by(line, FAR_FIRST[step]) for step in range(LINE)]

    def chip(i):
        return (dest_line[i // 2], (1 - pair) if i % 2 == 0 else pair)

    for i in range(2 * LINE):
        there, other = chip(i)
        fold(index_of(there, other, 1 - core), part.at[i])
        send(part.at[i], met.at[i], core_send.at[i], core_recv.at[i], sibling)
    for i in range(2 * LINE):
        there, other = chip(i)
        await_block(met.at[i], core_recv.at[i], core_send.at[i])
        fold(index_of(there, other, core), paired.at[LINE])
        add_strips(met.at[i], 0, rows, [met.at[i], paired.at[LINE]])
        if i % 2 == 0:
            send(met.at[i], paired.at[i // 2], pair_send.at[i // 2], pair_recv.at[i // 2], across)
    for step in range(LINE - 1):
        there = dest_line[step]
        way = jnp.where(there > line, 1, -1)
        behind = line - way
        held = (behind >= 0) & (behind < LINE)
        target = index_of(line + way, pair, core)
        slot = jnp.where((there == line + way) & (way < 0), LINE, there)
        await_block(paired.at[step], pair_recv.at[step], pair_send.at[step])
        add_strips(paired.at[step], 0, rows, [paired.at[step], met.at[2 * step + 1]])

        @pl.when(held)
        def _():
            await_block(passed.at[there], line_recv.at[there], line_send.at[step])
            add_strips(paired.at[step], 0, rows, [paired.at[step], passed.at[there]])

        send(paired.at[step], passed.at[slot], line_send.at[step], line_recv.at[slot], target)
    step = LINE - 1
    await_block(paired.at[step], pair_recv.at[step], pair_send.at[step])
    add_strips(out_ref, 0, rows, [paired.at[step], met.at[2 * step + 1]])
    for held, slot in ((line > 0, line), (line < LINE - 1, LINE)):

        @pl.when(held)
        def _():
            await_block(passed.at[slot], line_recv.at[slot], line_send.at[0])
            add_strips(out_ref, 0, rows, [out_ref, passed.at[slot]])

    for copy in sent:
        copy.wait_send()


TILE_GROUPS = 4
SCALE = (DN + DR) ** (-0.5)


def half_turn(values):
    lane = lax.broadcasted_iota(jnp.int32, values.shape, 1)
    lower = (lane // (DR // 2)) % 2 == 0
    return jnp.where(lower, pltpu.roll(values, 128 - DR // 2, 1), pltpu.roll(values, DR // 2, 1))


def group_mask(column_ref, row_ref):
    column, row = column_ref[...], row_ref[0]
    shape = (column.shape[0], row.shape[1])
    earlier = lax.broadcasted_iota(jnp.int32, shape, 1) <= lax.broadcasted_iota(
        jnp.int32, shape, 0
    )
    same = (column == row) | ((row % 4 == 0) & (column // 4 == row // 4))
    return earlier & same


def softmax_scores(query, key, mask):
    scores = jnp.where(mask, dot_right(query, key) * SCALE, -1e30)
    powers = jnp.exp(scores - jnp.max(scores, axis=-1, keepdims=True))
    return powers / jnp.sum(powers, axis=-1, keepdims=True)


def attention_forward_kernel(
    spans, x_ref, gain_ref, first_ref, latent_gain_ref, up_ref, trig_ref, column_ref, row_ref,
    output_ref, *refs,
):
    riders = len(spans)
    take = taker(refs)
    sources = [cut_rows(source, rows) for source, rows in zip(take(riders), spans)]
    normed_ref, query_ref, key_ref, value_ref, unit_ref, low_ref, scale_ref, attended_ref = take(8)
    (sum_ref,), targets = take(1), take(riders)
    buffers, semaphores, ride_sems = take(5), take(6), take(2)
    step = pl.program_id(0)

    @pl.when(step == 0)
    def _():
        others = lax.axis_size("dp") - 1 if riders else 0
        greet_dp(others)
        greet(*place_of(lax.axis_index("expert")), others)
        ride(sources, targets, *ride_sems)

    rank = up_ref.shape[0]
    inputs = x_ref[...].astype(F32)
    scale = lax.rsqrt(jnp.mean(inputs * inputs, axis=1, keepdims=True) + EPS)
    normed_ref[...] = (inputs * scale * gain_ref[...]).astype(BF)
    out = dot(normed_ref[...], first_ref[...])
    latent = out[:, DN : DN + rank]
    latent_scale = lax.rsqrt(jnp.mean(latent * latent, axis=1, keepdims=True) + EPS)
    scale_ref[...] = latent_scale
    unit = latent * latent_scale
    unit_ref[...] = unit.astype(BF)
    low_ref[...] = (unit * latent_gain_ref[...]).astype(BF)
    keys_values = dot(low_ref[...], up_ref[...])
    rope = out[:, DN + rank :]
    turned = rope * trig_ref[:, :128] + half_turn(rope) * trig_ref[:, 128:]
    lane = lax.broadcasted_iota(jnp.int32, turned.shape, 1)
    query_ref[:, :DN] = out[:, :DN].astype(BF)
    query_ref[:, DN:] = jnp.where(lane < DR, pltpu.roll(turned, DR, 1), 0.0).astype(BF)
    key_ref[:, :DN] = keys_values[:, :DN].astype(BF)
    key_ref[:, DN:] = jnp.where(lane < DR, turned, 0.0).astype(BF)
    value_ref[...] = keys_values[:, DN:].astype(BF)
    probs = softmax_scores(query_ref[...], key_ref[...], group_mask(column_ref, row_ref))
    attended_ref[...] = dot(probs.astype(BF), value_ref[...]).astype(BF)
    advance, finish, _, _ = step_scatter(step, buffers, semaphores)

    def produce(first, target):
        rows, width = target.shape

        @pl.loop(0, width // COLUMNS)
        def _(tile):
            columns = pl.ds(pl.multiple_of(tile * COLUMNS, COLUMNS), COLUMNS)
            target[:, columns] = dot(
                attended_ref[pl.ds(first, rows)], output_ref[:, columns]
            ).astype(BF)

    advance(produce)

    @pl.when(step == 2 * LINE - 1)
    def _():
        finish(sum_ref)
        for copy in ride(sources, targets, *ride_sems, start=False):
            copy.wait()


def attention_forward(
    x, gain, first_w, latent_gain, up_w, trig, column, row, output_w, riders, collective_id
):
    width, rank = first_w.shape[0], up_w.shape[0]
    span, rows = column.shape[0], row.shape[2]

    def tile(columns):
        return pl.BlockSpec((rows, columns), lambda i: (step_tile(i), 0))

    def fixed(shape):
        return pl.BlockSpec(shape, lambda i: (0, 0), pipeline_mode=pl.Buffered(1))

    anywhere = pl.BlockSpec(memory_space=pl.ANY)
    block = (rows // 2, width)
    carried, others = max(1, len(riders)), max(1, lax.axis_size("dp") - 1)
    outs = (width, 2 * DN, 2 * DN, DV, rank, rank, 1, DV)
    kinds = (BF, BF, BF, BF, BF, BF, F32, BF)
    return pl.pallas_call(
        lambda *refs: attention_forward_kernel([rider[1] for rider in riders], *refs),
        grid=(span // rows,),
        in_specs=[
            tile(width),
            fixed((1, width)),
            fixed(first_w.shape),
            fixed((1, rank)),
            fixed(up_w.shape),
            tile(trig.shape[1]),
            tile(1),
            pl.BlockSpec((1, 1, rows), lambda i: (step_tile(i), 0, 0)),
            fixed(output_w.shape),
        ]
        + [anywhere] * len(riders),
        out_specs=[tile(columns) for columns in outs]
        + [pl.BlockSpec(block, lambda i: (0, 0))]
        + [anywhere] * len(riders),
        out_shape=[jax.ShapeDtypeStruct((span, c), k) for c, k in zip(outs, kinds)]
        + [jax.ShapeDtypeStruct(block, F32)]
        + [landed(rider) for rider in riders],
        scratch_shapes=step_buffers(block)
        + [pltpu.SemaphoreType.DMA((carried, others)) for _ in range(2)],
        compiler_params=pltpu.CompilerParams(
            collective_id=collective_id, has_side_effects=True, vmem_limit_bytes=VMEM_LIMIT
        ),
        name="attention_forward",
    )(
        x, gain[None], first_w, latent_gain[None], up_w, trig, column, row, output_w,
        *[rider[0] for rider in riders],
    )


def attention_backward_kernel(
    latent_piece, small_rows, spans,
    r_ref, output_ref, attended_ref, query_ref, key_ref, value_ref, column_ref, row_ref, trig_ref,
    unit_ref, low_ref, scale_ref, latent_gain_ref, up_ref, normed_ref, first_ref,
    side_ref, gain_ref, down_now_ref, down_parts_ref, *refs,
):
    riders = len(spans)
    take = taker(refs)
    sources = [cut_rows(source, rows) for source, rows in zip(take(riders), spans)]
    (sum_ref, folded_ref, down_ref), (query_out, up_out, output_out) = take(3), take(3)
    own_targets, targets = take(4), take(riders)
    grad_ref, kv_ref, output_grad_ref, up_grad_ref, first_grad_ref, gain_grad_ref = take(6)
    query_full, query_low, up_low, output_low, small_ref, folded_low = take(6)
    fold_buffers, fold_semaphores = take(4), take(6)
    buffers, semaphores, ride_sems, out_sem, own_sems = take(5), take(6), take(2), take(1)[0], take(2)
    step = pl.program_id(0)
    rank = up_ref.shape[0]
    n_d, me_d = lax.axis_size("dp"), lax.axis_index("dp")
    experts = lax.axis_size("expert")

    @pl.when(step == 0)
    def _():
        greet_dp(n_d - 1)
        greet(*place_of(lax.axis_index("expert")), n_d - 1)
        ride(sources, targets, *ride_sems)
        output_grad_ref[...] = jnp.zeros_like(output_grad_ref)
        up_grad_ref[...] = jnp.zeros_like(up_grad_ref)
        first_grad_ref[...] = jnp.zeros_like(first_grad_ref)
        gain_grad_ref[...] = jnp.zeros_like(gain_grad_ref)

    down_total = down_now_ref[...]
    for ahead in range(1, n_d):
        down_total = down_total + down_parts_ref[ahead - 1].astype(F32)
    down_ref[...] = down_total
    attended_grad = dot_right(r_ref[...], output_ref[...]).astype(BF)
    output_grad_ref[...] += dot_left(attended_ref[...], r_ref[...])
    probs = softmax_scores(query_ref[...], key_ref[...], group_mask(column_ref, row_ref))
    kv_ref[:, DN:] = dot_left(probs.astype(BF), attended_grad).astype(BF)
    probs_grad = dot_right(attended_grad, value_ref[...])
    inner = jnp.sum(probs * probs_grad, axis=1, keepdims=True)
    score_grad = (probs * (probs_grad - inner)).astype(BF)
    query_grad = dot(score_grad, key_ref[...]) * SCALE
    key_grad = dot_left(score_grad, query_ref[...]) * SCALE
    kv_ref[:, :DN] = key_grad[:, :DN].astype(BF)
    grad_ref[:, :DN] = query_grad[:, :DN].astype(BF)
    rope = key_grad[:, DN:] + pltpu.roll(query_grad[:, DN:], DR, 1)
    rope = rope * trig_ref[:, :128] + half_turn(rope * trig_ref[:, 128:])
    grad_ref[:, DN + rank :] = rope.astype(BF)
    out_grad = dot_right(kv_ref[...], up_ref[...])
    unit = unit_ref[...].astype(F32)
    gain_grad_ref[...] += jnp.sum(out_grad * unit, axis=0, keepdims=True)
    scaled = out_grad * latent_gain_ref[...]
    inner = jnp.mean(scaled * unit, axis=1, keepdims=True)
    grad_ref[:, DN : DN + rank] = (scale_ref[...] * (scaled - unit * inner)).astype(BF)
    up_grad_ref[...] += dot_left(low_ref[...], kv_ref[...])
    first_grad_ref[...] += dot_left(normed_ref[...], grad_ref[...])
    advance, _, last_hop, last_sum = step_scatter(step, buffers, semaphores)

    def produce(first, target):
        rows, width = target.shape

        @pl.loop(0, width // COLUMNS)
        def _(tile):
            columns = pl.ds(pl.multiple_of(tile * COLUMNS, COLUMNS), COLUMNS)
            target[:, columns] = dot_right(
                grad_ref[pl.ds(first, rows)], first_ref[columns, :]
            ).astype(BF)

    advance(produce)

    def part(array, number, owner):
        size = array.shape[1 if number == 2 else 0] // n_d
        at = pl.ds(pl.multiple_of(owner * size, size), size)
        return array.at[:, at] if number == 2 else array.at[at]

    def own_copies():
        copies = []
        for number, low in enumerate((query_low, up_low, output_low)):
            for ahead in range(1, n_d):
                owner = lax.rem(me_d + ahead, n_d)
                copies.append((part(low, number, owner), number, ahead))
        for ahead in range(1, n_d):
            copies.append((folded_low, 3, ahead))
        return [
            pltpu.make_async_remote_copy(
                src_ref=source,
                dst_ref=own_targets[number].at[ahead - 1],
                send_sem=own_sems[0].at[number, ahead - 1],
                recv_sem=own_sems[1].at[number, ahead - 1],
                device_id={"dp": lax.rem(me_d + ahead, n_d)},
                device_id_type=MESH,
            )
            for source, number, ahead in copies
        ]

    @pl.when(step == 2 * LINE - 1)
    def _():
        last = DN + rank
        strip = 256

        @pl.loop(0, first_grad_ref.shape[0] // strip)
        def _(tile):
            first = pl.multiple_of(tile * strip, strip)
            at = pl.ds(first, strip)
            sums = first_grad_ref[at]
            rope = sums[:, last:]
            query_full[at, :DN] = sums[:, :DN]
            query_full[at, DN:] = pltpu.roll(rope, DR, 1)
            query_low[at, :DN] = sums[:, :DN].astype(BF)
            query_low[at, DN:] = pltpu.roll(rope, DR, 1).astype(BF)
            small_ref[at, :rank] = sums[:, DN:last].astype(BF)
            gain_sum = jnp.sum(sums * first_ref[at].astype(F32), axis=1, keepdims=True)
            gain_sum = gain_sum / gain_ref[at]
            row = lax.broadcasted_iota(jnp.int32, (strip, rank), 0) + first
            index = lax.broadcasted_iota(jnp.int32, (strip, rank), 1)
            place = (index // latent_piece) * small_rows + index % latent_piece
            latent_sum = jnp.sum(
                jnp.where(row == place, gain_grad_ref[...], 0.0), axis=1, keepdims=True
            )
            lane = lax.broadcasted_iota(jnp.int32, rope.shape, 1)
            mixed = jnp.where(lane < DR, rope, side_ref[at].astype(F32))
            mixed = jnp.where(lane == DR + experts + 1, gain_sum, mixed)
            mixed = jnp.where(lane == DR + experts + 2, latent_sum, mixed)
            small_ref[at, rank:] = mixed.astype(BF)

        up_low[...] = up_grad_ref[...].astype(BF)
        output_low[...] = output_grad_ref[...].astype(BF)
        outs = [
            pltpu.make_async_copy(query_full, query_out, out_sem.at[0]),
            pltpu.make_async_copy(up_grad_ref, up_out, out_sem.at[1]),
            pltpu.make_async_copy(output_grad_ref, output_out, out_sem.at[2]),
        ]
        for copy in outs:
            copy.start()
        moves = own_copies()
        for copy in moves[: 3 * (n_d - 1)]:
            copy.start()

        def fold(dest, target):
            wide = small_ref.shape[1]
            total = folded_ref.shape[0] // STRIP
            target[...] = jnp.zeros(target.shape, BF)
            for unit in range(n_d * small_rows // STRIP):
                owner, first = (unit * STRIP) // small_rows, (unit * STRIP) % small_rows
                start = pl.multiple_of((owner * experts + dest) * small_rows + first, STRIP)
                target[
                    (unit % total) * STRIP : (unit % total + 1) * STRIP,
                    (unit // total) * wide : (unit // total + 1) * wide,
                ] = small_ref[pl.ds(start, STRIP)]

        last_hop()
        scatter_folded(fold, folded_ref, fold_buffers, fold_semaphores)
        folded_low[...] = folded_ref[...].astype(BF)
        for copy in moves[3 * (n_d - 1) :]:
            copy.start()
        last_sum(sum_ref)
        for copy in moves + outs:
            copy.wait()
        for copy in ride(sources, targets, *ride_sems, start=False):
            copy.wait()


def attention_backward(
    residual_all, output_w, stored, column, row, trig, latent_gain, up_w, first_w, side, gain,
    latent_piece, small_rows, down_now, down_parts, riders, collective_id,
):
    normed, query, key, value, unit, low, scale, attended = stored
    width, rank = residual_all.shape[1], up_w.shape[0]
    rows = row.shape[2]
    n_d = lax.axis_size("dp")
    first_width = 2 * DN + rank
    block = (rows // 2, width)
    folded = (EXTRA_ROWS, width)
    small = (width, rank + 128)
    down_block = (down_now.shape[0] // (2 * LINE), down_now.shape[1])

    def tile(columns):
        return pl.BlockSpec((rows, columns), lambda i: (step_tile(i), 0))

    def fixed(shape):
        return pl.BlockSpec(shape, lambda i: (0, 0), pipeline_mode=pl.Buffered(1))

    anywhere = pl.BlockSpec(memory_space=pl.ANY)
    carried, others = max(1, len(riders)), max(1, n_d - 1)
    query_shape, up_shape, output_shape = (width, 2 * DN), up_w.shape, output_w.shape
    to_others = [
        (n_d - 1, query_shape[0] // n_d, query_shape[1]),
        (n_d - 1, up_shape[0] // n_d, up_shape[1]),
        (n_d - 1, output_shape[0], output_shape[1] // n_d),
        (n_d - 1,) + folded,
    ]
    return pl.pallas_call(
        lambda *refs: attention_backward_kernel(
            latent_piece, small_rows, [rider[1] for rider in riders], *refs
        ),
        grid=(2 * LINE,),
        in_specs=[
            tile(width),
            fixed(output_w.shape),
            tile(DV),
            tile(2 * DN),
            tile(2 * DN),
            tile(DV),
            tile(1),
            pl.BlockSpec((1, 1, rows), lambda i: (step_tile(i), 0, 0)),
            tile(trig.shape[1]),
            tile(rank),
            tile(rank),
            tile(1),
            fixed((1, rank)),
            fixed(up_w.shape),
            tile(width),
            fixed(first_w.shape),
            fixed(side.shape),
            fixed((width, 1)),
            pl.BlockSpec(down_block, lambda i: (i, 0)),
            pl.BlockSpec((n_d - 1,) + down_block, lambda i: (0, i, 0)),
        ]
        + [anywhere] * len(riders),
        out_specs=[
            pl.BlockSpec(block, lambda i: (0, 0)),
            pl.BlockSpec(folded, lambda i: (0, 0)),
            pl.BlockSpec(down_block, lambda i: (i, 0)),
        ]
        + [anywhere] * (7 + len(riders)),
        out_shape=[
            jax.ShapeDtypeStruct(shape, F32)
            for shape in (block, folded, down_now.shape, query_shape, up_shape, output_shape)
        ]
        + [jax.ShapeDtypeStruct(shape, BF) for shape in to_others]
        + [landed(rider) for rider in riders],
        scratch_shapes=[
            pltpu.VMEM((rows, first_width), BF),
            pltpu.VMEM((rows, DN + DV), BF),
            pltpu.VMEM(output_shape, F32),
            pltpu.VMEM(up_shape, F32),
            pltpu.VMEM((width, first_width), F32),
            pltpu.VMEM((1, rank), F32),
            pltpu.VMEM(query_shape, F32),
            pltpu.VMEM(query_shape, BF),
            pltpu.VMEM(up_shape, BF),
            pltpu.VMEM(output_shape, BF),
            pltpu.VMEM(small, BF),
            pltpu.VMEM(folded, BF),
            pltpu.VMEM((2 * LINE,) + folded, BF),
            pltpu.VMEM((2 * LINE,) + folded, BF),
            pltpu.VMEM((LINE + 1,) + folded, BF),
            pltpu.VMEM((LINE + 1,) + folded, BF),
            pltpu.SemaphoreType.DMA((2 * LINE,)),
            pltpu.SemaphoreType.DMA((2 * LINE,)),
            pltpu.SemaphoreType.DMA((LINE,)),
            pltpu.SemaphoreType.DMA((LINE,)),
            pltpu.SemaphoreType.DMA((LINE,)),
            pltpu.SemaphoreType.DMA((LINE + 1,)),
        ]
        + step_buffers(block)
        + [pltpu.SemaphoreType.DMA((carried, others)) for _ in range(2)]
        + [pltpu.SemaphoreType.DMA((3,))]
        + [pltpu.SemaphoreType.DMA((4, others)) for _ in range(2)],
        compiler_params=pltpu.CompilerParams(
            collective_id=collective_id, has_side_effects=True, vmem_limit_bytes=VMEM_LIMIT
        ),
        name="attention_backward",
    )(
        residual_all, output_w, attended, query, key, value, column, row, trig,
        unit, low, scale, latent_gain[None], up_w, normed, first_w, side,
        gain[:, None], down_now, down_parts, *[rider[0] for rider in riders],
    )


HIDDEN = 256
ROUTER_AT = 448


def logistic(values):
    return 0.5 * jnp.tanh(0.5 * values) + 0.5


def expert_layer_kernel(
    splits,
    ffn_ref, y_ref, code_row_ref, code_column_ref, wide_ref, shared_down_ref, *refs,
):
    take = taker(refs)
    own_weights, came = take(3), take(len(splits))
    (
        rows_ref, ups_ref, scaled_ref, gate_ref, up_ref, mixed_ref,
        down_grad_out, wide_grad_out, sum_ref,
    ) = take(9)
    (
        gate_w_ref, up_w_ref, down_w_ref, load_sem, out_sem, down_grad_ref, wide_grad_ref,
        grad_ref, left_ref, inner_ref, returned_ref, slot_gate_ref, slot_dot_ref,
        part, kept, met, paired, passed,
        core_send, core_recv, pair_send, pair_recv, line_send, line_recv,
    ) = take(24)
    step = pl.program_id(0)
    me = lax.axis_index("expert")
    experts = lax.axis_size("expert")
    line, pair, core = place_of(me)
    me_d, n_d = lax.axis_index("dp"), lax.axis_size("dp")
    groups, _, per = code_row_ref.shape
    slots = rows_ref.shape[0] // groups
    width = ffn_ref.shape[1]
    hidden = gate_w_ref.shape[1]

    wholes = (gate_w_ref, up_w_ref, down_w_ref)
    loads = []

    def load(source, number, owner, start, count):
        axis = 1 if number == 2 else 0
        size = own_weights[number].shape[axis]
        at = pl.multiple_of(owner * size, size)
        if axis == 0:
            place = wholes[number].at[pl.ds(at + start, count)]
        else:
            place = wholes[number].at[:, pl.ds(at, size)]
        loads.append(pltpu.make_async_copy(source, place, load_sem.at[len(loads)]))

    for number in range(3):
        load(own_weights[number], number, me_d, 0, own_weights[number].shape[0])
    for source, (number, first, end) in zip(came, splits):
        for ahead in range(1, n_d):
            owner = lax.rem(me_d - ahead + n_d, n_d)
            load(source.at[ahead - 1], number, owner, first, end - first)

    @pl.when(step == 0)
    def _():
        for copy in loads:
            copy.start()
        greet(line, pair, core)
        down_grad_ref[...] = jnp.zeros_like(down_grad_ref)
        wide_grad_ref[...] = jnp.zeros_like(wide_grad_ref)

    out = dot(ffn_ref[...], wide_ref[...])
    gates, ups = out[:, :HIDDEN], out[:, HIDDEN:]
    last = out[:, 2 * HIDDEN - 128 :]
    lane = lax.broadcasted_iota(jnp.int32, last.shape, 1)
    first_lane = ROUTER_AT - (2 * HIDDEN - 128)
    logits = jnp.where((lane >= first_lane) & (lane < first_lane + experts), last, -1e30)
    powers = jnp.exp(logits - jnp.max(logits, axis=1, keepdims=True))
    probs = powers / jnp.sum(powers, axis=1, keepdims=True)
    own_lane = (lane == first_lane + me).astype(F32)
    own_probs = jnp.sum(probs * own_lane, axis=1, keepdims=True)
    sigmoid = logistic(gates)
    silu = gates * sigmoid
    shared_low = (silu * ups).astype(BF)
    back = dot_right(y_ref[...], shared_down_ref[...])
    left_ref[:, :HIDDEN] = (back * ups * sigmoid * (1.0 + gates * (1.0 - sigmoid))).astype(BF)
    shared_up_low = back * silu
    left_ref[:, HIDDEN : 2 * HIDDEN - 128] = shared_up_low[:, : HIDDEN - 128].astype(BF)
    shared_last = shared_up_low[:, HIDDEN - 128 :]
    down_grad_ref[...] += dot_left(shared_low, y_ref[...])

    square = (per, per)
    diagonal = lax.broadcasted_iota(jnp.int32, square, 0) == lax.broadcasted_iota(
        jnp.int32, square, 1
    )
    for group in range(groups):
        tokens_at = pl.ds(group * per, per)
        slots_at = pl.ds(group * slots, slots)
        slot_ids = lax.broadcasted_iota(jnp.int32, (slots, per), 0)
        picks = slot_ids == code_row_ref[group]
        picks_low = picks.astype(F32).astype(BF)
        rows_ref[slots_at] = dot(picks_low, ffn_ref[tokens_at]).astype(BF)
        ups_ref[slots_at] = dot(picks_low, y_ref[tokens_at]).astype(BF)
        own_column = own_probs[group * per : (group + 1) * per]
        own_row = jnp.sum(jnp.where(diagonal, own_column, 0.0), axis=0, keepdims=True)
        slot_gate_ref[slots_at] = jnp.sum(
            jnp.where(picks, own_row, 0.0), axis=1, keepdims=True
        )
    slot_dot_ref[...] = jnp.zeros_like(slot_dot_ref)

    @pl.when(step == 0)
    def _():
        for copy in loads:
            copy.wait()

    def hidden_part(columns):
        gate_part = dot(rows_ref[...], gate_w_ref[:, columns])
        up_part = dot(rows_ref[...], up_w_ref[:, columns])
        raw = dot_right(ups_ref[...], down_w_ref[columns, :])
        slot_gate = slot_gate_ref[...]
        sigmoid = logistic(gate_part)
        silu = gate_part * sigmoid
        inner = silu * up_part
        slot_dot_ref[...] += jnp.sum(inner * raw, axis=1, keepdims=True)
        grad = raw * slot_gate
        inner_ref[:, columns] = inner.astype(BF)
        scaled_ref[:, columns] = (inner * slot_gate).astype(BF)
        gate_ref[:, columns] = (
            grad * up_part * sigmoid * (1.0 + gate_part * (1.0 - sigmoid))
        ).astype(BF)
        up_ref[:, columns] = (grad * silu).astype(BF)

    for first in range(0, hidden, HIDDEN):
        hidden_part(pl.ds(first, min(HIDDEN, hidden - first)))

    @pl.loop(0, width // COLUMNS)
    def _(tile):
        columns = pl.ds(pl.multiple_of(tile * COLUMNS, COLUMNS), COLUMNS)
        returned_ref[:, columns] = dot(inner_ref[...], down_w_ref[:, columns]).astype(BF)
        grad_ref[:, columns] = (
            dot_right(gate_ref[...], gate_w_ref[columns, :])
            + dot_right(up_ref[...], up_w_ref[columns, :])
        ).astype(BF)

    for group in range(groups):
        tokens_at = pl.ds(group * per, per)
        slots_at = pl.ds(group * slots, slots)
        own_column = own_probs[group * per : (group + 1) * per]
        slot_lane = lax.broadcasted_iota(jnp.int32, (per, slots), 1)
        picks = slot_lane == code_column_ref[tokens_at]
        pick_gate = jnp.where(picks, own_column, 0.0).astype(BF)
        mixed_ref[tokens_at] = (
            dot(shared_low[group * per : (group + 1) * per], shared_down_ref[...])
            + dot(pick_gate, returned_ref[slots_at])
        ).astype(BF)
        small = (slots, slots)
        eye = lax.broadcasted_iota(jnp.int32, small, 0) == lax.broadcasted_iota(
            jnp.int32, small, 1
        )
        dot_row = jnp.sum(jnp.where(eye, slot_dot_ref[slots_at], 0.0), axis=0, keepdims=True)
        row_dot = jnp.sum(jnp.where(picks, dot_row, 0.0), axis=1, keepdims=True)
        at = slice(group * per, (group + 1) * per)
        logit_grad = row_dot * own_column * (own_lane[at] - probs[at])
        high = logit_grad.astype(BF)
        rest = logit_grad - high.astype(F32)
        left_ref[tokens_at, 2 * HIDDEN - 128 :] = jnp.where(
            lane[at] < first_lane,
            shared_last[at],
            high.astype(F32) + pltpu.roll(rest, experts, 1),
        ).astype(BF)
    wide_grad_ref[...] += dot_left(ffn_ref[...], left_ref[...])

    advance, finish, _, _ = step_scatter(
        step, (part, kept, met, paired, passed),
        (core_send, core_recv, pair_send, pair_recv, line_send, line_recv),
    )
    rows = kept.shape[0]

    def produce(first, target):
        @pl.loop(0, width // COLUMNS)
        def _(tile):
            columns = pl.ds(pl.multiple_of(tile * COLUMNS, COLUMNS), COLUMNS)
            total = dot_right(left_ref[pl.ds(first, rows)], wide_ref[columns, :])
            for k in range(rows // per):
                group = first // per + k
                slot_lane = lax.broadcasted_iota(jnp.int32, (per, slots), 1)
                picks = slot_lane == code_column_ref[pl.ds(first + k * per, per)]
                scattered = dot(
                    picks.astype(F32).astype(BF),
                    grad_ref[pl.ds(group * slots, slots), columns],
                )
                target[pl.ds(k * per, per), columns] = (
                    total[k * per : (k + 1) * per] + scattered
                ).astype(BF)

    advance(produce)

    @pl.when(step == 2 * LINE - 1)
    def _():
        outs = [
            pltpu.make_async_copy(down_grad_ref, down_grad_out, out_sem.at[0]),
            pltpu.make_async_copy(wide_grad_ref, wide_grad_out, out_sem.at[1]),
        ]
        for copy in outs:
            copy.start()
        finish(sum_ref)
        for copy in outs:
            copy.wait()


def expert_layer(
    ffn_all, upstream_all, code, slots, wide, shared_down, weights, came, splits, collective_id
):
    groups, per = code.shape
    span, width = ffn_all.shape
    gate_w, up_w, down_w = weights
    hidden = gate_w.shape[1]
    n_d = lax.axis_size("dp")
    rows, slot_rows = TILE_GROUPS * per, TILE_GROUPS * slots
    total = groups * slots
    steps = 2 * LINE
    block = (rows // 2, width)

    def tile(count, columns):
        return pl.BlockSpec((count, columns), lambda i: (step_tile(i), 0))

    def fixed(shape):
        return pl.BlockSpec(shape, lambda i: (0, 0), pipeline_mode=pl.Buffered(1))

    anywhere = pl.BlockSpec(memory_space=pl.ANY)
    outs = [(total, width)] * 2 + [(total, hidden)] * 3 + [(span, width)]
    sums = [shared_down.shape, wide.shape]
    copies = 3 + len(came) * (n_d - 1)
    return pl.pallas_call(
        lambda *refs: expert_layer_kernel(splits, *refs),
        grid=(steps,),
        in_specs=[
            tile(rows, width),
            tile(rows, width),
            pl.BlockSpec((TILE_GROUPS, 1, per), lambda i: (step_tile(i), 0, 0)),
            tile(rows, 1),
            fixed(wide.shape),
            fixed(shared_down.shape),
        ]
        + [anywhere] * (3 + len(came)),
        out_specs=[
            tile(slot_rows if shape[0] == total else rows, shape[1]) for shape in outs
        ]
        + [anywhere] * 2
        + [pl.BlockSpec(block, lambda i: (0, 0))],
        out_shape=[jax.ShapeDtypeStruct(shape, BF) for shape in outs]
        + [jax.ShapeDtypeStruct(shape, F32) for shape in sums]
        + [jax.ShapeDtypeStruct(block, BF)],
        scratch_shapes=[
            pltpu.VMEM((gate_w.shape[0] * n_d, hidden), BF),
            pltpu.VMEM((up_w.shape[0] * n_d, hidden), BF),
            pltpu.VMEM((hidden, down_w.shape[1] * n_d), BF),
            pltpu.SemaphoreType.DMA((copies,)),
            pltpu.SemaphoreType.DMA((2,)),
            pltpu.VMEM(shared_down.shape, F32),
            pltpu.VMEM(wide.shape, F32),
            pltpu.VMEM((slot_rows, width), BF),
            pltpu.VMEM((rows, 2 * HIDDEN), BF),
            pltpu.VMEM((slot_rows, hidden), BF),
            pltpu.VMEM((slot_rows, width), BF),
            pltpu.VMEM((slot_rows, 1), F32),
            pltpu.VMEM((slot_rows, 1), F32),
        ]
        + step_buffers(block),
        compiler_params=pltpu.CompilerParams(
            collective_id=collective_id,
            has_side_effects=True,
            vmem_limit_bytes=63 * 1024 * 1024,
        ),
        name="expert_layer",
    )(
        ffn_all, upstream_all, code[:, None, :], code.reshape(span, 1), wide, shared_down,
        gate_w, up_w, down_w, *came,
    )


def on_device(
    tokens,
    segment,
    routes,
    drop_order,
    cotangent,
    attn_gain,
    query_weight,
    down_latent,
    latent_gain,
    up_latent,
    output_weight,
    ffn_gain,
    router_weight,
    shared_gate,
    shared_up,
    shared_down,
    expert_gate,
    expert_up,
    expert_down,
):
    n_e = lax.axis_size("expert")
    n_d = lax.axis_size("dp")
    me_e = lax.axis_index("expert")
    me_d = lax.axis_index("dp")
    micro, group_rows, width = tokens.shape
    own_rows = micro * group_rows
    span = n_e * own_rows
    groups = n_e * micro
    top = routes.shape[2]
    experts = n_e * expert_gate.shape[0]
    capacity = (5 * group_rows * top + 4 * experts - 1) // (4 * experts)
    slots = -(-capacity // 16) * 16
    rank_latent = latent_gain.shape[0] * n_e * n_d

    def gather(values):
        return lax.all_gather(values, "expert", axis=0, tiled=True)

    def scatter(values):
        return lax.psum_scatter(values, "expert", scatter_dimension=0, tiled=True)

    def whole(own, parts, axis):
        blocks = [own] + [parts[step - 1] for step in range(1, n_d)]
        ordered = [
            lax.select_n(lax.rem(me_d - owner + n_d, n_d), *blocks) for owner in range(n_d)
        ]
        return jnp.concatenate(ordered, axis=axis)

    def split_dp(values, axis):
        size = values.shape[axis] // n_d
        parts = []
        for step in range(n_d):
            at = lax.rem(me_d + step, n_d) * size
            parts.append(lax.dynamic_slice_in_dim(values, at, size, axis))
        return (stack([part.astype(BF) for part in parts[1:]]), parts[0])

    def stack(parts):
        return parts[0][None] if len(parts) == 1 else jnp.stack(parts)

    def add_all(total, parts):
        for step in range(n_d - 1):
            total = total + parts[step].astype(F32)
        return total

    small_rows = attn_gain.shape[0]
    latent_all_width = down_latent.shape[1]
    latent_piece = latent_gain.shape[0]
    packed = jnp.concatenate(
        [
            down_latent,
            router_weight,
            attn_gain[:, None],
            ffn_gain[:, None],
            jnp.pad(latent_gain, (0, small_rows - latent_piece))[:, None],
        ],
        axis=1,
    )
    packed = lax.all_gather(packed, ("dp", "expert"), axis=0, tiled=True)
    down_all = packed[:, :latent_all_width]
    router_all = packed[:, latent_all_width : latent_all_width + experts]
    rest = packed[:, latent_all_width + experts :].astype(F32)
    attn_gain_all = rest[:, 0]
    ffn_gain_all = rest[:, 1]
    latent_gain_all = rest[:, 2].reshape(n_e * n_d, small_rows)[:, :latent_piece].reshape(-1)

    chosen = jnp.sum(
        (routes[..., None] == jnp.arange(experts, dtype=jnp.int32)).astype(jnp.int32), axis=2
    )
    order = drop_order[:, 0]
    earlier = (order[:, None, :] < order[:, :, None]).astype(F32)
    rank = jnp.einsum("mtu,mue->mte", earlier, chosen.astype(F32)).astype(jnp.int32)
    code = jnp.where((chosen == 1) & (rank < capacity), rank, -1).reshape(own_rows, experts)

    tokens_own = tokens.reshape(own_rows, width)
    code_lanes = -(-experts // 128) * 128
    code_low = jnp.pad(code.astype(BF), ((0, 0), (0, code_lanes - experts)))
    own_gate, own_up, own_down = expert_gate[0], expert_up[0], expert_down[0]
    gate_first = own_gate.shape[0] * 3 // 8
    up_most = own_up.shape[0] * 7 // 8
    dense = (query_weight, up_latent, output_weight, shared_gate, shared_up, shared_down)
    came = gather_rows(
        jnp.concatenate([tokens_own, code_low], axis=1),
        5,
        riders=[(array, (0, array.shape[0])) for array in dense] + [(own_gate, (0, gate_first))],
    )
    tokens_all, gate_came = came[0], came[7]
    query_w, up_w, output_w, shared_gate_w, shared_up_w, shared_down_w = [
        whole(own, parts, axis)
        for own, parts, axis in zip(dense, came[1:7], (0, 0, 1, 0, 0, 1))
    ]
    upstream_own = cotangent.reshape(own_rows, width)
    upstream_later, tokens_all = lax.optimization_barrier((upstream_own, tokens_all))
    upstream_all = gather(upstream_later)
    code_all = tokens_all[:, width : width + experts].astype(jnp.int32)
    my_code = lax.dynamic_slice_in_dim(code_all, me_e, 1, 1).reshape(groups, group_rows)

    span_segment = (
        segment.reshape(micro, n_e, group_rows).transpose(1, 0, 2).reshape(groups, group_rows)
    )
    trig = angles(positions(span_segment), group_rows)
    marks = span_segment + 4 * jnp.arange(groups, dtype=jnp.int32)[:, None]
    column = marks.reshape(span, 1)
    row = marks.reshape(groups // TILE_GROUPS, 1, TILE_GROUPS * group_rows)
    first_w = jnp.concatenate(
        [
            query_w[:, :DN],
            down_all[:, :rank_latent],
            down_all[:, rank_latent:],
            query_w[:, DN:],
        ],
        axis=1,
    )
    came = attention_forward(
        tokens_all,
        attn_gain_all,
        first_w,
        latent_gain_all,
        up_w,
        trig,
        column,
        row,
        output_w,
        [(own_gate, (gate_first, own_gate.shape[0])), (own_up, (0, up_most))],
        2,
    )
    stored, attention_out, gate_came_last, up_came = came[:8], came[8], came[9], came[10]
    residual = tokens_own.astype(F32) + attention_out

    second_scale = rms_scale(residual)
    ffn_in = (residual * second_scale * ffn_gain_all).astype(BF)
    ffn_all, up_came_last, down_came = gather_rows(
        ffn_in,
        1,
        riders=[(own_up, (up_most, own_up.shape[0])), (own_down, (0, own_down.shape[0]))],
    )

    shared_hidden = shared_gate_w.shape[1]
    wide = jnp.concatenate(
        [
            jnp.pad(shared_gate_w, ((0, 0), (0, HIDDEN - shared_hidden))),
            jnp.pad(shared_up_w, ((0, 0), (0, ROUTER_AT - HIDDEN - shared_hidden))),
            router_all,
            jnp.pad(router_all, ((0, 0), (0, 2 * HIDDEN - ROUTER_AT - 2 * experts))),
        ],
        axis=1,
    )
    (
        expert_rows,
        slot_up,
        inner_scaled,
        gate_low,
        up_low,
        mixed_part,
        shared_down_grad,
        wide_grad,
        ffn_grad,
    ) = expert_layer(
        ffn_all,
        upstream_all,
        my_code,
        slots,
        wide,
        jnp.pad(shared_down_w, ((0, HIDDEN - shared_hidden), (0, 0))),
        (own_gate, own_up, own_down),
        (gate_came, gate_came_last, up_came, up_came_last, down_came),
        (
            (0, 0, gate_first),
            (0, gate_first, own_gate.shape[0]),
            (1, 0, up_most),
            (1, up_most, own_up.shape[0]),
            (2, 0, own_down.shape[0]),
        ),
        3,
    )
    ffn_grad = ffn_grad.astype(F32)
    mixed = residual + scatter(mixed_part).astype(F32)
    router_grad = (
        wide_grad[:, ROUTER_AT : ROUTER_AT + experts]
        + wide_grad[:, ROUTER_AT + experts : ROUTER_AT + 2 * experts]
    )
    shared_down_later, shared_down_now = split_dp(shared_down_grad[:shared_hidden], 1)
    shared_gate_later, shared_gate_now = split_dp(wide_grad[:, :shared_hidden], 0)
    shared_up_later, shared_up_now = split_dp(wide_grad[:, HIDDEN : HIDDEN + shared_hidden], 0)
    residual_part, ffn_gain_grad = norm_back(residual, second_scale, ffn_gain_all, ffn_grad)
    residual_grad = upstream_own.astype(F32) + residual_part
    (
        residual_all,
        shared_down_parts,
        shared_gate_parts,
        shared_up_parts,
        down_now,
        gate_now,
        up_now,
        down_parts,
        gate_parts_first,
        gate_later,
        up_later,
    ) = gather_rows(
        residual_grad.astype(BF),
        6,
        riders=[
            (later, None) for later in (shared_down_later, shared_gate_later, shared_up_later)
        ],
        products=(expert_rows, slot_up, inner_scaled, gate_low, up_low),
    )

    side = jnp.concatenate(
        [
            jnp.zeros((width, DR), F32),
            router_grad,
            ffn_gain_grad[:, None],
            jnp.zeros((width, 128 - DR - experts - 1), F32),
        ],
        axis=1,
    ).astype(BF)
    (
        normed_grad,
        folded,
        down_grad,
        query_full,
        up_latent_full,
        output_full,
        query_parts,
        latent_parts,
        output_parts,
        folded_parts,
        gate_parts_last,
        up_parts,
    ) = attention_backward(
        residual_all,
        output_w,
        stored,
        column,
        row,
        trig,
        latent_gain_all,
        up_w,
        first_w,
        side,
        attn_gain_all,
        latent_piece,
        small_rows,
        down_now,
        down_parts,
        [(gate_later, None), (up_later, None)],
        4,
    )

    def own_part(values, axis):
        size = values.shape[axis] // n_d
        return lax.dynamic_slice_in_dim(values, me_d * size, size, axis)

    query_grad = add_all(own_part(query_full, 0), query_parts)[:, : DN + DR]
    up_latent_grad = add_all(own_part(up_latent_full, 0), latent_parts)
    output_grad = add_all(own_part(output_full, 1), output_parts)
    small_width = rank_latent + 128
    folded = add_all(folded, folded_parts)
    small = jnp.concatenate(
        [folded[:, k * small_width : (k + 1) * small_width] for k in range(width // small_width)],
        axis=0,
    )
    small = lax.dynamic_slice_in_dim(small, me_d * small_rows, small_rows, 0)
    own_inputs = tokens_own.astype(F32)
    input_part, _ = norm_back(own_inputs, rms_scale(own_inputs), attn_gain_all, normed_grad)
    tokens_grad = residual_grad + input_part
    last = latent_all_width + experts
    shape = (micro, group_rows, width)
    return (
        mixed.reshape(shape),
        tokens_grad.reshape(shape),
        small[:, last + 1],
        query_grad,
        small[:, :latent_all_width],
        small[:latent_piece, last + 2],
        up_latent_grad,
        output_grad,
        small[:, last],
        small[:, latent_all_width:last],
        add_all(shared_gate_now, shared_gate_parts),
        add_all(shared_up_now, shared_up_parts),
        add_all(shared_down_now, shared_down_parts),
        add_all(gate_now, jnp.concatenate([gate_parts_first, gate_parts_last], axis=1))[None],
        add_all(up_now, up_parts)[None],
        down_grad[None],
    )


def solution(mesh):
    rows = P(None, ("dp", "expert"), None)
    split = P(("dp", "expert"))
    split_rows = P(("dp", "expert"), None)
    columns = P("dp", "expert")
    turned = P("expert", "dp")
    expert_in = P("expert", "dp", None)
    expert_out = P("expert", None, "dp")
    return jax.shard_map(
        on_device,
        mesh=mesh,
        in_specs=(
            rows,
            P(None, "dp"),
            rows,
            rows,
            rows,
            split,
            columns,
            split_rows,
            split,
            columns,
            turned,
            split,
            split_rows,
            columns,
            columns,
            turned,
            expert_in,
            expert_in,
            expert_out,
        ),
        out_specs=(
            rows,
            rows,
            split,
            columns,
            split_rows,
            split,
            columns,
            turned,
            split,
            split_rows,
            columns,
            columns,
            turned,
            expert_in,
            expert_in,
            expert_out,
        ),
        check_vma=False,
    )
```
